32 devices in a mesh: grp: 2 (over core), dp: 16 (over z, y, x).
Axes of the slice: x: 2, y: 2, z: 4, core: 2. Of those that a mesh axis runs over, the one named last changes fastest.
Arguments:
- tokens: bfloat16 [2, 25216, 768], P('grp', 'dp'), may hold values from -6 to 6
- frame_video: int32 [128], replicated, may hold values from 0 to 31, as said below
- caption_video: int32 [624], P('dp'), may hold values from 0 to 31, as said below
- caption_len: int32 [16, 39], P('dp'), may hold values from 1 to 77, 1576 in all within a row
- attn_norm_gain: float32 [2, 768], P('grp'), may hold values from 0.5 to 1.5
- attn_norm_shift: float32 [2, 768], P('grp'), may hold values from -1.5 to 1.5
- qkv_weight: bfloat16 [2, 768, 2304], P('grp'), may hold values from -0.21875 to 0.21875
- query_value_bias: float32 [2, 1536], P('grp'), may hold values from -1.5 to 1.5
- proj_weight: bfloat16 [2, 768, 768], P('grp'), may hold values from -0.875 to 0.875
- proj_bias: float32 [2, 768], P('grp'), may hold values from -1.5 to 1.5
- mlp_norm_gain: float32 [2, 768], P('grp'), may hold values from 0.5 to 1.5
- mlp_norm_shift: float32 [2, 768], P('grp'), may hold values from -1.5 to 1.5
- fc_in_weight: bfloat16 [2, 768, 3072], P('grp'), may hold values from -0.21875 to 0.21875
- fc_in_bias: float32 [2, 3072], P('grp'), may hold values from -1.5 to 1.5
- fc_out_weight: bfloat16 [2, 3072, 768], P('grp'), may hold values from -0.21875 to 0.21875
- fc_out_bias: float32 [2, 768], P('grp'), may hold values from -1.5 to 1.5
- side_in_weight: bfloat16 [2, 768, 768], P('grp'), may hold values from -0.21875 to 0.21875
- side_in_bias: float32 [2, 768], P('grp'), may hold values from -1.5 to 1.5
- side_norm_gain: float32 [2, 768], P('grp'), may hold values from 0.5 to 1.5
- side_norm_shift: float32 [2, 768], P('grp'), may hold values from -1.5 to 1.5
- side_qkv_weight: bfloat16 [2, 768, 2304], P('grp'), may hold values from -0.21875 to 0.21875
- side_out_weight: bfloat16 [2, 768, 768], P('grp'), may hold values from -0.4375 to 0.4375
- cotangent: bfloat16 [2, 25216, 768], P('grp', 'dp'), may hold values from -6 to 6
Outputs:
- out: bfloat16 [2, 25216, 768], P('grp', 'dp')
- grad_tokens: float32 [2, 25216, 768], P('grp', 'dp')
- grad_attn_norm_gain: float32 [2, 768], P('grp', 'dp')
- grad_attn_norm_shift: float32 [2, 768], P('grp', 'dp')
- grad_qkv_weight: float32 [2, 768, 2304], P('grp', 'dp')
- grad_query_value_bias: float32 [2, 1536], P('grp', 'dp')
- grad_proj_weight: float32 [2, 768, 768], P('grp', 'dp')
- grad_proj_bias: float32 [2, 768], P('grp', 'dp')
- grad_mlp_norm_gain: float32 [2, 768], P('grp', 'dp')
- grad_mlp_norm_shift: float32 [2, 768], P('grp', 'dp')
- grad_fc_in_weight: float32 [2, 768, 3072], P('grp', 'dp')
- grad_fc_in_bias: float32 [2, 3072], P('grp', 'dp')
- grad_fc_out_weight: float32 [2, 3072, 768], P('grp', 'dp')
- grad_fc_out_bias: float32 [2, 768], P('grp', 'dp')
- grad_side_in_weight: float32 [2, 768, 768], P('grp', 'dp')
- grad_side_in_bias: float32 [2, 768], P('grp', 'dp')
- grad_side_norm_gain: float32 [2, 768], P('grp', 'dp')
- grad_side_norm_shift: float32 [2, 768], P('grp', 'dp')
- grad_side_qkv_weight: float32 [2, 768, 2304], P('grp', 'dp')
- grad_side_out_weight: float32 [2, 768, 768], P('grp', 'dp')
The draws below stay inside these ranges and needn't reach their ends.
Inputs may be any that keep to these rules, and one draw needn't show every extreme that they name: `frame_video`: frames of one video are consecutive: each aligned block of 8 frames holds one video of 8 frames or two of 4, and the last block holds two; a video's number is that of its first block times 2, plus 1 for the second half of a split block. `caption_video`: each caption names a video that has frames; the first caption names the video of frame 0, the second and the last caption the video of the last frame.
All inputs are finite; a program needn't handle non-finite values.
Results may differ from the reference program's by a relative error of at most 0.03.
Values may be sent and summed in bfloat16 or wider, within the bound.
No kernel may reach another device: no remote copies, remote signals or barrier semaphores. Data moves between devices by JAX's collectives and lax.ppermute only.
A program may use at most 320 MiB of HBM per device.

```python
import math
import jax
import jax.numpy as jnp
import numpy as np
from jax import lax

D = 768
HEADS = 12
HD = 64
FF = 3072
TPF = 197
LEN = 77
FR_DEV = 8
CAPS_DEV = 39
FRAMES = 128
CAPTIONS = 624
N_DP = 16


def split_flags(key):
    flags = jax.random.randint(key, (FRAMES // 8,), 0, 2)
    return flags.at[FRAMES // 8 - 1].set(1)


def video_of(block_flags, frame_index):
    block_index = frame_index // 8
    return jnp.where(block_flags[block_index] == 1, frame_index // 4, block_index * 2).astype(jnp.int32)


def draw_frame_video(key, part):
    block_flags = split_flags(key)
    return video_of(block_flags, jnp.arange(FRAMES, dtype=jnp.int32))


def draw_caption_video(key, part):
    block_flags = split_flags(key)
    key = jax.random.fold_in(key, 7)
    picks = jax.random.randint(key, (CAPTIONS,), 0, FRAMES)
    picks = picks.at[0].set(0).at[1].set(FRAMES - 1).at[CAPTIONS - 1].set(FRAMES - 1)
    return video_of(block_flags, picks)


def block_scale(own_key, extent, pieces, low, top_value):
    gain, own = 1.0, jax.random.fold_in(own_key, 6)
    for position, blocks in pieces:
        draws = jnp.exp(jax.random.uniform(jax.random.fold_in(own, position), (blocks,), jnp.float32, low / len(pieces), top_value / len(pieces)))
        gain = gain * jnp.repeat(draws, extent[position] // blocks).reshape([-1 if axis == position else 1 for axis in range(len(extent))])
    return gain


def profile(number_of, total, limit, lean):
    weights = [(1 << 20) // math.isqrt(grade ** lean) + 1 for grade in range(2, number_of + 1)]
    spare, given = total - limit - (number_of - 1), [1] * (number_of - 1)
    while spare > 0:
        free = [i for i in range(number_of - 1) if given[i] < limit]
        mass, remaining = sum([weights[i] for i in free]), spare
        for i in free:
            addition = min(limit - given[i], max(1, remaining * weights[i] // mass), spare)
            given[i] = given[i] + addition
            spare = spare - addition
    return np.array([limit] + given)


def uneven_parts(own_key, number_of, total, limit, lean):
    if number_of == 2:
        one = jax.random.randint(own_key, (), max(1, total - limit), min(limit, total - 1) + 1)
        return jnp.stack([one, total - one])
    lengths = jnp.asarray(profile(number_of, total, limit, lean), jnp.int32)
    twos = (number_of - 1) // 2
    donor, receiver = lengths[1:1 + 2 * twos:2], lengths[2:2 + 2 * twos:2]
    margin = jnp.minimum(donor - 1, limit - receiver)
    shifted = jax.random.randint(jax.random.fold_in(own_key, 1), (twos,), 0, 1 << 20) % (margin + 1)
    lengths = lengths.at[1:1 + 2 * twos:2].set(donor - shifted).at[2:2 + 2 * twos:2].set(receiver + shifted)
    return lengths[jax.random.permutation(jax.random.fold_in(own_key, 2), number_of)]


def normal_values(own_key, shape, scale, most, shards=(), kind=jnp.bfloat16):
    values = jax.random.normal(own_key, shape, jnp.float32) * scale
    if len(shards) > 0:
        values = block_scale(own_key, shape, shards, -0.22, 0.18) * values
    return jnp.clip(values, min=-most, max=most).astype(kind)


def setup_inputs(seed: int = 0) -> dict:
    arg_keys = jax.random.split(jax.random.key(seed), 24)
    return {
        "tokens": normal_values(arg_keys[0], (2, N_DP * FR_DEV * TPF, D), 1.0, 6.0, ((0, 2), (1, 16))),
        "frame_video": draw_frame_video(jax.random.fold_in(arg_keys[23], 71), 0),
        "caption_video": draw_caption_video(jax.random.fold_in(arg_keys[23], 71), 0),
        "caption_len": jax.vmap(lambda own: uneven_parts(own, CAPS_DEV, FR_DEV * TPF, LEN, 1))(jax.random.split(arg_keys[3], N_DP)).reshape((N_DP, CAPS_DEV)).astype(jnp.int32),
        "attn_norm_gain": jnp.clip(1.0 + 0.1 * jax.random.normal(arg_keys[4], (2, D), jnp.float32), 0.5, 1.5),
        "attn_norm_shift": normal_values(arg_keys[5], (2, D), 0.3, 1.5, ((0, 2),), jnp.float32),
        "qkv_weight": normal_values(arg_keys[6], (2, D, 3 * D), D ** -0.5, 0.21875, ((0, 2),)),
        "query_value_bias": normal_values(arg_keys[7], (2, 2 * D), 0.3, 1.5, ((0, 2),), jnp.float32),
        "proj_weight": normal_values(arg_keys[8], (2, D, D), (D // 16) ** -0.5, 0.875, ((0, 2),)),
        "proj_bias": normal_values(arg_keys[9], (2, D), 0.3, 1.5, ((0, 2),), jnp.float32),
        "mlp_norm_gain": jnp.clip(1.0 + 0.1 * jax.random.normal(arg_keys[10], (2, D), jnp.float32), 0.5, 1.5),
        "mlp_norm_shift": normal_values(arg_keys[11], (2, D), 0.3, 1.5, ((0, 2),), jnp.float32),
        "fc_in_weight": normal_values(arg_keys[12], (2, D, FF), D ** -0.5, 0.21875, ((0, 2),)),
        "fc_in_bias": normal_values(arg_keys[13], (2, FF), 0.3, 1.5, ((0, 2),), jnp.float32),
        "fc_out_weight": normal_values(arg_keys[14], (2, FF, D), (FF // 4) ** -0.5, 0.21875, ((0, 2),)),
        "fc_out_bias": normal_values(arg_keys[15], (2, D), 0.3, 1.5, ((0, 2),), jnp.float32),
        "side_in_weight": normal_values(arg_keys[16], (2, D, D), D ** -0.5, 0.21875, ((0, 2),)),
        "side_in_bias": normal_values(arg_keys[17], (2, D), 0.3, 1.5, ((0, 2),), jnp.float32),
        "side_norm_gain": jnp.clip(1.0 + 0.1 * jax.random.normal(arg_keys[18], (2, D), jnp.float32), 0.5, 1.5),
        "side_norm_shift": normal_values(arg_keys[19], (2, D), 0.3, 1.5, ((0, 2),), jnp.float32),
        "side_qkv_weight": normal_values(arg_keys[20], (2, D, 3 * D), D ** -0.5, 0.21875, ((0, 2),)),
        "side_out_weight": normal_values(arg_keys[21], (2, D, D), (D // 4) ** -0.5, 0.4375, ((0, 2),)),
        "cotangent": normal_values(arg_keys[22], (2, N_DP * FR_DEV * TPF, D), 1.0, 6.0, ((0, 2), (1, 16))),
    }


@jax.custom_vjp
def low(v):
    return lax.optimization_barrier(v.astype(jnp.bfloat16)).astype(jnp.float32)

@jax.custom_vjp
def low_back(v):
    return v

def low_keep(v):
    return (low(v), None)

def low_pass(kept, grad):
    return (grad,)

def back_keep(v):
    return (v, None)

def back_low(kept, grad):
    return (low(grad),)
low.defvjp(low_keep, low_pass)
low_back.defvjp(back_keep, back_low)

def product(left_side, right_side):
    return jnp.einsum('...d,de->...e', left_side, right_side, precision=lax.Precision.HIGHEST)

def layer_norm(values, norm_gain, norm_shift):
    center = values - lax.optimization_barrier(jnp.mean(values, axis=-1, keepdims=True))
    spread = lax.rsqrt(lax.optimization_barrier(jnp.mean(center * center, axis=-1, keepdims=True)) + 1e-05)
    return center * spread * norm_gain + norm_shift

def quick_gelu(values):
    return values * jax.nn.sigmoid(1.702 * values)

def attend_heads(query_rows, key_rows, value_rows, allowed):
    scores = jnp.einsum('bqhe,bkhe->bhqk', query_rows, key_rows, precision=lax.Precision.HIGHEST) * HD ** (-0.5)
    scores = low_back(scores)
    if allowed is not None:
        scores = jnp.where(allowed, scores, -1e+30)
    soft_weights = jax.nn.softmax(scores, axis=-1)
    return jnp.einsum('bhqk,bkhe->bqhe', low(soft_weights), value_rows, precision=lax.Precision.HIGHEST)

def main_block(block_rows, main_params, allowed):
    attn_gain, attn_shift, qkv_weight, query_value_bias, proj_weight, proj_bias, mlp_gain, mlp_shift, fc_in_weight, fc_in_bias, fc_out_weight, fc_out_bias = main_params
    batch_size, length = (block_rows.shape[0], block_rows.shape[1])
    normed = low(layer_norm(block_rows, attn_gain, attn_shift))
    full_bias = jnp.concatenate([query_value_bias[:D], jnp.zeros((D,), jnp.float32), query_value_bias[D:]])
    projected = low_back(low(product(normed, qkv_weight) + full_bias))
    split_heads = projected.reshape(batch_size, length, 3, HEADS, HD)
    mixed_rows = attend_heads(split_heads[:, :, 0], split_heads[:, :, 1], split_heads[:, :, 2], allowed)
    mixed_rows = low_back(low(mixed_rows.reshape(batch_size, length, D)))
    middle = block_rows + low_back(product(mixed_rows, proj_weight) + proj_bias)
    normed_two = low(layer_norm(middle, mlp_gain, mlp_shift))
    pre_act = low_back(product(normed_two, fc_in_weight) + fc_in_bias)
    return middle + low_back(product(low(quick_gelu(pre_act)), fc_out_weight) + fc_out_bias)

def side_attend(query_rows, key_rows, value_rows, allowed):
    mixed_rows = attend_heads(query_rows.reshape(1, -1, HEADS, HD), key_rows.reshape(1, -1, HEADS, HD), value_rows.reshape(1, -1, HEADS, HD), allowed[None, None])
    return low_back(low(mixed_rows.reshape(-1, D)))

def side_start(source, side_params):
    start_rows = low_back(product(low(source), side_params[0]) + side_params[1])
    return (start_rows, low(layer_norm(start_rows, side_params[2], side_params[3])))

def video_side(source, frame_video, side_params):
    start_rows, normed = side_start(source, side_params)
    projected = low_back(low(product(normed, side_params[4])))
    mixed_rows = side_attend(projected[:, :D], projected[:, D:2 * D], projected[:, 2 * D:], frame_video[:, None] == frame_video[None, :])
    return low_back(start_rows + product(mixed_rows, side_params[5]))

def text_side(source, context, caption_video, frame_video, side_params):
    start_rows, normed = side_start(source, side_params)
    query_rows = low_back(low(product(normed, side_params[4][:, :D])))
    pair_rows = low_back(low(product(context, side_params[4][:, D:])))
    mixed_rows = side_attend(query_rows, pair_rows[:, :D], pair_rows[:, D:], caption_video[:, None] == frame_video[None, :])
    return low_back(start_rows + product(mixed_rows, side_params[5]))

def forward(tokens, frame_video, caption_video, caption_len, params):
    main_video = tuple((member[0] for member in params[:12]))
    main_text = tuple((member[1] for member in params[:12]))
    side_video = tuple((member[0] for member in params[12:]))
    side_text = tuple((member[1] for member in params[12:]))
    video_rows = tokens[0].reshape(N_DP, FR_DEV, TPF, D)
    messages = video_side(video_rows[:, :, 0].reshape(FRAMES, D), frame_video, side_video)
    frame_rows = jnp.concatenate([video_rows, messages.reshape(N_DP, FR_DEV, 1, D)], axis=2)

    def video_device(block_rows):
        return main_block(block_rows, main_video, None)[:, :TPF]
    video_out = lax.map(jax.checkpoint(video_device), frame_rows)
    caption_ends = jnp.cumsum(caption_len, axis=1) - 1
    places = jnp.arange(FR_DEV * TPF, dtype=jnp.int32)
    segment = lax.optimization_barrier(jnp.sum((places[None, :, None] > caption_ends[:, None, :]).astype(jnp.int32), axis=2))

    def text_device(device_pair):
        block_rows, seg_rows = device_pair
        allowed = (seg_rows[:, None] == seg_rows[None, :]) & (places[None, :] <= places[:, None])
        return main_block(block_rows[None], main_text, allowed[None, None])[0]
    hidden = lax.map(jax.checkpoint(text_device), (tokens[1].reshape(N_DP, FR_DEV * TPF, D), segment))
    hidden = hidden.reshape(-1, D)
    end_rows = (caption_ends + jnp.arange(N_DP, dtype=jnp.int32)[:, None] * (FR_DEV * TPF)).reshape(-1)
    prompts = text_side(hidden[end_rows], low(messages), caption_video, frame_video, side_text)
    text_out = hidden.at[end_rows].add(prompts)
    return jnp.stack([video_out.reshape(-1, D), text_out])

def reference(tokens, frame_video, caption_video, caption_len, attn_norm_gain, attn_norm_shift, qkv_weight, query_value_bias, proj_weight, proj_bias, mlp_norm_gain, mlp_norm_shift, fc_in_weight, fc_in_bias, fc_out_weight, fc_out_bias, side_in_weight, side_in_bias, side_norm_gain, side_norm_shift, side_qkv_weight, side_out_weight, cotangent):
    params = (attn_norm_gain, attn_norm_shift, qkv_weight, query_value_bias, proj_weight, proj_bias, mlp_norm_gain, mlp_norm_shift, fc_in_weight, fc_in_bias, fc_out_weight, fc_out_bias, side_in_weight, side_in_bias, side_norm_gain, side_norm_shift, side_qkv_weight, side_out_weight)
    floats = tuple((member.astype(jnp.float32) for member in params))

    def wrapped(token_values, *param_values):
        return forward(token_values, frame_video, caption_video, caption_len, param_values)
    outputs, back = jax.vjp(wrapped, tokens.astype(jnp.float32), *floats)
    grads = back(cotangent.astype(jnp.float32))
    return (outputs.astype(jnp.bfloat16), grads[0], grads[1], grads[2], grads[3], grads[4], grads[5], grads[6], grads[7], grads[8], grads[9], grads[10], grads[11], grads[12], grads[13], grads[14], grads[15], grads[16], grads[17], grads[18])
```

```python
import functools
import jax
import jax.numpy as jnp
from jax import lax
from jax.sharding import PartitionSpec as P

HEADS = 12
HD = 64
TPF = 197


def layer_norm(values, norm_gain, norm_shift):
    center = values - jnp.mean(values, axis=-1, keepdims=True)
    spread = lax.rsqrt(jnp.mean(center * center, axis=-1, keepdims=True) + 1e-05)
    return center * spread * norm_gain + norm_shift


def quick_gelu(values):
    return values * jax.nn.sigmoid(1.702 * values)


def product(left_side, right_side):
    return jnp.dot(left_side, right_side, preferred_element_type=jnp.float32)


def product_tn(left_side, right_side):
    return lax.dot_general(
        left_side, right_side, (((0,), (0,)), ((), ())), preferred_element_type=jnp.float32
    )


def product_nt(left_side, right_side):
    return lax.dot_general(
        left_side, right_side, (((1,), (1,)), ((), ())), preferred_element_type=jnp.float32
    )


def column_total(values):
    return jnp.sum(values.astype(jnp.float32), axis=0)


def soft_rows(scores):
    row_max = jnp.max(scores, axis=-1, keepdims=True)
    weights_exp = jnp.exp(scores - row_max)
    row_total = jnp.sum(weights_exp, axis=-1, keepdims=True)
    return (weights_exp / row_total, row_max + jnp.log(row_total))


def small_attend(query_rows, key_rows, value_rows, allowed):
    query_heads = query_rows.reshape(-1, HEADS, HD)
    key_heads = key_rows.reshape(-1, HEADS, HD)
    value_heads = value_rows.reshape(-1, HEADS, HD)
    scores = jnp.einsum(
        "qhe,khe->hqk", query_heads, key_heads, preferred_element_type=jnp.float32
    ) * HD ** (-0.5)
    soft_weights, log_total = soft_rows(jnp.where(allowed[None], scores, -1e30))
    mixed_heads = jnp.einsum(
        "hqk,khe->qhe",
        soft_weights.astype(jnp.bfloat16),
        value_heads,
        preferred_element_type=jnp.float32,
    )
    return (mixed_heads.reshape(query_rows.shape[0], -1).astype(jnp.bfloat16), soft_weights)


def small_attend_back(query_rows, key_rows, value_rows, soft_weights, grad_mixed):
    scale_value = HD ** (-0.5)
    query_heads = query_rows.reshape(-1, HEADS, HD)
    key_heads = key_rows.reshape(-1, HEADS, HD)
    value_heads = value_rows.reshape(-1, HEADS, HD)
    grad_heads = grad_mixed.reshape(-1, HEADS, HD)
    grad_soft = jnp.einsum(
        "qhe,khe->hqk", grad_heads, value_heads, preferred_element_type=jnp.float32
    )
    inner_sum = jnp.sum(soft_weights * grad_soft, axis=-1, keepdims=True)
    grad_scores = (soft_weights * (grad_soft - inner_sum)).astype(jnp.bfloat16)
    grad_query = (
        jnp.einsum("hqk,khe->qhe", grad_scores, key_heads, preferred_element_type=jnp.float32)
        * scale_value
    )
    grad_key = (
        jnp.einsum("hqk,qhe->khe", grad_scores, query_heads, preferred_element_type=jnp.float32)
        * scale_value
    )
    grad_value = jnp.einsum(
        "hqk,qhe->khe",
        soft_weights.astype(jnp.bfloat16),
        grad_heads,
        preferred_element_type=jnp.float32,
    )
    query_count = query_rows.shape[0]
    key_count = key_rows.shape[0]
    return (
        grad_query.reshape(query_count, -1),
        grad_key.reshape(key_count, -1),
        grad_value.reshape(key_count, -1),
    )


def frame_scores(projected, frame_count):
    split_heads = projected.reshape(frame_count, -1, 3, HEADS, HD)
    query_heads = split_heads[:, :, 0]
    key_heads = split_heads[:, :, 1]
    value_heads = split_heads[:, :, 2]
    scores = jnp.einsum(
        "fqhe,fkhe->fhqk", query_heads, key_heads, preferred_element_type=jnp.float32
    ) * HD ** (-0.5)
    return (query_heads, key_heads, value_heads, scores)


def frame_attend(projected, frame_count):
    query_heads, key_heads, value_heads, scores = frame_scores(projected, frame_count)
    soft_weights, log_total = soft_rows(scores)
    mixed_heads = jnp.einsum(
        "fhqk,fkhe->fqhe",
        soft_weights.astype(jnp.bfloat16),
        value_heads,
        preferred_element_type=jnp.float32,
    )
    return (mixed_heads.reshape(projected.shape[0], -1).astype(jnp.bfloat16), log_total)


def frame_attend_back(projected, log_total, grad_mixed, frame_count):
    scale_value = HD ** (-0.5)
    query_heads, key_heads, value_heads, scores = frame_scores(projected, frame_count)
    soft_weights = jnp.exp(scores - log_total)
    grad_heads = grad_mixed.reshape(frame_count, -1, HEADS, HD)
    grad_soft = jnp.einsum(
        "fqhe,fkhe->fhqk", grad_heads, value_heads, preferred_element_type=jnp.float32
    )
    inner_sum = jnp.sum(soft_weights * grad_soft, axis=-1, keepdims=True)
    grad_scores = (soft_weights * (grad_soft - inner_sum)).astype(jnp.bfloat16)
    grad_query = (
        jnp.einsum("fhqk,fkhe->fqhe", grad_scores, key_heads, preferred_element_type=jnp.float32)
        * scale_value
    )
    grad_key = (
        jnp.einsum("fhqk,fqhe->fkhe", grad_scores, query_heads, preferred_element_type=jnp.float32)
        * scale_value
    )
    grad_value = jnp.einsum(
        "fhqk,fqhe->fkhe",
        soft_weights.astype(jnp.bfloat16),
        grad_heads,
        preferred_element_type=jnp.float32,
    )
    return jnp.stack([grad_query, grad_key, grad_value], axis=2).reshape(projected.shape[0], -1)


def padded_count(row_count):
    return -(-row_count // 512) * 512


def packed_prepare(projected, segment):
    row_count = projected.shape[0]
    padding_rows = padded_count(row_count) - row_count
    split_heads = projected.reshape(row_count, 3, HEADS, HD)
    query_all = jnp.pad(split_heads[:, 0], ((0, padding_rows), (0, 0), (0, 0)))
    pair_all = jnp.pad(split_heads[:, 1:], ((128, padding_rows), (0, 0), (0, 0), (0, 0)))
    query_segment = jnp.pad(segment, (0, padding_rows), constant_values=-2)
    key_segment = jnp.pad(segment, (128, padding_rows), constant_values=-1)
    return (query_all, pair_all, query_segment, key_segment)


def packed_block(prepared, block_index):
    query_all, pair_all, query_segment, key_segment = prepared
    block_start = block_index * 512
    query_heads = lax.dynamic_slice_in_dim(query_all, block_start, 512, 0).reshape(
        4, 128, HEADS, HD
    )
    pair_window = lax.dynamic_slice_in_dim(pair_all, block_start, 640, 0)
    pair_heads = jnp.stack([pair_window[offset : offset + 256] for offset in range(0, 512, 128)])
    query_labels = lax.dynamic_slice_in_dim(query_segment, block_start, 512, 0).reshape(4, 128)
    label_window = lax.dynamic_slice_in_dim(key_segment, block_start, 640, 0)
    key_labels = jnp.stack([label_window[offset : offset + 256] for offset in range(0, 512, 128)])
    query_place = block_start + jnp.arange(512, dtype=jnp.int32).reshape(4, 128)
    key_place = (
        block_start
        - 128
        + jnp.arange(256, dtype=jnp.int32)[None, :]
        + 128 * jnp.arange(4, dtype=jnp.int32)[:, None]
    )
    allowed = (query_labels[:, :, None] == key_labels[:, None, :]) & (
        key_place[:, None, :] <= query_place[:, :, None]
    )
    scores = jnp.einsum(
        "sqhe,skhe->shqk", query_heads, pair_heads[:, :, 0], preferred_element_type=jnp.float32
    )
    scores = jnp.where(allowed[:, None], scores * HD ** (-0.5), -1e30)
    return (query_heads, pair_heads, scores)


def packed_attend(projected, segment):
    row_count = projected.shape[0]
    prepared = packed_prepare(projected, segment)
    block_count = padded_count(row_count) // 512

    def one_block(block_index):
        query_heads, pair_heads, scores = packed_block(prepared, block_index)
        soft_weights, log_total = soft_rows(scores)
        mixed_heads = jnp.einsum(
            "shqk,skhe->sqhe",
            soft_weights.astype(jnp.bfloat16),
            pair_heads[:, :, 1],
            preferred_element_type=jnp.float32,
        )
        return (mixed_heads.reshape(512, -1).astype(jnp.bfloat16), log_total)

    mixed_rows, log_total = lax.map(one_block, jnp.arange(block_count, dtype=jnp.int32))
    return (mixed_rows.reshape(block_count * 512, -1)[:row_count], log_total)


def packed_attend_back(projected, log_total, grad_mixed, segment):
    scale_value = HD ** (-0.5)
    row_count = projected.shape[0]
    total_rows = padded_count(row_count)
    prepared = packed_prepare(projected, segment)
    block_count = total_rows // 512
    grad_padded = jnp.pad(grad_mixed, ((0, total_rows - row_count), (0, 0)))

    def one_block(grad_pairs, block_index):
        query_heads, pair_heads, scores = packed_block(prepared, block_index)
        soft_weights = jnp.exp(scores - log_total[block_index])
        block_start = block_index * 512
        grad_heads = lax.dynamic_slice_in_dim(grad_padded, block_start, 512, 0).reshape(
            4, 128, HEADS, HD
        )
        grad_soft = jnp.einsum(
            "sqhe,skhe->shqk", grad_heads, pair_heads[:, :, 1], preferred_element_type=jnp.float32
        )
        inner_sum = jnp.sum(soft_weights * grad_soft, axis=-1, keepdims=True)
        grad_scores = (soft_weights * (grad_soft - inner_sum)).astype(jnp.bfloat16)
        grad_query = (
            jnp.einsum(
                "shqk,skhe->sqhe",
                grad_scores,
                pair_heads[:, :, 0],
                preferred_element_type=jnp.float32,
            )
            * scale_value
        )
        grad_key = (
            jnp.einsum(
                "shqk,sqhe->skhe", grad_scores, query_heads, preferred_element_type=jnp.float32
            )
            * scale_value
        )
        grad_value = jnp.einsum(
            "shqk,sqhe->skhe",
            soft_weights.astype(jnp.bfloat16),
            grad_heads,
            preferred_element_type=jnp.float32,
        )
        grad_local = jnp.stack([grad_key, grad_value], axis=2)
        window_grad = sum(
            (
                jnp.pad(grad_local[offset // 128], ((offset, 384 - offset), (0, 0), (0, 0), (0, 0)))
                for offset in range(0, 512, 128)
            )
        )
        window = lax.dynamic_slice_in_dim(grad_pairs, block_start, 640, 0)
        grad_pairs = lax.dynamic_update_slice_in_dim(
            grad_pairs, window + window_grad, block_start, 0
        )
        return (grad_pairs, grad_query.reshape(512, HEADS, HD))

    grad_pairs, grad_query = lax.scan(
        one_block,
        jnp.zeros((total_rows + 128, 2, HEADS, HD), jnp.float32),
        jnp.arange(block_count, dtype=jnp.int32),
    )
    grad_query = grad_query.reshape(total_rows, 1, HEADS, HD)[:row_count]
    return jnp.concatenate([grad_query, grad_pairs[128 : 128 + row_count]], axis=1).reshape(
        row_count, -1
    )


def main_forward(row_values, main_params, attend):
    (
        attn_gain,
        attn_shift,
        qkv_weight,
        query_value_bias,
        proj_weight,
        proj_bias,
        mlp_gain,
        mlp_shift,
        fc_in_weight,
        fc_in_bias,
        fc_out_weight,
        fc_out_bias,
    ) = main_params
    model_width = row_values.shape[1]
    normed = layer_norm(row_values, attn_gain, attn_shift).astype(jnp.bfloat16)
    full_bias = jnp.concatenate(
        [
            query_value_bias[:model_width],
            jnp.zeros((model_width,), jnp.float32),
            query_value_bias[model_width:],
        ]
    )
    projected = (product(normed, qkv_weight) + full_bias).astype(jnp.bfloat16)
    mixed_rows, log_total = attend(projected)
    middle = row_values + product(mixed_rows, proj_weight) + proj_bias
    normed_two = layer_norm(middle, mlp_gain, mlp_shift).astype(jnp.bfloat16)
    pre_act = product(normed_two, fc_in_weight) + fc_in_bias
    activation = quick_gelu(pre_act).astype(jnp.bfloat16)
    block_out = middle + product(activation, fc_out_weight) + fc_out_bias
    return (
        block_out,
        (normed, projected, mixed_rows, log_total, middle, normed_two, pre_act, activation),
    )


def main_backward(row_values, grad_out, main_params, stored, attend_back):
    (
        attn_gain,
        attn_shift,
        qkv_weight,
        query_value_bias,
        proj_weight,
        proj_bias,
        mlp_gain,
        mlp_shift,
        fc_in_weight,
        fc_in_bias,
        fc_out_weight,
        fc_out_bias,
    ) = main_params
    normed, projected, mixed_rows, log_total, middle, normed_two, pre_act, activation = stored
    model_width = row_values.shape[1]
    grad_branch = grad_out.astype(jnp.bfloat16)
    grad_fc_out = product_tn(activation, grad_branch)
    grad_fc_out_bias = column_total(grad_branch)
    unused_value, gelu_back = jax.vjp(quick_gelu, pre_act)
    grad_pre = gelu_back(product_nt(grad_branch, fc_out_weight))[0].astype(jnp.bfloat16)
    grad_fc_in = product_tn(normed_two, grad_pre)
    grad_fc_in_bias = column_total(grad_pre)
    unused_norm, norm_back = jax.vjp(layer_norm, middle, mlp_gain, mlp_shift)
    grad_middle, grad_mlp_gain, grad_mlp_shift = norm_back(product_nt(grad_pre, fc_in_weight))
    grad_middle = grad_middle + grad_out
    grad_attn_branch = grad_middle.astype(jnp.bfloat16)
    grad_proj = product_tn(mixed_rows, grad_attn_branch)
    grad_proj_bias = column_total(grad_attn_branch)
    grad_mixed = product_nt(grad_attn_branch, proj_weight).astype(jnp.bfloat16)
    grad_projected = attend_back(projected, log_total, grad_mixed).astype(jnp.bfloat16)
    grad_qkv = product_tn(normed, grad_projected)
    bias_totals = column_total(grad_projected)
    grad_qv_bias = jnp.concatenate([bias_totals[:model_width], bias_totals[2 * model_width :]])
    unused_first, norm_back_first = jax.vjp(layer_norm, row_values, attn_gain, attn_shift)
    grad_rows, grad_attn_gain, grad_attn_shift = norm_back_first(
        product_nt(grad_projected, qkv_weight)
    )
    return (
        grad_rows + grad_middle,
        (
            grad_attn_gain,
            grad_attn_shift,
            grad_qkv,
            grad_qv_bias,
            grad_proj,
            grad_proj_bias,
            grad_mlp_gain,
            grad_mlp_shift,
            grad_fc_in,
            grad_fc_in_bias,
            grad_fc_out,
            grad_fc_out_bias,
        ),
    )


def side_open(source, side_params):
    start_rows = product(source, side_params[0]) + side_params[1]
    return (start_rows, layer_norm(start_rows, side_params[2], side_params[3]).astype(jnp.bfloat16))


def side_close(start_rows, grad_direct, grad_normed, side_params):
    unused_norm, norm_back = jax.vjp(layer_norm, start_rows, side_params[2], side_params[3])
    grad_start, grad_gain, grad_shift = norm_back(grad_normed)
    return ((grad_start + grad_direct).astype(jnp.bfloat16), grad_gain, grad_shift)


def video_side(source, frame_ids, side_params):
    model_width = source.shape[1]
    start_rows, normed = side_open(source, side_params)
    projected = product(normed, side_params[4]).astype(jnp.bfloat16)
    mixed_rows, soft_weights = small_attend(
        projected[:, :model_width],
        projected[:, model_width : 2 * model_width],
        projected[:, 2 * model_width :],
        frame_ids[:, None] == frame_ids[None, :],
    )
    message = start_rows + product(mixed_rows, side_params[5])
    return (message, (start_rows, normed, projected, mixed_rows, soft_weights))


def video_side_back(source, side_params, stored, grad_message):
    start_rows, normed, projected, mixed_rows, soft_weights = stored
    model_width = source.shape[1]
    grad_round = grad_message.astype(jnp.bfloat16)
    grad_mixed = product_nt(grad_round, side_params[5]).astype(jnp.bfloat16)
    grad_parts = small_attend_back(
        projected[:, :model_width],
        projected[:, model_width : 2 * model_width],
        projected[:, 2 * model_width :],
        soft_weights,
        grad_mixed,
    )
    grad_projected = jnp.concatenate(grad_parts, axis=1).astype(jnp.bfloat16)
    grad_start, grad_gain, grad_shift = side_close(
        start_rows,
        grad_round.astype(jnp.float32),
        product_nt(grad_projected, side_params[4]),
        side_params,
    )
    grad_source = product_nt(grad_start, side_params[0])
    rows = jnp.concatenate([grad_start, grad_projected, grad_round], axis=1)
    return (grad_source, rows, (column_total(grad_start), grad_gain, grad_shift))


def text_side(source, context, caption_ids, frame_ids, side_params):
    model_width = source.shape[1]
    start_rows, normed = side_open(source, side_params)
    query_rows = product(normed, side_params[4][:, :model_width]).astype(jnp.bfloat16)
    pair_rows = product(context, side_params[4][:, model_width:]).astype(jnp.bfloat16)
    mixed_rows, soft_weights = small_attend(
        query_rows,
        pair_rows[:, :model_width],
        pair_rows[:, model_width:],
        caption_ids[:, None] == frame_ids[None, :],
    )
    prompt = start_rows + product(mixed_rows, side_params[5])
    return (prompt, (start_rows, normed, query_rows, pair_rows, mixed_rows, soft_weights))


def text_side_back(source, side_params, stored, grad_prompt):
    start_rows, normed, query_rows, pair_rows, mixed_rows, soft_weights = stored
    model_width = source.shape[1]
    grad_round = grad_prompt.astype(jnp.bfloat16)
    grad_out_weight = product_tn(mixed_rows, grad_round)
    grad_mixed = product_nt(grad_round, side_params[5]).astype(jnp.bfloat16)
    grad_query, grad_key, grad_value = small_attend_back(
        query_rows, pair_rows[:, :model_width], pair_rows[:, model_width:], soft_weights, grad_mixed
    )
    grad_query = grad_query.astype(jnp.bfloat16)
    grad_start, grad_gain, grad_shift = side_close(
        start_rows,
        grad_round.astype(jnp.float32),
        product_nt(grad_query, side_params[4][:, :model_width]),
        side_params,
    )
    weights = [product_tn(source, grad_start), product_tn(normed, grad_query), grad_out_weight]
    return (
        product_nt(grad_start, side_params[0]),
        jnp.concatenate([grad_key, grad_value], axis=1),
        jnp.concatenate(weights, axis=1).astype(jnp.bfloat16),
        (column_total(grad_start), grad_gain, grad_shift),
    )


def pair_list(size, distance):
    return [(place, place ^ distance) for place in range(size)]


def group_pairs(size, distance, group):
    return [(group * size + place, group * size + (place ^ distance)) for place in range(size)]


def bit_count(size):
    return size.bit_length() - 1


def halve_scatter(parts, size, order, send):
    me = lax.axis_index("dp")
    bits = list(range(bit_count(size)))[::-1]
    view = parts.reshape((2,) * len(bits) + parts.shape[1:])
    for step, bit in enumerate(order):
        axis = bits.index(bit)
        bits.remove(bit)
        mine = (me >> bit) & 1
        keep = lax.dynamic_index_in_dim(view, mine, axis, keepdims=False)
        other = lax.dynamic_index_in_dim(view, 1 - mine, axis, keepdims=False)
        total = keep.astype(jnp.float32) + send(other, 1 << bit).astype(jnp.float32)
        view = total if step == len(order) - 1 else total.astype(parts.dtype)
    return view


def scatter_matrix(matrix, size):
    rows, columns = matrix.shape
    parts = matrix.astype(jnp.bfloat16).reshape(size, rows // size, columns)
    order = list(range(bit_count(size)))
    other = [1, 0] + order[2:]

    def send(values, distance):
        return lax.ppermute(values, "dp", pair_list(size, distance))

    half = columns // 2
    return jnp.concatenate(
        [
            halve_scatter(parts[:, :, :half], size, order, send),
            halve_scatter(parts[:, :, half:], size, other, send),
        ],
        axis=1,
    )


def double_gather(values, size, send):
    for bit in range(bit_count(size)):
        values = jnp.concatenate([values, send(values, 1 << bit)], axis=0)
    return values

def on_device(
    size,
    tokens,
    frame_video,
    caption_video,
    caption_len,
    attn_norm_gain,
    attn_norm_shift,
    qkv_weight,
    query_value_bias,
    proj_weight,
    proj_bias,
    mlp_norm_gain,
    mlp_norm_shift,
    fc_in_weight,
    fc_in_bias,
    fc_out_weight,
    fc_out_bias,
    side_in_weight,
    side_in_bias,
    side_norm_gain,
    side_norm_shift,
    side_qkv_weight,
    side_out_weight,
    cotangent,
):
    main_params = tuple(
        (
            member[0]
            for member in (
                attn_norm_gain,
                attn_norm_shift,
                qkv_weight,
                query_value_bias,
                proj_weight,
                proj_bias,
                mlp_norm_gain,
                mlp_norm_shift,
                fc_in_weight,
                fc_in_bias,
                fc_out_weight,
                fc_out_bias,
            )
        )
    )
    side_params = tuple(
        (
            member[0]
            for member in (
                side_in_weight,
                side_in_bias,
                side_norm_gain,
                side_norm_shift,
                side_qkv_weight,
                side_out_weight,
            )
        )
    )
    token_rows = tokens[0]
    cotangent_rows = cotangent[0]
    row_count, model_width = token_rows.shape
    frame_count = row_count // TPF
    me = lax.axis_index("dp")
    is_video = lax.axis_index("grp") == 0

    def to_text(values):
        return lax.ppermute(values, ("grp", "dp"), [(i, size + i) for i in range(size)])

    def to_video(values):
        return lax.ppermute(values, ("grp", "dp"), [(size + i, i) for i in range(size)])

    def in_all(values, distance):
        return lax.ppermute(values, "dp", pair_list(size, distance))

    def in_video(values, distance):
        return lax.ppermute(values, ("grp", "dp"), group_pairs(size, distance, 0))

    def in_text(values, distance):
        return lax.ppermute(values, ("grp", "dp"), group_pairs(size, distance, 1))

    frame_order = frame_video.reshape(size, frame_count)[me ^ jnp.arange(size)]
    frame_ids = frame_order[0]
    frame_order = frame_order.reshape(-1)
    source = token_rows.reshape(frame_count, TPF, model_width)[:, 0]
    message, side_stored = video_side(source, frame_ids, side_params)
    arrived = to_text(message.astype(jnp.bfloat16))
    packed = jnp.concatenate([arrived, source, side_stored[1], side_stored[3]], axis=1)
    packed = double_gather(packed, size, in_all)
    context = packed[:, :model_width]
    caption_ends = jnp.cumsum(caption_len[0]) - 1
    places = jnp.arange(row_count, dtype=jnp.int32)
    segment = jnp.sum((places[:, None] > caption_ends[None, :]).astype(jnp.int32), axis=1)

    def video_branch():
        frame_rows = jnp.concatenate(
            [
                token_rows.reshape(frame_count, TPF, model_width).astype(jnp.float32),
                message[:, None, :],
            ],
            axis=1,
        ).reshape(-1, model_width)

        def attend(projected):
            return frame_attend(projected, frame_count)

        def attend_back(projected, log_total, grad_mixed):
            return frame_attend_back(projected, log_total, grad_mixed, frame_count)

        block_out, stored = main_forward(frame_rows, main_params, attend)
        shaped = block_out.reshape(frame_count, TPF + 1, model_width)
        out_rows = shaped[:, :TPF].reshape(row_count, model_width).astype(jnp.bfloat16)
        grad_out = jnp.concatenate(
            [
                cotangent_rows.reshape(frame_count, TPF, model_width).astype(jnp.float32),
                jnp.zeros((frame_count, 1, model_width), jnp.float32),
            ],
            axis=1,
        )
        grad_rows, main_grads = main_backward(
            frame_rows, grad_out.reshape(-1, model_width), main_params, stored, attend_back
        )
        grad_rows = grad_rows.reshape(frame_count, TPF + 1, model_width)
        vector = jnp.zeros((model_width,), jnp.float32)
        return (
            out_rows,
            grad_rows[:, :TPF].reshape(row_count, model_width),
            main_grads,
            jnp.zeros((model_width, 3 * model_width), jnp.bfloat16),
            jnp.zeros((context.shape[0], 2 * model_width), jnp.float32),
            (vector, vector, vector),
            grad_rows[:, TPF],
        )

    def text_branch():

        def attend(projected):
            return packed_attend(projected, segment)

        def attend_back(projected, log_total, grad_mixed):
            return packed_attend_back(projected, log_total, grad_mixed, segment)

        row_values = token_rows.astype(jnp.float32)
        block_out, stored = main_forward(row_values, main_params, attend)
        text_source = block_out[caption_ends].astype(jnp.bfloat16)
        prompt, text_stored = text_side(
            text_source, context, caption_video, frame_order, side_params
        )
        out_rows = block_out.at[caption_ends].add(prompt).astype(jnp.bfloat16)
        grad_out = cotangent_rows.astype(jnp.float32)
        grad_source, grad_pair, side_grads, side_vectors = text_side_back(
            text_source, side_params, text_stored, grad_out[caption_ends]
        )
        grad_rows, main_grads = main_backward(
            row_values, grad_out.at[caption_ends].add(grad_source), main_params, stored, attend_back
        )
        return (
            out_rows,
            grad_rows,
            main_grads,
            side_grads,
            grad_pair,
            side_vectors,
            jnp.zeros((frame_count, model_width), jnp.float32),
        )

    out_rows, grad_tokens, main_grads, text_weights, grad_pair, text_vectors, grad_message = (
        lax.cond(is_video, video_branch, text_branch)
    )
    for bit in range(bit_count(size)):
        distance = frame_count << bit
        lanes = grad_pair.reshape(-1, 2, distance, 2 * model_width)
        swapped = in_text(lanes[:, ::-1].reshape(grad_pair.shape).astype(jnp.bfloat16), 1 << bit)
        grad_pair = grad_pair + swapped.astype(jnp.float32)
    grad_pair = grad_pair.astype(jnp.bfloat16)
    received = to_video(product_nt(grad_pair[:frame_count], side_params[4][:, model_width:]))
    grad_source, grad_lines, video_vectors = video_side_back(
        source, side_params, side_stored, grad_message + received
    )
    class_rows = jnp.zeros((frame_count, TPF, model_width), jnp.float32).at[:, 0].set(grad_source)
    grad_tokens = grad_tokens + jnp.where(is_video, class_rows.reshape(row_count, model_width), 0.0)
    own_width = model_width // size
    grad_lines = double_gather(grad_lines, size, in_video)
    inputs = lax.dynamic_slice_in_dim(
        packed.reshape(-1, 4, model_width), me * own_width, own_width, 2
    )
    side_parts = halve_scatter(
        text_weights.reshape(size, own_width, 3 * model_width),
        size,
        list(range(bit_count(size))),
        in_text,
    )
    pair_part = product_tn(inputs[:, 0], grad_pair)
    grad_in_weight = jnp.where(
        is_video, product_tn(inputs[:, 1], grad_lines[:, :model_width]), side_parts[:, :model_width]
    )
    grad_side_qkv = jnp.where(
        is_video,
        product_tn(inputs[:, 2], grad_lines[:, model_width : 4 * model_width]),
        jnp.concatenate([side_parts[:, model_width : 2 * model_width], pair_part], axis=1),
    )
    grad_side_out = jnp.where(
        is_video,
        product_tn(inputs[:, 3], grad_lines[:, 4 * model_width :]),
        side_parts[:, 2 * model_width :],
    )
    side_vectors = tuple(
        (jnp.where(is_video, one, two) for one, two in zip(video_vectors, text_vectors))
    )
    (
        grad_attn_gain,
        grad_attn_shift,
        grad_qkv,
        grad_qv_bias,
        grad_proj,
        grad_proj_bias,
        grad_mlp_gain,
        grad_mlp_shift,
        grad_fc_in,
        grad_fc_in_bias,
        grad_fc_out,
        grad_fc_out_bias,
    ) = main_grads
    vectors = (
        grad_attn_gain,
        grad_attn_shift,
        grad_qv_bias,
        grad_proj_bias,
        grad_mlp_gain,
        grad_mlp_shift,
        grad_fc_in_bias,
        grad_fc_out_bias,
    ) + side_vectors
    widths = [member.shape[0] // size for member in vectors]
    lines = jnp.concatenate([member.reshape(size, -1) for member in vectors], axis=1)
    line = halve_scatter(lines[:, None, :], size, list(range(bit_count(size))), in_all)[0]
    starts = [sum(widths[:place]) for place in range(len(widths))]
    (
        grad_attn_gain,
        grad_attn_shift,
        grad_qv_bias,
        grad_proj_bias,
        grad_mlp_gain,
        grad_mlp_shift,
        grad_fc_in_bias,
        grad_fc_out_bias,
        grad_in_bias,
        grad_side_gain,
        grad_side_shift,
    ) = [line[start : start + width] for start, width in zip(starts, widths)]
    summed = (
        grad_attn_gain,
        grad_attn_shift,
        scatter_matrix(grad_qkv, size),
        grad_qv_bias,
        scatter_matrix(grad_proj, size),
        grad_proj_bias,
        grad_mlp_gain,
        grad_mlp_shift,
        scatter_matrix(grad_fc_in, size),
        grad_fc_in_bias,
        scatter_matrix(grad_fc_out, size),
        grad_fc_out_bias,
        grad_in_weight,
        grad_in_bias,
        grad_side_gain,
        grad_side_shift,
        grad_side_qkv,
        grad_side_out,
    )
    return tuple([out_rows[None], grad_tokens[None]] + [member[None] for member in summed])


def solution(mesh):
    placed = (
        P("grp", "dp", None),
        P(),
        P("dp"),
        P("dp", None),
        P("grp", None),
        P("grp", None),
        P("grp", None, None),
        P("grp", None),
        P("grp", None, None),
        P("grp", None),
        P("grp", None),
        P("grp", None),
        P("grp", None, None),
        P("grp", None),
        P("grp", None, None),
        P("grp", None),
        P("grp", None, None),
        P("grp", None),
        P("grp", None),
        P("grp", None),
        P("grp", None, None),
        P("grp", None, None),
        P("grp", "dp", None),
    )
    return jax.shard_map(
        functools.partial(on_device, mesh.shape["dp"]),
        mesh=mesh,
        in_specs=placed,
        out_specs=(
            P("grp", "dp", None),
            P("grp", "dp", None),
            P("grp", "dp"),
            P("grp", "dp"),
            P("grp", "dp", None),
            P("grp", "dp"),
            P("grp", "dp", None),
            P("grp", "dp"),
            P("grp", "dp"),
            P("grp", "dp"),
            P("grp", "dp", None),
            P("grp", "dp"),
            P("grp", "dp", None),
            P("grp", "dp"),
            P("grp", "dp", None),
            P("grp", "dp"),
            P("grp", "dp"),
            P("grp", "dp"),
            P("grp", "dp", None),
            P("grp", "dp", None),
        ),
        check_vma=False,
    )
```

```python
import functools

import jax
import jax.numpy as jnp
from jax import lax
from jax.experimental import pallas as pl
from jax.experimental.pallas import tpu as pltpu
from jax.sharding import PartitionSpec as P

HEADS = 12
HD = 64
TPF = 197
FRAME = 208
PRIOR = 80
VMEM_BYTES = 58 * 2**20
SUB_BLOCKS = ((0, 112, -80, 192), (112, 96, 32, 176))


def product(left_side, right_side):
    return jnp.dot(left_side, right_side, preferred_element_type=jnp.float32)


def product_tn(left_side, right_side):
    return lax.dot_general(
        left_side, right_side, (((0,), (0,)), ((), ())), preferred_element_type=jnp.float32
    )


def product_nt(left_side, right_side):
    return lax.dot_general(
        left_side, right_side, (((1,), (1,)), ((), ())), preferred_element_type=jnp.float32
    )


def norm_parts(values):
    center = values - jnp.mean(values, axis=-1, keepdims=True)
    spread = lax.rsqrt(jnp.mean(center * center, axis=-1, keepdims=True) + 1e-05)
    return (center * spread, spread)


def norm_back(unit, spread, gain, grad):
    grad_unit = grad * gain
    first = jnp.mean(grad_unit, axis=-1, keepdims=True)
    second = jnp.mean(grad_unit * unit, axis=-1, keepdims=True)
    return spread * (grad_unit - first - unit * second)


def column_sum(values):
    return jnp.sum(values, axis=0, keepdims=True)


def lane_is_low(shape):
    return lax.broadcasted_iota(jnp.int32, shape, len(shape) - 1) < HD


def with_message(rows, is_video, message_row):
    first = TPF // 8 * 8
    middle = rows[first : first + 8]
    place = lax.broadcasted_iota(jnp.int32, middle.shape, 0)
    middle = jnp.where((place == TPF - first) & is_video, message_row, middle)
    return jnp.concatenate([rows[:first], middle, rows[first + 8 :]], axis=0)


def attend_pair(query, key, value, bias):
    count = query.shape[0]
    low = lane_is_low(query.shape)
    query = query * jnp.asarray(HD**-0.5, query.dtype)
    zero = jnp.zeros_like(query)
    stacked = jnp.concatenate([jnp.where(low, query, zero), jnp.where(low, zero, query)], axis=0)
    scores = product_nt(stacked, key)
    weights = []
    for head in range(2):
        one = scores[head * count : (head + 1) * count] + bias
        weights.append(jnp.exp(one - jnp.max(one, axis=-1, keepdims=True)).astype(jnp.bfloat16))
    wide = jnp.concatenate([value, jnp.ones_like(value)], axis=1)
    summed = product(jnp.concatenate(weights, axis=0), wide)
    mixed = summed[:, :128] / summed[:, 128:]
    return jnp.where(low, mixed[:count], mixed[count:]).astype(jnp.bfloat16)


def attend_pair_back(query, key, value, grad, bias):
    count = key.shape[0]
    low = lane_is_low(key.shape)
    query = query * jnp.asarray(HD**-0.5, query.dtype)
    zero = jnp.zeros_like(key)
    keys = jnp.concatenate([jnp.where(low, key, zero), jnp.where(low, zero, key)], axis=0)
    values = jnp.concatenate([jnp.where(low, value, zero), jnp.where(low, zero, value)], axis=0)
    scores = product_nt(keys, query)
    grad_soft = product_nt(values, grad)
    soft_parts, grad_parts = [], []
    for head in range(2):
        one = scores[head * count : (head + 1) * count] + bias
        one = jnp.exp(one - jnp.max(one, axis=0, keepdims=True))
        soft = one * (1.0 / jnp.sum(one, axis=0, keepdims=True))
        inner = soft * grad_soft[head * count : (head + 1) * count]
        grad_parts.append((inner - soft * column_sum(inner)).astype(jnp.bfloat16))
        soft_parts.append(soft.astype(jnp.bfloat16))
    grad_scores = jnp.concatenate(grad_parts, axis=0)
    grad_value = product(jnp.concatenate(soft_parts, axis=0), grad)
    grad_key = product(grad_scores, query)
    grad_query = product_tn(grad_scores, keys) * HD**-0.5
    return (
        grad_query,
        jnp.where(low, grad_key[:count], grad_key[count:]),
        jnp.where(low, grad_value[:count], grad_value[count:]),
    )


def forward_kernel(
    frames,
    flag_ref,
    token_ref,
    message_ref,
    first_ref,
    gain_one,
    shift_one,
    qkv_weight,
    qkv_bias,
    proj_weight,
    proj_bias,
    gain_two,
    shift_two,
    fc_in_weight,
    fc_in_bias,
    fc_out_weight,
    fc_out_bias,
    normed_ref,
    projected_ref,
    mixed_ref,
    middle_ref,
    normed_two_ref,
    act_ref,
    slope_ref,
    block_ref,
    held,
):
    step = pl.program_id(0)
    is_video = flag_ref[0] == 0
    width = token_ref.shape[1]
    rows = frames * FRAME
    parts = []
    for frame in range(frames):
        part = token_ref[frame * FRAME : (frame + 1) * FRAME, :].astype(jnp.float32)
        message = message_ref[pl.ds(step * frames + frame, 1), :]
        parts.append(with_message(part, is_video, message))
    hidden = jnp.concatenate(parts, axis=0)
    unit, _ = norm_parts(hidden)
    normed = (unit * gain_one[...] + shift_one[...]).astype(jnp.bfloat16)
    normed_ref[...] = normed

    @pl.when(step == 0)
    def _():
        held[0:PRIOR, :] = jnp.zeros((PRIOR, held.shape[1]), held.dtype)

    @pl.when(step > 0)
    def _():
        held[0:PRIOR, :] = held[rows : rows + PRIOR, :]

    for start in range(0, 3 * width, width):
        columns = slice(start, start + width)
        part = (product(normed, qkv_weight[:, columns]) + qkv_bias[:, columns]).astype(jnp.bfloat16)
        held[PRIOR:, columns] = part
        projected_ref[:, columns] = part

    def attend(frame, query_start, query_count, key_start, key_count, bias):
        query_rows = pl.ds(PRIOR + frame * FRAME + query_start, query_count)
        key_rows = pl.ds(PRIOR + frame * FRAME + key_start, key_count)
        for pair in range(0, width, 128):
            mixed_ref[pl.ds(frame * FRAME + query_start, query_count), pair : pair + 128] = attend_pair(
                held[query_rows, pair : pair + 128],
                held[key_rows, width + pair : width + pair + 128],
                held[key_rows, 2 * width + pair : 2 * width + pair + 128],
                bias,
            )

    @pl.when(is_video)
    def _():
        place = lax.broadcasted_iota(jnp.int32, (FRAME, FRAME), 1)
        bias = jnp.where(place <= TPF, 0.0, -1e30)
        for frame in range(frames):
            attend(frame, 0, FRAME, 0, FRAME, bias)

    @pl.when(jnp.logical_not(is_video))
    def _():
        for frame in range(frames):
            for query_start, query_count, key_start, key_count in SUB_BLOCKS:
                base = step * rows + frame * FRAME
                shape = (query_count, key_count)
                key_place = base + key_start + lax.broadcasted_iota(jnp.int32, shape, 1)
                query_place = base + query_start + lax.broadcasted_iota(jnp.int32, shape, 0)
                first = first_ref[pl.ds(frame * FRAME + query_start, query_count), :]
                allowed = (key_place >= first) & (key_place <= query_place)
                bias = jnp.where(allowed, 0.0, -1e30)
                attend(frame, query_start, query_count, key_start, key_count, bias)

    middle = hidden + product(mixed_ref[...], proj_weight[...]) + proj_bias[...]
    middle_ref[...] = middle.astype(jnp.bfloat16)
    unit, _ = norm_parts(middle)
    normed = (unit * gain_two[...] + shift_two[...]).astype(jnp.bfloat16)
    normed_two_ref[...] = normed
    total = middle + fc_out_bias[...]
    for start in range(0, fc_in_weight.shape[1], width):
        columns = slice(start, start + width)
        pre = product(normed, fc_in_weight[:, columns]) + fc_in_bias[:, columns]
        gate = 0.5 + 0.5 * jnp.tanh(0.851 * pre)
        value = pre * gate
        act = value.astype(jnp.bfloat16)
        act_ref[:, columns] = act
        slope_ref[:, columns] = (gate + 1.702 * value * (1.0 - gate)).astype(jnp.bfloat16)
        total = total + product(act, fc_out_weight[columns, :])
    block_ref[...] = total.astype(jnp.bfloat16)


def whole(shape):
    return pl.BlockSpec(
        shape, lambda *_: (0,) * len(shape), pipeline_mode=pl.Buffered(buffer_count=1)
    )


def forward(flag, tokens, message, first, params, frames=2):
    count, width = tokens.shape
    rows = frames * FRAME
    hidden = params[8].shape[1]

    def by_rows(columns):
        return pl.BlockSpec((rows, columns), lambda i, _: (i, 0))

    widths = (width, 3 * width, width, width, width, hidden, hidden, width)
    return pl.pallas_call(
        functools.partial(forward_kernel, frames),
        grid_spec=pltpu.PrefetchScalarGridSpec(
            num_scalar_prefetch=1,
            grid=(count // rows,),
            in_specs=[by_rows(width), whole(message.shape), by_rows(1)]
            + [whole(member.shape) for member in params],
            out_specs=[by_rows(columns) for columns in widths],
            scratch_shapes=[pltpu.VMEM((rows + PRIOR, 3 * width), jnp.bfloat16)],
        ),
        out_shape=[jax.ShapeDtypeStruct((count, columns), jnp.bfloat16) for columns in widths],
        compiler_params=pltpu.CompilerParams(vmem_limit_bytes=VMEM_BYTES),
        name="forward",
    )(flag, tokens, message, first, *params)


def out_weight_kernel(act_ref, grad_ref, weight_ref, bias_ref):
    weight_ref[...] = product_tn(act_ref[...], grad_ref[...]).astype(jnp.bfloat16)

    @pl.when(pl.program_id(0) == 0)
    def _():
        bias_ref[...] = column_sum(grad_ref[...].astype(jnp.float32))


def out_weight_grad(act, grad, tile=512):
    count, hidden = act.shape
    width = grad.shape[1]
    return pl.pallas_call(
        out_weight_kernel,
        grid=(hidden // tile,),
        in_specs=[pl.BlockSpec((count, tile), lambda i: (0, i)), whole(grad.shape)],
        out_specs=[pl.BlockSpec((tile, width), lambda i: (i, 0)), whole((1, width))],
        out_shape=[
            jax.ShapeDtypeStruct((hidden, width), jnp.bfloat16),
            jax.ShapeDtypeStruct((1, width), jnp.float32),
        ],
        compiler_params=pltpu.CompilerParams(vmem_limit_bytes=VMEM_BYTES),
        name="out_weight_grad",
    )(act, grad)


def mlp_back_kernel(
    chunk,
    grad_ref,
    slope_ref,
    normed_ref,
    middle_ref,
    mixed_ref,
    fc_out_weight,
    fc_in_weight,
    proj_weight,
    gain_ref,
    weight_ref,
    bias_ref,
    grad_middle_ref,
    grad_mixed_ref,
    proj_weight_ref,
    vector_ref,
    grad_pre,
    total,
):
    step = pl.program_id(0)
    count = grad_ref.shape[0]
    bias = jnp.zeros(bias_ref.shape, jnp.float32)
    for start in range(0, count, chunk):
        rows = slice(start, start + chunk)
        part = product_nt(grad_ref[rows, :], fc_out_weight[...])
        part = (part * slope_ref[rows, :].astype(jnp.float32)).astype(jnp.bfloat16)
        grad_pre[rows, :] = part
        bias = bias + column_sum(part.astype(jnp.float32))
        back = product_nt(part, fc_in_weight[...])

        @pl.when(step == 0)
        def _():
            total[rows, :] = back

        @pl.when(step > 0)
        def _():
            total[rows, :] = total[rows, :] + back

    bias_ref[...] = bias
    weight_ref[...] = product_tn(normed_ref[...], grad_pre[...]).astype(jnp.bfloat16)

    @pl.when(step == pl.num_programs(0) - 1)
    def _():
        gain = gain_ref[...]
        width = gain.shape[1]
        sums = [jnp.zeros((1, width), jnp.float32) for _ in range(3)]
        for start in range(0, count, chunk):
            rows = slice(start, start + chunk)
            unit, spread = norm_parts(middle_ref[rows, :].astype(jnp.float32))
            back = total[rows, :]
            grad_middle = norm_back(unit, spread, gain, back) + grad_ref[rows, :].astype(jnp.float32)
            grad_middle = grad_middle.astype(jnp.bfloat16)
            grad_middle_ref[rows, :] = grad_middle
            grad_mixed_ref[rows, :] = product_nt(grad_middle, proj_weight[...]).astype(jnp.bfloat16)
            sums[0] = sums[0] + column_sum(back * unit)
            sums[1] = sums[1] + column_sum(back)
            sums[2] = sums[2] + column_sum(grad_middle.astype(jnp.float32))
        vector_ref[...] = jnp.concatenate(sums, axis=0)
        proj_weight_ref[...] = product_tn(mixed_ref[...], grad_middle_ref[...]).astype(jnp.bfloat16)


def mlp_back(grad, slope, normed, middle, mixed, fc_out_weight, fc_in_weight, proj_weight, gain, tile=768):
    count, width = grad.shape
    hidden = slope.shape[1]
    rows = (count, width)
    return pl.pallas_call(
        functools.partial(mlp_back_kernel, 2 * FRAME),
        grid=(hidden // tile,),
        in_specs=[
            whole(rows),
            pl.BlockSpec((count, tile), lambda i: (0, i)),
            whole(rows),
            whole(rows),
            whole(rows),
            pl.BlockSpec((tile, width), lambda i: (i, 0)),
            pl.BlockSpec((width, tile), lambda i: (0, i)),
            whole(proj_weight.shape),
            whole(gain.shape),
        ],
        out_specs=[
            pl.BlockSpec((width, tile), lambda i: (0, i)),
            pl.BlockSpec((1, tile), lambda i: (0, i)),
            whole(rows),
            whole(rows),
            whole((width, width)),
            whole((3, width)),
        ],
        out_shape=[
            jax.ShapeDtypeStruct((width, hidden), jnp.bfloat16),
            jax.ShapeDtypeStruct((1, hidden), jnp.float32),
            jax.ShapeDtypeStruct(rows, jnp.bfloat16),
            jax.ShapeDtypeStruct(rows, jnp.bfloat16),
            jax.ShapeDtypeStruct((width, width), jnp.bfloat16),
            jax.ShapeDtypeStruct((3, width), jnp.float32),
        ],
        scratch_shapes=[pltpu.VMEM((count, tile), jnp.bfloat16), pltpu.VMEM(rows, jnp.float32)],
        compiler_params=pltpu.CompilerParams(vmem_limit_bytes=VMEM_BYTES),
        name="mlp_back",
    )(grad, slope, normed, middle, mixed, fc_out_weight, fc_in_weight, proj_weight, gain)


def attend_back_kernel(flag_ref, projected_ref, grad_ref, first_ref, out_ref, held, pending, carry):
    step = pl.program_id(0)
    blocks = pl.num_programs(0) - 1
    is_video = flag_ref[0] == 0
    width = grad_ref.shape[1]

    @pl.when(step == 0)
    def _():
        held[...] = jnp.zeros(held.shape, held.dtype)
        carry[...] = jnp.zeros(carry.shape, carry.dtype)

    @pl.when(step > 0)
    def _():
        out_ref[...] = pending[...]

    def add_prior(columns, values):
        rows = slice(FRAME - PRIOR, FRAME)
        out_ref[rows, columns] = (carry[:, columns] + values).astype(jnp.bfloat16)

    @pl.when((step < blocks) & is_video)
    def _():
        place = lax.broadcasted_iota(jnp.int32, (FRAME, FRAME), 0)
        bias = jnp.where(place <= TPF, 0.0, -1e30)
        for pair in range(0, width, 128):
            places = [slice(start + pair, start + pair + 128) for start in (0, width, 2 * width)]
            grads = attend_pair_back(
                projected_ref[:, places[0]],
                projected_ref[:, places[1]],
                projected_ref[:, places[2]],
                grad_ref[:, pair : pair + 128],
                bias,
            )
            for columns, values in zip(places, grads):
                pending[:, columns] = values.astype(jnp.bfloat16)

    @pl.when((step < blocks) & jnp.logical_not(is_video))
    def _():
        held[PRIOR:, :] = projected_ref[...]
        biases = []
        for query_start, query_count, key_start, key_count in SUB_BLOCKS:
            base = step * FRAME
            shape = (key_count, query_count)
            key_place = base + key_start + lax.broadcasted_iota(jnp.int32, shape, 0)
            query_place = base + query_start + lax.broadcasted_iota(jnp.int32, shape, 1)
            first = first_ref[0, :, query_start : query_start + query_count]
            allowed = (key_place >= first) & (key_place <= query_place)
            biases.append(jnp.where(allowed, 0.0, -1e30))
        for pair in range(0, width, 128):
            places = [slice(start + pair, start + pair + 128) for start in (0, width, 2 * width)]
            results = []
            for bias, block in zip(biases, SUB_BLOCKS):
                query_start, query_count, key_start, key_count = block
                key_rows = slice(PRIOR + key_start, PRIOR + key_start + key_count)
                query_rows = slice(query_start, query_start + query_count)
                grads = attend_pair_back(
                    projected_ref[query_rows, places[0]],
                    held[key_rows, places[1]],
                    held[key_rows, places[2]],
                    grad_ref[query_rows, pair : pair + 128],
                    bias,
                )
                pending[query_rows, places[0]] = grads[0].astype(jnp.bfloat16)
                results.append(grads[1:])
            for place in range(2):
                early, late = results[0][place], results[1][place]
                overlap = SUB_BLOCKS[1][2]
                reach = SUB_BLOCKS[0][1]
                columns = places[1 + place]
                own = jnp.concatenate(
                    [
                        early[PRIOR : PRIOR + overlap],
                        early[PRIOR + overlap :] + late[: reach - overlap],
                        late[reach - overlap :],
                    ],
                    axis=0,
                )
                add_prior(columns, early[:PRIOR])
                pending[:, columns] = own.astype(jnp.bfloat16)
                carry[:, columns] = own[FRAME - PRIOR :]
        held[0:PRIOR, :] = projected_ref[FRAME - PRIOR :, :]


def attend_back(flag, projected, grad_mixed, first):
    count, wide = projected.shape
    width = grad_mixed.shape[1]
    blocks = count // FRAME

    def ahead(i, _):
        return (jnp.minimum(i, blocks - 1), 0)

    return pl.pallas_call(
        attend_back_kernel,
        grid_spec=pltpu.PrefetchScalarGridSpec(
            num_scalar_prefetch=1,
            grid=(blocks + 1,),
            in_specs=[
                pl.BlockSpec((FRAME, wide), ahead),
                pl.BlockSpec((FRAME, width), ahead),
                pl.BlockSpec((1, 1, FRAME), lambda i, _: (jnp.minimum(i, blocks - 1), 0, 0)),
            ],
            out_specs=pl.BlockSpec((FRAME, wide), lambda i, _: (jnp.maximum(i - 1, 0), 0)),
            scratch_shapes=[
                pltpu.VMEM((FRAME + PRIOR, wide), jnp.bfloat16),
                pltpu.VMEM((FRAME, wide), jnp.bfloat16),
                pltpu.VMEM((PRIOR, wide), jnp.float32),
            ],
        ),
        out_shape=jax.ShapeDtypeStruct((count, wide), jnp.bfloat16),
        compiler_params=pltpu.CompilerParams(vmem_limit_bytes=VMEM_BYTES),
        name="attend_back",
    )(flag, projected, grad_mixed, first)


def qkv_weight_kernel(normed_ref, grad_ref, weight_ref, bias_ref):
    weight_ref[...] = product_tn(normed_ref[...], grad_ref[...]).astype(jnp.bfloat16)
    bias_ref[...] = column_sum(grad_ref[...].astype(jnp.float32))


def qkv_weight_grad(normed, grad, tile=768):
    count, width = normed.shape
    wide = grad.shape[1]
    return pl.pallas_call(
        qkv_weight_kernel,
        grid=(wide // tile,),
        in_specs=[whole(normed.shape), pl.BlockSpec((count, tile), lambda i: (0, i))],
        out_specs=[
            pl.BlockSpec((width, tile), lambda i: (0, i)),
            pl.BlockSpec((1, tile), lambda i: (0, i)),
        ],
        out_shape=[
            jax.ShapeDtypeStruct((width, wide), jnp.bfloat16),
            jax.ShapeDtypeStruct((1, wide), jnp.float32),
        ],
        compiler_params=pltpu.CompilerParams(vmem_limit_bytes=VMEM_BYTES),
        name="qkv_weight_grad",
    )(normed, grad)


def token_grad_kernel(
    frames, flag_ref, grad_ref, token_ref, message_ref, middle_ref, weight_ref, gain_ref, out_ref, vector_ref
):
    step = pl.program_id(0)
    is_video = flag_ref[0] == 0
    back = product_nt(grad_ref[...], weight_ref[...])
    parts = []
    for frame in range(frames):
        part = token_ref[frame * FRAME : (frame + 1) * FRAME, :].astype(jnp.float32)
        message = message_ref[pl.ds(step * frames + frame, 1), :]
        parts.append(with_message(part, is_video, message))
    unit, spread = norm_parts(jnp.concatenate(parts, axis=0))
    out_ref[...] = norm_back(unit, spread, gain_ref[...], back) + middle_ref[...].astype(jnp.float32)
    sums = jnp.concatenate([column_sum(back * unit), column_sum(back)], axis=0)

    @pl.when(step == 0)
    def _():
        vector_ref[...] = sums

    @pl.when(step > 0)
    def _():
        vector_ref[...] = vector_ref[...] + sums


def token_grad(flag, grad, tokens, message, grad_middle, weight, gain, frames=2):
    count, width = tokens.shape
    rows = frames * FRAME

    def by_rows(columns):
        return pl.BlockSpec((rows, columns), lambda i, _: (i, 0))

    return pl.pallas_call(
        functools.partial(token_grad_kernel, frames),
        grid_spec=pltpu.PrefetchScalarGridSpec(
            num_scalar_prefetch=1,
            grid=(count // rows,),
            in_specs=[
                by_rows(grad.shape[1]),
                by_rows(width),
                whole(message.shape),
                by_rows(width),
                whole(weight.shape),
                whole(gain.shape),
            ],
            out_specs=[by_rows(width), whole((2, width))],
        ),
        out_shape=[
            jax.ShapeDtypeStruct((count, width), jnp.float32),
            jax.ShapeDtypeStruct((2, width), jnp.float32),
        ],
        compiler_params=pltpu.CompilerParams(vmem_limit_bytes=VMEM_BYTES),
        name="token_grad",
    )(flag, grad, tokens, message, grad_middle, weight, gain)


def layer_norm(values, norm_gain, norm_shift):
    center = values - jnp.mean(values, axis=-1, keepdims=True)
    spread = lax.rsqrt(jnp.mean(center * center, axis=-1, keepdims=True) + 1e-05)
    return center * spread * norm_gain + norm_shift


def column_total(values):
    return jnp.sum(values.astype(jnp.float32), axis=0)


def soft_rows(scores):
    row_max = jnp.max(scores, axis=-1, keepdims=True)
    weights_exp = jnp.exp(scores - row_max)
    row_total = jnp.sum(weights_exp, axis=-1, keepdims=True)
    return (weights_exp / row_total, row_max + jnp.log(row_total))


def small_attend(query_rows, key_rows, value_rows, allowed):
    query_heads = query_rows.reshape(-1, HEADS, HD)
    key_heads = key_rows.reshape(-1, HEADS, HD)
    value_heads = value_rows.reshape(-1, HEADS, HD)
    scores = jnp.einsum(
        "qhe,khe->hqk", query_heads, key_heads, preferred_element_type=jnp.float32
    ) * HD ** (-0.5)
    soft_weights, log_total = soft_rows(jnp.where(allowed[None], scores, -1e30))
    mixed_heads = jnp.einsum(
        "hqk,khe->qhe",
        soft_weights.astype(jnp.bfloat16),
        value_heads,
        preferred_element_type=jnp.float32,
    )
    return (mixed_heads.reshape(query_rows.shape[0], -1).astype(jnp.bfloat16), soft_weights)


def small_attend_back(query_rows, key_rows, value_rows, soft_weights, grad_mixed):
    scale_value = HD ** (-0.5)
    query_heads = query_rows.reshape(-1, HEADS, HD)
    key_heads = key_rows.reshape(-1, HEADS, HD)
    value_heads = value_rows.reshape(-1, HEADS, HD)
    grad_heads = grad_mixed.reshape(-1, HEADS, HD)
    grad_soft = jnp.einsum(
        "qhe,khe->hqk", grad_heads, value_heads, preferred_element_type=jnp.float32
    )
    inner_sum = jnp.sum(soft_weights * grad_soft, axis=-1, keepdims=True)
    grad_scores = (soft_weights * (grad_soft - inner_sum)).astype(jnp.bfloat16)
    grad_query = (
        jnp.einsum("hqk,khe->qhe", grad_scores, key_heads, preferred_element_type=jnp.float32)
        * scale_value
    )
    grad_key = (
        jnp.einsum("hqk,qhe->khe", grad_scores, query_heads, preferred_element_type=jnp.float32)
        * scale_value
    )
    grad_value = jnp.einsum(
        "hqk,qhe->khe",
        soft_weights.astype(jnp.bfloat16),
        grad_heads,
        preferred_element_type=jnp.float32,
    )
    query_count = query_rows.shape[0]
    key_count = key_rows.shape[0]
    return (
        grad_query.reshape(query_count, -1),
        grad_key.reshape(key_count, -1),
        grad_value.reshape(key_count, -1),
    )


def side_open(source, side_params):
    start_rows = product(source, side_params[0]) + side_params[1]
    return (start_rows, layer_norm(start_rows, side_params[2], side_params[3]).astype(jnp.bfloat16))


def side_close(start_rows, grad_direct, grad_normed, side_params):
    unused_norm, norm_back = jax.vjp(layer_norm, start_rows, side_params[2], side_params[3])
    grad_start, grad_gain, grad_shift = norm_back(grad_normed)
    return ((grad_start + grad_direct).astype(jnp.bfloat16), grad_gain, grad_shift)


def video_side(source, frame_ids, side_params):
    model_width = source.shape[1]
    start_rows, normed = side_open(source, side_params)
    projected = product(normed, side_params[4]).astype(jnp.bfloat16)
    mixed_rows, soft_weights = small_attend(
        projected[:, :model_width],
        projected[:, model_width : 2 * model_width],
        projected[:, 2 * model_width :],
        frame_ids[:, None] == frame_ids[None, :],
    )
    message = start_rows + product(mixed_rows, side_params[5])
    return (message, (start_rows, normed, projected, mixed_rows, soft_weights))


def video_side_back(source, side_params, stored, grad_message):
    start_rows, normed, projected, mixed_rows, soft_weights = stored
    model_width = source.shape[1]
    grad_round = grad_message.astype(jnp.bfloat16)
    grad_mixed = product_nt(grad_round, side_params[5]).astype(jnp.bfloat16)
    grad_parts = small_attend_back(
        projected[:, :model_width],
        projected[:, model_width : 2 * model_width],
        projected[:, 2 * model_width :],
        soft_weights,
        grad_mixed,
    )
    grad_projected = jnp.concatenate(grad_parts, axis=1).astype(jnp.bfloat16)
    grad_start, grad_gain, grad_shift = side_close(
        start_rows,
        grad_round.astype(jnp.float32),
        product_nt(grad_projected, side_params[4]),
        side_params,
    )
    grad_source = product_nt(grad_start, side_params[0])
    rows = jnp.concatenate([grad_start, grad_projected, grad_round], axis=1)
    return (grad_source, rows, (column_total(grad_start), grad_gain, grad_shift))


def text_side(source, context, caption_ids, frame_ids, side_params):
    model_width = source.shape[1]
    start_rows, normed = side_open(source, side_params)
    query_rows = product(normed, side_params[4][:, :model_width]).astype(jnp.bfloat16)
    pair_rows = product(context, side_params[4][:, model_width:]).astype(jnp.bfloat16)
    mixed_rows, soft_weights = small_attend(
        query_rows,
        pair_rows[:, :model_width],
        pair_rows[:, model_width:],
        caption_ids[:, None] == frame_ids[None, :],
    )
    prompt = start_rows + product(mixed_rows, side_params[5])
    return (prompt, (start_rows, normed, query_rows, pair_rows, mixed_rows, soft_weights))


def text_side_back(source, side_params, stored, grad_prompt):
    start_rows, normed, query_rows, pair_rows, mixed_rows, soft_weights = stored
    model_width = source.shape[1]
    grad_round = grad_prompt.astype(jnp.bfloat16)
    grad_out_weight = product_tn(mixed_rows, grad_round)
    grad_mixed = product_nt(grad_round, side_params[5]).astype(jnp.bfloat16)
    grad_query, grad_key, grad_value = small_attend_back(
        query_rows, pair_rows[:, :model_width], pair_rows[:, model_width:], soft_weights, grad_mixed
    )
    grad_query = grad_query.astype(jnp.bfloat16)
    grad_start, grad_gain, grad_shift = side_close(
        start_rows,
        grad_round.astype(jnp.float32),
        product_nt(grad_query, side_params[4][:, :model_width]),
        side_params,
    )
    weights = [product_tn(source, grad_start), product_tn(normed, grad_query), grad_out_weight]
    return (
        product_nt(grad_start, side_params[0]),
        jnp.concatenate([grad_key, grad_value], axis=1),
        jnp.concatenate(weights, axis=1).astype(jnp.bfloat16),
        (column_total(grad_start), grad_gain, grad_shift),
    )


def pair_list(size, distance):
    return [(place, place ^ distance) for place in range(size)]


def group_pairs(size, distance, group):
    return [(group * size + place, group * size + (place ^ distance)) for place in range(size)]


def bit_count(size):
    return size.bit_length() - 1


def halve_scatter(parts, size, order, send):
    me = lax.axis_index("dp")
    bits = list(range(bit_count(size)))[::-1]
    view = parts.reshape((2,) * len(bits) + parts.shape[1:])
    for step, bit in enumerate(order):
        axis = bits.index(bit)
        bits.remove(bit)
        mine = (me >> bit) & 1
        keep = lax.dynamic_index_in_dim(view, mine, axis, keepdims=False)
        other = lax.dynamic_index_in_dim(view, 1 - mine, axis, keepdims=False)
        total = keep.astype(jnp.float32) + send(other, 1 << bit).astype(jnp.float32)
        view = total if step == len(order) - 1 else total.astype(parts.dtype)
    return view


def scatter_matrix(matrix, size):
    rows, columns = matrix.shape
    parts = matrix.astype(jnp.bfloat16).reshape(size, rows // size, columns)
    order = list(range(bit_count(size)))
    other = [1, 0] + order[2:]

    def send(values, distance):
        return lax.ppermute(values, "dp", pair_list(size, distance))

    half = columns // 2
    return jnp.concatenate(
        [
            halve_scatter(parts[:, :, :half], size, order, send),
            halve_scatter(parts[:, :, half:], size, other, send),
        ],
        axis=1,
    )


def double_gather(values, size, send):
    for bit in range(bit_count(size)):
        values = jnp.concatenate([values, send(values, 1 << bit)], axis=0)
    return values


def pad_frames(rows, is_video):
    frames = rows.shape[0] // TPF
    video = jnp.pad(rows.reshape(frames, TPF, -1), ((0, 0), (0, FRAME - TPF), (0, 0)))
    text = jnp.pad(rows, ((0, frames * (FRAME - TPF)), (0, 0)))
    return jnp.where(is_video, video.reshape(frames * FRAME, -1), text)


def trim_frames(rows, is_video):
    frames = rows.shape[0] // FRAME
    video = rows.reshape(frames, FRAME, -1)[:, :TPF].reshape(frames * TPF, -1)
    return jnp.where(is_video, video, rows[: frames * TPF])


def on_device(
    size,
    tokens,
    frame_video,
    caption_video,
    caption_len,
    attn_norm_gain,
    attn_norm_shift,
    qkv_weight,
    query_value_bias,
    proj_weight,
    proj_bias,
    mlp_norm_gain,
    mlp_norm_shift,
    fc_in_weight,
    fc_in_bias,
    fc_out_weight,
    fc_out_bias,
    side_in_weight,
    side_in_bias,
    side_norm_gain,
    side_norm_shift,
    side_qkv_weight,
    side_out_weight,
    cotangent,
):
    main_params = tuple(
        (
            member[0]
            for member in (
                attn_norm_gain,
                attn_norm_shift,
                qkv_weight,
                query_value_bias,
                proj_weight,
                proj_bias,
                mlp_norm_gain,
                mlp_norm_shift,
                fc_in_weight,
                fc_in_bias,
                fc_out_weight,
                fc_out_bias,
            )
        )
    )
    side_params = tuple(
        (
            member[0]
            for member in (
                side_in_weight,
                side_in_bias,
                side_norm_gain,
                side_norm_shift,
                side_qkv_weight,
                side_out_weight,
            )
        )
    )
    token_rows = tokens[0]
    cotangent_rows = cotangent[0]
    row_count, model_width = token_rows.shape
    frame_count = row_count // TPF
    me = lax.axis_index("dp")
    is_video = lax.axis_index("grp") == 0

    def to_text(values):
        return lax.ppermute(values, ("grp", "dp"), [(i, size + i) for i in range(size)])

    def to_video(values):
        return lax.ppermute(values, ("grp", "dp"), [(size + i, i) for i in range(size)])

    def in_all(values, distance):
        return lax.ppermute(values, "dp", pair_list(size, distance))

    def in_video(values, distance):
        return lax.ppermute(values, ("grp", "dp"), group_pairs(size, distance, 0))

    def in_text(values, distance):
        return lax.ppermute(values, ("grp", "dp"), group_pairs(size, distance, 1))

    frame_order = frame_video.reshape(size, frame_count)[me ^ jnp.arange(size)]
    frame_ids = frame_order[0]
    frame_order = frame_order.reshape(-1)
    source = token_rows.reshape(frame_count, TPF, model_width)[:, 0]
    message, side_stored = video_side(source, frame_ids, side_params)
    arrived = to_text(message.astype(jnp.bfloat16))
    packed = jnp.concatenate([arrived, source, side_stored[1], side_stored[3]], axis=1)
    packed = double_gather(packed, size, in_all)
    context = packed[:, :model_width]
    caption_ends = jnp.cumsum(caption_len[0]) - 1
    places = jnp.arange(frame_count * FRAME, dtype=jnp.int32)
    caption_starts = jnp.concatenate([caption_ends + 1 - caption_len[0], jnp.full((1,), row_count)])
    first = jnp.max(
        jnp.where(places[:, None] >= caption_starts[None, :], caption_starts[None, :], 0), axis=1
    ).astype(jnp.int32)
    flag = lax.axis_index("grp").astype(jnp.int32).reshape(1)
    bias = main_params[3]
    full_bias = jnp.concatenate(
        [bias[:model_width], jnp.zeros((model_width,), jnp.float32), bias[model_width:]]
    )
    params = tuple(
        (
            member if member.ndim == 2 else member[None]
            for member in main_params[:3] + (full_bias,) + main_params[4:]
        )
    )
    token_pad = pad_frames(token_rows, is_video)
    grad_pad = pad_frames(cotangent_rows, is_video)
    normed, projected, mixed, middle, normed_two, act, slope, block_rows = forward(
        flag, token_pad, message, first[:, None], params
    )

    def video_branch():
        vector = jnp.zeros((model_width,), jnp.float32)
        return (
            block_rows,
            grad_pad,
            jnp.zeros((model_width, 3 * model_width), jnp.bfloat16),
            jnp.zeros((context.shape[0], 2 * model_width), jnp.float32),
            (vector, vector, vector),
        )

    def text_branch():
        text_source = block_rows[caption_ends]
        prompt, text_stored = text_side(
            text_source, context, caption_video, frame_order, side_params
        )
        ends = (text_source.astype(jnp.float32) + prompt).astype(jnp.bfloat16)
        grad_ends = grad_pad[caption_ends].astype(jnp.float32)
        grad_source, grad_pair, side_grads, side_vectors = text_side_back(
            text_source, side_params, text_stored, grad_ends
        )
        return (
            block_rows.at[caption_ends].set(ends),
            grad_pad.at[caption_ends].set((grad_ends + grad_source).astype(jnp.bfloat16)),
            side_grads,
            grad_pair,
            side_vectors,
        )

    block_rows, grad_out, text_weights, grad_pair, text_vectors = lax.cond(
        is_video, video_branch, text_branch
    )
    out_rows = trim_frames(block_rows, is_video)
    grad_fc_out, grad_fc_out_bias = out_weight_grad(act, grad_out)
    grad_fc_out = scatter_matrix(grad_fc_out, size)
    grad_fc_in, grad_fc_in_bias, grad_middle, grad_mixed, grad_proj, middle_vectors = mlp_back(
        grad_out, slope, normed_two, middle, mixed, params[10], params[8], params[4], params[6]
    )
    grad_fc_in = scatter_matrix(grad_fc_in, size)
    grad_proj = scatter_matrix(grad_proj, size)
    grad_projected = attend_back(flag, projected, grad_mixed, first.reshape(frame_count, 1, FRAME))
    grad_qkv, bias_totals = qkv_weight_grad(normed, grad_projected)
    grad_qkv = scatter_matrix(grad_qkv, size)
    grad_pad_tokens, first_vectors = token_grad(
        flag, grad_projected, token_pad, message, grad_middle, params[2], params[0]
    )
    grad_tokens = trim_frames(grad_pad_tokens, is_video)
    grad_message = grad_pad_tokens.reshape(frame_count, FRAME, model_width)[:, TPF]
    bias_totals = bias_totals[0]
    grad_qv_bias = jnp.concatenate([bias_totals[:model_width], bias_totals[2 * model_width :]])
    grad_attn_gain, grad_attn_shift = first_vectors
    grad_mlp_gain, grad_mlp_shift, grad_proj_bias = middle_vectors
    grad_fc_in_bias = grad_fc_in_bias[0]
    grad_fc_out_bias = grad_fc_out_bias[0]
    for bit in range(bit_count(size)):
        distance = frame_count << bit
        lanes = grad_pair.reshape(-1, 2, distance, 2 * model_width)
        swapped = in_text(lanes[:, ::-1].reshape(grad_pair.shape).astype(jnp.bfloat16), 1 << bit)
        grad_pair = grad_pair + swapped.astype(jnp.float32)
    grad_pair = grad_pair.astype(jnp.bfloat16)
    received = to_video(product_nt(grad_pair[:frame_count], side_params[4][:, model_width:]))
    grad_source, grad_lines, video_vectors = video_side_back(
        source, side_params, side_stored, grad_message + received
    )
    class_rows = jnp.zeros((frame_count, TPF, model_width), jnp.float32).at[:, 0].set(grad_source)
    grad_tokens = grad_tokens + jnp.where(is_video, class_rows.reshape(row_count, model_width), 0.0)
    own_width = model_width // size
    grad_lines = double_gather(grad_lines, size, in_video)
    inputs = lax.dynamic_slice_in_dim(
        packed.reshape(-1, 4, model_width), me * own_width, own_width, 2
    )
    side_parts = halve_scatter(
        text_weights.reshape(size, own_width, 3 * model_width),
        size,
        list(range(bit_count(size))),
        in_text,
    )
    pair_part = product_tn(inputs[:, 0], grad_pair)
    grad_in_weight = jnp.where(
        is_video, product_tn(inputs[:, 1], grad_lines[:, :model_width]), side_parts[:, :model_width]
    )
    grad_side_qkv = jnp.where(
        is_video,
        product_tn(inputs[:, 2], grad_lines[:, model_width : 4 * model_width]),
        jnp.concatenate([side_parts[:, model_width : 2 * model_width], pair_part], axis=1),
    )
    grad_side_out = jnp.where(
        is_video,
        product_tn(inputs[:, 3], grad_lines[:, 4 * model_width :]),
        side_parts[:, 2 * model_width :],
    )
    side_vectors = tuple(
        (jnp.where(is_video, one, two) for one, two in zip(video_vectors, text_vectors))
    )
    vectors = (
        grad_attn_gain,
        grad_attn_shift,
        grad_qv_bias,
        grad_proj_bias,
        grad_mlp_gain,
        grad_mlp_shift,
        grad_fc_in_bias,
        grad_fc_out_bias,
    ) + side_vectors
    widths = [member.shape[0] // size for member in vectors]
    lines = jnp.concatenate([member.reshape(size, -1) for member in vectors], axis=1)
    line = halve_scatter(lines[:, None, :], size, list(range(bit_count(size))), in_all)[0]
    starts = [sum(widths[:place]) for place in range(len(widths))]
    (
        grad_attn_gain,
        grad_attn_shift,
        grad_qv_bias,
        grad_proj_bias,
        grad_mlp_gain,
        grad_mlp_shift,
        grad_fc_in_bias,
        grad_fc_out_bias,
        grad_in_bias,
        grad_side_gain,
        grad_side_shift,
    ) = [line[start : start + width] for start, width in zip(starts, widths)]
    summed = (
        grad_attn_gain,
        grad_attn_shift,
        grad_qkv,
        grad_qv_bias,
        grad_proj,
        grad_proj_bias,
        grad_mlp_gain,
        grad_mlp_shift,
        grad_fc_in,
        grad_fc_in_bias,
        grad_fc_out,
        grad_fc_out_bias,
        grad_in_weight,
        grad_in_bias,
        grad_side_gain,
        grad_side_shift,
        grad_side_qkv,
        grad_side_out,
    )
    return tuple([out_rows[None], grad_tokens[None]] + [member[None] for member in summed])


def solution(mesh):
    placed = (
        P("grp", "dp", None),
        P(),
        P("dp"),
        P("dp", None),
        P("grp", None),
        P("grp", None),
        P("grp", None, None),
        P("grp", None),
        P("grp", None, None),
        P("grp", None),
        P("grp", None),
        P("grp", None),
        P("grp", None, None),
        P("grp", None),
        P("grp", None, None),
        P("grp", None),
        P("grp", None, None),
        P("grp", None),
        P("grp", None),
        P("grp", None),
        P("grp", None, None),
        P("grp", None, None),
        P("grp", "dp", None),
    )
    return jax.shard_map(
        functools.partial(on_device, mesh.shape["dp"]),
        mesh=mesh,
        in_specs=placed,
        out_specs=(
            P("grp", "dp", None),
            P("grp", "dp", None),
            P("grp", "dp"),
            P("grp", "dp"),
            P("grp", "dp", None),
            P("grp", "dp"),
            P("grp", "dp", None),
            P("grp", "dp"),
            P("grp", "dp"),
            P("grp", "dp"),
            P("grp", "dp", None),
            P("grp", "dp"),
            P("grp", "dp", None),
            P("grp", "dp"),
            P("grp", "dp", None),
            P("grp", "dp"),
            P("grp", "dp"),
            P("grp", "dp"),
            P("grp", "dp", None),
            P("grp", "dp", None),
        ),
        check_vma=False,
    )
```

```python
import functools

import jax
import jax.numpy as jnp
from jax import lax
from jax.experimental import pallas as pl
from jax.experimental.pallas import tpu as pltpu
from jax.sharding import PartitionSpec as P

HEADS = 12
HD = 64
TPF = 197
FRAME = 208
PRIOR = 80
VMEM_BYTES = 58 * 2**20
SUB_BLOCKS = ((0, 112, -80, 192), (112, 96, 32, 176))


def product(left_side, right_side):
    return jnp.dot(left_side, right_side, preferred_element_type=jnp.float32)


def product_tn(left_side, right_side):
    return lax.dot_general(
        left_side, right_side, (((0,), (0,)), ((), ())), preferred_element_type=jnp.float32
    )


def product_nt(left_side, right_side):
    return lax.dot_general(
        left_side, right_side, (((1,), (1,)), ((), ())), preferred_element_type=jnp.float32
    )


def cost(flops, size):
    return pl.CostEstimate(flops=int(flops), bytes_accessed=int(size), transcendentals=0)


def split_shapes(size, rows, columns):
    return [
        jax.ShapeDtypeStruct((size // 2, rows // size, columns // 2), jnp.bfloat16) for _ in range(4)
    ]


def write_split(values, first_block, me, refs):
    send_left, keep_left, send_right, keep_right = refs
    block_rows, half = send_left.shape[1:]
    for place in range(values.shape[0] // block_rows):
        block = first_block + place
        rows = slice(place * block_rows, (place + 1) * block_rows)
        left = values[rows, :half]
        right = values[rows, half:]
        differs = block ^ me
        left_place = block >> 1
        right_place = ((block >> 2) << 1) | (block & 1)

        def put(condition, ref, index, part):
            @pl.when(condition)
            def _():
                ref[index] = part

        put((differs & 1) == 1, send_left, left_place, left)
        put((differs & 1) == 0, keep_left, left_place, left)
        put((differs & 2) == 2, send_right, right_place, right)
        put((differs & 2) == 0, keep_right, right_place, right)


def write_columns(values, step, me, refs):
    send_left, keep_left, send_right, keep_right = refs
    count, block_rows, half = send_left.shape
    tile = values.shape[1]
    per_half = half // tile
    columns = pl.ds(pl.multiple_of((step % per_half) * tile, tile), tile)

    def put(condition, ref, index, part):
        @pl.when(condition)
        def _():
            ref[index, :, columns] = part

    for block in range(2 * count):
        part = values[block * block_rows : (block + 1) * block_rows]
        differs = block ^ me
        left = step < per_half
        right = step >= per_half
        put(left & ((differs & 1) == 1), send_left, block >> 1, part)
        put(left & ((differs & 1) == 0), keep_left, block >> 1, part)
        place = ((block >> 2) << 1) | (block & 1)
        put(right & ((differs & 2) == 2), send_right, place, part)
        put(right & ((differs & 2) == 0), keep_right, place, part)


def combine_kernel(bits, me_ref, *refs):
    count = len(bits)
    sources, results = refs[: 2 * count], list(refs[2 * count :])
    for place, bit in enumerate(bits):
        keep, arrived = sources[2 * place], sources[2 * place + 1]

        def total(index):
            return keep[index].astype(jnp.float32) + arrived[index].astype(jnp.float32)

        if bit is None:
            columns = keep.shape[2]
            if place % 2 == 0:
                out = results.pop(0)
            out[:, (place % 2) * columns : (place % 2 + 1) * columns] = total(0)
        else:
            send, held = results.pop(0), results.pop(0)
            mine = (me_ref[0] >> bit) & 1
            for index in range(held.shape[0]):
                held[index] = total(2 * index + mine).astype(held.dtype)
                send[index] = total(2 * index + 1 - mine).astype(send.dtype)


def combine(me, streams):
    shapes, size = [], 0
    for place, (keep, arrived, bit) in enumerate(streams):
        size += 3 * keep.size * 2
        if bit is None:
            if place % 2 == 0:
                shapes.append(jax.ShapeDtypeStruct((keep.shape[1], 2 * keep.shape[2]), jnp.float32))
        else:
            half = jax.ShapeDtypeStruct((keep.shape[0] // 2,) + keep.shape[1:], keep.dtype)
            shapes += [half, half]
    operands = [value for keep, arrived, _ in streams for value in (keep, arrived)]
    return pl.pallas_call(
        functools.partial(combine_kernel, tuple(bit for _, _, bit in streams)),
        in_specs=[pl.BlockSpec(memory_space=pltpu.SMEM)]
        + [pl.BlockSpec(memory_space=pltpu.VMEM) for _ in operands],
        out_specs=[pl.BlockSpec(memory_space=pltpu.VMEM) for _ in shapes],
        out_shape=shapes,
        compiler_params=pltpu.CompilerParams(vmem_limit_bytes=VMEM_BYTES),
        cost_estimate=cost(size, size),
        name="combine",
    )(me, *operands)


def norm_parts(values):
    center = values - jnp.mean(values, axis=-1, keepdims=True)
    spread = lax.rsqrt(jnp.mean(center * center, axis=-1, keepdims=True) + 1e-05)
    return (center * spread, spread)


def norm_back(unit, spread, gain, grad):
    grad_unit = grad * gain
    first = jnp.mean(grad_unit, axis=-1, keepdims=True)
    second = jnp.mean(grad_unit * unit, axis=-1, keepdims=True)
    return spread * (grad_unit - first - unit * second)


def column_sum(values):
    return jnp.sum(values, axis=0, keepdims=True)


def lane_is_low(shape):
    return lax.broadcasted_iota(jnp.int32, shape, len(shape) - 1) < HD


def frame_start(is_video, frame):
    return jnp.where(is_video, TPF, FRAME) * frame


def load_rows(buffer, start):
    base = start // 16 * 16
    window = buffer[pl.ds(pl.multiple_of(base, 16), FRAME + 24), :].astype(jnp.float32)
    return pltpu.roll(window, (FRAME + 24 - (start - base)) % (FRAME + 24), axis=0)[:FRAME]


def store_rows(buffer, start, values):
    base = pl.multiple_of(start // 16 * 16, 16)
    pad = jnp.zeros((24, values.shape[1]), jnp.float32)
    moved = pltpu.roll(jnp.concatenate([values, pad], axis=0), start - base, axis=0)
    old = buffer[pl.ds(base, 16), :].astype(jnp.float32)
    place = lax.broadcasted_iota(jnp.int32, old.shape, 0)
    first = jnp.where(place < start - base, old, moved[:16])
    buffer[pl.ds(base, 16), :] = first.astype(buffer.dtype)
    buffer[pl.ds(base + 16, FRAME), :] = moved[16 : FRAME + 16].astype(buffer.dtype)


def frame_tail(rows, is_video, last_row):
    first = TPF // 8 * 8
    tail = rows[first:]
    place = lax.broadcasted_iota(jnp.int32, tail.shape, 0) + first
    video = jnp.where(place == TPF, last_row, jnp.where(place < TPF, tail, 0.0))
    return jnp.concatenate([rows[:first], jnp.where(is_video, video, tail)], axis=0)


def head_mask(shape, head):
    lane = lax.broadcasted_iota(jnp.int32, shape, len(shape) - 1)
    return (lane >= head * HD) & (lane < (head + 1) * HD)


def stack_heads(rows):
    zero = jnp.zeros_like(rows)
    return jnp.concatenate(
        [jnp.where(head_mask(rows.shape, head), rows, zero) for head in range(HEADS)], axis=0
    )


def pick_heads(stacked):
    count = stacked.shape[0] // HEADS
    total = jnp.zeros((count, stacked.shape[1]), jnp.float32)
    for head in range(HEADS):
        part = stacked[head * count : (head + 1) * count]
        total = total + jnp.where(head_mask(part.shape, head), part, 0.0)
    return total


def side_weights(query, key, allowed):
    stacked = stack_heads(query * jnp.asarray(HD**-0.5, query.dtype))
    bias = jnp.where(allowed, 0.0, -1e30)
    scores = product_nt(stacked, key) + jnp.concatenate([bias] * HEADS, axis=0)
    weights = jnp.exp(scores - jnp.max(scores, axis=-1, keepdims=True))
    return (stacked, weights / jnp.sum(weights, axis=-1, keepdims=True))


def side_attend(query, key, value, allowed):
    _, weights = side_weights(query, key, allowed)
    return pick_heads(product(weights.astype(jnp.bfloat16), value)).astype(jnp.bfloat16)


def side_attend_back(query, key, value, allowed, grad):
    stacked, weights = side_weights(query, key, allowed)
    grads = stack_heads(grad)
    grad_soft = product_nt(grads, value)
    inner = jnp.sum(weights * grad_soft, axis=-1, keepdims=True)
    grad_scores = (weights * (grad_soft - inner)).astype(jnp.bfloat16)
    return (
        pick_heads(product(grad_scores, key)) * HD**-0.5,
        product_tn(grad_scores, stacked),
        product_tn(weights.astype(jnp.bfloat16), grads),
    )


def attend_pair(query, key, value, bias):
    count = query.shape[0]
    low = lane_is_low(query.shape)
    query = query * jnp.asarray(HD**-0.5, query.dtype)
    zero = jnp.zeros_like(query)
    stacked = jnp.concatenate([jnp.where(low, query, zero), jnp.where(low, zero, query)], axis=0)
    scores = product_nt(stacked, key)
    weights = []
    for head in range(2):
        one = scores[head * count : (head + 1) * count] + bias
        weights.append(jnp.exp(one - jnp.max(one, axis=-1, keepdims=True)).astype(jnp.bfloat16))
    wide = jnp.concatenate([value, jnp.ones_like(value)], axis=1)
    summed = product(jnp.concatenate(weights, axis=0), wide)
    mixed = summed[:, :128] / summed[:, 128:]
    return jnp.where(low, mixed[:count], mixed[count:]).astype(jnp.bfloat16)


def attend_pair_back(query, key, value, grad, bias):
    count = key.shape[0]
    low = lane_is_low(key.shape)
    query = query * jnp.asarray(HD**-0.5, query.dtype)
    zero = jnp.zeros_like(key)
    keys = jnp.concatenate([jnp.where(low, key, zero), jnp.where(low, zero, key)], axis=0)
    values = jnp.concatenate([jnp.where(low, value, zero), jnp.where(low, zero, value)], axis=0)
    scores = product_nt(keys, query)
    grad_soft = product_nt(values, grad)
    soft_parts, grad_parts = [], []
    for head in range(2):
        one = scores[head * count : (head + 1) * count] + bias
        one = jnp.exp(one - jnp.max(one, axis=0, keepdims=True))
        soft = one * (1.0 / jnp.sum(one, axis=0, keepdims=True))
        inner = soft * grad_soft[head * count : (head + 1) * count]
        grad_parts.append((inner - soft * column_sum(inner)).astype(jnp.bfloat16))
        soft_parts.append(soft.astype(jnp.bfloat16))
    grad_scores = jnp.concatenate(grad_parts, axis=0)
    grad_value = product(jnp.concatenate(soft_parts, axis=0), grad)
    grad_key = product(grad_scores, query)
    grad_query = product_tn(grad_scores, keys) * HD**-0.5
    return (
        grad_query,
        jnp.where(low, grad_key[:count], grad_key[count:]),
        jnp.where(low, grad_value[:count], grad_value[count:]),
    )


def forward_kernel(
    frames,
    flag_ref,
    token_ref,
    message_ref,
    first_ref,
    gain_one,
    shift_one,
    qkv_weight,
    qkv_bias,
    proj_weight,
    proj_bias,
    gain_two,
    shift_two,
    fc_in_weight,
    fc_in_bias,
    fc_out_weight,
    fc_out_bias,
    normed_ref,
    projected_ref,
    mixed_ref,
    middle_ref,
    normed_two_ref,
    act_ref,
    slope_ref,
    hidden_ref,
    block_ref,
    held,
    source,
    target,
):
    step = pl.program_id(0)
    is_video = flag_ref[0] == 0
    count, width = token_ref.shape
    rows = frames * FRAME

    @pl.when(step == 0)
    def _():
        source[0:count, :] = token_ref[...]
        source[count:, :] = jnp.zeros((source.shape[0] - count, width), source.dtype)

    parts = []
    for frame in range(frames):
        part = load_rows(source, frame_start(is_video, step * frames + frame))
        message = message_ref[pl.ds(step * frames + frame, 1), :]
        parts.append(frame_tail(part, is_video, message))
    hidden = jnp.concatenate(parts, axis=0)
    hidden_ref[...] = hidden.astype(jnp.bfloat16)
    unit, _ = norm_parts(hidden)
    normed = (unit * gain_one[...] + shift_one[...]).astype(jnp.bfloat16)
    normed_ref[...] = normed

    @pl.when(step == 0)
    def _():
        held[0:PRIOR, :] = jnp.zeros((PRIOR, held.shape[1]), held.dtype)

    @pl.when(step > 0)
    def _():
        held[0:PRIOR, :] = held[rows : rows + PRIOR, :]

    for start in range(0, 3 * width, width):
        columns = slice(start, start + width)
        part = (product(normed, qkv_weight[:, columns]) + qkv_bias[:, columns]).astype(jnp.bfloat16)
        held[PRIOR:, columns] = part
        projected_ref[:, columns] = part

    def attend(frame, query_start, query_count, key_start, key_count, bias):
        query_rows = pl.ds(PRIOR + frame * FRAME + query_start, query_count)
        key_rows = pl.ds(PRIOR + frame * FRAME + key_start, key_count)
        for pair in range(0, width, 128):
            mixed_ref[pl.ds(frame * FRAME + query_start, query_count), pair : pair + 128] = attend_pair(
                held[query_rows, pair : pair + 128],
                held[key_rows, width + pair : width + pair + 128],
                held[key_rows, 2 * width + pair : 2 * width + pair + 128],
                bias,
            )

    @pl.when(is_video)
    def _():
        place = lax.broadcasted_iota(jnp.int32, (FRAME, FRAME), 1)
        bias = jnp.where(place <= TPF, 0.0, -1e30)
        for frame in range(frames):
            attend(frame, 0, FRAME, 0, FRAME, bias)

    @pl.when(jnp.logical_not(is_video))
    def _():
        for frame in range(frames):
            for query_start, query_count, key_start, key_count in SUB_BLOCKS:
                base = step * rows + frame * FRAME
                shape = (query_count, key_count)
                key_place = base + key_start + lax.broadcasted_iota(jnp.int32, shape, 1)
                query_place = base + query_start + lax.broadcasted_iota(jnp.int32, shape, 0)
                first = first_ref[pl.ds(frame * FRAME + query_start, query_count), :]
                allowed = (key_place >= first) & (key_place <= query_place)
                bias = jnp.where(allowed, 0.0, -1e30)
                attend(frame, query_start, query_count, key_start, key_count, bias)

    middle = hidden + product(mixed_ref[...], proj_weight[...]) + proj_bias[...]
    middle_ref[...] = middle.astype(jnp.bfloat16)
    unit, _ = norm_parts(middle)
    normed = (unit * gain_two[...] + shift_two[...]).astype(jnp.bfloat16)
    normed_two_ref[...] = normed
    total = middle + fc_out_bias[...]
    for start in range(0, fc_in_weight.shape[1], width):
        columns = slice(start, start + width)
        pre = product(normed, fc_in_weight[:, columns]) + fc_in_bias[:, columns]
        gate = 0.5 + 0.5 * jnp.tanh(0.851 * pre)
        value = pre * gate
        act = value.astype(jnp.bfloat16)
        act_ref[:, columns] = act
        slope_ref[:, columns] = (gate + 1.702 * value * (1.0 - gate)).astype(jnp.bfloat16)
        total = total + product(act, fc_out_weight[columns, :])
    for frame in range(frames):
        start = frame_start(is_video, step * frames + frame)
        store_rows(target, start, total[frame * FRAME : (frame + 1) * FRAME])

    @pl.when(step == pl.num_programs(0) - 1)
    def _():
        block_ref[...] = target[0:count, :]


def whole(shape):
    return pl.BlockSpec(
        shape, lambda *_: (0,) * len(shape), pipeline_mode=pl.Buffered(buffer_count=1)
    )


def forward(flag, tokens, message, first, params, frames=2):
    token_count, width = tokens.shape
    count = token_count // TPF * FRAME
    rows = frames * FRAME
    hidden = params[8].shape[1]

    def by_rows(columns):
        return pl.BlockSpec((rows, columns), lambda i, _: (i, 0))

    widths = (width, 3 * width, width, width, width, hidden, hidden, width)
    return pl.pallas_call(
        functools.partial(forward_kernel, frames),
        grid_spec=pltpu.PrefetchScalarGridSpec(
            num_scalar_prefetch=1,
            grid=(count // rows,),
            in_specs=[whole(tokens.shape), whole(message.shape), by_rows(1)]
            + [whole(member.shape) for member in params],
            out_specs=[by_rows(columns) for columns in widths] + [whole(tokens.shape)],
            scratch_shapes=[
                pltpu.VMEM((rows + PRIOR, 3 * width), jnp.bfloat16),
                pltpu.VMEM((count + 32, width), jnp.bfloat16),
                pltpu.VMEM((count + 32, width), jnp.bfloat16),
            ],
        ),
        out_shape=[jax.ShapeDtypeStruct((count, columns), jnp.bfloat16) for columns in widths]
        + [jax.ShapeDtypeStruct(tokens.shape, jnp.bfloat16)],
        compiler_params=pltpu.CompilerParams(vmem_limit_bytes=VMEM_BYTES),
        cost_estimate=cost(2 * count * width * (4 * width + 2 * hidden), 2 * count * sum(widths)),
        name="forward",
    )(flag, tokens, message, first, *params)


def out_weight_kernel(me_ref, act_ref, grad_ref, bias_ref, *weight_refs):
    step = pl.program_id(0)
    part = product_tn(act_ref[...], grad_ref[...]).astype(jnp.bfloat16)
    write_split(part, step * (part.shape[0] // weight_refs[0].shape[1]), me_ref[0], weight_refs)

    @pl.when(step == 0)
    def _():
        bias_ref[...] = column_sum(grad_ref[...].astype(jnp.float32))


def out_weight_grad(me, size, act, grad, tile=768):
    count, hidden = act.shape
    width = grad.shape[1]
    splits = split_shapes(size, hidden, width)
    return pl.pallas_call(
        out_weight_kernel,
        grid_spec=pltpu.PrefetchScalarGridSpec(
            num_scalar_prefetch=1,
            grid=(hidden // tile,),
            in_specs=[pl.BlockSpec((count, tile), lambda i, _: (0, i)), whole(grad.shape)],
            out_specs=[whole((1, width))] + [whole(split.shape) for split in splits],
        ),
        out_shape=[jax.ShapeDtypeStruct((1, width), jnp.float32)] + splits,
        compiler_params=pltpu.CompilerParams(vmem_limit_bytes=VMEM_BYTES),
        cost_estimate=cost(2 * count * hidden * width, 2 * count * hidden),
        name="out_weight_grad",
    )(me, act, grad)


def mlp_back_kernel(
    chunk,
    me_ref,
    grad_ref,
    slope_ref,
    normed_ref,
    middle_ref,
    mixed_ref,
    fc_out_weight,
    fc_in_weight,
    proj_weight,
    gain_ref,
    bias_ref,
    grad_middle_ref,
    grad_mixed_ref,
    vector_ref,
    *refs,
):
    in_refs, proj_refs, (grad_pre, total) = refs[:4], refs[4:8], refs[8:]
    step = pl.program_id(0)
    count = grad_ref.shape[0]
    bias = jnp.zeros(bias_ref.shape, jnp.float32)
    for start in range(0, count, chunk):
        rows = slice(start, start + chunk)
        part = product_nt(grad_ref[rows, :], fc_out_weight[...])
        part = (part * slope_ref[rows, :].astype(jnp.float32)).astype(jnp.bfloat16)
        grad_pre[rows, :] = part
        bias = bias + column_sum(part.astype(jnp.float32))
        back = product_nt(part, fc_in_weight[...])

        @pl.when(step == 0)
        def _():
            total[rows, :] = back

        @pl.when(step > 0)
        def _():
            total[rows, :] = total[rows, :] + back

    bias_ref[...] = bias
    part = product_tn(normed_ref[...], grad_pre[...]).astype(jnp.bfloat16)
    write_columns(part, step, me_ref[0], in_refs)

    @pl.when(step == pl.num_programs(0) - 1)
    def _():
        gain = gain_ref[...]
        width = gain.shape[1]
        sums = [jnp.zeros((1, width), jnp.float32) for _ in range(3)]
        for start in range(0, count, chunk):
            rows = slice(start, start + chunk)
            unit, spread = norm_parts(middle_ref[rows, :].astype(jnp.float32))
            back = total[rows, :]
            grad_middle = norm_back(unit, spread, gain, back) + grad_ref[rows, :].astype(jnp.float32)
            grad_middle = grad_middle.astype(jnp.bfloat16)
            grad_middle_ref[rows, :] = grad_middle
            grad_mixed_ref[rows, :] = product_nt(grad_middle, proj_weight[...]).astype(jnp.bfloat16)
            sums[0] = sums[0] + column_sum(back * unit)
            sums[1] = sums[1] + column_sum(back)
            sums[2] = sums[2] + column_sum(grad_middle.astype(jnp.float32))
        vector_ref[...] = jnp.concatenate(sums, axis=0)
        part = product_tn(mixed_ref[...], grad_middle_ref[...]).astype(jnp.bfloat16)
        write_split(part, 0, me_ref[0], proj_refs)


def mlp_back(me, size, grad, slope, normed, middle, mixed, fc_out_weight, fc_in_weight, proj_weight, gain, tile=768):
    count, width = grad.shape
    hidden = slope.shape[1]
    rows = (count, width)
    splits = split_shapes(size, width, hidden) + split_shapes(size, width, width)
    return pl.pallas_call(
        functools.partial(mlp_back_kernel, 2 * FRAME),
        grid_spec=pltpu.PrefetchScalarGridSpec(
            num_scalar_prefetch=1,
            grid=(hidden // tile,),
            in_specs=[
                whole(rows),
                pl.BlockSpec((count, tile), lambda i, _: (0, i)),
                whole(rows),
                whole(rows),
                whole(rows),
                pl.BlockSpec((tile, width), lambda i, _: (i, 0)),
                pl.BlockSpec((width, tile), lambda i, _: (0, i)),
                whole(proj_weight.shape),
                whole(gain.shape),
            ],
            out_specs=[
                pl.BlockSpec((1, tile), lambda i, _: (0, i)),
                whole(rows),
                whole(rows),
                whole((3, width)),
            ]
            + [whole(split.shape) for split in splits],
            scratch_shapes=[pltpu.VMEM((count, tile), jnp.bfloat16), pltpu.VMEM(rows, jnp.float32)],
        ),
        out_shape=[
            jax.ShapeDtypeStruct((1, hidden), jnp.float32),
            jax.ShapeDtypeStruct(rows, jnp.bfloat16),
            jax.ShapeDtypeStruct(rows, jnp.bfloat16),
            jax.ShapeDtypeStruct((3, width), jnp.float32),
        ]
        + splits,
        compiler_params=pltpu.CompilerParams(vmem_limit_bytes=VMEM_BYTES),
        cost_estimate=cost(2 * count * width * (3 * hidden + 2 * width), 2 * count * hidden),
        name="mlp_back",
    )(me, grad, slope, normed, middle, mixed, fc_out_weight, fc_in_weight, proj_weight, gain)


def attend_back_kernel(flag_ref, projected_ref, grad_ref, first_ref, out_ref, held, pending, carry):
    step = pl.program_id(0)
    blocks = pl.num_programs(0) - 1
    is_video = flag_ref[0] == 0
    width = grad_ref.shape[1]

    @pl.when(step == 0)
    def _():
        held[...] = jnp.zeros(held.shape, held.dtype)
        carry[...] = jnp.zeros(carry.shape, carry.dtype)

    @pl.when(step > 0)
    def _():
        out_ref[...] = pending[...]

    def add_prior(columns, values):
        rows = slice(FRAME - PRIOR, FRAME)
        out_ref[rows, columns] = (carry[:, columns] + values).astype(jnp.bfloat16)

    @pl.when((step < blocks) & is_video)
    def _():
        place = lax.broadcasted_iota(jnp.int32, (FRAME, FRAME), 0)
        bias = jnp.where(place <= TPF, 0.0, -1e30)
        for pair in range(0, width, 128):
            places = [slice(start + pair, start + pair + 128) for start in (0, width, 2 * width)]
            grads = attend_pair_back(
                projected_ref[:, places[0]],
                projected_ref[:, places[1]],
                projected_ref[:, places[2]],
                grad_ref[:, pair : pair + 128],
                bias,
            )
            for columns, values in zip(places, grads):
                pending[:, columns] = values.astype(jnp.bfloat16)

    @pl.when((step < blocks) & jnp.logical_not(is_video))
    def _():
        held[PRIOR:, :] = projected_ref[...]
        biases = []
        for query_start, query_count, key_start, key_count in SUB_BLOCKS:
            base = step * FRAME
            shape = (key_count, query_count)
            key_place = base + key_start + lax.broadcasted_iota(jnp.int32, shape, 0)
            query_place = base + query_start + lax.broadcasted_iota(jnp.int32, shape, 1)
            first = first_ref[0, :, query_start : query_start + query_count]
            allowed = (key_place >= first) & (key_place <= query_place)
            biases.append(jnp.where(allowed, 0.0, -1e30))
        for pair in range(0, width, 128):
            places = [slice(start + pair, start + pair + 128) for start in (0, width, 2 * width)]
            results = []
            for bias, block in zip(biases, SUB_BLOCKS):
                query_start, query_count, key_start, key_count = block
                key_rows = slice(PRIOR + key_start, PRIOR + key_start + key_count)
                query_rows = slice(query_start, query_start + query_count)
                grads = attend_pair_back(
                    projected_ref[query_rows, places[0]],
                    held[key_rows, places[1]],
                    held[key_rows, places[2]],
                    grad_ref[query_rows, pair : pair + 128],
                    bias,
                )
                pending[query_rows, places[0]] = grads[0].astype(jnp.bfloat16)
                results.append(grads[1:])
            for place in range(2):
                early, late = results[0][place], results[1][place]
                overlap = SUB_BLOCKS[1][2]
                reach = SUB_BLOCKS[0][1]
                columns = places[1 + place]
                own = jnp.concatenate(
                    [
                        early[PRIOR : PRIOR + overlap],
                        early[PRIOR + overlap :] + late[: reach - overlap],
                        late[reach - overlap :],
                    ],
                    axis=0,
                )
                add_prior(columns, early[:PRIOR])
                pending[:, columns] = own.astype(jnp.bfloat16)
                carry[:, columns] = own[FRAME - PRIOR :]
        held[0:PRIOR, :] = projected_ref[FRAME - PRIOR :, :]


def attend_back(flag, projected, grad_mixed, first):
    count, wide = projected.shape
    width = grad_mixed.shape[1]
    blocks = count // FRAME

    def ahead(i, _):
        return (jnp.minimum(i, blocks - 1), 0)

    return pl.pallas_call(
        attend_back_kernel,
        grid_spec=pltpu.PrefetchScalarGridSpec(
            num_scalar_prefetch=1,
            grid=(blocks + 1,),
            in_specs=[
                pl.BlockSpec((FRAME, wide), ahead),
                pl.BlockSpec((FRAME, width), ahead),
                pl.BlockSpec((1, 1, FRAME), lambda i, _: (jnp.minimum(i, blocks - 1), 0, 0)),
            ],
            out_specs=pl.BlockSpec((FRAME, wide), lambda i, _: (jnp.maximum(i - 1, 0), 0)),
            scratch_shapes=[
                pltpu.VMEM((FRAME + PRIOR, wide), jnp.bfloat16),
                pltpu.VMEM((FRAME, wide), jnp.bfloat16),
                pltpu.VMEM((PRIOR, wide), jnp.float32),
            ],
        ),
        out_shape=jax.ShapeDtypeStruct((count, wide), jnp.bfloat16),
        compiler_params=pltpu.CompilerParams(vmem_limit_bytes=VMEM_BYTES),
        cost_estimate=cost(2 * count * width * 5 * FRAME * 4, 4 * count * wide),
        name="attend_back",
    )(flag, projected, grad_mixed, first)


def qkv_weight_kernel(me_ref, normed_ref, grad_ref, bias_ref, *weight_refs):
    part = product_tn(normed_ref[...], grad_ref[...]).astype(jnp.bfloat16)
    write_columns(part, pl.program_id(0), me_ref[0], weight_refs)
    bias_ref[...] = column_sum(grad_ref[...].astype(jnp.float32))


def qkv_weight_grad(me, size, normed, grad, tile=384):
    count, width = normed.shape
    wide = grad.shape[1]
    splits = split_shapes(size, width, wide)
    return pl.pallas_call(
        qkv_weight_kernel,
        grid_spec=pltpu.PrefetchScalarGridSpec(
            num_scalar_prefetch=1,
            grid=(wide // tile,),
            in_specs=[whole(normed.shape), pl.BlockSpec((count, tile), lambda i, _: (0, i))],
            out_specs=[pl.BlockSpec((1, tile), lambda i, _: (0, i))]
            + [whole(split.shape) for split in splits],
        ),
        out_shape=[jax.ShapeDtypeStruct((1, wide), jnp.float32)] + splits,
        compiler_params=pltpu.CompilerParams(vmem_limit_bytes=VMEM_BYTES),
        cost_estimate=cost(2 * count * width * wide, 2 * count * wide),
        name="qkv_weight_grad",
    )(me, normed, grad)


def token_grad_kernel(
    frames, flag_ref, grad_ref, hidden_ref, middle_ref, source_ref, weight_ref, gain_ref, out_ref, vector_ref, target
):
    step = pl.program_id(0)
    is_video = flag_ref[0] == 0
    back = product_nt(grad_ref[...], weight_ref[...])
    unit, spread = norm_parts(hidden_ref[...].astype(jnp.float32))
    grads = norm_back(unit, spread, gain_ref[...], back) + middle_ref[...].astype(jnp.float32)
    for frame in range(frames):
        part = grads[frame * FRAME : (frame + 1) * FRAME]
        place = lax.broadcasted_iota(jnp.int32, (8, part.shape[1]), 0)
        extra = jnp.where(is_video & (place == 0), source_ref[pl.ds(step * frames + frame, 1), :], 0.0)
        part = jnp.concatenate([part[:8] + extra, part[8:]], axis=0)
        store_rows(target, frame_start(is_video, step * frames + frame), part)
    sums = jnp.concatenate([column_sum(back * unit), column_sum(back)], axis=0)

    @pl.when(step == 0)
    def _():
        vector_ref[...] = sums

    @pl.when(step > 0)
    def _():
        vector_ref[...] = vector_ref[...] + sums

    @pl.when(step == pl.num_programs(0) - 1)
    def _():
        out_ref[...] = target[0 : out_ref.shape[0], :]


def token_grad(flag, grad, hidden, grad_middle, grad_source, weight, gain, frames=2):
    count, width = hidden.shape
    rows = frames * FRAME
    tokens = (count // FRAME * TPF, width)

    def by_rows(columns):
        return pl.BlockSpec((rows, columns), lambda i, _: (i, 0))

    return pl.pallas_call(
        functools.partial(token_grad_kernel, frames),
        grid_spec=pltpu.PrefetchScalarGridSpec(
            num_scalar_prefetch=1,
            grid=(count // rows,),
            in_specs=[
                by_rows(grad.shape[1]),
                by_rows(width),
                by_rows(width),
                whole(grad_source.shape),
                whole(weight.shape),
                whole(gain.shape),
            ],
            out_specs=[whole(tokens), whole((2, width))],
            scratch_shapes=[pltpu.VMEM((count + 32, width), jnp.float32)],
        ),
        out_shape=[
            jax.ShapeDtypeStruct(tokens, jnp.float32),
            jax.ShapeDtypeStruct((2, width), jnp.float32),
        ],
        compiler_params=pltpu.CompilerParams(vmem_limit_bytes=VMEM_BYTES),
        cost_estimate=cost(2 * count * width * 3 * width, 4 * count * width),
        name="token_grad",
    )(flag, grad, hidden, grad_middle, grad_source, weight, gain)


def message_kernel(flag_ref, token_ref, ids_row, ids_column, in_weight, in_bias, gain, shift, qkv_weight, out_weight, message_ref, packed_ref, start_ref, projected_ref):
    frames, width = message_ref.shape

    @pl.when(flag_ref[0] == 0)
    def _():
        parts = []
        for frame in range(frames):
            row = frame * TPF
            base = row // 16 * 16
            tile = token_ref[base : base + 16, :].astype(jnp.float32)
            parts.append(tile[row - base : row - base + 1])
        source = jnp.concatenate(parts, axis=0).astype(jnp.bfloat16)
        start = product(source, in_weight[...]) + in_bias[...]
        unit, _ = norm_parts(start)
        normed = (unit * gain[...] + shift[...]).astype(jnp.bfloat16)
        projected = product(normed, qkv_weight[...]).astype(jnp.bfloat16)
        mixed = side_attend(
            projected[:, :width],
            projected[:, width : 2 * width],
            projected[:, 2 * width :],
            ids_column[...] == ids_row[...],
        )
        message = start + product(mixed, out_weight[...])
        message_ref[...] = message
        start_ref[...] = start
        projected_ref[...] = projected
        packed_ref[...] = jnp.concatenate([message.astype(jnp.bfloat16), source, normed, mixed], axis=1)

    @pl.when(flag_ref[0] != 0)
    def _():
        message_ref[...] = jnp.zeros(message_ref.shape, message_ref.dtype)
        packed_ref[...] = jnp.zeros(packed_ref.shape, packed_ref.dtype)
        start_ref[...] = jnp.zeros(start_ref.shape, start_ref.dtype)
        projected_ref[...] = jnp.zeros(projected_ref.shape, projected_ref.dtype)


def in_vmem(count):
    return [pl.BlockSpec(memory_space=pltpu.VMEM) for _ in range(count)]


def call_once(kernel, name, flops, scalars, operands, shapes):
    return pl.pallas_call(
        kernel,
        in_specs=[pl.BlockSpec(memory_space=pltpu.SMEM) for _ in scalars] + in_vmem(len(operands)),
        out_specs=in_vmem(len(shapes)),
        out_shape=[jax.ShapeDtypeStruct(shape, dtype) for shape, dtype in shapes],
        compiler_params=pltpu.CompilerParams(vmem_limit_bytes=VMEM_BYTES),
        cost_estimate=cost(flops, sum(value.size * 2 for value in operands)),
        name=name,
    )(*scalars, *operands)


def make_message(flag, tokens, frame_ids, side_params):
    frames = frame_ids.shape[0]
    width = tokens.shape[1]
    shapes = [
        ((frames, width), jnp.float32),
        ((frames, 4 * width), jnp.bfloat16),
        ((frames, width), jnp.float32),
        ((frames, 3 * width), jnp.bfloat16),
    ]
    operands = (tokens, frame_ids[None, :], frame_ids[:, None]) + side_params
    return call_once(message_kernel, "message", 1e10, (flag,), operands, shapes)


def prompt_kernel(
    flag_ref,
    me_ref,
    block_ref,
    cotangent_ref,
    context_ref,
    ends_column,
    caption_ids,
    frame_ids,
    in_weight,
    in_bias,
    gain,
    shift,
    qkv_weight,
    out_weight,
    out_ref,
    grad_out_ref,
    pair_ref,
    vector_ref,
    send_ref,
    keep_ref,
    padded,
):
    count, width = block_ref.shape
    frames = count // TPF
    is_video = flag_ref[0] == 0

    @pl.when(is_video)
    def _():
        out_ref[...] = block_ref[...]
        padded[0:count, :] = cotangent_ref[...]
        padded[count:, :] = jnp.zeros((padded.shape[0] - count, width), padded.dtype)
        for frame in range(frames):
            rows = load_rows(padded, frame * TPF)
            rows = frame_tail(rows, True, 0.0)
            grad_out_ref[frame * FRAME : (frame + 1) * FRAME, :] = rows.astype(jnp.bfloat16)
        vector_ref[...] = jnp.zeros(vector_ref.shape, vector_ref.dtype)

    @pl.when(jnp.logical_not(is_video))
    def _():
        captions = ends_column.shape[0]
        place = lax.broadcasted_iota(jnp.int32, (captions, count), 1)
        chosen = (place == ends_column[...]).astype(jnp.bfloat16)
        source = product(chosen, block_ref[...]).astype(jnp.bfloat16)
        grad_ends = product(chosen, cotangent_ref[...])
        start = product(source, in_weight[...]) + in_bias[...]
        unit, spread = norm_parts(start)
        normed = (unit * gain[...] + shift[...]).astype(jnp.bfloat16)
        query = product(normed, qkv_weight[:, :width]).astype(jnp.bfloat16)
        context = context_ref[:, :width]
        pair = product(context, qkv_weight[:, width:]).astype(jnp.bfloat16)
        key, value = pair[:, :width], pair[:, width:]
        allowed = caption_ids[...] == frame_ids[...]
        mixed = side_attend(query, key, value, allowed)
        prompt = start + product(mixed, out_weight[...])
        high = prompt.astype(jnp.bfloat16)
        lower = (prompt - high.astype(jnp.float32)).astype(jnp.bfloat16)
        added = product_tn(chosen, jnp.concatenate([high, lower], axis=1))
        added = added[:, :width] + added[:, width:]
        out_ref[...] = (block_ref[...].astype(jnp.float32) + added).astype(jnp.bfloat16)
        grad_round = grad_ends.astype(jnp.bfloat16)
        grad_mixed = product_nt(grad_round, out_weight[...]).astype(jnp.bfloat16)
        grad_query, grad_key, grad_value = side_attend_back(query, key, value, allowed, grad_mixed)
        grad_query = grad_query.astype(jnp.bfloat16)
        pair_ref[:, :width] = grad_key
        pair_ref[:, width:] = grad_value
        grad_normed = product_nt(grad_query, qkv_weight[:, :width])
        grad_start = norm_back(unit, spread, gain[...], grad_normed) + grad_round.astype(jnp.float32)
        grad_start = grad_start.astype(jnp.bfloat16)
        vector_ref[...] = jnp.concatenate(
            [
                column_sum(grad_start.astype(jnp.float32)),
                column_sum(grad_normed * unit),
                column_sum(grad_normed),
            ],
            axis=0,
        )
        grad_source = product_nt(grad_start, in_weight[...])
        added = product_tn(chosen, grad_source.astype(jnp.bfloat16))
        grad_out_ref[0:count, :] = (cotangent_ref[...].astype(jnp.float32) + added).astype(jnp.bfloat16)
        grad_out_ref[count:, :] = jnp.zeros((frames * FRAME - count, width), jnp.bfloat16)
        block_rows = send_ref.shape[1]
        mine = me_ref[0] & 1
        for third, (left, right) in enumerate(
            ((source, grad_start), (normed, grad_query), (mixed, grad_round))
        ):
            part = product_tn(left, right).astype(jnp.bfloat16)
            columns = slice(third * width, (third + 1) * width)
            for block in range(width // block_rows):
                rows = part[block * block_rows : (block + 1) * block_rows]

                @pl.when((block & 1) != mine)
                def _():
                    send_ref[block >> 1, :, columns] = rows

                @pl.when((block & 1) == mine)
                def _():
                    keep_ref[block >> 1, :, columns] = rows


def make_prompt(flag, me, size, block, cotangent, context, ends, caption_ids, frame_ids, side_params):
    count, width = block.shape
    padded = count // TPF * FRAME
    frames = context.shape[0]
    split = (size // 2, width // size, 3 * width)
    shapes = [
        ((count, width), jnp.bfloat16),
        ((padded, width), jnp.bfloat16),
        ((frames, 2 * width), jnp.float32),
        ((3, width), jnp.float32),
        (split, jnp.bfloat16),
        (split, jnp.bfloat16),
    ]
    spare = -ends.shape[0] % 16
    ends = jnp.pad(ends, (0, spare), constant_values=-1)[:, None]
    caption_ids = jnp.pad(caption_ids, (0, spare), constant_values=-1)[:, None]
    operands = (block, cotangent, context, ends, caption_ids, frame_ids[None, :]) + side_params
    return pl.pallas_call(
        prompt_kernel,
        in_specs=[pl.BlockSpec(memory_space=pltpu.SMEM)] * 2 + in_vmem(len(operands)),
        out_specs=in_vmem(len(shapes)),
        out_shape=[jax.ShapeDtypeStruct(shape, dtype) for shape, dtype in shapes],
        scratch_shapes=[pltpu.VMEM((padded + 32, width), jnp.bfloat16)],
        compiler_params=pltpu.CompilerParams(vmem_limit_bytes=VMEM_BYTES),
        cost_estimate=cost(1e10, 2 * count * width * 8),
        name="prompt",
    )(flag, me, *operands)


def message_back_kernel(frames, flag_ref, *refs):
    grads, middles, rest = refs[:frames], refs[frames : 2 * frames], refs[2 * frames :]
    (
        message_ref,
        received_ref,
        start_ref,
        projected_ref,
        ids_row,
        ids_column,
        main_weight,
        main_gain,
        in_weight,
        gain,
        qkv_weight,
        out_weight,
        source_ref,
        line_ref,
        vector_ref,
    ) = rest
    width = message_ref.shape[1]

    @pl.when(flag_ref[0] == 0)
    def _():
        row = TPF % 16
        grad = jnp.concatenate(
            [one[...].astype(jnp.float32)[row : row + 1] for one in grads], axis=0
        ).astype(jnp.bfloat16)
        middle = jnp.concatenate(
            [one[...].astype(jnp.float32)[row : row + 1] for one in middles], axis=0
        )
        unit, spread = norm_parts(message_ref[...])
        back = norm_back(unit, spread, main_gain[...], product_nt(grad, main_weight[...]))
        grad_round = (back + middle + received_ref[...]).astype(jnp.bfloat16)
        grad_mixed = product_nt(grad_round, out_weight[...]).astype(jnp.bfloat16)
        projected = projected_ref[...]
        grad_parts = side_attend_back(
            projected[:, :width],
            projected[:, width : 2 * width],
            projected[:, 2 * width :],
            ids_column[...] == ids_row[...],
            grad_mixed,
        )
        grad_projected = jnp.concatenate(grad_parts, axis=1).astype(jnp.bfloat16)
        unit, spread = norm_parts(start_ref[...])
        grad_normed = product_nt(grad_projected, qkv_weight[...])
        grad_start = norm_back(unit, spread, gain[...], grad_normed) + grad_round.astype(jnp.float32)
        grad_start = grad_start.astype(jnp.bfloat16)
        source_ref[...] = product_nt(grad_start, in_weight[...])
        line_ref[...] = jnp.concatenate([grad_start, grad_projected, grad_round], axis=1)
        vector_ref[...] = jnp.concatenate(
            [
                column_sum(grad_start.astype(jnp.float32)),
                column_sum(grad_normed * unit),
                column_sum(grad_normed),
            ],
            axis=0,
        )

    @pl.when(flag_ref[0] != 0)
    def _():
        source_ref[...] = jnp.zeros(source_ref.shape, source_ref.dtype)
        line_ref[...] = jnp.zeros(line_ref.shape, line_ref.dtype)
        vector_ref[...] = jnp.zeros(vector_ref.shape, vector_ref.dtype)


def message_back(flag, grad_projected, grad_middle, operands):
    width = grad_middle.shape[1]
    frames = grad_middle.shape[0] // FRAME
    shapes = [
        jax.ShapeDtypeStruct((frames, width), jnp.float32),
        jax.ShapeDtypeStruct((frames, 5 * width), jnp.bfloat16),
        jax.ShapeDtypeStruct((3, width), jnp.float32),
    ]

    def last_rows(columns):
        return [
            pl.BlockSpec(
                (16, columns),
                functools.partial(lambda place, *_: (place, 0), (frame * FRAME + TPF) // 16),
                pipeline_mode=pl.Buffered(buffer_count=1),
            )
            for frame in range(frames)
        ]

    return pl.pallas_call(
        functools.partial(message_back_kernel, frames),
        grid_spec=pltpu.PrefetchScalarGridSpec(
            num_scalar_prefetch=1,
            grid=(1,),
            in_specs=last_rows(3 * width)
            + last_rows(width)
            + [whole(value.shape) for value in operands],
            out_specs=[whole(shape.shape) for shape in shapes],
        ),
        out_shape=shapes,
        compiler_params=pltpu.CompilerParams(vmem_limit_bytes=VMEM_BYTES),
        cost_estimate=cost(1e10, 10**7),
        name="message_back",
    )(flag, *([grad_projected] * frames), *([grad_middle] * frames), *operands)


def side_weight_kernel(flag_ref, me_ref, packed_ref, line_ref, pair_ref, keep_ref, arrived_ref, in_ref, qkv_ref, out_ref):
    own, width = in_ref.shape

    def own_columns(place):
        part = packed_ref[:, place * width : (place + 1) * width].astype(jnp.float32)
        return pltpu.roll(part, (width - me_ref[0] * own) % width, axis=1)[:, :own].astype(jnp.bfloat16)

    @pl.when(flag_ref[0] == 0)
    def _():
        in_ref[...] = product_tn(own_columns(1), line_ref[:, :width])
        qkv_ref[...] = product_tn(own_columns(2), line_ref[:, width : 4 * width])
        out_ref[...] = product_tn(own_columns(3), line_ref[:, 4 * width :])

    @pl.when(flag_ref[0] != 0)
    def _():
        total = keep_ref[0].astype(jnp.float32) + arrived_ref[0].astype(jnp.float32)
        in_ref[...] = total[:, :width]
        qkv_ref[:, :width] = total[:, width : 2 * width]
        qkv_ref[:, width:] = product_tn(own_columns(0), pair_ref[...])
        out_ref[...] = total[:, 2 * width :]


def side_weight_grads(flag, me, size, packed, lines, pair, keep, arrived):
    width = packed.shape[1] // 4
    own = width // size
    shapes = [((own, width), jnp.float32), ((own, 3 * width), jnp.float32), ((own, width), jnp.float32)]
    operands = (packed, lines, pair, keep, arrived)
    return call_once(side_weight_kernel, "side_weight_grads", 1e9, (flag, me), operands, shapes)


def vector_kernel(size, widths, me_ref, line_ref, arrived_ref, *out_refs):
    start = 0
    for width, out_ref in zip(widths, out_refs):
        own = width // size
        columns = slice(start, start + width)
        total = line_ref[:, columns] + arrived_ref[:, columns]
        total = jnp.broadcast_to(total, (8, width))
        out_ref[...] = pltpu.roll(total, (width - me_ref[0] * own) % width, axis=1)[0:1, :own]
        start += width


def own_vectors(me, size, line, arrived, widths):
    shapes = [((1, width // size), jnp.float32) for width in widths]
    kernel = functools.partial(vector_kernel, size, tuple(widths))
    return call_once(kernel, "own_vectors", 1e6, (me,), (line, arrived), shapes)


def pair_list(size, distance):
    return [(place, place ^ distance) for place in range(size)]


def group_pairs(size, distance, group):
    return [(group * size + place, group * size + (place ^ distance)) for place in range(size)]


def bit_count(size):
    return size.bit_length() - 1


def gather_order(size):
    return list(range(bit_count(size)))[::-1]


def gathered_devices(me, size):
    places = jnp.arange(size)
    offsets = jnp.zeros((size,), jnp.int32)
    for step, bit in enumerate(gather_order(size)):
        offsets = offsets + (((places >> step) & 1) << bit)
    return me ^ offsets


def double_gather(values, size, send):
    for bit in gather_order(size):
        values = jnp.concatenate([values, send(values, 1 << bit)], axis=0)
    return values


class Halving:
    def __init__(self, keep, sent, order, send):
        self.keep, self.order, self.send = keep, list(order), send
        self.done = False
        self.launch(sent)

    def launch(self, sent):
        self.arrived = self.send(sent, 1 << self.order.pop(0))


def advance(me, streams, ready=None):
    streams = [one for one in streams if not one.done]
    streams = [one for one in streams if not one.order] + [one for one in streams if one.order]
    held, arrived, ready = lax.optimization_barrier(
        ([one.keep for one in streams], [one.arrived for one in streams], ready)
    )
    bits = [one.order[0] if one.order else None for one in streams]
    results = combine(me, list(zip(held, arrived, bits)))
    results, ready = lax.optimization_barrier((list(results), ready))
    for place, (one, bit) in enumerate(zip(streams, bits)):
        if bit is None:
            one.done = True
            if place % 2 == 0:
                one.result = results.pop(0)
        else:
            sent, one.keep = results.pop(0), results.pop(0)
            one.launch(sent)
    return ready


def on_device(
    size,
    tokens,
    frame_video,
    caption_video,
    caption_len,
    attn_norm_gain,
    attn_norm_shift,
    qkv_weight,
    query_value_bias,
    proj_weight,
    proj_bias,
    mlp_norm_gain,
    mlp_norm_shift,
    fc_in_weight,
    fc_in_bias,
    fc_out_weight,
    fc_out_bias,
    side_in_weight,
    side_in_bias,
    side_norm_gain,
    side_norm_shift,
    side_qkv_weight,
    side_out_weight,
    cotangent,
):
    main_params = tuple(
        (
            member[0]
            for member in (
                attn_norm_gain,
                attn_norm_shift,
                qkv_weight,
                query_value_bias,
                proj_weight,
                proj_bias,
                mlp_norm_gain,
                mlp_norm_shift,
                fc_in_weight,
                fc_in_bias,
                fc_out_weight,
                fc_out_bias,
            )
        )
    )
    side_params = tuple(
        (
            member[0]
            for member in (
                side_in_weight,
                side_in_bias,
                side_norm_gain,
                side_norm_shift,
                side_qkv_weight,
                side_out_weight,
            )
        )
    )
    token_rows = tokens[0]
    cotangent_rows = cotangent[0]
    row_count, model_width = token_rows.shape
    frame_count = row_count // TPF
    me = lax.axis_index("dp")
    is_video = lax.axis_index("grp") == 0

    def to_text(values):
        return lax.ppermute(values, ("grp", "dp"), [(i, size + i) for i in range(size)])

    def to_video(values):
        return lax.ppermute(values, ("grp", "dp"), [(size + i, i) for i in range(size)])

    def in_all(values, distance):
        return lax.ppermute(values, "dp", pair_list(size, distance))

    def in_video(values, distance):
        return lax.ppermute(values, ("grp", "dp"), group_pairs(size, distance, 0))

    def in_text(values, distance):
        return lax.ppermute(values, ("grp", "dp"), group_pairs(size, distance, 1))

    flag = lax.axis_index("grp").astype(jnp.int32).reshape(1)
    me_one = me.astype(jnp.int32).reshape(1)
    side_rows = tuple((member if member.ndim == 2 else member[None] for member in side_params))
    frame_order = frame_video.reshape(size, frame_count)[gathered_devices(me, size)]
    frame_ids = frame_order[0]
    message, packed, side_start, side_projected = make_message(
        flag, token_rows, frame_ids, side_rows
    )
    arrived = to_text(packed[:, :model_width])
    packed = jnp.concatenate([arrived, packed[:, model_width:]], axis=1)
    packed = double_gather(packed, size, in_all)
    caption_ends = jnp.cumsum(caption_len[0]) - 1
    places = jnp.arange(frame_count * FRAME, dtype=jnp.int32)
    caption_starts = jnp.concatenate([caption_ends + 1 - caption_len[0], jnp.full((1,), row_count)])
    first = jnp.max(
        jnp.where(places[:, None] >= caption_starts[None, :], caption_starts[None, :], 0), axis=1
    ).astype(jnp.int32)
    bias = main_params[3]
    full_bias = jnp.concatenate(
        [bias[:model_width], jnp.zeros((model_width,), jnp.float32), bias[model_width:]]
    )
    params = tuple(
        (
            member if member.ndim == 2 else member[None]
            for member in main_params[:3] + (full_bias,) + main_params[4:]
        )
    )
    normed, projected, mixed, middle, normed_two, act, slope, hidden, block_rows = forward(
        flag, token_rows, message, first[:, None], params
    )
    out_rows, grad_out, grad_pair, text_vectors, *parts = make_prompt(
        flag,
        me_one,
        size,
        block_rows,
        cotangent_rows,
        packed,
        caption_ends,
        caption_video,
        frame_order.reshape(-1),
        side_rows,
    )
    left_order = list(range(bit_count(size)))
    right_order = [1, 0] + left_order[2:]

    def two_streams(parts):
        send_left, keep_left, send_right, keep_right = parts
        return [
            Halving(keep_left, send_left, left_order, in_all),
            Halving(keep_right, send_right, right_order, in_all),
        ]

    side_stream = Halving(parts[1], parts[0], left_order, in_text)
    pair_steps = list(enumerate(gather_order(size)))

    def pair_send(values):
        step, bit = pair_steps[0]
        lanes = values.reshape(-1, 2, frame_count << step, 2 * model_width)
        return in_text(lanes[:, ::-1].reshape(values.shape).astype(jnp.bfloat16), 1 << bit)

    def pair_add(values, arrived, ready):
        values, arrived, ready = lax.optimization_barrier((values, arrived, ready))
        values = values + arrived.astype(jnp.float32)
        values, ready = lax.optimization_barrier((values, ready))
        pair_steps.pop(0)
        return (values, pair_send(values) if pair_steps else None, ready)

    pair_arrived = pair_send(grad_pair)
    grad_fc_out_bias, *parts = out_weight_grad(me_one, size, act, grad_out)
    out_streams = two_streams(parts)
    grad_pair, pair_arrived, grad_out = pair_add(grad_pair, pair_arrived, grad_out)
    grad_fc_in_bias, grad_middle, grad_mixed, middle_vectors, *parts = mlp_back(
        me_one, size, grad_out, slope, normed_two, middle, mixed, params[10], params[8], params[4], params[6]
    )
    in_streams = two_streams(parts[:4])
    proj_streams = two_streams(parts[4:])
    grad_pair, pair_arrived, grad_mixed = pair_add(grad_pair, pair_arrived, grad_mixed)
    grad_mixed = advance(me_one, out_streams + [side_stream], grad_mixed)
    grad_projected = attend_back(flag, projected, grad_mixed, first.reshape(frame_count, 1, FRAME))
    while pair_steps:
        grad_pair, pair_arrived, grad_projected = pair_add(grad_pair, pair_arrived, grad_projected)
    grad_projected = advance(
        me_one, out_streams + in_streams + proj_streams + [side_stream], grad_projected
    )
    grad_pair = grad_pair.astype(jnp.bfloat16)
    received = to_video(product_nt(grad_pair[:frame_count], side_params[4][:, model_width:]))
    bias_totals, *parts = qkv_weight_grad(me_one, size, normed, grad_projected)
    qkv_streams = two_streams(parts)
    grad_projected = advance(
        me_one, out_streams + in_streams + proj_streams + [side_stream], grad_projected
    )
    grad_source, grad_lines, video_vectors = message_back(
        flag,
        grad_projected,
        grad_middle,
        (message, received, side_start, side_projected, frame_ids[None, :], frame_ids[:, None])
        + (params[2], params[0], side_rows[0], side_rows[2], side_rows[4], side_rows[5]),
    )
    grad_source = advance(
        me_one, out_streams + in_streams + proj_streams + qkv_streams, grad_source
    )
    grad_tokens, first_vectors = token_grad(
        flag, grad_projected, hidden, grad_middle, grad_source, params[2], params[0]
    )
    grad_lines = double_gather(grad_lines, size, in_video)
    bias_totals = bias_totals[0]
    vectors = (
        first_vectors[0],
        first_vectors[1],
        jnp.concatenate([bias_totals[:model_width], bias_totals[2 * model_width :]]),
        middle_vectors[2],
        middle_vectors[0],
        middle_vectors[1],
        grad_fc_in_bias[0],
        grad_fc_out_bias[0],
    ) + tuple((video_vectors[place] + text_vectors[place] for place in range(3)))
    widths = [member.shape[0] for member in vectors]
    line = jnp.concatenate(vectors)[None]
    for bit in gather_order(size)[:-1]:
        line = line + in_all(line, 1 << bit)
    line_arrived = in_all(line, 1)
    streams = out_streams + in_streams + proj_streams + qkv_streams
    while not all(one.done for one in streams):
        advance(me_one, streams + ([side_stream] if side_stream.order else []))
    while side_stream.order:
        advance(me_one, [side_stream])
    grad_in_weight, grad_side_qkv, grad_side_out = side_weight_grads(
        flag, me_one, size, packed, grad_lines, grad_pair, side_stream.keep, side_stream.arrived
    )
    (
        grad_attn_gain,
        grad_attn_shift,
        grad_qv_bias,
        grad_proj_bias,
        grad_mlp_gain,
        grad_mlp_shift,
        grad_fc_in_bias,
        grad_fc_out_bias,
        grad_in_bias,
        grad_side_gain,
        grad_side_shift,
    ) = own_vectors(me_one, size, line, line_arrived, widths)
    summed = (
        grad_attn_gain,
        grad_attn_shift,
        qkv_streams[0].result[None],
        grad_qv_bias,
        proj_streams[0].result[None],
        grad_proj_bias,
        grad_mlp_gain,
        grad_mlp_shift,
        in_streams[0].result[None],
        grad_fc_in_bias,
        out_streams[0].result[None],
        grad_fc_out_bias,
        grad_in_weight[None],
        grad_in_bias,
        grad_side_gain,
        grad_side_shift,
        grad_side_qkv[None],
        grad_side_out[None],
    )
    return tuple([out_rows[None], grad_tokens[None]] + list(summed))


def solution(mesh):
    placed = (
        P("grp", "dp", None),
        P(),
        P("dp"),
        P("dp", None),
        P("grp", None),
        P("grp", None),
        P("grp", None, None),
        P("grp", None),
        P("grp", None, None),
        P("grp", None),
        P("grp", None),
        P("grp", None),
        P("grp", None, None),
        P("grp", None),
        P("grp", None, None),
        P("grp", None),
        P("grp", None, None),
        P("grp", None),
        P("grp", None),
        P("grp", None),
        P("grp", None, None),
        P("grp", None, None),
        P("grp", "dp", None),
    )
    return jax.shard_map(
        functools.partial(on_device, mesh.shape["dp"]),
        mesh=mesh,
        in_specs=placed,
        out_specs=(
            P("grp", "dp", None),
            P("grp", "dp", None),
            P("grp", "dp"),
            P("grp", "dp"),
            P("grp", "dp", None),
            P("grp", "dp"),
            P("grp", "dp", None),
            P("grp", "dp"),
            P("grp", "dp"),
            P("grp", "dp"),
            P("grp", "dp", None),
            P("grp", "dp"),
            P("grp", "dp", None),
            P("grp", "dp"),
            P("grp", "dp", None),
            P("grp", "dp"),
            P("grp", "dp"),
            P("grp", "dp"),
            P("grp", "dp", None),
            P("grp", "dp", None),
        ),
        check_vma=False,
    )
```

```python
import functools

import jax
import jax.numpy as jnp
from jax import lax
from jax.experimental import pallas as pl
from jax.experimental.pallas import tpu as pltpu
from jax.sharding import PartitionSpec as P

HEADS = 12
HD = 64
TPF = 197
FRAME = 208
PRIOR = 80
CHUNK = 384
VMEM_BYTES = 58 * 2**20
SUB_BLOCKS = ((0, 112, -80, 192), (112, 96, 32, 176))


def product(left_side, right_side):
    return jnp.dot(left_side, right_side, preferred_element_type=jnp.float32)


def product_tn(left_side, right_side):
    return lax.dot_general(
        left_side, right_side, (((0,), (0,)), ((), ())), preferred_element_type=jnp.float32
    )


def product_nt(left_side, right_side):
    return lax.dot_general(
        left_side, right_side, (((1,), (1,)), ((), ())), preferred_element_type=jnp.float32
    )


def cost(flops, size):
    return pl.CostEstimate(flops=int(flops), bytes_accessed=int(size), transcendentals=0)


def padded_rows(rows):
    return -(-rows // 16) * 16


def split_shapes(size, rows):
    return [jax.ShapeDtypeStruct((size // 2, rows, CHUNK), jnp.bfloat16) for _ in range(4)]


def store_block(stage, side, block, me, row, values):
    differs = block ^ me
    right = side == 1
    sent = jnp.where(right, (differs >> 1) & 1, differs & 1)
    place = jnp.where(right, ((block >> 2) << 1) | (block & 1), block >> 1)
    stage[side, sent, place, pl.ds(row, values.shape[0]), :] = values


def flush(stage, side, outs, sems):
    return [
        pltpu.make_async_copy(stage.at[side, sent], outs[2 * side + 1 - sent], sems.at[2 * side + sent])
        for sent in range(2)
    ]


def stage_shapes(size, rows):
    return [
        pltpu.VMEM((2, 2, size // 2, rows, CHUNK), jnp.bfloat16),
        pltpu.SemaphoreType.DMA((4,)),
    ]


def in_hbm(count):
    return [pl.BlockSpec(memory_space=pl.ANY) for _ in range(count)]


def combine_kernel(kinds, me_ref, *refs):
    refs = list(refs)
    sources = [[refs.pop(0) for _ in range(kind[1])] for kind in kinds]
    for (name, _, detail), parts in zip(kinds, sources):

        def total(side, index):
            keep, arrived = parts[2 * side], parts[2 * side + 1]
            return keep[index].astype(jnp.float32) + arrived[index].astype(jnp.float32)

        if name == "raw":
            refs.pop(0)[...] = total(0, 0)
        elif name == "add":
            refs.pop(0)[...] = parts[0][...] + parts[1][...]
        elif name == "stack":
            refs.pop(0)[...] = jnp.concatenate([parts[0][...], parts[1][...]], axis=0)
        elif name == "end":
            value = total(0, 0)
            half = value.shape[0] // 2
            start = 0
            for rows, chunks in detail:
                out = refs.pop(0)
                for side in range(2):
                    for chunk in range(chunks):
                        row = side * half + start + chunk * padded_rows(rows)
                        column = (side * chunks + chunk) * CHUNK
                        out[:, column : column + CHUNK] = value[row : row + rows]
                start += chunks * padded_rows(rows)
        else:
            send, held = refs.pop(0), refs.pop(0)
            mine = (me_ref[0] >> detail) & 1
            rows = parts[0].shape[1]
            for side in range(len(parts) // 2):
                place = slice(side * rows, (side + 1) * rows)
                for index in range(held.shape[0]):
                    held[index, place, :] = total(side, 2 * index + mine).astype(held.dtype)
                    send[index, place, :] = total(side, 2 * index + 1 - mine).astype(send.dtype)


def combine(me, items):
    shapes, kinds, operands = [], [], []
    for name, values, detail in items:
        kinds.append((name, len(values), detail))
        operands += values
        rows = values[0].shape[1]
        if name == "raw":
            shapes.append(jax.ShapeDtypeStruct((rows, CHUNK), jnp.float32))
        elif name in ("add", "stack"):
            times = 2 if name == "stack" else 1
            shape = (times * values[0].shape[0], values[0].shape[1])
            shapes.append(jax.ShapeDtypeStruct(shape, values[0].dtype))
        elif name == "end":
            for own, chunks in detail:
                shapes.append(jax.ShapeDtypeStruct((own, 2 * chunks * CHUNK), jnp.float32))
        else:
            sides = len(values) // 2
            half = (values[0].shape[0] // 2, sides * rows, CHUNK)
            shapes += [jax.ShapeDtypeStruct(half, jnp.bfloat16)] * 2
    size = 3 * sum(value.size for value in operands)
    return pl.pallas_call(
        functools.partial(combine_kernel, tuple(kinds)),
        in_specs=[pl.BlockSpec(memory_space=pltpu.SMEM)] + in_vmem(len(operands)),
        out_specs=in_vmem(len(shapes)),
        out_shape=shapes,
        compiler_params=pltpu.CompilerParams(vmem_limit_bytes=30 * 2**20),
        cost_estimate=cost(size, size),
        name="combine",
    )(me, *operands)


def in_vmem(count):
    return [pl.BlockSpec(memory_space=pltpu.VMEM) for _ in range(count)]


def norm_parts(values):
    center = values - jnp.mean(values, axis=-1, keepdims=True)
    spread = lax.rsqrt(jnp.mean(center * center, axis=-1, keepdims=True) + 1e-05)
    return (center * spread, spread)


def norm_back(unit, spread, gain, grad):
    grad_unit = grad * gain
    first = jnp.mean(grad_unit, axis=-1, keepdims=True)
    second = jnp.mean(grad_unit * unit, axis=-1, keepdims=True)
    return spread * (grad_unit - first - unit * second)


def column_sum(values):
    return jnp.sum(values, axis=0, keepdims=True)


def lane_is_low(shape):
    return lax.broadcasted_iota(jnp.int32, shape, len(shape) - 1) < HD


def frame_start(is_video, frame):
    return jnp.where(is_video, TPF, FRAME) * frame


def load_rows(buffer, start):
    base = start // 16 * 16
    window = buffer[pl.ds(pl.multiple_of(base, 16), FRAME + 24), :].astype(jnp.float32)
    return pltpu.roll(window, (FRAME + 24 - (start - base)) % (FRAME + 24), axis=0)[:FRAME]


def store_rows(buffer, start, values):
    base = pl.multiple_of(start // 16 * 16, 16)
    pad = jnp.zeros((24, values.shape[1]), jnp.float32)
    moved = pltpu.roll(jnp.concatenate([values, pad], axis=0), start - base, axis=0)
    old = buffer[pl.ds(base, 16), :].astype(jnp.float32)
    place = lax.broadcasted_iota(jnp.int32, old.shape, 0)
    first = jnp.where(place < start - base, old, moved[:16])
    buffer[pl.ds(base, 16), :] = first.astype(buffer.dtype)
    buffer[pl.ds(base + 16, FRAME), :] = moved[16 : FRAME + 16].astype(buffer.dtype)


def frame_tail(rows, is_video, last_row):
    first = TPF // 8 * 8
    tail = rows[first:]
    place = lax.broadcasted_iota(jnp.int32, tail.shape, 0) + first
    video = jnp.where(place == TPF, last_row, jnp.where(place < TPF, tail, 0.0))
    return jnp.concatenate([rows[:first], jnp.where(is_video, video, tail)], axis=0)


def head_mask(shape, head):
    lane = lax.broadcasted_iota(jnp.int32, shape, len(shape) - 1)
    return (lane >= head * HD) & (lane < (head + 1) * HD)


def stack_heads(rows):
    zero = jnp.zeros_like(rows)
    return jnp.concatenate(
        [jnp.where(head_mask(rows.shape, head), rows, zero) for head in range(HEADS)], axis=0
    )


def pick_heads(stacked):
    count = stacked.shape[0] // HEADS
    total = jnp.zeros((count, stacked.shape[1]), jnp.float32)
    for head in range(HEADS):
        part = stacked[head * count : (head + 1) * count]
        total = total + jnp.where(head_mask(part.shape, head), part, 0.0)
    return total


def side_weights(query, key, allowed):
    stacked = stack_heads(query * jnp.asarray(HD**-0.5, query.dtype))
    bias = jnp.where(allowed, 0.0, -1e30)
    scores = product_nt(stacked, key) + jnp.concatenate([bias] * HEADS, axis=0)
    weights = jnp.exp(scores - jnp.max(scores, axis=-1, keepdims=True))
    return (stacked, weights / jnp.sum(weights, axis=-1, keepdims=True))


def side_attend(query, key, value, allowed):
    _, weights = side_weights(query, key, allowed)
    return pick_heads(product(weights.astype(jnp.bfloat16), value)).astype(jnp.bfloat16)


def side_attend_back(query, key, value, allowed, grad):
    stacked, weights = side_weights(query, key, allowed)
    grads = stack_heads(grad)
    grad_soft = product_nt(grads, value)
    inner = jnp.sum(weights * grad_soft, axis=-1, keepdims=True)
    grad_scores = (weights * (grad_soft - inner)).astype(jnp.bfloat16)
    return (
        pick_heads(product(grad_scores, key)) * HD**-0.5,
        product_tn(grad_scores, stacked),
        product_tn(weights.astype(jnp.bfloat16), grads),
    )


def attend_pair(query, key, value, bias):
    count = query.shape[0]
    low = lane_is_low(query.shape)
    query = query * jnp.asarray(HD**-0.5, query.dtype)
    zero = jnp.zeros_like(query)
    stacked = jnp.concatenate([jnp.where(low, query, zero), jnp.where(low, zero, query)], axis=0)
    scores = product_nt(stacked, key)
    weights = []
    for head in range(2):
        one = scores[head * count : (head + 1) * count] + bias
        weights.append(jnp.exp(one - jnp.max(one, axis=-1, keepdims=True)).astype(jnp.bfloat16))
    wide = jnp.concatenate([value, jnp.ones_like(value)], axis=1)
    summed = product(jnp.concatenate(weights, axis=0), wide)
    mixed = summed[:, :128] / summed[:, 128:]
    return jnp.where(low, mixed[:count], mixed[count:]).astype(jnp.bfloat16)


def attend_pair_back(query, key, value, grad, bias):
    count = key.shape[0]
    low = lane_is_low(key.shape)
    query = query * jnp.asarray(HD**-0.5, query.dtype)
    zero = jnp.zeros_like(key)
    keys = jnp.concatenate([jnp.where(low, key, zero), jnp.where(low, zero, key)], axis=0)
    values = jnp.concatenate([jnp.where(low, value, zero), jnp.where(low, zero, value)], axis=0)
    scores = product_nt(keys, query)
    grad_soft = product_nt(values, grad)
    soft_parts, grad_parts = [], []
    for head in range(2):
        one = scores[head * count : (head + 1) * count] + bias
        one = jnp.exp(one - jnp.max(one, axis=0, keepdims=True))
        soft = one * (1.0 / jnp.sum(one, axis=0, keepdims=True))
        inner = soft * grad_soft[head * count : (head + 1) * count]
        grad_parts.append((inner - soft * column_sum(inner)).astype(jnp.bfloat16))
        soft_parts.append(soft.astype(jnp.bfloat16))
    grad_scores = jnp.concatenate(grad_parts, axis=0)
    grad_value = product(jnp.concatenate(soft_parts, axis=0), grad)
    grad_key = product(grad_scores, query)
    grad_query = product_tn(grad_scores, keys) * HD**-0.5
    return (
        grad_query,
        jnp.where(low, grad_key[:count], grad_key[count:]),
        jnp.where(low, grad_value[:count], grad_value[count:]),
    )


def forward_kernel(
    frames,
    flag_ref,
    token_ref,
    message_ref,
    first_ref,
    gain_one,
    shift_one,
    qkv_weight,
    qkv_bias,
    proj_weight,
    proj_bias,
    gain_two,
    shift_two,
    fc_in_weight,
    fc_in_bias,
    fc_out_weight,
    fc_out_bias,
    normed_ref,
    projected_ref,
    mixed_ref,
    middle_ref,
    normed_two_ref,
    act_ref,
    slope_ref,
    hidden_ref,
    block_ref,
    held,
    source,
    target,
):
    step = pl.program_id(0)
    is_video = flag_ref[0] == 0
    count, width = token_ref.shape
    rows = frames * FRAME

    @pl.when(step == 0)
    def _():
        source[0:count, :] = token_ref[...]
        source[count:, :] = jnp.zeros((source.shape[0] - count, width), source.dtype)

    parts = []
    for frame in range(frames):
        part = load_rows(source, frame_start(is_video, step * frames + frame))
        message = message_ref[pl.ds(step * frames + frame, 1), :]
        parts.append(frame_tail(part, is_video, message))
    hidden = jnp.concatenate(parts, axis=0)
    hidden_ref[...] = hidden.astype(jnp.bfloat16)
    unit, _ = norm_parts(hidden)
    normed = (unit * gain_one[...] + shift_one[...]).astype(jnp.bfloat16)
    normed_ref[...] = normed

    @pl.when(step == 0)
    def _():
        held[0:PRIOR, :] = jnp.zeros((PRIOR, held.shape[1]), held.dtype)

    @pl.when(step > 0)
    def _():
        held[0:PRIOR, :] = held[rows : rows + PRIOR, :]

    for start in range(0, 3 * width, width):
        columns = slice(start, start + width)
        part = (product(normed, qkv_weight[:, columns]) + qkv_bias[:, columns]).astype(jnp.bfloat16)
        held[PRIOR:, columns] = part
        projected_ref[:, columns] = part

    def attend(frame, query_start, query_count, key_start, key_count, bias):
        query_rows = pl.ds(PRIOR + frame * FRAME + query_start, query_count)
        key_rows = pl.ds(PRIOR + frame * FRAME + key_start, key_count)
        for pair in range(0, width, 128):
            mixed_ref[pl.ds(frame * FRAME + query_start, query_count), pair : pair + 128] = attend_pair(
                held[query_rows, pair : pair + 128],
                held[key_rows, width + pair : width + pair + 128],
                held[key_rows, 2 * width + pair : 2 * width + pair + 128],
                bias,
            )

    @pl.when(is_video)
    def _():
        place = lax.broadcasted_iota(jnp.int32, (FRAME, FRAME), 1)
        bias = jnp.where(place <= TPF, 0.0, -1e30)
        for frame in range(frames):
            attend(frame, 0, FRAME, 0, FRAME, bias)

    @pl.when(jnp.logical_not(is_video))
    def _():
        for frame in range(frames):
            for query_start, query_count, key_start, key_count in SUB_BLOCKS:
                base = step * rows + frame * FRAME
                shape = (query_count, key_count)
                key_place = base + key_start + lax.broadcasted_iota(jnp.int32, shape, 1)
                query_place = base + query_start + lax.broadcasted_iota(jnp.int32, shape, 0)
                first = first_ref[pl.ds(frame * FRAME + query_start, query_count), :]
                allowed = (key_place >= first) & (key_place <= query_place)
                bias = jnp.where(allowed, 0.0, -1e30)
                attend(frame, query_start, query_count, key_start, key_count, bias)

    middle = hidden + product(mixed_ref[...], proj_weight[...]) + proj_bias[...]
    middle_ref[...] = middle.astype(jnp.bfloat16)
    unit, _ = norm_parts(middle)
    normed = (unit * gain_two[...] + shift_two[...]).astype(jnp.bfloat16)
    normed_two_ref[...] = normed
    total = middle + fc_out_bias[...]
    for start in range(0, fc_in_weight.shape[1], width):
        columns = slice(start, start + width)
        pre = product(normed, fc_in_weight[:, columns]) + fc_in_bias[:, columns]
        gate = 0.5 + 0.5 * jnp.tanh(0.851 * pre)
        value = pre * gate
        act = value.astype(jnp.bfloat16)
        act_ref[:, columns] = act
        slope_ref[:, columns] = (gate + 1.702 * value * (1.0 - gate)).astype(jnp.bfloat16)
        total = total + product(act, fc_out_weight[columns, :])
    for frame in range(frames):
        start = frame_start(is_video, step * frames + frame)
        store_rows(target, start, total[frame * FRAME : (frame + 1) * FRAME])

    @pl.when(step == pl.num_programs(0) - 1)
    def _():
        block_ref[...] = target[0:count, :]


def whole(shape):
    return pl.BlockSpec(
        shape, lambda *_: (0,) * len(shape), pipeline_mode=pl.Buffered(buffer_count=1)
    )


def forward(flag, tokens, message, first, params, frames=2):
    token_count, width = tokens.shape
    count = token_count // TPF * FRAME
    rows = frames * FRAME
    hidden = params[8].shape[1]

    def by_rows(columns):
        return pl.BlockSpec((rows, columns), lambda i, _: (i, 0))

    widths = (width, 3 * width, width, width, width, hidden, hidden, width)
    return pl.pallas_call(
        functools.partial(forward_kernel, frames),
        grid_spec=pltpu.PrefetchScalarGridSpec(
            num_scalar_prefetch=1,
            grid=(count // rows,),
            in_specs=[whole(tokens.shape), whole(message.shape), by_rows(1)]
            + [whole(member.shape) for member in params],
            out_specs=[by_rows(columns) for columns in widths] + [whole(tokens.shape)],
            scratch_shapes=[
                pltpu.VMEM((rows + PRIOR, 3 * width), jnp.bfloat16),
                pltpu.VMEM((count + 32, width), jnp.bfloat16),
                pltpu.VMEM((count + 32, width), jnp.bfloat16),
            ],
        ),
        out_shape=[jax.ShapeDtypeStruct((count, columns), jnp.bfloat16) for columns in widths]
        + [jax.ShapeDtypeStruct(tokens.shape, jnp.bfloat16)],
        compiler_params=pltpu.CompilerParams(vmem_limit_bytes=VMEM_BYTES),
        cost_estimate=cost(2 * count * width * (4 * width + 2 * hidden), 2 * count * sum(widths)),
        name="forward",
    )(flag, tokens, message, first, *params)


def out_weight_kernel(me_ref, act_ref, grad_ref, bias_ref, *refs):
    outs, (stage, sems) = refs[:4], refs[4:]
    step = pl.program_id(0)
    rows = stage.shape[3]
    part = product_tn(act_ref[...], grad_ref[...]).astype(jnp.bfloat16)
    for index in range(part.shape[0] // rows):
        block = step * (part.shape[0] // rows) + index
        for side in range(2):
            values = part[index * rows : (index + 1) * rows, side * CHUNK : (side + 1) * CHUNK]
            store_block(stage, side, block, me_ref[0], 0, values)

    @pl.when(step == 0)
    def _():
        bias_ref[...] = column_sum(grad_ref[...].astype(jnp.float32))

    @pl.when(step == pl.num_programs(0) - 1)
    def _():
        copies = flush(stage, 0, outs, sems) + flush(stage, 1, outs, sems)
        for copy in copies:
            copy.start()
        for copy in copies:
            copy.wait()


def out_weight_grad(me, size, act, grad, tile=768):
    count, hidden = act.shape
    width = grad.shape[1]
    rows = hidden // size
    return pl.pallas_call(
        out_weight_kernel,
        grid_spec=pltpu.PrefetchScalarGridSpec(
            num_scalar_prefetch=1,
            grid=(hidden // tile,),
            in_specs=[pl.BlockSpec((count, tile), lambda i, _: (0, i)), whole(grad.shape)],
            out_specs=[whole((1, width))] + in_hbm(4),
            scratch_shapes=stage_shapes(size, rows),
        ),
        out_shape=[jax.ShapeDtypeStruct((1, width), jnp.float32)] + split_shapes(size, rows),
        compiler_params=pltpu.CompilerParams(vmem_limit_bytes=46 * 2**20),
        cost_estimate=cost(2 * count * hidden * width, 2 * count * hidden),
        name="out_weight_grad",
    )(me, act, grad)


def mlp_back_kernel(
    chunk,
    me_ref,
    grad_ref,
    slope_ref,
    normed_ref,
    middle_ref,
    mixed_ref,
    fc_out_weight,
    fc_in_weight,
    proj_weight,
    gain_ref,
    bias_ref,
    grad_middle_ref,
    grad_mixed_ref,
    vector_ref,
    *refs,
):
    outs, (grad_pre, total, stage, sems) = refs[:4], refs[4:]
    step = pl.program_id(0)
    count = grad_ref.shape[0]
    last = pl.num_programs(0) - 1

    def back_rows(index, bias):
        rows = pl.ds(pl.multiple_of(index * chunk, chunk), chunk)
        part = product_nt(grad_ref[rows, :], fc_out_weight[...])
        part = (part * slope_ref[rows, :].astype(jnp.float32)).astype(jnp.bfloat16)
        grad_pre[rows, :] = part
        back = product_nt(part, fc_in_weight[...])

        @pl.when(step == 0)
        def _():
            total[rows, :] = back

        @pl.when(step > 0)
        def _():
            total[rows, :] = total[rows, :] + back

        return bias + column_sum(part.astype(jnp.float32))

    bias = jnp.zeros(bias_ref.shape, jnp.float32)
    bias_ref[...] = lax.fori_loop(0, count // chunk, back_rows, bias)
    blocks = 2 * stage.shape[2]
    own = normed_ref.shape[1] // blocks
    spaced = padded_rows(own)
    per_half = (last + 1) // 2
    side = step // per_half
    chunks = grad_pre.shape[1] // CHUNK
    first_chunk = (step - side * per_half) * chunks

    def weight_columns(index, carry):
        columns = pl.ds(pl.multiple_of(index * CHUNK, CHUNK), CHUNK)
        part = product_tn(normed_ref[...], grad_pre[:, columns]).astype(jnp.bfloat16)
        row = pl.multiple_of((first_chunk + index) * spaced, 16)
        for block in range(blocks):
            values = part[block * own : (block + 1) * own]
            store_block(stage, side, block, me_ref[0], row, values)
        return carry

    lax.fori_loop(0, chunks, weight_columns, 0)

    @pl.when(step == last)
    def _():
        gain = gain_ref[...]

        def norm_rows(index, sums):
            rows = pl.ds(pl.multiple_of(index * chunk, chunk), chunk)
            unit, spread = norm_parts(middle_ref[rows, :].astype(jnp.float32))
            back = total[rows, :]
            grad_middle = norm_back(unit, spread, gain, back) + grad_ref[rows, :].astype(jnp.float32)
            grad_middle = grad_middle.astype(jnp.bfloat16)
            grad_middle_ref[rows, :] = grad_middle
            grad_mixed_ref[rows, :] = product_nt(grad_middle, proj_weight[...]).astype(jnp.bfloat16)
            parts = (back * unit, back, grad_middle.astype(jnp.float32))
            return tuple((one + column_sum(part) for one, part in zip(sums, parts)))

        empty = jnp.zeros(gain.shape, jnp.float32)
        sums = lax.fori_loop(0, count // chunk, norm_rows, (empty, empty, empty))
        vector_ref[...] = jnp.concatenate(sums, axis=0)
        part = product_tn(mixed_ref[...], grad_middle_ref[...]).astype(jnp.bfloat16)
        row = stage.shape[3] - spaced
        for block in range(blocks):
            for side in range(2):
                values = part[block * own : (block + 1) * own, side * CHUNK : (side + 1) * CHUNK]
                store_block(stage, side, block, me_ref[0], row, values)
        copies = flush(stage, 0, outs, sems) + flush(stage, 1, outs, sems)
        for copy in copies:
            copy.start()
        for copy in copies:
            copy.wait()


def mlp_back(me, size, grad, slope, normed, middle, mixed, fc_out_weight, fc_in_weight, proj_weight, gain, tile=768):
    count, width = grad.shape
    hidden = slope.shape[1]
    rows = (count, width)
    own = (hidden // (2 * CHUNK) + width // (2 * CHUNK)) * padded_rows(width // size)
    return pl.pallas_call(
        functools.partial(mlp_back_kernel, 2 * FRAME),
        grid_spec=pltpu.PrefetchScalarGridSpec(
            num_scalar_prefetch=1,
            grid=(hidden // tile,),
            in_specs=[
                whole(rows),
                pl.BlockSpec((count, tile), lambda i, _: (0, i)),
                whole(rows),
                whole(rows),
                whole(rows),
                pl.BlockSpec((tile, width), lambda i, _: (i, 0)),
                pl.BlockSpec((width, tile), lambda i, _: (0, i)),
                whole(proj_weight.shape),
                whole(gain.shape),
            ],
            out_specs=[
                pl.BlockSpec((1, tile), lambda i, _: (0, i)),
                whole(rows),
                whole(rows),
                whole((3, width)),
            ]
            + in_hbm(4),
            scratch_shapes=[pltpu.VMEM((count, tile), jnp.bfloat16), pltpu.VMEM(rows, jnp.float32)]
            + stage_shapes(size, own),
        ),
        out_shape=[
            jax.ShapeDtypeStruct((1, hidden), jnp.float32),
            jax.ShapeDtypeStruct(rows, jnp.bfloat16),
            jax.ShapeDtypeStruct(rows, jnp.bfloat16),
            jax.ShapeDtypeStruct((3, width), jnp.float32),
        ]
        + split_shapes(size, own),
        compiler_params=pltpu.CompilerParams(vmem_limit_bytes=50 * 2**20),
        cost_estimate=cost(2 * count * width * (3 * hidden + 2 * width), 2 * count * hidden),
        name="mlp_back",
    )(me, grad, slope, normed, middle, mixed, fc_out_weight, fc_in_weight, proj_weight, gain)


def attend_back_kernel(flag_ref, projected_ref, grad_ref, first_ref, out_ref, held, pending, carry):
    step = pl.program_id(0)
    blocks = pl.num_programs(0) - 1
    is_video = flag_ref[0] == 0
    width = grad_ref.shape[1]

    @pl.when(step == 0)
    def _():
        held[...] = jnp.zeros(held.shape, held.dtype)
        carry[...] = jnp.zeros(carry.shape, carry.dtype)

    @pl.when(step > 0)
    def _():
        out_ref[...] = pending[...]

    def add_prior(columns, values):
        rows = slice(FRAME - PRIOR, FRAME)
        out_ref[rows, columns] = (carry[:, columns] + values).astype(jnp.bfloat16)

    @pl.when((step < blocks) & is_video)
    def _():
        place = lax.broadcasted_iota(jnp.int32, (FRAME, FRAME), 0)
        bias = jnp.where(place <= TPF, 0.0, -1e30)
        for pair in range(0, width, 128):
            places = [slice(start + pair, start + pair + 128) for start in (0, width, 2 * width)]
            grads = attend_pair_back(
                projected_ref[:, places[0]],
                projected_ref[:, places[1]],
                projected_ref[:, places[2]],
                grad_ref[:, pair : pair + 128],
                bias,
            )
            for columns, values in zip(places, grads):
                pending[:, columns] = values.astype(jnp.bfloat16)

    @pl.when((step < blocks) & jnp.logical_not(is_video))
    def _():
        held[PRIOR:, :] = projected_ref[...]
        biases = []
        for query_start, query_count, key_start, key_count in SUB_BLOCKS:
            base = step * FRAME
            shape = (key_count, query_count)
            key_place = base + key_start + lax.broadcasted_iota(jnp.int32, shape, 0)
            query_place = base + query_start + lax.broadcasted_iota(jnp.int32, shape, 1)
            first = first_ref[0, :, query_start : query_start + query_count]
            allowed = (key_place >= first) & (key_place <= query_place)
            biases.append(jnp.where(allowed, 0.0, -1e30))
        for pair in range(0, width, 128):
            places = [slice(start + pair, start + pair + 128) for start in (0, width, 2 * width)]
            results = []
            for bias, block in zip(biases, SUB_BLOCKS):
                query_start, query_count, key_start, key_count = block
                key_rows = slice(PRIOR + key_start, PRIOR + key_start + key_count)
                query_rows = slice(query_start, query_start + query_count)
                grads = attend_pair_back(
                    projected_ref[query_rows, places[0]],
                    held[key_rows, places[1]],
                    held[key_rows, places[2]],
                    grad_ref[query_rows, pair : pair + 128],
                    bias,
                )
                pending[query_rows, places[0]] = grads[0].astype(jnp.bfloat16)
                results.append(grads[1:])
            for place in range(2):
                early, late = results[0][place], results[1][place]
                overlap = SUB_BLOCKS[1][2]
                reach = SUB_BLOCKS[0][1]
                columns = places[1 + place]
                own = jnp.concatenate(
                    [
                        early[PRIOR : PRIOR + overlap],
                        early[PRIOR + overlap :] + late[: reach - overlap],
                        late[reach - overlap :],
                    ],
                    axis=0,
                )
                add_prior(columns, early[:PRIOR])
                pending[:, columns] = own.astype(jnp.bfloat16)
                carry[:, columns] = own[FRAME - PRIOR :]
        held[0:PRIOR, :] = projected_ref[FRAME - PRIOR :, :]


def attend_back(flag, projected, grad_mixed, first):
    count, wide = projected.shape
    width = grad_mixed.shape[1]
    blocks = count // FRAME

    def ahead(i, _):
        return (jnp.minimum(i, blocks - 1), 0)

    return pl.pallas_call(
        attend_back_kernel,
        grid_spec=pltpu.PrefetchScalarGridSpec(
            num_scalar_prefetch=1,
            grid=(blocks + 1,),
            in_specs=[
                pl.BlockSpec((FRAME, wide), ahead),
                pl.BlockSpec((FRAME, width), ahead),
                pl.BlockSpec((1, 1, FRAME), lambda i, _: (jnp.minimum(i, blocks - 1), 0, 0)),
            ],
            out_specs=pl.BlockSpec((FRAME, wide), lambda i, _: (jnp.maximum(i - 1, 0), 0)),
            scratch_shapes=[
                pltpu.VMEM((FRAME + PRIOR, wide), jnp.bfloat16),
                pltpu.VMEM((FRAME, wide), jnp.bfloat16),
                pltpu.VMEM((PRIOR, wide), jnp.float32),
            ],
        ),
        out_shape=jax.ShapeDtypeStruct((count, wide), jnp.bfloat16),
        compiler_params=pltpu.CompilerParams(vmem_limit_bytes=46 * 2**20),
        cost_estimate=cost(2 * count * width * 5 * FRAME * 4, 4 * count * wide),
        name="attend_back",
    )(flag, projected, grad_mixed, first)


def two_terms(values):
    high = values.astype(jnp.bfloat16)
    return (high, (values - high.astype(jnp.float32)).astype(jnp.bfloat16))


def row_product(values, weight):
    spread = [jnp.broadcast_to(one, (8, one.shape[1])) for one in two_terms(values)]
    return (product_nt(spread[0], weight) + product_nt(spread[1], weight))[0:1]


def qkv_weight_kernel(me_ref, normed_ref, grad_ref, weight_ref, gain_ref, shift_ref, bias_ref, vector_ref, *refs):
    outs, (sums, stage, sems) = refs[:4], refs[4:]
    step = pl.program_id(0)
    last = pl.num_programs(0) - 1
    part = product_tn(normed_ref[...], grad_ref[...])
    bias = column_sum(grad_ref[...].astype(jnp.float32))
    bias_ref[...] = bias
    weight = weight_ref[...]
    shift = row_product(bias, weight)
    ones = jnp.ones((8, part.shape[1]), jnp.bfloat16)
    high, lower = two_terms(part * weight.astype(jnp.float32))
    scaled = (product_nt(ones, high) + product_nt(ones, lower))[0:1]
    both = jnp.concatenate([scaled, shift], axis=0)

    @pl.when(step == 0)
    def _():
        sums[...] = both

    @pl.when(step > 0)
    def _():
        sums[...] = sums[...] + both

    part = part.astype(jnp.bfloat16)
    blocks = 2 * stage.shape[2]
    rows = part.shape[0] // blocks
    per_half = (last + 1) // 2
    side = step // per_half
    row = pl.multiple_of((step - side * per_half) * padded_rows(rows), 16)
    for block in range(blocks):
        store_block(stage, side, block, me_ref[0], row, part[block * rows : (block + 1) * rows])

    @pl.when(step == last)
    def _():
        copies = flush(stage, 0, outs, sems) + flush(stage, 1, outs, sems)
        for copy in copies:
            copy.start()
        shift_total = sums[1:2, :]
        gain_total = (sums[0:1, :] - shift_ref[...] * shift_total) / gain_ref[...]
        vector_ref[...] = jnp.concatenate([gain_total, shift_total], axis=0)
        for copy in copies:
            copy.wait()


def qkv_weight_grad(me, size, normed, grad, weight, gain, shift):
    count, width = normed.shape
    wide = grad.shape[1]
    own = wide // (2 * CHUNK) * padded_rows(width // size)
    return pl.pallas_call(
        qkv_weight_kernel,
        grid_spec=pltpu.PrefetchScalarGridSpec(
            num_scalar_prefetch=1,
            grid=(wide // CHUNK,),
            in_specs=[
                whole(normed.shape),
                pl.BlockSpec((count, CHUNK), lambda i, _: (0, i)),
                pl.BlockSpec((width, CHUNK), lambda i, _: (0, i)),
                whole(gain.shape),
                whole(shift.shape),
            ],
            out_specs=[pl.BlockSpec((1, CHUNK), lambda i, _: (0, i)), whole((2, width))] + in_hbm(4),
            scratch_shapes=[pltpu.VMEM((2, width), jnp.float32)] + stage_shapes(size, own),
        ),
        out_shape=[
            jax.ShapeDtypeStruct((1, wide), jnp.float32),
            jax.ShapeDtypeStruct((2, width), jnp.float32),
        ]
        + split_shapes(size, own),
        compiler_params=pltpu.CompilerParams(vmem_limit_bytes=46 * 2**20),
        cost_estimate=cost(2 * count * width * wide, 2 * count * wide),
        name="qkv_weight_grad",
    )(me, normed, grad, weight, gain, shift)


def token_grad_kernel(
    frames, flag_ref, grad_ref, hidden_ref, middle_ref, source_ref, weight_ref, gain_ref, out_ref, target
):
    step = pl.program_id(0)
    is_video = flag_ref[0] == 0
    back = product_nt(grad_ref[...], weight_ref[...])
    unit, spread = norm_parts(hidden_ref[...].astype(jnp.float32))
    grads = norm_back(unit, spread, gain_ref[...], back) + middle_ref[...].astype(jnp.float32)
    for frame in range(frames):
        part = grads[frame * FRAME : (frame + 1) * FRAME]
        place = lax.broadcasted_iota(jnp.int32, (8, part.shape[1]), 0)
        extra = jnp.where(is_video & (place == 0), source_ref[pl.ds(step * frames + frame, 1), :], 0.0)
        part = jnp.concatenate([part[:8] + extra, part[8:]], axis=0)
        store_rows(target, frame_start(is_video, step * frames + frame), part)
    @pl.when(step == pl.num_programs(0) - 1)
    def _():
        out_ref[...] = target[0 : out_ref.shape[0], :]


def token_grad(flag, grad, hidden, grad_middle, grad_source, weight, gain, frames=2):
    count, width = hidden.shape
    rows = frames * FRAME
    tokens = (count // FRAME * TPF, width)

    def by_rows(columns):
        return pl.BlockSpec((rows, columns), lambda i, _: (i, 0))

    return pl.pallas_call(
        functools.partial(token_grad_kernel, frames),
        grid_spec=pltpu.PrefetchScalarGridSpec(
            num_scalar_prefetch=1,
            grid=(count // rows,),
            in_specs=[
                by_rows(grad.shape[1]),
                by_rows(width),
                by_rows(width),
                whole(grad_source.shape),
                whole(weight.shape),
                whole(gain.shape),
            ],
            out_specs=whole(tokens),
            scratch_shapes=[pltpu.VMEM((count + 32, width), jnp.float32)],
        ),
        out_shape=jax.ShapeDtypeStruct(tokens, jnp.float32),
        compiler_params=pltpu.CompilerParams(vmem_limit_bytes=46 * 2**20),
        cost_estimate=cost(2 * count * width * 3 * width, 4 * count * width),
        name="token_grad",
    )(flag, grad, hidden, grad_middle, grad_source, weight, gain)


def message_kernel(flag_ref, token_ref, ids_row, ids_column, in_weight, in_bias, gain, shift, qkv_weight, out_weight, message_ref, packed_ref, start_ref, projected_ref):
    frames, width = message_ref.shape

    @pl.when(flag_ref[0] == 0)
    def _():
        parts = []
        for frame in range(frames):
            row = frame * TPF
            base = row // 16 * 16
            tile = token_ref[base : base + 16, :].astype(jnp.float32)
            parts.append(tile[row - base : row - base + 1])
        source = jnp.concatenate(parts, axis=0).astype(jnp.bfloat16)
        start = product(source, in_weight[...]) + in_bias[...]
        unit, _ = norm_parts(start)
        normed = (unit * gain[...] + shift[...]).astype(jnp.bfloat16)
        projected = product(normed, qkv_weight[...]).astype(jnp.bfloat16)
        mixed = side_attend(
            projected[:, :width],
            projected[:, width : 2 * width],
            projected[:, 2 * width :],
            ids_column[...] == ids_row[...],
        )
        message = start + product(mixed, out_weight[...])
        message_ref[...] = message
        start_ref[...] = start
        projected_ref[...] = projected
        packed_ref[...] = jnp.concatenate([message.astype(jnp.bfloat16), source, normed, mixed], axis=1)

    @pl.when(flag_ref[0] != 0)
    def _():
        message_ref[...] = jnp.zeros(message_ref.shape, message_ref.dtype)
        packed_ref[...] = jnp.zeros(packed_ref.shape, packed_ref.dtype)
        start_ref[...] = jnp.zeros(start_ref.shape, start_ref.dtype)
        projected_ref[...] = jnp.zeros(projected_ref.shape, projected_ref.dtype)


def call_once(kernel, name, flops, scalars, operands, shapes):
    return pl.pallas_call(
        kernel,
        in_specs=[pl.BlockSpec(memory_space=pltpu.SMEM) for _ in scalars] + in_vmem(len(operands)),
        out_specs=in_vmem(len(shapes)),
        out_shape=[jax.ShapeDtypeStruct(shape, dtype) for shape, dtype in shapes],
        compiler_params=pltpu.CompilerParams(vmem_limit_bytes=VMEM_BYTES),
        cost_estimate=cost(flops, sum(value.size * 2 for value in operands)),
        name=name,
    )(*scalars, *operands)


def make_message(flag, tokens, frame_ids, side_params):
    frames = frame_ids.shape[0]
    width = tokens.shape[1]
    shapes = [
        ((frames, width), jnp.float32),
        ((frames, 4 * width), jnp.bfloat16),
        ((frames, width), jnp.float32),
        ((frames, 3 * width), jnp.bfloat16),
    ]
    operands = (tokens, frame_ids[None, :], frame_ids[:, None]) + side_params
    return call_once(message_kernel, "message", 1e10, (flag,), operands, shapes)


def prompt_kernel(
    flag_ref,
    me_ref,
    block_ref,
    cotangent_ref,
    context_ref,
    ends_column,
    caption_ids,
    frame_ids,
    in_weight,
    in_bias,
    gain,
    shift,
    qkv_weight,
    out_weight,
    out_ref,
    grad_out_ref,
    vector_ref,
    send_ref,
    keep_ref,
    padded,
):
    count, width = block_ref.shape
    frames = count // TPF
    is_video = flag_ref[0] == 0

    @pl.when(is_video)
    def _():
        out_ref[...] = block_ref[...]
        padded[0:count, :] = cotangent_ref[...]
        padded[count:, :] = jnp.zeros((padded.shape[0] - count, width), padded.dtype)
        for frame in range(frames):
            rows = load_rows(padded, frame * TPF)
            rows = frame_tail(rows, True, 0.0)
            grad_out_ref[frame * FRAME : (frame + 1) * FRAME, :] = rows.astype(jnp.bfloat16)
        vector_ref[...] = jnp.zeros(vector_ref.shape, vector_ref.dtype)

    @pl.when(jnp.logical_not(is_video))
    def _():
        captions = ends_column.shape[0]
        place = lax.broadcasted_iota(jnp.int32, (captions, count), 1)
        chosen = (place == ends_column[...]).astype(jnp.bfloat16)
        source = product(chosen, block_ref[...]).astype(jnp.bfloat16)
        grad_ends = product(chosen, cotangent_ref[...])
        start = product(source, in_weight[...]) + in_bias[...]
        unit, spread = norm_parts(start)
        normed = (unit * gain[...] + shift[...]).astype(jnp.bfloat16)
        query = product(normed, qkv_weight[:, :width]).astype(jnp.bfloat16)
        context = context_ref[:, :width]
        pair = product(context, qkv_weight[:, width:]).astype(jnp.bfloat16)
        key, value = pair[:, :width], pair[:, width:]
        allowed = caption_ids[...] == frame_ids[...]
        mixed = side_attend(query, key, value, allowed)
        prompt = start + product(mixed, out_weight[...])
        high = prompt.astype(jnp.bfloat16)
        lower = (prompt - high.astype(jnp.float32)).astype(jnp.bfloat16)
        added = product_tn(chosen, jnp.concatenate([high, lower], axis=1))
        added = added[:, :width] + added[:, width:]
        out_ref[...] = (block_ref[...].astype(jnp.float32) + added).astype(jnp.bfloat16)
        grad_round = grad_ends.astype(jnp.bfloat16)
        grad_mixed = product_nt(grad_round, out_weight[...]).astype(jnp.bfloat16)
        grad_query, grad_key, grad_value = side_attend_back(query, key, value, allowed, grad_mixed)
        grad_query = grad_query.astype(jnp.bfloat16)
        mine = (me_ref[0] >> 1) & 1

        def put(block, row, values):
            place = ((block >> 2) << 1) | (block & 1)
            values = values.astype(jnp.bfloat16)

            @pl.when(((block >> 1) & 1) != mine)
            def _():
                send_ref[place, row : row + values.shape[0], :] = values

            @pl.when(((block >> 1) & 1) == mine)
            def _():
                keep_ref[place, row : row + values.shape[0], :] = values

        blocks = 2 * send_ref.shape[0]
        own = context_ref.shape[0] // blocks
        chunks = width // CHUNK
        grad_pair = jnp.concatenate([grad_key, grad_value], axis=1)
        devices = gathered_offsets(blocks)
        for block in range(blocks):
            part = grad_pair[block * own : (block + 1) * own]
            parts = [part[:, chunk * CHUNK : (chunk + 1) * CHUNK] for chunk in range(2 * chunks)]
            put(devices[block] ^ me_ref[0], send_ref.shape[1] - 2 * chunks * own, jnp.concatenate(parts, axis=0))
        grad_normed = product_nt(grad_query, qkv_weight[:, :width])
        grad_start = norm_back(unit, spread, gain[...], grad_normed) + grad_round.astype(jnp.float32)
        grad_start = grad_start.astype(jnp.bfloat16)
        vector_ref[...] = jnp.concatenate(
            [
                column_sum(grad_start.astype(jnp.float32)),
                column_sum(grad_normed * unit),
                column_sum(grad_normed),
            ],
            axis=0,
        )
        grad_source = product_nt(grad_start, in_weight[...])
        added = product_tn(chosen, grad_source.astype(jnp.bfloat16))
        grad_out_ref[0:count, :] = (cotangent_ref[...].astype(jnp.float32) + added).astype(jnp.bfloat16)
        grad_out_ref[count:, :] = jnp.zeros((frames * FRAME - count, width), jnp.bfloat16)
        rows = width // blocks
        for third, (left, right) in enumerate(
            ((source, grad_start), (normed, grad_query), (mixed, grad_round))
        ):
            part = product_tn(left, right).astype(jnp.bfloat16)
            for chunk in range(chunks):
                row = (third * chunks + chunk) * padded_rows(rows)
                columns = slice(chunk * CHUNK, (chunk + 1) * CHUNK)
                for block in range(blocks):
                    put(block, row, part[block * rows : (block + 1) * rows, columns])


def make_prompt(flag, me, size, block, cotangent, context, ends, caption_ids, frame_ids, side_params):
    count, width = block.shape
    padded = count // TPF * FRAME
    chunks = width // CHUNK
    rows = 3 * chunks * padded_rows(width // size) + 2 * chunks * (context.shape[0] // size)
    split = (size // 2, rows, CHUNK)
    shapes = [
        ((count, width), jnp.bfloat16),
        ((padded, width), jnp.bfloat16),
        ((3, width), jnp.float32),
        (split, jnp.bfloat16),
        (split, jnp.bfloat16),
    ]
    spare = -ends.shape[0] % 16
    ends = jnp.pad(ends, (0, spare), constant_values=-1)[:, None]
    caption_ids = jnp.pad(caption_ids, (0, spare), constant_values=-1)[:, None]
    operands = (block, cotangent, context, ends, caption_ids, frame_ids[None, :]) + side_params
    return pl.pallas_call(
        prompt_kernel,
        in_specs=[pl.BlockSpec(memory_space=pltpu.SMEM)] * 2 + in_vmem(len(operands)),
        out_specs=in_vmem(len(shapes)),
        out_shape=[jax.ShapeDtypeStruct(shape, dtype) for shape, dtype in shapes],
        scratch_shapes=[pltpu.VMEM((padded + 32, width), jnp.bfloat16)],
        compiler_params=pltpu.CompilerParams(vmem_limit_bytes=VMEM_BYTES),
        cost_estimate=cost(1e10, 2 * count * width * 8),
        name="prompt",
    )(flag, me, *operands)


def message_back_kernel(frames, flag_ref, *refs):
    grads, middles, rest = refs[:frames], refs[frames : 2 * frames], refs[2 * frames :]
    (
        message_ref,
        received_ref,
        start_ref,
        projected_ref,
        ids_row,
        ids_column,
        main_weight,
        main_gain,
        in_weight,
        gain,
        qkv_weight,
        out_weight,
        pair_ref,
        source_ref,
        line_ref,
    ) = rest
    width = message_ref.shape[1]

    @pl.when(flag_ref[0] == 0)
    def _():
        row = TPF % 16
        grad = jnp.concatenate(
            [one[...].astype(jnp.float32)[row : row + 1] for one in grads], axis=0
        ).astype(jnp.bfloat16)
        middle = jnp.concatenate(
            [one[...].astype(jnp.float32)[row : row + 1] for one in middles], axis=0
        )
        unit, spread = norm_parts(message_ref[...])
        back = norm_back(unit, spread, main_gain[...], product_nt(grad, main_weight[...]))
        grad_round = (back + middle + received_ref[...]).astype(jnp.bfloat16)
        grad_mixed = product_nt(grad_round, out_weight[...]).astype(jnp.bfloat16)
        projected = projected_ref[...]
        grad_parts = side_attend_back(
            projected[:, :width],
            projected[:, width : 2 * width],
            projected[:, 2 * width :],
            ids_column[...] == ids_row[...],
            grad_mixed,
        )
        grad_projected = jnp.concatenate(grad_parts, axis=1).astype(jnp.bfloat16)
        unit, spread = norm_parts(start_ref[...])
        grad_normed = product_nt(grad_projected, qkv_weight[...])
        grad_start = norm_back(unit, spread, gain[...], grad_normed) + grad_round.astype(jnp.float32)
        grad_start = grad_start.astype(jnp.bfloat16)
        source_ref[...] = product_nt(grad_start, in_weight[...])
        line_ref[...] = jnp.concatenate([grad_start, grad_projected, grad_round], axis=1)

    @pl.when(flag_ref[0] != 0)
    def _():
        source_ref[...] = jnp.zeros(source_ref.shape, source_ref.dtype)
        line_ref[:, : 2 * width] = pair_ref[...]
        line_ref[:, 2 * width :] = jnp.zeros((line_ref.shape[0], 3 * width), line_ref.dtype)


def message_back(flag, grad_projected, grad_middle, operands):
    width = grad_middle.shape[1]
    frames = grad_middle.shape[0] // FRAME
    shapes = [
        jax.ShapeDtypeStruct((frames, width), jnp.float32),
        jax.ShapeDtypeStruct((frames, 5 * width), jnp.bfloat16),
    ]

    def last_rows(columns):
        return [
            pl.BlockSpec(
                (16, columns),
                functools.partial(lambda place, *_: (place, 0), (frame * FRAME + TPF) // 16),
                pipeline_mode=pl.Buffered(buffer_count=1),
            )
            for frame in range(frames)
        ]

    return pl.pallas_call(
        functools.partial(message_back_kernel, frames),
        grid_spec=pltpu.PrefetchScalarGridSpec(
            num_scalar_prefetch=1,
            grid=(1,),
            in_specs=last_rows(3 * width)
            + last_rows(width)
            + [whole(value.shape) for value in operands],
            out_specs=[whole(shape.shape) for shape in shapes],
        ),
        out_shape=shapes,
        compiler_params=pltpu.CompilerParams(vmem_limit_bytes=46 * 2**20),
        cost_estimate=cost(1e10, 10**7),
        name="message_back",
    )(flag, *([grad_projected] * frames), *([grad_middle] * frames), *operands)


def pair_kernel(flag_ref, side_ref, weight_ref, *refs):
    vectors, (pair_ref, context_ref, line_ref) = refs[:-3], refs[-3:]
    rows, width = context_ref.shape
    start = 0
    for place, one in enumerate(vectors):
        for row in range(one.shape[0]):
            line_ref[:, start : start + one.shape[1]] = one[row : row + 1, :]
            start += one.shape[1]
    chunks = pair_ref.shape[1] // CHUNK
    first = side_ref.shape[0] - chunks * rows

    @pl.when(flag_ref[0] != 0)
    def _():
        parts = [side_ref[first + rows * chunk : first + rows * (chunk + 1), :] for chunk in range(chunks)]
        pair = jnp.concatenate(parts, axis=1).astype(jnp.bfloat16)
        pair_ref[...] = pair
        context_ref[...] = product_nt(pair, weight_ref[:, width:])

    @pl.when(flag_ref[0] == 0)
    def _():
        pair_ref[...] = jnp.zeros(pair_ref.shape, pair_ref.dtype)
        context_ref[...] = jnp.zeros(context_ref.shape, context_ref.dtype)


def pair_grad(flag, side, weight, frames, vectors):
    width = weight.shape[0]
    shapes = [
        ((frames, 2 * width), jnp.bfloat16),
        ((frames, width), jnp.float32),
        ((1, sum(one.size for one in vectors)), jnp.float32),
    ]
    return call_once(pair_kernel, "pair_grad", 1e9, (flag,), (side, weight) + vectors, shapes)


def side_weight_kernel(
    flag_ref,
    me_ref,
    packed_ref,
    line_ref,
    side_ref,
    weight_ref,
    gain_ref,
    shift_ref,
    in_ref,
    qkv_ref,
    out_ref,
    vector_ref,
):
    own, width = in_ref.shape

    def own_columns(place):
        part = packed_ref[:, place * width : (place + 1) * width].astype(jnp.float32)
        return pltpu.roll(part, (width - me_ref[0] * own) % width, axis=1)[:, :own].astype(jnp.bfloat16)

    @pl.when(flag_ref[0] == 0)
    def _():
        in_ref[...] = product_tn(own_columns(1), line_ref[:, :width])
        qkv_ref[...] = product_tn(own_columns(2), line_ref[:, width : 4 * width])
        out_ref[...] = product_tn(own_columns(3), line_ref[:, 4 * width :])
        lines = line_ref[...].astype(jnp.float32)
        vector_ref[0:1, :] = column_sum(lines[:, :width])
        unit = packed_ref[:, 2 * width : 3 * width].astype(jnp.float32) - shift_ref[...]
        grad_normed = product_nt(line_ref[:, width : 4 * width], weight_ref[...])
        vector_ref[1:2, :] = column_sum(grad_normed * unit) / gain_ref[...]
        vector_ref[2:3, :] = column_sum(grad_normed)

    @pl.when(flag_ref[0] != 0)
    def _():
        chunks = width // CHUNK
        spaced = padded_rows(own)

        def matrix(third):
            rows = [(third * chunks + chunk) * spaced for chunk in range(chunks)]
            return jnp.concatenate([side_ref[row : row + own, :] for row in rows], axis=1)

        in_ref[...] = matrix(0)
        qkv_ref[:, :width] = matrix(1)
        qkv_ref[:, width:] = product_tn(own_columns(0), line_ref[:, : 2 * width])
        out_ref[...] = matrix(2)
        vector_ref[...] = jnp.zeros(vector_ref.shape, vector_ref.dtype)


def side_weight_grads(flag, me, size, packed, lines, side, weight, gain, shift):
    width = packed.shape[1] // 4
    own = width // size
    shapes = [
        ((own, width), jnp.float32),
        ((own, 3 * width), jnp.float32),
        ((own, width), jnp.float32),
        ((3, width), jnp.float32),
    ]
    operands = (packed, lines, side, weight, gain, shift)
    return call_once(side_weight_kernel, "side_weight_grads", 1e9, (flag, me), operands, shapes)


def vector_kernel(size, widths, flag_ref, me_ref, line_ref, side_ref, *out_refs):
    start = 0
    third = out_refs[0].shape[1] * size
    for place, (width, out_ref) in enumerate(zip(widths, out_refs)):
        total = line_ref[:, start : start + width]
        start += width
        if place == 2:
            total = jnp.concatenate([total[:, :third], total[:, 2 * third :]], axis=1)
            width = 2 * third
        own = width // size
        side = place - (len(widths) - 3)
        if side >= 0:
            total = jnp.where(flag_ref[0] == 0, side_ref[side : side + 1, :], total)
        total = jnp.broadcast_to(total, (8, width))
        out_ref[...] = pltpu.roll(total, (width - me_ref[0] * own) % width, axis=1)[0:1, :own]


def own_vectors(flag, me, size, line, side, widths):
    shapes = [((1, width // size), jnp.float32) for width in widths]
    shapes[2] = ((1, 2 * widths[0] // size), jnp.float32)
    kernel = functools.partial(vector_kernel, size, tuple(widths))
    return call_once(kernel, "own_vectors", 1e6, (flag, me), (line, side), shapes)


def pair_list(size, distance):
    return [(place, place ^ distance) for place in range(size)]


def group_pairs(size, distance, group):
    return [(group * size + place, group * size + (place ^ distance)) for place in range(size)]


def bit_count(size):
    return size.bit_length() - 1


def gather_order(size):
    return list(range(bit_count(size)))[::-1]


def gathered_offsets(size):
    return [
        sum((((place >> step) & 1) << bit for step, bit in enumerate(gather_order(size))))
        for place in range(size)
    ]


def gathered_devices(me, size):
    return me ^ jnp.array(gathered_offsets(size), jnp.int32)


def double_gather(values, size, send):
    for bit in gather_order(size):
        values = jnp.concatenate([values, send(values, 1 << bit)], axis=0)
    return values


class Sum:
    def __init__(self, size, send, parts, layout):
        self.send, self.layout = send, layout
        self.bits = list(range(2, bit_count(size)))
        self.orders = [[0, 1], [1, 0]]
        self.keeps, self.arrived = [], []
        for side in range(2):
            self.launch(parts[2 * side], parts[2 * side + 1], self.orders[side].pop(0))

    def launch(self, sent, kept, bit):
        self.keeps.append(kept)
        self.arrived.append(self.send(sent, 1 << bit))

    def values(self):
        return [value for pair in zip(self.keeps, self.arrived) for value in pair]

    def items(self):
        values = self.values()
        if self.orders[0]:
            return [("split", values[2 * side : 2 * side + 2], self.orders[side][0]) for side in range(2)]
        if self.bits:
            return [("split", values, self.bits[0])]
        return [("end", values, self.layout)]

    def take(self, results):
        self.keeps, self.arrived = [], []
        if self.orders[0]:
            for side in range(2):
                self.launch(results.pop(0), results.pop(0), self.orders[side].pop(0))
        elif self.bits:
            self.launch(results.pop(0), results.pop(0), self.bits.pop(0))
        else:
            self.result = [results.pop(0) for _ in self.layout]


class PlainSum:
    def __init__(self, size, send, sent, kept):
        self.send, self.kept = send, kept
        self.bits = [bit for bit in range(bit_count(size)) if bit != 1]
        self.arrived = send(sent, 2)

    def items(self):
        if self.bits:
            return [("split", [self.kept, self.arrived], self.bits[0])]
        return [("raw", [self.kept, self.arrived], None)]

    def take(self, results):
        if self.bits:
            sent, self.kept = results.pop(0), results.pop(0)
            self.arrived = self.send(sent, 1 << self.bits.pop(0))
        else:
            self.result = results.pop(0)


class Spread:
    def __init__(self, size, send, values, kind):
        self.kind, self.send, self.held = kind, send, values
        self.bits = gather_order(size)
        self.arrived = send(values, 1 << self.bits.pop(0))

    def items(self):
        return [(self.kind, [self.held, self.arrived], None)]

    def take(self, results):
        self.held = results.pop(0)
        if self.bits:
            self.arrived = self.send(self.held, 1 << self.bits.pop(0))
        else:
            self.result = self.held


def tie(first, second):
    return lax.optimization_barrier((first, second))


def advance(me, streams, after, before=None):
    streams = [one for one in streams if not hasattr(one, "result")]
    if not streams:
        return (after, before)
    items = [one.items() for one in streams]
    flat = [item for one in items for item in one]
    operands, after = tie([item[1] for item in flat], after)
    results = combine(me, [(item[0], values, item[2]) for item, values in zip(flat, operands)])
    results, before = tie(list(results), before)
    for one in streams:
        one.take(results)
    return (after, before)


def on_device(
    size,
    tokens,
    frame_video,
    caption_video,
    caption_len,
    attn_norm_gain,
    attn_norm_shift,
    qkv_weight,
    query_value_bias,
    proj_weight,
    proj_bias,
    mlp_norm_gain,
    mlp_norm_shift,
    fc_in_weight,
    fc_in_bias,
    fc_out_weight,
    fc_out_bias,
    side_in_weight,
    side_in_bias,
    side_norm_gain,
    side_norm_shift,
    side_qkv_weight,
    side_out_weight,
    cotangent,
):
    main_params = tuple(
        (
            member[0]
            for member in (
                attn_norm_gain,
                attn_norm_shift,
                qkv_weight,
                query_value_bias,
                proj_weight,
                proj_bias,
                mlp_norm_gain,
                mlp_norm_shift,
                fc_in_weight,
                fc_in_bias,
                fc_out_weight,
                fc_out_bias,
            )
        )
    )
    side_params = tuple(
        (
            member[0]
            for member in (
                side_in_weight,
                side_in_bias,
                side_norm_gain,
                side_norm_shift,
                side_qkv_weight,
                side_out_weight,
            )
        )
    )
    token_rows = tokens[0]
    cotangent_rows = cotangent[0]
    row_count, model_width = token_rows.shape
    frame_count = row_count // TPF
    me = lax.axis_index("dp")
    is_video = lax.axis_index("grp") == 0

    def to_text(values):
        return lax.ppermute(values, ("grp", "dp"), [(i, size + i) for i in range(size)])

    def to_video(values):
        return lax.ppermute(values, ("grp", "dp"), [(size + i, i) for i in range(size)])

    def in_all(values, distance):
        return lax.ppermute(values, "dp", pair_list(size, distance))

    def in_video(values, distance):
        return lax.ppermute(values, ("grp", "dp"), group_pairs(size, distance, 0))

    def in_text(values, distance):
        return lax.ppermute(values, ("grp", "dp"), group_pairs(size, distance, 1))

    flag = lax.axis_index("grp").astype(jnp.int32).reshape(1)
    me_one = me.astype(jnp.int32).reshape(1)
    side_rows = tuple((member if member.ndim == 2 else member[None] for member in side_params))
    frame_order = frame_video.reshape(size, frame_count)[gathered_devices(me, size)]
    frame_ids = frame_order[0]
    message, packed, side_start, side_projected = make_message(
        flag, token_rows, frame_ids, side_rows
    )
    arrived = to_text(packed[:, :model_width])
    packed = jnp.concatenate([arrived, packed[:, model_width:]], axis=1)
    packed = double_gather(packed, size, in_all)
    caption_ends = jnp.cumsum(caption_len[0]) - 1
    places = jnp.arange(frame_count * FRAME, dtype=jnp.int32)
    caption_starts = jnp.concatenate([caption_ends + 1 - caption_len[0], jnp.full((1,), row_count)])
    first = jnp.max(
        jnp.where(places[:, None] >= caption_starts[None, :], caption_starts[None, :], 0), axis=1
    ).astype(jnp.int32)
    bias = main_params[3]
    full_bias = jnp.concatenate(
        [bias[:model_width], jnp.zeros((model_width,), jnp.float32), bias[model_width:]]
    )
    params = tuple(
        (
            member if member.ndim == 2 else member[None]
            for member in main_params[:3] + (full_bias,) + main_params[4:]
        )
    )
    normed, projected, mixed, middle, normed_two, act, slope, hidden, block_rows = forward(
        flag, token_rows, message, first[:, None], params
    )
    out_rows, grad_out, text_vectors, *parts = make_prompt(
        flag,
        me_one,
        size,
        block_rows,
        cotangent_rows,
        packed,
        caption_ends,
        caption_video,
        frame_order.reshape(-1),
        side_rows,
    )
    own_width = model_width // size
    side_sum = PlainSum(size, in_text, parts[0], parts[1])
    grad_fc_out_bias, *parts = out_weight_grad(me_one, size, act, grad_out)
    parts, grad_out = tie(parts, grad_out)
    out_sum = Sum(size, in_all, parts, [(fc_out_weight.shape[1] // size, 1)])
    _, grad_out = advance(me_one, [side_sum], parts[1], grad_out)
    grad_fc_in_bias, grad_middle, grad_mixed, middle_vectors, *parts = mlp_back(
        me_one, size, grad_out, slope, normed_two, middle, mixed, params[10], params[8], params[4], params[6]
    )
    chunks = model_width // (2 * CHUNK)
    in_sum = Sum(size, in_all, parts, [(own_width, 4 * chunks), (own_width, chunks)])
    _, grad_mixed = advance(me_one, [out_sum, side_sum], grad_middle, grad_mixed)
    grad_projected = attend_back(flag, projected, grad_mixed, first.reshape(frame_count, 1, FRAME))
    grad_projected, normed = advance(me_one, [out_sum, in_sum, side_sum], grad_projected, normed)
    bias_totals, first_vectors, *parts = qkv_weight_grad(
        me_one, size, normed, grad_projected, params[2], params[0], params[1]
    )
    qkv_sum = Sum(size, in_all, parts, [(own_width, 3 * chunks)])
    bias_totals, grad_middle = advance(
        me_one, [out_sum, in_sum, side_sum], bias_totals, grad_middle
    )
    while not hasattr(side_sum, "result"):
        advance(me_one, [side_sum], bias_totals)
    vectors = (
        first_vectors,
        bias_totals,
        middle_vectors,
        grad_fc_in_bias,
        grad_fc_out_bias,
        text_vectors,
    )
    pair_rows, context_grad, line = pair_grad(
        flag, side_sum.result, side_rows[4], frame_count, vectors
    )
    received = to_video(context_grad)
    grad_source, grad_lines = message_back(
        flag,
        grad_projected,
        grad_middle,
        (message, received, side_start, side_projected, frame_ids[None, :], frame_ids[:, None])
        + (params[2], params[0], side_rows[0], side_rows[2], side_rows[4], side_rows[5], pair_rows),
    )
    widths = [model_width] * 2 + [3 * model_width] + [model_width] * 3
    widths += [grad_fc_in_bias.shape[1]] + [model_width] * 4
    (line, grad_lines), grad_source = tie((line, grad_lines), grad_source)
    line_sum = Spread(size, in_all, line, "add")
    all_lines = Spread(size, in_all, grad_lines, "stack")
    _, grad_source = advance(me_one, [out_sum, in_sum, qkv_sum], grad_source, grad_source)
    grad_tokens = token_grad(
        flag, grad_projected, hidden, grad_middle, grad_source, params[2], params[0]
    )
    streams = [out_sum, in_sum, qkv_sum, line_sum, all_lines]
    while not all((hasattr(one, "result") for one in streams)):
        grad_tokens, _ = advance(me_one, streams, grad_tokens)
    grad_in_weight, grad_side_qkv, grad_side_out, video_vectors = side_weight_grads(
        flag, me_one, size, packed, all_lines.result, side_sum.result, side_rows[4], side_rows[2], side_rows[3]
    )
    (
        grad_attn_gain,
        grad_attn_shift,
        grad_qv_bias,
        grad_mlp_gain,
        grad_mlp_shift,
        grad_proj_bias,
        grad_fc_in_bias,
        grad_fc_out_bias,
        grad_in_bias,
        grad_side_gain,
        grad_side_shift,
    ) = own_vectors(flag, me_one, size, line_sum.result, video_vectors, widths)
    summed = (
        grad_attn_gain,
        grad_attn_shift,
        qkv_sum.result[0][None],
        grad_qv_bias,
        in_sum.result[1][None],
        grad_proj_bias,
        grad_mlp_gain,
        grad_mlp_shift,
        in_sum.result[0][None],
        grad_fc_in_bias,
        out_sum.result[0][None],
        grad_fc_out_bias,
        grad_in_weight[None],
        grad_in_bias,
        grad_side_gain,
        grad_side_shift,
        grad_side_qkv[None],
        grad_side_out[None],
    )
    return tuple([out_rows[None], grad_tokens[None]] + list(summed))


def solution(mesh):
    placed = (
        P("grp", "dp", None),
        P(),
        P("dp"),
        P("dp", None),
        P("grp", None),
        P("grp", None),
        P("grp", None, None),
        P("grp", None),
        P("grp", None, None),
        P("grp", None),
        P("grp", None),
        P("grp", None),
        P("grp", None, None),
        P("grp", None),
        P("grp", None, None),
        P("grp", None),
        P("grp", None, None),
        P("grp", None),
        P("grp", None),
        P("grp", None),
        P("grp", None, None),
        P("grp", None, None),
        P("grp", "dp", None),
    )
    return jax.shard_map(
        functools.partial(on_device, mesh.shape["dp"]),
        mesh=mesh,
        in_specs=placed,
        out_specs=(
            P("grp", "dp", None),
            P("grp", "dp", None),
            P("grp", "dp"),
            P("grp", "dp"),
            P("grp", "dp", None),
            P("grp", "dp"),
            P("grp", "dp", None),
            P("grp", "dp"),
            P("grp", "dp"),
            P("grp", "dp"),
            P("grp", "dp", None),
            P("grp", "dp"),
            P("grp", "dp", None),
            P("grp", "dp"),
            P("grp", "dp", None),
            P("grp", "dp"),
            P("grp", "dp"),
            P("grp", "dp"),
            P("grp", "dp", None),
            P("grp", "dp", None),
        ),
        check_vma=False,
    )
```

```python
import functools

import jax
import jax.numpy as jnp
from jax import lax
from jax.experimental import pallas as pl
from jax.experimental.pallas import tpu as pltpu
from jax.sharding import PartitionSpec as P

HEADS = 12
HD = 64
TPF = 197
FRAME = 208
PRIOR = 80
CHUNK = 384
VMEM_BYTES = 58 * 2**20
SUB_BLOCKS = ((0, 112, -80, 192), (112, 96, 32, 176))


def product(left_side, right_side):
    return jnp.dot(left_side, right_side, preferred_element_type=jnp.float32)


def product_tn(left_side, right_side):
    return lax.dot_general(
        left_side, right_side, (((0,), (0,)), ((), ())), preferred_element_type=jnp.float32
    )


def product_nt(left_side, right_side):
    return lax.dot_general(
        left_side, right_side, (((1,), (1,)), ((), ())), preferred_element_type=jnp.float32
    )


def cost(flops, size):
    return pl.CostEstimate(flops=int(flops), bytes_accessed=int(size), transcendentals=0)


def padded_rows(rows):
    return -(-rows // 16) * 16


def split_shapes(size, rows):
    return [jax.ShapeDtypeStruct((size // 2, rows, CHUNK), jnp.bfloat16) for _ in range(4)]


def store_block(stage, side, block, me, row, values):
    differs = block ^ me
    right = side == 1
    sent = jnp.where(right, (differs >> 1) & 1, differs & 1)
    place = jnp.where(right, ((block >> 2) << 1) | (block & 1), block >> 1)
    stage[side, sent, place, pl.ds(row, values.shape[0]), :] = values


def stage_shapes(size, rows, steps):
    return [
        pltpu.VMEM((2, 2, size // 2, rows, CHUNK), jnp.bfloat16),
        pltpu.SemaphoreType.DMA((steps, 4)),
    ]


def rows_out(stage, outs, sems, step, side, row, count):
    rows = pl.ds(row, count)
    return [
        pltpu.make_async_copy(
            stage.at[side, sent, :, rows, :],
            outs[2 * side + 1 - sent].at[:, rows, :],
            sems.at[step, sent],
        )
        for sent in range(2)
    ]


def start_rows(stage, outs, sems, step, side, row, count):
    for index in range(2):

        @pl.when(side == index)
        def _():
            for copy in rows_out(stage, outs, sems, step, index, row, count):
                copy.start()


def wait_rows(stage, outs, sems, step, side, row, count):
    for copy in rows_out(stage, outs, sems, step, side, row, count):
        copy.wait()


def in_hbm(count):
    return [pl.BlockSpec(memory_space=pl.ANY) for _ in range(count)]


def combine_kernel(kinds, me_ref, *refs):
    refs = list(refs)
    sources = [[refs.pop(0) for _ in range(kind[1])] for kind in kinds]
    for (name, _, detail), parts in zip(kinds, sources):

        def total(side, index):
            keep, arrived = parts[2 * side], parts[2 * side + 1]
            return keep[index].astype(jnp.float32) + arrived[index].astype(jnp.float32)

        if name == "raw":
            refs.pop(0)[...] = total(0, 0)
        elif name == "add":
            refs.pop(0)[...] = sum((part[...] for part in parts[1:]), parts[0][...])
        elif name == "stack":
            refs.pop(0)[...] = jnp.concatenate([part[...] for part in parts], axis=0)
        elif name == "end":
            value = total(0, 0)
            half = value.shape[0] // 2
            start = 0
            for rows, chunks in detail:
                out = refs.pop(0)
                for side in range(2):
                    for chunk in range(chunks):
                        row = side * half + start + chunk * padded_rows(rows)
                        column = (side * chunks + chunk) * CHUNK
                        out[:, column : column + CHUNK] = value[row : row + rows]
                start += chunks * padded_rows(rows)
        else:
            send, held = refs.pop(0), refs.pop(0)
            mine = (me_ref[0] >> detail) & 1
            rows = parts[0].shape[1]
            for side in range(len(parts) // 2):
                place = slice(side * rows, (side + 1) * rows)
                for index in range(held.shape[0]):
                    held[index, place, :] = total(side, 2 * index + mine).astype(held.dtype)
                    send[index, place, :] = total(side, 2 * index + 1 - mine).astype(send.dtype)


def combine(me, items):
    shapes, kinds, operands = [], [], []
    for name, values, detail in items:
        kinds.append((name, len(values), detail))
        operands += values
        rows = values[0].shape[1]
        if name == "raw":
            shapes.append(jax.ShapeDtypeStruct((rows, CHUNK), jnp.float32))
        elif name in ("add", "stack"):
            times = len(values) if name == "stack" else 1
            shape = (times * values[0].shape[0], values[0].shape[1])
            shapes.append(jax.ShapeDtypeStruct(shape, values[0].dtype))
        elif name == "end":
            for own, chunks in detail:
                shapes.append(jax.ShapeDtypeStruct((own, 2 * chunks * CHUNK), jnp.float32))
        else:
            sides = len(values) // 2
            half = (values[0].shape[0] // 2, sides * rows, CHUNK)
            shapes += [jax.ShapeDtypeStruct(half, jnp.bfloat16)] * 2
    size = 3 * sum(value.size for value in operands)
    return pl.pallas_call(
        functools.partial(combine_kernel, tuple(kinds)),
        in_specs=[pl.BlockSpec(memory_space=pltpu.SMEM)] + in_vmem(len(operands)),
        out_specs=in_vmem(len(shapes)),
        out_shape=shapes,
        compiler_params=pltpu.CompilerParams(vmem_limit_bytes=30 * 2**20),
        cost_estimate=cost(size, size),
        name="combine",
    )(me, *operands)


def in_vmem(count):
    return [pl.BlockSpec(memory_space=pltpu.VMEM) for _ in range(count)]


def norm_parts(values):
    center = values - jnp.mean(values, axis=-1, keepdims=True)
    spread = lax.rsqrt(jnp.mean(center * center, axis=-1, keepdims=True) + 1e-05)
    return (center * spread, spread)


def norm_back(unit, spread, gain, grad):
    grad_unit = grad * gain
    first = jnp.mean(grad_unit, axis=-1, keepdims=True)
    second = jnp.mean(grad_unit * unit, axis=-1, keepdims=True)
    return spread * (grad_unit - first - unit * second)


def column_sum(values):
    return jnp.sum(values, axis=0, keepdims=True)


def lane_is_low(shape):
    return lax.broadcasted_iota(jnp.int32, shape, len(shape) - 1) < HD


def frame_start(is_video, frame):
    return jnp.where(is_video, TPF, FRAME) * frame


def load_rows(buffer, start):
    base = start // 16 * 16
    window = buffer[pl.ds(pl.multiple_of(base, 16), FRAME + 24), :].astype(jnp.float32)
    return pltpu.roll(window, (FRAME + 24 - (start - base)) % (FRAME + 24), axis=0)[:FRAME]


def store_rows(buffer, start, values):
    base = pl.multiple_of(start // 16 * 16, 16)
    pad = jnp.zeros((24, values.shape[1]), jnp.float32)
    moved = pltpu.roll(jnp.concatenate([values, pad], axis=0), start - base, axis=0)
    old = buffer[pl.ds(base, 16), :].astype(jnp.float32)
    place = lax.broadcasted_iota(jnp.int32, old.shape, 0)
    first = jnp.where(place < start - base, old, moved[:16])
    buffer[pl.ds(base, 16), :] = first.astype(buffer.dtype)
    buffer[pl.ds(base + 16, FRAME), :] = moved[16 : FRAME + 16].astype(buffer.dtype)


def frame_tail(rows, is_video, last_row):
    first = TPF // 8 * 8
    tail = rows[first:]
    place = lax.broadcasted_iota(jnp.int32, tail.shape, 0) + first
    video = jnp.where(place == TPF, last_row, jnp.where(place < TPF, tail, 0.0))
    return jnp.concatenate([rows[:first], jnp.where(is_video, video, tail)], axis=0)


def head_mask(shape, head):
    lane = lax.broadcasted_iota(jnp.int32, shape, len(shape) - 1)
    return (lane >= head * HD) & (lane < (head + 1) * HD)


def stack_heads(rows):
    zero = jnp.zeros_like(rows)
    return jnp.concatenate(
        [jnp.where(head_mask(rows.shape, head), rows, zero) for head in range(HEADS)], axis=0
    )


def pick_heads(stacked):
    count = stacked.shape[0] // HEADS
    total = jnp.zeros((count, stacked.shape[1]), jnp.float32)
    for head in range(HEADS):
        part = stacked[head * count : (head + 1) * count]
        total = total + jnp.where(head_mask(part.shape, head), part, 0.0)
    return total


def side_weights(query, key, allowed):
    stacked = stack_heads(query * jnp.asarray(HD**-0.5, query.dtype))
    bias = jnp.where(allowed, 0.0, -1e30)
    scores = product_nt(stacked, key) + jnp.concatenate([bias] * HEADS, axis=0)
    weights = jnp.exp(scores - jnp.max(scores, axis=-1, keepdims=True))
    return (stacked, weights / jnp.sum(weights, axis=-1, keepdims=True))


def side_attend(query, key, value, allowed):
    _, weights = side_weights(query, key, allowed)
    return pick_heads(product(weights.astype(jnp.bfloat16), value)).astype(jnp.bfloat16)


def side_attend_back(query, key, value, allowed, grad):
    stacked, weights = side_weights(query, key, allowed)
    grads = stack_heads(grad)
    grad_soft = product_nt(grads, value)
    inner = jnp.sum(weights * grad_soft, axis=-1, keepdims=True)
    grad_scores = (weights * (grad_soft - inner)).astype(jnp.bfloat16)
    return (
        pick_heads(product(grad_scores, key)) * HD**-0.5,
        product_tn(grad_scores, stacked),
        product_tn(weights.astype(jnp.bfloat16), grads),
    )


def attend_pair(query, key, value, bias):
    count = query.shape[0]
    low = lane_is_low(query.shape)
    query = query * jnp.asarray(HD**-0.5, query.dtype)
    zero = jnp.zeros_like(query)
    stacked = jnp.concatenate([jnp.where(low, query, zero), jnp.where(low, zero, query)], axis=0)
    scores = product_nt(stacked, key)
    weights = []
    for head in range(2):
        one = scores[head * count : (head + 1) * count] + bias
        weights.append(jnp.exp(one - jnp.max(one, axis=-1, keepdims=True)).astype(jnp.bfloat16))
    wide = jnp.concatenate([value, jnp.ones_like(value)], axis=1)
    summed = product(jnp.concatenate(weights, axis=0), wide)
    mixed = summed[:, :128] / summed[:, 128:]
    return jnp.where(low, mixed[:count], mixed[count:]).astype(jnp.bfloat16)


def attend_back_group(parts):
    masked, scores, softs, grad_scores = [], [], [], []
    for query, key, value, grad, bias in parts:
        low = lane_is_low(query.shape)
        query = query * jnp.asarray(HD**-0.5, query.dtype)
        zero = jnp.zeros_like(query)
        queries = jnp.concatenate([jnp.where(low, query, zero), jnp.where(low, zero, query)], axis=0)
        grads = jnp.concatenate([jnp.where(low, grad, zero), jnp.where(low, zero, grad)], axis=0)
        masked.append((queries, grads))
    for (query, key, value, grad, bias), (queries, grads) in zip(parts, masked):
        scores.append((product_nt(key, queries) + bias, product_nt(value, grads)))
    for one, grad_soft in scores:
        soft = jnp.exp(one - jnp.max(one, axis=0, keepdims=True))
        soft = soft * (1.0 / column_sum(soft))
        inner = soft * grad_soft
        grad_scores.append((inner - soft * column_sum(inner)).astype(jnp.bfloat16))
        softs.append(soft.astype(jnp.bfloat16))
    results = []
    for (query, key, value, grad, bias), (queries, grads), soft, back in zip(parts, masked, softs, grad_scores):
        count = query.shape[0]
        grad_query = product_tn(back, key) * HD**-0.5
        grad_query = jnp.where(lane_is_low(query.shape), grad_query[:count], grad_query[count:])
        results.append((grad_query, product(back, queries), product(soft, grads)))
    return results


def forward_kernel(
    frames,
    flag_ref,
    token_ref,
    message_ref,
    first_ref,
    gain_one,
    shift_one,
    qkv_weight,
    qkv_bias,
    proj_weight,
    proj_bias,
    gain_two,
    shift_two,
    fc_in_weight,
    fc_in_bias,
    fc_out_weight,
    fc_out_bias,
    normed_ref,
    projected_ref,
    mixed_ref,
    middle_ref,
    normed_two_ref,
    act_ref,
    slope_ref,
    hidden_ref,
    block_ref,
    held,
    source,
    target,
):
    step = pl.program_id(0)
    is_video = flag_ref[0] == 0
    count, width = token_ref.shape
    rows = frames * FRAME

    @pl.when(step == 0)
    def _():
        source[0:count, :] = token_ref[...]
        source[count:, :] = jnp.zeros((source.shape[0] - count, width), source.dtype)

    parts = []
    for frame in range(frames):
        part = load_rows(source, frame_start(is_video, step * frames + frame))
        message = message_ref[pl.ds(step * frames + frame, 1), :]
        parts.append(frame_tail(part, is_video, message))
    hidden = jnp.concatenate(parts, axis=0)
    hidden_ref[...] = hidden.astype(jnp.bfloat16)
    unit, _ = norm_parts(hidden)
    normed = (unit * gain_one[...] + shift_one[...]).astype(jnp.bfloat16)
    normed_ref[...] = normed

    @pl.when(step == 0)
    def _():
        held[0:PRIOR, :] = jnp.zeros((PRIOR, held.shape[1]), held.dtype)

    @pl.when(step > 0)
    def _():
        held[0:PRIOR, :] = held[rows : rows + PRIOR, :]

    for start in range(0, 3 * width, width):
        columns = slice(start, start + width)
        part = (product(normed, qkv_weight[:, columns]) + qkv_bias[:, columns]).astype(jnp.bfloat16)
        held[PRIOR:, columns] = part
        projected_ref[:, columns] = part

    def attend(frame, query_start, query_count, key_start, key_count, bias):
        query_rows = pl.ds(PRIOR + frame * FRAME + query_start, query_count)
        key_rows = pl.ds(PRIOR + frame * FRAME + key_start, key_count)
        for pair in range(0, width, 128):
            mixed_ref[pl.ds(frame * FRAME + query_start, query_count), pair : pair + 128] = attend_pair(
                held[query_rows, pair : pair + 128],
                held[key_rows, width + pair : width + pair + 128],
                held[key_rows, 2 * width + pair : 2 * width + pair + 128],
                bias,
            )

    @pl.when(is_video)
    def _():
        place = lax.broadcasted_iota(jnp.int32, (FRAME, FRAME), 1)
        bias = jnp.where(place <= TPF, 0.0, -1e30)
        for frame in range(frames):
            attend(frame, 0, FRAME, 0, FRAME, bias)

    @pl.when(jnp.logical_not(is_video))
    def _():
        for frame in range(frames):
            for query_start, query_count, key_start, key_count in SUB_BLOCKS:
                base = step * rows + frame * FRAME
                shape = (query_count, key_count)
                key_place = base + key_start + lax.broadcasted_iota(jnp.int32, shape, 1)
                query_place = base + query_start + lax.broadcasted_iota(jnp.int32, shape, 0)
                first = first_ref[pl.ds(frame * FRAME + query_start, query_count), :]
                allowed = (key_place >= first) & (key_place <= query_place)
                bias = jnp.where(allowed, 0.0, -1e30)
                attend(frame, query_start, query_count, key_start, key_count, bias)

    middle = hidden + product(mixed_ref[...], proj_weight[...]) + proj_bias[...]
    middle_ref[...] = middle.astype(jnp.bfloat16)
    unit, _ = norm_parts(middle)
    normed = (unit * gain_two[...] + shift_two[...]).astype(jnp.bfloat16)
    normed_two_ref[...] = normed
    total = middle + fc_out_bias[...]
    for start in range(0, fc_in_weight.shape[1], width):
        columns = slice(start, start + width)
        pre = product(normed, fc_in_weight[:, columns]) + fc_in_bias[:, columns]
        gate = 0.5 + 0.5 * jnp.tanh(0.851 * pre)
        value = pre * gate
        act = value.astype(jnp.bfloat16)
        act_ref[:, columns] = act
        slope_ref[:, columns] = (gate + 1.702 * value * (1.0 - gate)).astype(jnp.bfloat16)
        total = total + product(act, fc_out_weight[columns, :])
    for frame in range(frames):
        start = frame_start(is_video, step * frames + frame)
        store_rows(target, start, total[frame * FRAME : (frame + 1) * FRAME])

    @pl.when(step == pl.num_programs(0) - 1)
    def _():
        block_ref[...] = target[0:count, :]


def whole(shape):
    return pl.BlockSpec(
        shape, lambda *_: (0,) * len(shape), pipeline_mode=pl.Buffered(buffer_count=1)
    )


def forward(flag, tokens, message, first, params, frames=2):
    token_count, width = tokens.shape
    count = token_count // TPF * FRAME
    rows = frames * FRAME
    hidden = params[8].shape[1]

    def by_rows(columns):
        return pl.BlockSpec((rows, columns), lambda i, _: (i, 0))

    widths = (width, 3 * width, width, width, width, hidden, hidden, width)
    return pl.pallas_call(
        functools.partial(forward_kernel, frames),
        grid_spec=pltpu.PrefetchScalarGridSpec(
            num_scalar_prefetch=1,
            grid=(count // rows,),
            in_specs=[whole(tokens.shape), whole(message.shape), by_rows(1)]
            + [whole(member.shape) for member in params],
            out_specs=[by_rows(columns) for columns in widths] + [whole(tokens.shape)],
            scratch_shapes=[
                pltpu.VMEM((rows + PRIOR, 3 * width), jnp.bfloat16),
                pltpu.VMEM((count + 32, width), jnp.bfloat16),
                pltpu.VMEM((count + 32, width), jnp.bfloat16),
            ],
        ),
        out_shape=[jax.ShapeDtypeStruct((count, columns), jnp.bfloat16) for columns in widths]
        + [jax.ShapeDtypeStruct(tokens.shape, jnp.bfloat16)],
        compiler_params=pltpu.CompilerParams(vmem_limit_bytes=VMEM_BYTES),
        cost_estimate=cost(2 * count * width * (4 * width + 2 * hidden), 2 * count * sum(widths)),
        name="forward",
    )(flag, tokens, message, first, *params)


def out_weight_kernel(me_ref, act_ref, grad_ref, bias_ref, *refs):
    outs, (stage, sems) = refs[:4], refs[4:]
    step = pl.program_id(0)
    rows = stage.shape[3]
    part = product_tn(act_ref[...], grad_ref[...]).astype(jnp.bfloat16)
    for index in range(part.shape[0] // rows):
        block = step * (part.shape[0] // rows) + index
        for side in range(2):
            values = part[index * rows : (index + 1) * rows, side * CHUNK : (side + 1) * CHUNK]
            store_block(stage, side, block, me_ref[0], 0, values)

    @pl.when(step == 0)
    def _():
        bias_ref[...] = column_sum(grad_ref[...].astype(jnp.float32))

    @pl.when(step == pl.num_programs(0) - 1)
    def _():
        copies = [
            pltpu.make_async_copy(stage.at[index // 2, index % 2], outs[index + 1 - 2 * (index % 2)], sems.at[0, index])
            for index in range(4)
        ]
        for copy in copies:
            copy.start()
        for copy in copies:
            copy.wait()


def out_weight_grad(me, size, act, grad, tile=768):
    count, hidden = act.shape
    width = grad.shape[1]
    rows = hidden // size
    return pl.pallas_call(
        out_weight_kernel,
        grid_spec=pltpu.PrefetchScalarGridSpec(
            num_scalar_prefetch=1,
            grid=(hidden // tile,),
            in_specs=[pl.BlockSpec((count, tile), lambda i, _: (0, i)), whole(grad.shape)],
            out_specs=[whole((1, width))] + in_hbm(4),
            scratch_shapes=stage_shapes(size, rows, 1),
        ),
        out_shape=[jax.ShapeDtypeStruct((1, width), jnp.float32)] + split_shapes(size, rows),
        compiler_params=pltpu.CompilerParams(vmem_limit_bytes=46 * 2**20),
        cost_estimate=cost(2 * count * hidden * width, 2 * count * hidden),
        name="out_weight_grad",
    )(me, act, grad)


def pre_grad_kernel(grad_ref, slope_ref, weight_ref, out_ref, bias_ref):
    hidden = weight_ref.shape[0]

    @pl.when(pl.program_id(0) == 0)
    def _():
        bias_ref[...] = jnp.zeros(bias_ref.shape, bias_ref.dtype)

    for start in range(0, hidden, 768):
        columns = slice(start, start + 768)
        part = product_nt(grad_ref[...], weight_ref[columns, :])
        part = (part * slope_ref[:, columns].astype(jnp.float32)).astype(jnp.bfloat16)
        out_ref[:, columns] = part
        bias_ref[:, columns] = bias_ref[:, columns] + column_sum(part.astype(jnp.float32))


def pre_grad(grad, slope, weight):
    count, width = grad.shape
    hidden = slope.shape[1]
    rows = 2 * FRAME
    return pl.pallas_call(
        pre_grad_kernel,
        grid=(count // rows,),
        in_specs=[
            pl.BlockSpec((rows, width), lambda i: (i, 0)),
            pl.BlockSpec((rows, hidden), lambda i: (i, 0)),
            whole(weight.shape),
        ],
        out_specs=[pl.BlockSpec((rows, hidden), lambda i: (i, 0)), whole((1, hidden))],
        out_shape=[
            jax.ShapeDtypeStruct((count, hidden), jnp.bfloat16),
            jax.ShapeDtypeStruct((1, hidden), jnp.float32),
        ],
        compiler_params=pltpu.CompilerParams(vmem_limit_bytes=46 * 2**20),
        cost_estimate=cost(2 * count * hidden * width, 4 * count * hidden),
        name="pre_grad",
    )(grad, slope, weight)


def middle_grad_kernel(grad_pre_ref, grad_ref, middle_ref, in_weight, proj_weight, gain_ref, out_ref, mixed_ref, vector_ref):
    back = product_nt(grad_pre_ref[...], in_weight[...])
    unit, spread = norm_parts(middle_ref[...].astype(jnp.float32))
    grad = norm_back(unit, spread, gain_ref[...], back) + grad_ref[...].astype(jnp.float32)
    grad = grad.astype(jnp.bfloat16)
    out_ref[...] = grad
    mixed_ref[...] = product_nt(grad, proj_weight[...]).astype(jnp.bfloat16)
    sums = [column_sum(part) for part in (back * unit, back, grad.astype(jnp.float32))]
    sums = jnp.concatenate(sums, axis=0)

    @pl.when(pl.program_id(0) == 0)
    def _():
        vector_ref[...] = sums

    @pl.when(pl.program_id(0) > 0)
    def _():
        vector_ref[...] = vector_ref[...] + sums


def middle_grad(grad_pre, grad, middle, in_weight, proj_weight, gain):
    count, width = grad.shape
    hidden = grad_pre.shape[1]
    rows = 2 * FRAME

    def by_rows(columns):
        return pl.BlockSpec((rows, columns), lambda i: (i, 0))

    return pl.pallas_call(
        middle_grad_kernel,
        grid=(count // rows,),
        in_specs=[by_rows(hidden), by_rows(width), by_rows(width)]
        + [whole(value.shape) for value in (in_weight, proj_weight, gain)],
        out_specs=[by_rows(width), by_rows(width), whole((3, width))],
        out_shape=[
            jax.ShapeDtypeStruct((count, width), jnp.bfloat16),
            jax.ShapeDtypeStruct((count, width), jnp.bfloat16),
            jax.ShapeDtypeStruct((3, width), jnp.float32),
        ],
        compiler_params=pltpu.CompilerParams(vmem_limit_bytes=46 * 2**20),
        cost_estimate=cost(2 * count * width * (hidden + width), 2 * count * hidden),
        name="middle_grad",
    )(grad_pre, grad, middle, in_weight, proj_weight, gain)


def in_weight_kernel(me_ref, normed_ref, grad_pre_ref, mixed_ref, grad_ref, *refs):
    outs, (stage, sems) = refs[:4], refs[4:]
    step = pl.program_id(0)
    steps = pl.num_programs(0)
    blocks = 2 * stage.shape[2]
    own = normed_ref.shape[1] // blocks
    spaced = padded_rows(own)
    chunks = grad_pre_ref.shape[1] // CHUNK
    per_half = (stage.shape[3] // spaced - 1) // chunks
    side = step // per_half
    first_row = (step - side * per_half) * chunks * spaced

    @pl.when(step < steps - 1)
    def _():
        part = product_tn(normed_ref[...], grad_pre_ref[...]).astype(jnp.bfloat16)
        for chunk in range(chunks):
            row = pl.multiple_of(first_row + chunk * spaced, 16)
            columns = slice(chunk * CHUNK, (chunk + 1) * CHUNK)
            for block in range(blocks):
                values = part[block * own : (block + 1) * own, columns]
                store_block(stage, side, block, me_ref[0], row, values)
        start_rows(stage, outs, sems, step, side, pl.multiple_of(first_row, 16), chunks * spaced)

    @pl.when(step == steps - 1)
    def _():
        part = product_tn(mixed_ref[...], grad_ref[...]).astype(jnp.bfloat16)
        row = stage.shape[3] - spaced
        for block in range(blocks):
            for half in range(2):
                values = part[block * own : (block + 1) * own, half * CHUNK : (half + 1) * CHUNK]
                store_block(stage, half, block, me_ref[0], row, values)
        last = []
        for half in range(2):
            last += rows_out(stage, outs, sems, 2 * per_half + half, half, row, spaced)
        for copy in last:
            copy.start()
        for done in range(2 * per_half):
            first = done % per_half * chunks * spaced
            wait_rows(stage, outs, sems, done, done // per_half, first, chunks * spaced)
        for copy in last:
            copy.wait()


def in_weight_grad(me, size, normed, grad_pre, mixed, grad_middle, tile=768):
    count, width = normed.shape
    hidden = grad_pre.shape[1]
    own = (hidden // (2 * CHUNK) + width // (2 * CHUNK)) * padded_rows(width // size)
    steps = hidden // tile
    return pl.pallas_call(
        in_weight_kernel,
        grid_spec=pltpu.PrefetchScalarGridSpec(
            num_scalar_prefetch=1,
            grid=(steps + 1,),
            in_specs=[
                whole(normed.shape),
                pl.BlockSpec((count, tile), lambda i, _: (0, jnp.minimum(i, steps - 1))),
                whole(mixed.shape),
                whole(grad_middle.shape),
            ],
            out_specs=in_hbm(4),
            scratch_shapes=stage_shapes(size, own, steps + 2),
        ),
        out_shape=split_shapes(size, own),
        compiler_params=pltpu.CompilerParams(vmem_limit_bytes=46 * 2**20),
        cost_estimate=cost(2 * count * width * (hidden + width), 2 * count * hidden),
        name="in_weight_grad",
    )(me, normed, grad_pre, mixed, grad_middle)


def attend_back_kernel(flag_ref, projected_ref, grad_ref, first_ref, out_ref, held, pending, carry):
    step = pl.program_id(0)
    blocks = pl.num_programs(0) - 1
    is_video = flag_ref[0] == 0
    width = grad_ref.shape[1]

    @pl.when(step == 0)
    def _():
        held[...] = jnp.zeros(held.shape, held.dtype)
        carry[...] = jnp.zeros(carry.shape, carry.dtype)

    @pl.when(step > 0)
    def _():
        out_ref[...] = pending[...]

    def add_prior(columns, values):
        rows = slice(FRAME - PRIOR, FRAME)
        out_ref[rows, columns] = (carry[:, columns] + values).astype(jnp.bfloat16)

    @pl.when((step < blocks) & is_video)
    def _():
        place = lax.broadcasted_iota(jnp.int32, (FRAME, 2 * FRAME), 0)
        bias = jnp.where(place <= TPF, 0.0, -1e30)
        for first_pair in range(0, width, 128 * 3):
            pairs = range(first_pair, first_pair + 128 * 3, 128)
            places = [
                [slice(start + pair, start + pair + 128) for start in (0, width, 2 * width)] for pair in pairs
            ]
            parts = [
                tuple((projected_ref[:, columns] for columns in place)) + (grad_ref[:, place[0]], bias)
                for place in places
            ]
            for place, grads in zip(places, attend_back_group(parts)):
                for columns, values in zip(place, grads):
                    pending[:, columns] = values.astype(jnp.bfloat16)

    @pl.when((step < blocks) & jnp.logical_not(is_video))
    def _():
        held[PRIOR:, :] = projected_ref[...]
        biases = []
        for query_start, query_count, key_start, key_count in SUB_BLOCKS:
            base = step * FRAME
            shape = (key_count, query_count)
            key_place = base + key_start + lax.broadcasted_iota(jnp.int32, shape, 0)
            query_place = base + query_start + lax.broadcasted_iota(jnp.int32, shape, 1)
            first = first_ref[0, :, query_start : query_start + query_count]
            allowed = (key_place >= first) & (key_place <= query_place)
            bias = jnp.where(allowed, 0.0, -1e30)
            biases.append(jnp.concatenate([bias, bias], axis=1))
        for first_pair in range(0, width, 128 * 3):
            pairs = range(first_pair, first_pair + 128 * 3, 128)
            places, parts = [], []
            for pair in pairs:
                place = [slice(start + pair, start + pair + 128) for start in (0, width, 2 * width)]
                places.append(place)
                for bias, block in zip(biases, SUB_BLOCKS):
                    query_start, query_count, key_start, key_count = block
                    key_rows = slice(PRIOR + key_start, PRIOR + key_start + key_count)
                    query_rows = slice(query_start, query_start + query_count)
                    parts.append(
                        (
                            projected_ref[query_rows, place[0]],
                            held[key_rows, place[1]],
                            held[key_rows, place[2]],
                            grad_ref[query_rows, place[0]],
                            bias,
                        )
                    )
            results = attend_back_group(parts)
            for index, place in enumerate(places):
                pair_results = results[2 * index : 2 * index + 2]
                for grads, block in zip(pair_results, SUB_BLOCKS):
                    pending[block[0] : block[0] + block[1], place[0]] = grads[0].astype(jnp.bfloat16)
                for kind in (1, 2):
                    early, late = pair_results[0][kind], pair_results[1][kind]
                    overlap = SUB_BLOCKS[1][2]
                    reach = SUB_BLOCKS[0][1]
                    own = jnp.concatenate(
                        [
                            early[PRIOR : PRIOR + overlap],
                            early[PRIOR + overlap :] + late[: reach - overlap],
                            late[reach - overlap :],
                        ],
                        axis=0,
                    )
                    add_prior(place[kind], early[:PRIOR])
                    pending[:, place[kind]] = own.astype(jnp.bfloat16)
                    carry[:, place[kind]] = own[FRAME - PRIOR :]
        held[0:PRIOR, :] = projected_ref[FRAME - PRIOR :, :]


def attend_back(flag, projected, grad_mixed, first):
    count, wide = projected.shape
    width = grad_mixed.shape[1]
    blocks = count // FRAME

    def ahead(i, _):
        return (jnp.minimum(i, blocks - 1), 0)

    return pl.pallas_call(
        attend_back_kernel,
        grid_spec=pltpu.PrefetchScalarGridSpec(
            num_scalar_prefetch=1,
            grid=(blocks + 1,),
            in_specs=[
                pl.BlockSpec((FRAME, wide), ahead),
                pl.BlockSpec((FRAME, width), ahead),
                pl.BlockSpec((1, 1, FRAME), lambda i, _: (jnp.minimum(i, blocks - 1), 0, 0)),
            ],
            out_specs=pl.BlockSpec((FRAME, wide), lambda i, _: (jnp.maximum(i - 1, 0), 0)),
            scratch_shapes=[
                pltpu.VMEM((FRAME + PRIOR, wide), jnp.bfloat16),
                pltpu.VMEM((FRAME, wide), jnp.bfloat16),
                pltpu.VMEM((PRIOR, wide), jnp.float32),
            ],
        ),
        out_shape=jax.ShapeDtypeStruct((count, wide), jnp.bfloat16),
        compiler_params=pltpu.CompilerParams(vmem_limit_bytes=46 * 2**20),
        cost_estimate=cost(2 * count * width * 5 * FRAME * 4, 4 * count * wide),
        name="attend_back",
    )(flag, projected, grad_mixed, first)


def two_terms(values):
    high = values.astype(jnp.bfloat16)
    return (high, (values - high.astype(jnp.float32)).astype(jnp.bfloat16))


def row_product(values, weight):
    spread = [jnp.broadcast_to(one, (8, one.shape[1])) for one in two_terms(values)]
    return (product_nt(spread[0], weight) + product_nt(spread[1], weight))[0:1]


def qkv_weight_kernel(me_ref, normed_ref, grad_ref, weight_ref, gain_ref, shift_ref, bias_ref, vector_ref, *refs):
    outs, (sums, stage, sems) = refs[:4], refs[4:]
    step = pl.program_id(0)
    last = pl.num_programs(0) - 1
    part = product_tn(normed_ref[...], grad_ref[...])
    bias = column_sum(grad_ref[...].astype(jnp.float32))
    bias_ref[...] = bias
    weight = weight_ref[...]
    shift = row_product(bias, weight)
    ones = jnp.ones((8, part.shape[1]), jnp.bfloat16)
    high, lower = two_terms(part * weight.astype(jnp.float32))
    scaled = (product_nt(ones, high) + product_nt(ones, lower))[0:1]
    both = jnp.concatenate([scaled, shift], axis=0)

    @pl.when(step == 0)
    def _():
        sums[...] = both

    @pl.when(step > 0)
    def _():
        sums[...] = sums[...] + both

    part = part.astype(jnp.bfloat16)
    blocks = 2 * stage.shape[2]
    rows = part.shape[0] // blocks
    per_half = (last + 1) // 2
    side = step // per_half
    row = pl.multiple_of((step - side * per_half) * padded_rows(rows), 16)
    for block in range(blocks):
        store_block(stage, side, block, me_ref[0], row, part[block * rows : (block + 1) * rows])
    spaced = padded_rows(rows)
    start_rows(stage, outs, sems, step, side, row, spaced)

    @pl.when(step == last)
    def _():
        shift_total = sums[1:2, :]
        gain_total = (sums[0:1, :] - shift_ref[...] * shift_total) / gain_ref[...]
        vector_ref[...] = jnp.concatenate([gain_total, shift_total], axis=0)
        half = stage.shape[3] // spaced
        for done in range(2 * half):
            wait_rows(stage, outs, sems, done, done // half, done % half * spaced, spaced)


def qkv_weight_grad(me, size, normed, grad, weight, gain, shift):
    count, width = normed.shape
    wide = grad.shape[1]
    own = wide // (2 * CHUNK) * padded_rows(width // size)
    return pl.pallas_call(
        qkv_weight_kernel,
        grid_spec=pltpu.PrefetchScalarGridSpec(
            num_scalar_prefetch=1,
            grid=(wide // CHUNK,),
            in_specs=[
                whole(normed.shape),
                pl.BlockSpec((count, CHUNK), lambda i, _: (0, i)),
                pl.BlockSpec((width, CHUNK), lambda i, _: (0, i)),
                whole(gain.shape),
                whole(shift.shape),
            ],
            out_specs=[pl.BlockSpec((1, CHUNK), lambda i, _: (0, i)), whole((2, width))] + in_hbm(4),
            scratch_shapes=[pltpu.VMEM((2, width), jnp.float32)]
            + stage_shapes(size, own, wide // CHUNK),
        ),
        out_shape=[
            jax.ShapeDtypeStruct((1, wide), jnp.float32),
            jax.ShapeDtypeStruct((2, width), jnp.float32),
        ]
        + split_shapes(size, own),
        compiler_params=pltpu.CompilerParams(vmem_limit_bytes=46 * 2**20),
        cost_estimate=cost(2 * count * width * wide, 2 * count * wide),
        name="qkv_weight_grad",
    )(me, normed, grad, weight, gain, shift)


def token_grad_kernel(
    part, split, flag_ref, grad_ref, hidden_ref, middle_ref, source_ref, weight_ref, gain_ref, *refs
):
    if part == 0:
        out_ref, shared_ref, target, sem = refs
    else:
        before_ref, other_ref, out_ref, target, sem = refs
    frames = source_ref.shape[0] // 2
    is_video = flag_ref[0] == 0
    origin = part * split
    step = pl.program_id(0)
    if part == 1:

        @pl.when(step == 0)
        def _():
            target[0 : before_ref.shape[0], :] = before_ref[...]

    back = product_nt(grad_ref[...], weight_ref[...])
    unit, spread = norm_parts(hidden_ref[...].astype(jnp.float32))
    grads = norm_back(unit, spread, gain_ref[...], back) + middle_ref[...].astype(jnp.float32)
    per_step = grads.shape[0] // FRAME
    for frame in range(per_step):
        rows = grads[frame * FRAME : (frame + 1) * FRAME]
        index = part * frames + step * per_step + frame
        place = lax.broadcasted_iota(jnp.int32, (8, rows.shape[1]), 0)
        extra = jnp.where(is_video & (place == 0), source_ref[pl.ds(index, 1), :], 0.0)
        rows = jnp.concatenate([rows[:8] + extra, rows[8:]], axis=0)
        store_rows(target, frame_start(is_video, index) - origin, rows)

    @pl.when(step == pl.num_programs(0) - 1)
    def _():
        count = split if part == 0 else out_ref.shape[0] - split
        copy = pltpu.make_async_copy(
            target.at[pl.ds(0, count)], out_ref.at[pl.ds(origin, count)], sem
        )
        copy.start()
        if part == 0:
            shared_ref[...] = target[split : split + shared_ref.shape[0], :]
        copy.wait()


def token_grad(part, flag, grad, hidden, grad_middle, grad_source, weight, gain, before=None, frames=2):
    count, width = hidden.shape
    rows = frames * FRAME
    tokens = (count // FRAME * TPF, width)
    steps = count // rows // 2
    split = grad_source.shape[0] // 2 * TPF // 16 * 16
    shared = (-(-(grad_source.shape[0] // 2 * FRAME - split) // 16) * 16, width)
    more = () if part == 0 else before

    def by_rows(columns):
        return pl.BlockSpec((rows, columns), lambda i, _: (i + part * steps, 0))

    out_shape = [jax.ShapeDtypeStruct(tokens, jnp.float32)]
    out_specs = in_hbm(1)
    if part == 0:
        out_shape.append(jax.ShapeDtypeStruct(shared, jnp.float32))
        out_specs = out_specs + [whole(shared)]
    results = pl.pallas_call(
        functools.partial(token_grad_kernel, part, split),
        grid_spec=pltpu.PrefetchScalarGridSpec(
            num_scalar_prefetch=1,
            grid=(steps,),
            in_specs=[
                by_rows(grad.shape[1]),
                by_rows(width),
                by_rows(width),
                whole(grad_source.shape),
                whole(weight.shape),
                whole(gain.shape),
            ]
            + ([whole(shared)] + in_hbm(1) if part == 1 else []),
            out_specs=out_specs,
            scratch_shapes=[
                pltpu.VMEM((count // 2 + FRAME, width), jnp.float32),
                pltpu.SemaphoreType.DMA(()),
            ],
        ),
        out_shape=out_shape,
        input_output_aliases={8: 0} if part == 1 else {},
        compiler_params=pltpu.CompilerParams(vmem_limit_bytes=46 * 2**20),
        cost_estimate=cost(count * width * 3 * width, 2 * count * width),
        name="token_grad",
    )(flag, grad, hidden, grad_middle, grad_source, weight, gain, *more)
    return (results[1], results[0]) if part == 0 else results[0]


def message_kernel(flag_ref, token_ref, ids_row, ids_column, in_weight, in_bias, gain, shift, qkv_weight, out_weight, message_ref, packed_ref, start_ref, projected_ref):
    frames, width = message_ref.shape

    @pl.when(flag_ref[0] == 0)
    def _():
        parts = []
        for frame in range(frames):
            row = frame * TPF
            base = row // 16 * 16
            tile = token_ref[base : base + 16, :].astype(jnp.float32)
            parts.append(tile[row - base : row - base + 1])
        source = jnp.concatenate(parts, axis=0).astype(jnp.bfloat16)
        start = product(source, in_weight[...]) + in_bias[...]
        unit, _ = norm_parts(start)
        normed = (unit * gain[...] + shift[...]).astype(jnp.bfloat16)
        projected = product(normed, qkv_weight[...]).astype(jnp.bfloat16)
        mixed = side_attend(
            projected[:, :width],
            projected[:, width : 2 * width],
            projected[:, 2 * width :],
            ids_column[...] == ids_row[...],
        )
        message = start + product(mixed, out_weight[...])
        message_ref[...] = message
        start_ref[...] = start
        projected_ref[...] = projected
        packed_ref[...] = jnp.concatenate([message.astype(jnp.bfloat16), source, normed, mixed], axis=1)

    @pl.when(flag_ref[0] != 0)
    def _():
        message_ref[...] = jnp.zeros(message_ref.shape, message_ref.dtype)
        packed_ref[...] = jnp.zeros(packed_ref.shape, packed_ref.dtype)
        start_ref[...] = jnp.zeros(start_ref.shape, start_ref.dtype)
        projected_ref[...] = jnp.zeros(projected_ref.shape, projected_ref.dtype)


def call_once(kernel, name, flops, scalars, operands, shapes):
    return pl.pallas_call(
        kernel,
        in_specs=[pl.BlockSpec(memory_space=pltpu.SMEM) for _ in scalars] + in_vmem(len(operands)),
        out_specs=in_vmem(len(shapes)),
        out_shape=[jax.ShapeDtypeStruct(shape, dtype) for shape, dtype in shapes],
        compiler_params=pltpu.CompilerParams(vmem_limit_bytes=VMEM_BYTES),
        cost_estimate=cost(flops, sum(value.size * 2 for value in operands)),
        name=name,
    )(*scalars, *operands)


def make_message(flag, tokens, frame_ids, side_params):
    frames = frame_ids.shape[0]
    width = tokens.shape[1]
    shapes = [
        ((frames, width), jnp.float32),
        ((frames, 4 * width), jnp.bfloat16),
        ((frames, width), jnp.float32),
        ((frames, 3 * width), jnp.bfloat16),
    ]
    operands = (tokens, frame_ids[None, :], frame_ids[:, None]) + side_params
    return call_once(message_kernel, "message", 1e10, (flag,), operands, shapes)


def prompt_kernel(
    flag_ref,
    me_ref,
    block_ref,
    cotangent_ref,
    context_ref,
    ends_column,
    caption_ids,
    frame_ids,
    in_weight,
    in_bias,
    gain,
    shift,
    qkv_weight,
    out_weight,
    out_ref,
    grad_out_ref,
    vector_ref,
    send_ref,
    keep_ref,
    padded,
):
    count, width = block_ref.shape
    frames = count // TPF
    is_video = flag_ref[0] == 0

    @pl.when(is_video)
    def _():
        out_ref[...] = block_ref[...]
        padded[0:count, :] = cotangent_ref[...]
        padded[count:, :] = jnp.zeros((padded.shape[0] - count, width), padded.dtype)
        for frame in range(frames):
            rows = load_rows(padded, frame * TPF)
            rows = frame_tail(rows, True, 0.0)
            grad_out_ref[frame * FRAME : (frame + 1) * FRAME, :] = rows.astype(jnp.bfloat16)
        vector_ref[...] = jnp.zeros(vector_ref.shape, vector_ref.dtype)

    @pl.when(jnp.logical_not(is_video))
    def _():
        captions = ends_column.shape[0]
        place = lax.broadcasted_iota(jnp.int32, (captions, count), 1)
        chosen = (place == ends_column[...]).astype(jnp.bfloat16)
        source = product(chosen, block_ref[...]).astype(jnp.bfloat16)
        grad_ends = product(chosen, cotangent_ref[...])
        start = product(source, in_weight[...]) + in_bias[...]
        unit, spread = norm_parts(start)
        normed = (unit * gain[...] + shift[...]).astype(jnp.bfloat16)
        query = product(normed, qkv_weight[:, :width]).astype(jnp.bfloat16)
        context = context_ref[:, :width]
        pair = product(context, qkv_weight[:, width:]).astype(jnp.bfloat16)
        key, value = pair[:, :width], pair[:, width:]
        allowed = caption_ids[...] == frame_ids[...]
        mixed = side_attend(query, key, value, allowed)
        prompt = start + product(mixed, out_weight[...])
        high = prompt.astype(jnp.bfloat16)
        lower = (prompt - high.astype(jnp.float32)).astype(jnp.bfloat16)
        added = product_tn(chosen, jnp.concatenate([high, lower], axis=1))
        added = added[:, :width] + added[:, width:]
        out_ref[...] = (block_ref[...].astype(jnp.float32) + added).astype(jnp.bfloat16)
        grad_round = grad_ends.astype(jnp.bfloat16)
        grad_mixed = product_nt(grad_round, out_weight[...]).astype(jnp.bfloat16)
        grad_query, grad_key, grad_value = side_attend_back(query, key, value, allowed, grad_mixed)
        grad_query = grad_query.astype(jnp.bfloat16)
        mine = (me_ref[0] >> 1) & 1

        def put(block, row, values):
            place = ((block >> 2) << 1) | (block & 1)
            values = values.astype(jnp.bfloat16)

            @pl.when(((block >> 1) & 1) != mine)
            def _():
                send_ref[place, row : row + values.shape[0], :] = values

            @pl.when(((block >> 1) & 1) == mine)
            def _():
                keep_ref[place, row : row + values.shape[0], :] = values

        blocks = 2 * send_ref.shape[0]
        own = context_ref.shape[0] // blocks
        chunks = width // CHUNK
        grad_pair = jnp.concatenate([grad_key, grad_value], axis=1)
        devices = gathered_offsets(blocks)
        for block in range(blocks):
            part = grad_pair[block * own : (block + 1) * own]
            parts = [part[:, chunk * CHUNK : (chunk + 1) * CHUNK] for chunk in range(2 * chunks)]
            put(devices[block] ^ me_ref[0], send_ref.shape[1] - 2 * chunks * own, jnp.concatenate(parts, axis=0))
        grad_normed = product_nt(grad_query, qkv_weight[:, :width])
        grad_start = norm_back(unit, spread, gain[...], grad_normed) + grad_round.astype(jnp.float32)
        grad_start = grad_start.astype(jnp.bfloat16)
        vector_ref[...] = jnp.concatenate(
            [
                column_sum(grad_start.astype(jnp.float32)),
                column_sum(grad_normed * unit),
                column_sum(grad_normed),
            ],
            axis=0,
        )
        grad_source = product_nt(grad_start, in_weight[...])
        added = product_tn(chosen, grad_source.astype(jnp.bfloat16))
        grad_out_ref[0:count, :] = (cotangent_ref[...].astype(jnp.float32) + added).astype(jnp.bfloat16)
        grad_out_ref[count:, :] = jnp.zeros((frames * FRAME - count, width), jnp.bfloat16)
        rows = width // blocks
        for third, (left, right) in enumerate(
            ((source, grad_start), (normed, grad_query), (mixed, grad_round))
        ):
            part = product_tn(left, right).astype(jnp.bfloat16)
            for chunk in range(chunks):
                row = (third * chunks + chunk) * padded_rows(rows)
                columns = slice(chunk * CHUNK, (chunk + 1) * CHUNK)
                for block in range(blocks):
                    put(block, row, part[block * rows : (block + 1) * rows, columns])


def make_prompt(flag, me, size, block, cotangent, context, ends, caption_ids, frame_ids, side_params):
    count, width = block.shape
    padded = count // TPF * FRAME
    chunks = width // CHUNK
    rows = 3 * chunks * padded_rows(width // size) + 2 * chunks * (context.shape[0] // size)
    split = (size // 2, rows, CHUNK)
    shapes = [
        ((count, width), jnp.bfloat16),
        ((padded, width), jnp.bfloat16),
        ((3, width), jnp.float32),
        (split, jnp.bfloat16),
        (split, jnp.bfloat16),
    ]
    spare = -ends.shape[0] % 16
    ends = jnp.pad(ends, (0, spare), constant_values=-1)[:, None]
    caption_ids = jnp.pad(caption_ids, (0, spare), constant_values=-1)[:, None]
    operands = (block, cotangent, context, ends, caption_ids, frame_ids[None, :]) + side_params
    return pl.pallas_call(
        prompt_kernel,
        in_specs=[pl.BlockSpec(memory_space=pltpu.SMEM)] * 2 + in_vmem(len(operands)),
        out_specs=in_vmem(len(shapes)),
        out_shape=[jax.ShapeDtypeStruct(shape, dtype) for shape, dtype in shapes],
        scratch_shapes=[pltpu.VMEM((padded + 32, width), jnp.bfloat16)],
        compiler_params=pltpu.CompilerParams(vmem_limit_bytes=VMEM_BYTES),
        cost_estimate=cost(1e10, 2 * count * width * 8),
        name="prompt",
    )(flag, me, *operands)


def message_back_kernel(frames, flag_ref, *refs):
    grads, middles, rest = refs[:frames], refs[frames : 2 * frames], refs[2 * frames :]
    (
        message_ref,
        received_ref,
        start_ref,
        projected_ref,
        ids_row,
        ids_column,
        main_weight,
        main_gain,
        in_weight,
        gain,
        qkv_weight,
        out_weight,
        pair_ref,
        source_ref,
        line_ref,
    ) = rest
    width = message_ref.shape[1]

    @pl.when(flag_ref[0] == 0)
    def _():
        row = TPF % 16
        grad = jnp.concatenate(
            [one[...].astype(jnp.float32)[row : row + 1] for one in grads], axis=0
        ).astype(jnp.bfloat16)
        middle = jnp.concatenate(
            [one[...].astype(jnp.float32)[row : row + 1] for one in middles], axis=0
        )
        unit, spread = norm_parts(message_ref[...])
        back = norm_back(unit, spread, main_gain[...], product_nt(grad, main_weight[...]))
        grad_round = (back + middle + received_ref[...]).astype(jnp.bfloat16)
        grad_mixed = product_nt(grad_round, out_weight[...]).astype(jnp.bfloat16)
        projected = projected_ref[...]
        grad_parts = side_attend_back(
            projected[:, :width],
            projected[:, width : 2 * width],
            projected[:, 2 * width :],
            ids_column[...] == ids_row[...],
            grad_mixed,
        )
        grad_projected = jnp.concatenate(grad_parts, axis=1).astype(jnp.bfloat16)
        unit, spread = norm_parts(start_ref[...])
        grad_normed = product_nt(grad_projected, qkv_weight[...])
        grad_start = norm_back(unit, spread, gain[...], grad_normed) + grad_round.astype(jnp.float32)
        grad_start = grad_start.astype(jnp.bfloat16)
        source_ref[...] = product_nt(grad_start, in_weight[...])
        line_ref[...] = jnp.concatenate([grad_start, grad_projected, grad_round], axis=1)

    @pl.when(flag_ref[0] != 0)
    def _():
        source_ref[...] = jnp.zeros(source_ref.shape, source_ref.dtype)
        line_ref[:, : 2 * width] = pair_ref[...]
        line_ref[:, 2 * width :] = jnp.zeros((line_ref.shape[0], 3 * width), line_ref.dtype)


def message_back(flag, grad_projected, grad_middle, operands):
    width = grad_middle.shape[1]
    frames = grad_middle.shape[0] // FRAME
    shapes = [
        jax.ShapeDtypeStruct((frames, width), jnp.float32),
        jax.ShapeDtypeStruct((frames, 5 * width), jnp.bfloat16),
    ]

    def last_rows(columns):
        return [
            pl.BlockSpec(
                (16, columns),
                functools.partial(lambda place, *_: (place, 0), (frame * FRAME + TPF) // 16),
                pipeline_mode=pl.Buffered(buffer_count=1),
            )
            for frame in range(frames)
        ]

    return pl.pallas_call(
        functools.partial(message_back_kernel, frames),
        grid_spec=pltpu.PrefetchScalarGridSpec(
            num_scalar_prefetch=1,
            grid=(1,),
            in_specs=last_rows(3 * width)
            + last_rows(width)
            + [whole(value.shape) for value in operands],
            out_specs=[whole(shape.shape) for shape in shapes],
        ),
        out_shape=shapes,
        compiler_params=pltpu.CompilerParams(vmem_limit_bytes=46 * 2**20),
        cost_estimate=cost(1e10, 10**7),
        name="message_back",
    )(flag, *([grad_projected] * frames), *([grad_middle] * frames), *operands)


def pair_kernel(flag_ref, side_ref, weight_ref, pair_ref, context_ref):
    rows, width = context_ref.shape
    chunks = pair_ref.shape[1] // CHUNK
    first = side_ref.shape[0] - chunks * rows

    @pl.when(flag_ref[0] != 0)
    def _():
        parts = [side_ref[first + rows * chunk : first + rows * (chunk + 1), :] for chunk in range(chunks)]
        pair = jnp.concatenate(parts, axis=1).astype(jnp.bfloat16)
        pair_ref[...] = pair
        context_ref[...] = product_nt(pair, weight_ref[:, width:])

    @pl.when(flag_ref[0] == 0)
    def _():
        pair_ref[...] = jnp.zeros(pair_ref.shape, pair_ref.dtype)
        context_ref[...] = jnp.zeros(context_ref.shape, context_ref.dtype)


def pair_grad(flag, side, weight, frames):
    width = weight.shape[0]
    shapes = [((frames, 2 * width), jnp.bfloat16), ((frames, width), jnp.float32)]
    return call_once(pair_kernel, "pair_grad", 1e9, (flag,), (side, weight), shapes)


def pack_kernel(*refs):
    start = 0
    for one in refs[:-1]:
        for row in range(one.shape[0]):
            refs[-1][:, start : start + one.shape[1]] = one[row : row + 1, :]
            start += one.shape[1]


def pack_vectors(vectors):
    shapes = [((1, sum(one.size for one in vectors)), jnp.float32)]
    return call_once(pack_kernel, "pack_vectors", 1e6, (), vectors, shapes)[0]


def side_weight_kernel(
    flag_ref,
    me_ref,
    context_ref,
    packed_ref,
    line_ref,
    side_ref,
    weight_ref,
    gain_ref,
    shift_ref,
    in_ref,
    qkv_ref,
    out_ref,
    vector_ref,
):
    own, width = in_ref.shape

    def own_columns(ref, place):
        part = ref[:, place * width : (place + 1) * width].astype(jnp.float32)
        return pltpu.roll(part, (width - me_ref[0] * own) % width, axis=1)[:, :own].astype(jnp.bfloat16)

    @pl.when(flag_ref[0] == 0)
    def _():
        in_ref[...] = product_tn(own_columns(packed_ref, 0), line_ref[:, :width])
        qkv_ref[...] = product_tn(own_columns(packed_ref, 1), line_ref[:, width : 4 * width])
        out_ref[...] = product_tn(own_columns(packed_ref, 2), line_ref[:, 4 * width :])
        lines = line_ref[...].astype(jnp.float32)
        vector_ref[0:1, :] = column_sum(lines[:, :width])
        unit = packed_ref[:, width : 2 * width].astype(jnp.float32) - shift_ref[...]
        grad_normed = product_nt(line_ref[:, width : 4 * width], weight_ref[...])
        vector_ref[1:2, :] = column_sum(grad_normed * unit) / gain_ref[...]
        vector_ref[2:3, :] = column_sum(grad_normed)

    @pl.when(flag_ref[0] != 0)
    def _():
        chunks = width // CHUNK
        spaced = padded_rows(own)

        def matrix(third):
            rows = [(third * chunks + chunk) * spaced for chunk in range(chunks)]
            return jnp.concatenate([side_ref[row : row + own, :] for row in rows], axis=1)

        in_ref[...] = matrix(0)
        qkv_ref[:, :width] = matrix(1)
        qkv_ref[:, width:] = product_tn(own_columns(context_ref, 0), line_ref[:, : 2 * width])
        out_ref[...] = matrix(2)
        vector_ref[...] = jnp.zeros(vector_ref.shape, vector_ref.dtype)


def side_weight_grads(flag, me, size, context, packed, lines, side, weight, gain, shift):
    width = context.shape[1]
    own = width // size
    shapes = [
        ((own, width), jnp.float32),
        ((own, 3 * width), jnp.float32),
        ((own, width), jnp.float32),
        ((3, width), jnp.float32),
    ]
    operands = (context, packed, lines, side, weight, gain, shift)
    return call_once(side_weight_kernel, "side_weight_grads", 1e9, (flag, me), operands, shapes)


def vector_kernel(size, widths, flag_ref, me_ref, line_ref, side_ref, *out_refs):
    start = 0
    third = out_refs[0].shape[1] * size
    for place, (width, out_ref) in enumerate(zip(widths, out_refs)):
        total = line_ref[:, start : start + width]
        start += width
        if place == 2:
            total = jnp.concatenate([total[:, :third], total[:, 2 * third :]], axis=1)
            width = 2 * third
        own = width // size
        side = place - (len(widths) - 3)
        if side >= 0:
            total = jnp.where(flag_ref[0] == 0, side_ref[side : side + 1, :], total)
        total = jnp.broadcast_to(total, (8, width))
        out_ref[...] = pltpu.roll(total, (width - me_ref[0] * own) % width, axis=1)[0:1, :own]


def own_vectors(flag, me, size, line, side, widths):
    shapes = [((1, width // size), jnp.float32) for width in widths]
    shapes[2] = ((1, 2 * widths[0] // size), jnp.float32)
    kernel = functools.partial(vector_kernel, size, tuple(widths))
    return call_once(kernel, "own_vectors", 1e6, (flag, me), (line, side), shapes)


def pair_list(size, distance):
    return [(place, place ^ distance) for place in range(size)]


def group_pairs(size, distance, group):
    return [(group * size + place, group * size + (place ^ distance)) for place in range(size)]


def bit_count(size):
    return size.bit_length() - 1


def gather_order(size):
    return list(range(bit_count(size)))[::-1]


def gathered_offsets(size):
    return [
        sum((((place >> step) & 1) << bit for step, bit in enumerate(gather_order(size))))
        for place in range(size)
    ]


def gathered_devices(me, size):
    return me ^ jnp.array(gathered_offsets(size), jnp.int32)


def double_gather(values, size, send):
    for bit in gather_order(size):
        values = jnp.concatenate([values, send(values, 1 << bit)], axis=0)
    return values


class Sum:
    def __init__(self, size, send, parts, layout):
        self.send, self.layout = send, layout
        self.bits = list(range(2, bit_count(size)))
        self.orders = [[0, 1], [1, 0]]
        self.keeps, self.arrived = [], []
        for side in range(2):
            self.launch(parts[2 * side], parts[2 * side + 1], self.orders[side].pop(0))

    def launch(self, sent, kept, bit):
        self.keeps.append(kept)
        self.arrived.append(self.send(sent, 1 << bit))

    def values(self):
        return [value for pair in zip(self.keeps, self.arrived) for value in pair]

    def items(self):
        values = self.values()
        if self.orders[0]:
            return [("split", values[2 * side : 2 * side + 2], self.orders[side][0]) for side in range(2)]
        if self.bits:
            return [("split", values, self.bits[0])]
        return [("end", values, self.layout)]

    def take(self, results):
        self.keeps, self.arrived = [], []
        if self.orders[0]:
            for side in range(2):
                self.launch(results.pop(0), results.pop(0), self.orders[side].pop(0))
        elif self.bits:
            self.launch(results.pop(0), results.pop(0), self.bits.pop(0))
        else:
            self.result = [results.pop(0) for _ in self.layout]


class PlainSum:
    def __init__(self, size, send, sent, kept):
        self.send, self.kept = send, kept
        self.bits = [bit for bit in range(bit_count(size)) if bit != 1]
        self.arrived = send(sent, 2)

    def items(self):
        if self.bits:
            return [("split", [self.kept, self.arrived], self.bits[0])]
        return [("raw", [self.kept, self.arrived], None)]

    def take(self, results):
        if self.bits:
            sent, self.kept = results.pop(0), results.pop(0)
            self.arrived = self.send(sent, 1 << self.bits.pop(0))
        else:
            self.result = results.pop(0)


class Spread:
    def __init__(self, size, send, values, kind, plane=False):
        self.kind, self.send, self.held = kind, send, values
        self.steps = [[1 << bit] for bit in gather_order(size)]
        if plane:
            self.steps = self.steps[:-2] + [[2, 1, 3]]
        self.launch()

    def launch(self):
        self.arrived = [self.send(self.held, distance) for distance in self.steps.pop(0)]

    def items(self):
        return [(self.kind, [self.held] + self.arrived, None)]

    def take(self, results):
        self.held = results.pop(0)
        if self.steps:
            self.launch()
        else:
            self.result = self.held


def tie(first, second):
    return lax.optimization_barrier((first, second))


def advance(me, streams, after, before=None):
    streams = [one for one in streams if not hasattr(one, "result")]
    if not streams:
        return (after, before)
    items = [one.items() for one in streams]
    flat = [item for one in items for item in one]
    operands, after = tie([item[1] for item in flat], after)
    results = combine(me, [(item[0], values, item[2]) for item, values in zip(flat, operands)])
    results, before = tie(list(results), before)
    for one in streams:
        one.take(results)
    return (after, before)


def on_device(
    size,
    tokens,
    frame_video,
    caption_video,
    caption_len,
    attn_norm_gain,
    attn_norm_shift,
    qkv_weight,
    query_value_bias,
    proj_weight,
    proj_bias,
    mlp_norm_gain,
    mlp_norm_shift,
    fc_in_weight,
    fc_in_bias,
    fc_out_weight,
    fc_out_bias,
    side_in_weight,
    side_in_bias,
    side_norm_gain,
    side_norm_shift,
    side_qkv_weight,
    side_out_weight,
    cotangent,
):
    main_params = tuple(
        (
            member[0]
            for member in (
                attn_norm_gain,
                attn_norm_shift,
                qkv_weight,
                query_value_bias,
                proj_weight,
                proj_bias,
                mlp_norm_gain,
                mlp_norm_shift,
                fc_in_weight,
                fc_in_bias,
                fc_out_weight,
                fc_out_bias,
            )
        )
    )
    side_params = tuple(
        (
            member[0]
            for member in (
                side_in_weight,
                side_in_bias,
                side_norm_gain,
                side_norm_shift,
                side_qkv_weight,
                side_out_weight,
            )
        )
    )
    token_rows = tokens[0]
    cotangent_rows = cotangent[0]
    row_count, model_width = token_rows.shape
    frame_count = row_count // TPF
    me = lax.axis_index("dp")
    is_video = lax.axis_index("grp") == 0

    def to_text(values):
        return lax.ppermute(values, ("grp", "dp"), [(i, size + i) for i in range(size)])

    def to_video(values):
        return lax.ppermute(values, ("grp", "dp"), [(size + i, i) for i in range(size)])

    def in_all(values, distance):
        return lax.ppermute(values, "dp", pair_list(size, distance))

    def in_video(values, distance):
        return lax.ppermute(values, ("grp", "dp"), group_pairs(size, distance, 0))

    def in_text(values, distance):
        return lax.ppermute(values, ("grp", "dp"), group_pairs(size, distance, 1))

    flag = lax.axis_index("grp").astype(jnp.int32).reshape(1)
    me_one = me.astype(jnp.int32).reshape(1)
    side_rows = tuple((member if member.ndim == 2 else member[None] for member in side_params))
    frame_order = frame_video.reshape(size, frame_count)[gathered_devices(me, size)]
    frame_ids = frame_order[0]
    message, packed, side_start, side_projected = make_message(
        flag, token_rows, frame_ids, side_rows
    )
    context = to_text(packed[:, :model_width])
    side_inputs = packed[:, model_width:]
    caption_ends = jnp.cumsum(caption_len[0]) - 1
    places = jnp.arange(frame_count * FRAME, dtype=jnp.int32)
    caption_starts = jnp.concatenate([caption_ends + 1 - caption_len[0], jnp.full((1,), row_count)])
    first = jnp.max(
        jnp.where(places[:, None] >= caption_starts[None, :], caption_starts[None, :], 0), axis=1
    ).astype(jnp.int32)
    bias = main_params[3]
    full_bias = jnp.concatenate(
        [bias[:model_width], jnp.zeros((model_width,), jnp.float32), bias[model_width:]]
    )
    params = tuple(
        (
            member if member.ndim == 2 else member[None]
            for member in main_params[:3] + (full_bias,) + main_params[4:]
        )
    )
    normed, projected, mixed, middle, normed_two, act, slope, hidden, block_rows = forward(
        flag, token_rows, message, first[:, None], params
    )
    context = double_gather(context, size, in_text)
    out_rows, grad_out, text_vectors, *parts = make_prompt(
        flag,
        me_one,
        size,
        block_rows,
        cotangent_rows,
        context,
        caption_ends,
        caption_video,
        frame_order.reshape(-1),
        side_rows,
    )
    own_width = model_width // size
    side_sum = PlainSum(size, in_text, parts[0], parts[1])
    grad_fc_out_bias, *parts = out_weight_grad(me_one, size, act, grad_out)
    parts, grad_out = tie(parts, grad_out)
    out_sum = Sum(size, in_all, parts, [(fc_out_weight.shape[1] // size, 1)])
    grad_out, side_inputs = tie(grad_out, side_inputs)
    all_inputs = Spread(size, in_video, side_inputs, "stack")
    grad_pre, grad_fc_in_bias = pre_grad(grad_out, slope, params[10])
    grad_pre, _ = advance(me_one, [side_sum, all_inputs], grad_pre)
    grad_middle, grad_mixed, middle_vectors = middle_grad(
        grad_pre, grad_out, middle, params[8], params[4], params[6]
    )
    grad_middle, normed_two = advance(
        me_one, [out_sum, side_sum, all_inputs], grad_middle, normed_two
    )
    parts = in_weight_grad(me_one, size, normed_two, grad_pre, mixed, grad_middle)
    chunks = model_width // (2 * CHUNK)
    parts, grad_mixed = tie(parts, grad_mixed)
    in_sum = Sum(size, in_all, parts, [(own_width, 4 * chunks), (own_width, chunks)])
    _, grad_mixed = advance(me_one, [out_sum, side_sum, all_inputs], parts, grad_mixed)
    grad_projected = attend_back(flag, projected, grad_mixed, first.reshape(frame_count, 1, FRAME))
    grad_projected, normed = advance(
        me_one, [out_sum, in_sum, side_sum, all_inputs], grad_projected, normed
    )
    while not hasattr(side_sum, "result"):
        advance(me_one, [side_sum, all_inputs], grad_projected)
    pair_rows, context_grad = pair_grad(flag, side_sum.result, side_rows[4], frame_count)
    received = to_video(context_grad)
    bias_totals, first_vectors, *parts = qkv_weight_grad(
        me_one, size, normed, grad_projected, params[2], params[0], params[1]
    )
    qkv_sum = Sum(size, in_all, parts, [(own_width, 3 * chunks)])
    line = pack_vectors(
        (
            first_vectors,
            bias_totals,
            middle_vectors,
            grad_fc_in_bias,
            grad_fc_out_bias,
            text_vectors,
        )
    )
    line_sum = Spread(size, in_all, line, "add")
    bias_totals, grad_middle = advance(me_one, [out_sum, in_sum], bias_totals, grad_middle)
    grad_source, grad_lines = message_back(
        flag,
        grad_projected,
        grad_middle,
        (message, received, side_start, side_projected, frame_ids[None, :], frame_ids[:, None])
        + (params[2], params[0], side_rows[0], side_rows[2], side_rows[4], side_rows[5], pair_rows),
    )
    widths = [model_width] * 2 + [3 * model_width] + [model_width] * 3
    widths += [grad_fc_in_bias.shape[1]] + [model_width] * 4
    all_lines = Spread(size, in_all, grad_lines, "stack", plane=True)
    streams = [out_sum, in_sum, qkv_sum, line_sum]
    _, grad_source = advance(me_one, streams, grad_source, grad_source)
    token_operands = (hidden, grad_middle, grad_source, params[2], params[0])
    before = token_grad(0, flag, grad_projected, *token_operands)
    streams = [out_sum, in_sum, qkv_sum, line_sum, all_lines]
    before, _ = advance(me_one, streams, before)
    grad_tokens = token_grad(1, flag, grad_projected, *token_operands, before=before)
    while not all((hasattr(one, "result") for one in streams)):
        grad_tokens, _ = advance(me_one, streams, grad_tokens)
    grad_in_weight, grad_side_qkv, grad_side_out, video_vectors = side_weight_grads(
        flag,
        me_one,
        size,
        context,
        all_inputs.result,
        all_lines.result,
        side_sum.result,
        side_rows[4],
        side_rows[2],
        side_rows[3],
    )
    (
        grad_attn_gain,
        grad_attn_shift,
        grad_qv_bias,
        grad_mlp_gain,
        grad_mlp_shift,
        grad_proj_bias,
        grad_fc_in_bias,
        grad_fc_out_bias,
        grad_in_bias,
        grad_side_gain,
        grad_side_shift,
    ) = own_vectors(flag, me_one, size, line_sum.result, video_vectors, widths)
    summed = (
        grad_attn_gain,
        grad_attn_shift,
        qkv_sum.result[0][None],
        grad_qv_bias,
        in_sum.result[1][None],
        grad_proj_bias,
        grad_mlp_gain,
        grad_mlp_shift,
        in_sum.result[0][None],
        grad_fc_in_bias,
        out_sum.result[0][None],
        grad_fc_out_bias,
        grad_in_weight[None],
        grad_in_bias,
        grad_side_gain,
        grad_side_shift,
        grad_side_qkv[None],
        grad_side_out[None],
    )
    return tuple([out_rows[None], grad_tokens[None]] + list(summed))


def solution(mesh):
    placed = (
        P("grp", "dp", None),
        P(),
        P("dp"),
        P("dp", None),
        P("grp", None),
        P("grp", None),
        P("grp", None, None),
        P("grp", None),
        P("grp", None, None),
        P("grp", None),
        P("grp", None),
        P("grp", None),
        P("grp", None, None),
        P("grp", None),
        P("grp", None, None),
        P("grp", None),
        P("grp", None, None),
        P("grp", None),
        P("grp", None),
        P("grp", None),
        P("grp", None, None),
        P("grp", None, None),
        P("grp", "dp", None),
    )
    return jax.shard_map(
        functools.partial(on_device, mesh.shape["dp"]),
        mesh=mesh,
        in_specs=placed,
        out_specs=(
            P("grp", "dp", None),
            P("grp", "dp", None),
            P("grp", "dp"),
            P("grp", "dp"),
            P("grp", "dp", None),
            P("grp", "dp"),
            P("grp", "dp", None),
            P("grp", "dp"),
            P("grp", "dp"),
            P("grp", "dp"),
            P("grp", "dp", None),
            P("grp", "dp"),
            P("grp", "dp", None),
            P("grp", "dp"),
            P("grp", "dp", None),
            P("grp", "dp"),
            P("grp", "dp"),
            P("grp", "dp"),
            P("grp", "dp", None),
            P("grp", "dp", None),
        ),
        check_vma=False,
    )
```

```python
import functools

import jax
import jax.numpy as jnp
from jax import lax
from jax.experimental import pallas as pl
from jax.experimental.pallas import tpu as pltpu
from jax.sharding import PartitionSpec as P

HEADS = 12
HD = 64
TPF = 197
FRAME = 208
PRIOR = 80
CHUNK = 384
VMEM_BYTES = 58 * 2**20
SUB_BLOCKS = ((0, 112, -80, 192), (112, 96, 32, 176))


def product(left_side, right_side):
    return jnp.dot(left_side, right_side, preferred_element_type=jnp.float32)


def product_tn(left_side, right_side):
    return lax.dot_general(
        left_side, right_side, (((0,), (0,)), ((), ())), preferred_element_type=jnp.float32
    )


def product_nt(left_side, right_side):
    return lax.dot_general(
        left_side, right_side, (((1,), (1,)), ((), ())), preferred_element_type=jnp.float32
    )


def cost(flops, size):
    return pl.CostEstimate(flops=int(flops), bytes_accessed=int(size), transcendentals=0)


def padded_rows(rows):
    return -(-rows // 16) * 16


def split_shapes(size, rows):
    return [jax.ShapeDtypeStruct((size // 2, rows, CHUNK), jnp.bfloat16) for _ in range(4)]


def store_block(stage, side, block, me, row, values):
    differs = block ^ me
    right = side == 1
    sent = jnp.where(right, (differs >> 1) & 1, differs & 1)
    place = jnp.where(right, ((block >> 2) << 1) | (block & 1), block >> 1)
    stage[side, sent, place, pl.ds(row, values.shape[0]), :] = values


def stage_shapes(size, rows, steps):
    return [
        pltpu.VMEM((2, 2, size // 2, rows, CHUNK), jnp.bfloat16),
        pltpu.SemaphoreType.DMA((steps, 4)),
    ]


def rows_out(stage, outs, sems, step, side, row, count):
    rows = pl.ds(row, count)
    return [
        pltpu.make_async_copy(
            stage.at[side, sent, :, rows, :],
            outs[2 * side + 1 - sent].at[:, rows, :],
            sems.at[step, sent],
        )
        for sent in range(2)
    ]


def start_rows(stage, outs, sems, step, side, row, count):
    for index in range(2):

        @pl.when(side == index)
        def _():
            for copy in rows_out(stage, outs, sems, step, index, row, count):
                copy.start()


def wait_rows(stage, outs, sems, step, side, row, count):
    for copy in rows_out(stage, outs, sems, step, side, row, count):
        copy.wait()


def in_hbm(count):
    return [pl.BlockSpec(memory_space=pl.ANY) for _ in range(count)]


def combine_kernel(kinds, me_ref, *refs):
    refs = list(refs)
    sources = [[refs.pop(0) for _ in range(kind[1])] for kind in kinds]
    for (name, _, detail), parts in zip(kinds, sources):

        def total(side, index):
            keep, arrived = parts[2 * side], parts[2 * side + 1]
            return keep[index].astype(jnp.float32) + arrived[index].astype(jnp.float32)

        if name == "raw":
            refs.pop(0)[...] = total(0, 0)
        elif name == "add":
            refs.pop(0)[...] = sum((part[...] for part in parts[1:]), parts[0][...])
        elif name == "stack":
            refs.pop(0)[...] = jnp.concatenate([part[...] for part in parts], axis=0)
        elif name == "fan":
            mine = (me_ref[0] >> detail) & 3
            rows = parts[0].shape[1]
            for offset in range(4):
                out = refs.pop(0)
                for side in range(len(parts) // 2):
                    value = total(side, mine ^ offset)
                    out[side * rows : (side + 1) * rows, :] = value.astype(out.dtype)
        elif name == "end":
            if len(parts[0].shape) == 2:
                value = sum((part[...].astype(jnp.float32) for part in parts[1:]), parts[0][...].astype(jnp.float32))
            else:
                value = total(0, 0)
            half = value.shape[0] // 2
            start = 0
            for rows, chunks in detail:
                out = refs.pop(0)
                for side in range(2):
                    for chunk in range(chunks):
                        row = side * half + start + chunk * padded_rows(rows)
                        column = (side * chunks + chunk) * CHUNK
                        out[:, column : column + CHUNK] = value[row : row + rows]
                start += chunks * padded_rows(rows)
        else:
            send, held = refs.pop(0), refs.pop(0)
            mine = (me_ref[0] >> detail) & 1
            rows = parts[0].shape[1]
            for side in range(len(parts) // 2):
                place = slice(side * rows, (side + 1) * rows)
                for index in range(held.shape[0]):
                    held[index, place, :] = total(side, 2 * index + mine).astype(held.dtype)
                    send[index, place, :] = total(side, 2 * index + 1 - mine).astype(send.dtype)


def combine(me, items):
    shapes, kinds, operands = [], [], []
    for name, values, detail in items:
        kinds.append((name, len(values), detail))
        operands += values
        rows = values[0].shape[1]
        if name == "fan":
            shape = (len(values) // 2 * rows, CHUNK)
            shapes += [jax.ShapeDtypeStruct(shape, jnp.bfloat16)] * 4
        elif name == "raw":
            shapes.append(jax.ShapeDtypeStruct((rows, CHUNK), jnp.float32))
        elif name in ("add", "stack"):
            times = len(values) if name == "stack" else 1
            shape = (times * values[0].shape[0], values[0].shape[1])
            shapes.append(jax.ShapeDtypeStruct(shape, values[0].dtype))
        elif name == "end":
            for own, chunks in detail:
                shapes.append(jax.ShapeDtypeStruct((own, 2 * chunks * CHUNK), jnp.float32))
        else:
            sides = len(values) // 2
            half = (values[0].shape[0] // 2, sides * rows, CHUNK)
            shapes += [jax.ShapeDtypeStruct(half, jnp.bfloat16)] * 2
    size = 3 * sum(value.size for value in operands)
    return pl.pallas_call(
        functools.partial(combine_kernel, tuple(kinds)),
        in_specs=[pl.BlockSpec(memory_space=pltpu.SMEM)] + in_vmem(len(operands)),
        out_specs=in_vmem(len(shapes)),
        out_shape=shapes,
        compiler_params=pltpu.CompilerParams(vmem_limit_bytes=30 * 2**20),
        cost_estimate=cost(size, size),
        name="combine",
    )(me, *operands)


def in_vmem(count):
    return [pl.BlockSpec(memory_space=pltpu.VMEM) for _ in range(count)]


def norm_parts(values):
    center = values - jnp.mean(values, axis=-1, keepdims=True)
    spread = lax.rsqrt(jnp.mean(center * center, axis=-1, keepdims=True) + 1e-05)
    return (center * spread, spread)


def norm_back(unit, spread, gain, grad):
    grad_unit = grad * gain
    first = jnp.mean(grad_unit, axis=-1, keepdims=True)
    second = jnp.mean(grad_unit * unit, axis=-1, keepdims=True)
    return spread * (grad_unit - first - unit * second)


def column_sum(values):
    return jnp.sum(values, axis=0, keepdims=True)


def lane_is_low(shape):
    return lax.broadcasted_iota(jnp.int32, shape, len(shape) - 1) < HD


def frame_start(is_video, frame):
    return jnp.where(is_video, TPF, FRAME) * frame


def load_rows(buffer, start):
    base = start // 16 * 16
    window = buffer[pl.ds(pl.multiple_of(base, 16), FRAME + 24), :].astype(jnp.float32)
    return pltpu.roll(window, (FRAME + 24 - (start - base)) % (FRAME + 24), axis=0)[:FRAME]


def store_rows(buffer, start, values):
    base = pl.multiple_of(start // 16 * 16, 16)
    pad = jnp.zeros((24, values.shape[1]), jnp.float32)
    moved = pltpu.roll(jnp.concatenate([values, pad], axis=0), start - base, axis=0)
    old = buffer[pl.ds(base, 16), :].astype(jnp.float32)
    place = lax.broadcasted_iota(jnp.int32, old.shape, 0)
    first = jnp.where(place < start - base, old, moved[:16])
    buffer[pl.ds(base, 16), :] = first.astype(buffer.dtype)
    buffer[pl.ds(base + 16, FRAME), :] = moved[16 : FRAME + 16].astype(buffer.dtype)


def frame_tail(rows, is_video, last_row):
    first = TPF // 8 * 8
    tail = rows[first:]
    place = lax.broadcasted_iota(jnp.int32, tail.shape, 0) + first
    video = jnp.where(place == TPF, last_row, jnp.where(place < TPF, tail, 0.0))
    return jnp.concatenate([rows[:first], jnp.where(is_video, video, tail)], axis=0)


def head_mask(shape, head):
    lane = lax.broadcasted_iota(jnp.int32, shape, len(shape) - 1)
    return (lane >= head * HD) & (lane < (head + 1) * HD)


def stack_heads(rows):
    zero = jnp.zeros_like(rows)
    return jnp.concatenate(
        [jnp.where(head_mask(rows.shape, head), rows, zero) for head in range(HEADS)], axis=0
    )


def pick_heads(stacked):
    count = stacked.shape[0] // HEADS
    total = jnp.zeros((count, stacked.shape[1]), jnp.float32)
    for head in range(HEADS):
        part = stacked[head * count : (head + 1) * count]
        total = total + jnp.where(head_mask(part.shape, head), part, 0.0)
    return total


def side_weights(query, key, allowed):
    stacked = stack_heads(query * jnp.asarray(HD**-0.5, query.dtype))
    bias = jnp.where(allowed, 0.0, -1e30)
    scores = product_nt(stacked, key) + jnp.concatenate([bias] * HEADS, axis=0)
    weights = jnp.exp(scores - jnp.max(scores, axis=-1, keepdims=True))
    return (stacked, weights / jnp.sum(weights, axis=-1, keepdims=True))


def side_attend(query, key, value, allowed):
    _, weights = side_weights(query, key, allowed)
    return pick_heads(product(weights.astype(jnp.bfloat16), value)).astype(jnp.bfloat16)


def side_attend_back(query, key, value, allowed, grad):
    stacked, weights = side_weights(query, key, allowed)
    grads = stack_heads(grad)
    grad_soft = product_nt(grads, value)
    inner = jnp.sum(weights * grad_soft, axis=-1, keepdims=True)
    grad_scores = (weights * (grad_soft - inner)).astype(jnp.bfloat16)
    return (
        pick_heads(product(grad_scores, key)) * HD**-0.5,
        product_tn(grad_scores, stacked),
        product_tn(weights.astype(jnp.bfloat16), grads),
    )


def attend_pair(query, key, value, bias):
    count = query.shape[0]
    low = lane_is_low(query.shape)
    query = query * jnp.asarray(HD**-0.5, query.dtype)
    zero = jnp.zeros_like(query)
    stacked = jnp.concatenate([jnp.where(low, query, zero), jnp.where(low, zero, query)], axis=0)
    scores = product_nt(stacked, key)
    weights = []
    for head in range(2):
        one = scores[head * count : (head + 1) * count] + bias
        weights.append(jnp.exp(one - jnp.max(one, axis=-1, keepdims=True)).astype(jnp.bfloat16))
    wide = jnp.concatenate([value, jnp.ones_like(value)], axis=1)
    summed = product(jnp.concatenate(weights, axis=0), wide)
    mixed = summed[:, :128] / summed[:, 128:]
    return jnp.where(low, mixed[:count], mixed[count:]).astype(jnp.bfloat16)


def attend_back_group(parts):
    masked, scores, softs, grad_scores = [], [], [], []
    for query, key, value, grad, bias in parts:
        low = lane_is_low(query.shape)
        query = query * jnp.asarray(HD**-0.5, query.dtype)
        zero = jnp.zeros_like(query)
        queries = jnp.concatenate([jnp.where(low, query, zero), jnp.where(low, zero, query)], axis=0)
        grads = jnp.concatenate([jnp.where(low, grad, zero), jnp.where(low, zero, grad)], axis=0)
        masked.append((queries, grads))
    for (query, key, value, grad, bias), (queries, grads) in zip(parts, masked):
        scores.append((product_nt(key, queries) + bias, product_nt(value, grads)))
    for one, grad_soft in scores:
        soft = jnp.exp(one - jnp.max(one, axis=0, keepdims=True))
        soft = soft * (1.0 / column_sum(soft))
        inner = soft * grad_soft
        grad_scores.append((inner - soft * column_sum(inner)).astype(jnp.bfloat16))
        softs.append(soft.astype(jnp.bfloat16))
    results = []
    for (query, key, value, grad, bias), (queries, grads), soft, back in zip(parts, masked, softs, grad_scores):
        count = query.shape[0]
        grad_query = product_tn(back, key) * HD**-0.5
        grad_query = jnp.where(lane_is_low(query.shape), grad_query[:count], grad_query[count:])
        results.append((grad_query, product(back, queries), product(soft, grads)))
    return results


def forward_kernel(
    frames,
    flag_ref,
    token_ref,
    message_ref,
    first_ref,
    gain_one,
    shift_one,
    qkv_source,
    qkv_bias,
    proj_source,
    proj_bias,
    gain_two,
    shift_two,
    fc_in_source,
    fc_in_bias,
    fc_out_source,
    fc_out_bias,
    normed_ref,
    projected_ref,
    mixed_ref,
    middle_ref,
    normed_two_ref,
    act_ref,
    slope_ref,
    hidden_ref,
    block_ref,
    held,
    source,
    target,
    next_hidden,
    next_normed,
    qkv_weight,
    proj_weight,
    fc_in_weight,
    fc_out_weight,
    sems,
):
    step = pl.program_id(0)
    last = pl.num_programs(0) - 1
    is_video = flag_ref[0] == 0
    count, width = token_ref.shape
    rows = frames * FRAME
    loads = [
        pltpu.make_async_copy(origin, place, sems.at[index])
        for index, (origin, place) in enumerate(
            (
                (qkv_source, qkv_weight),
                (proj_source, proj_weight),
                (fc_in_source, fc_in_weight),
                (fc_out_source, fc_out_weight),
            )
        )
    ]

    def prepare(index):
        for frame in range(frames):
            part = load_rows(source, frame_start(is_video, index * frames + frame))
            message = message_ref[pl.ds(index * frames + frame, 1), :]
            part = frame_tail(part, is_video, message)
            place = slice(frame * FRAME, (frame + 1) * FRAME)
            next_hidden[place, :] = part
            unit, _ = norm_parts(part)
            next_normed[place, :] = (unit * gain_one[...] + shift_one[...]).astype(jnp.bfloat16)

    @pl.when(step == 0)
    def _():
        for load in loads:
            load.start()
        source[0:count, :] = token_ref[...]
        source[count:, :] = jnp.zeros((source.shape[0] - count, width), source.dtype)
        prepare(0)
        loads[0].wait()

    hidden = next_hidden[...]
    hidden_ref[...] = hidden.astype(jnp.bfloat16)
    normed = next_normed[...]
    normed_ref[...] = normed

    @pl.when(step == 0)
    def _():
        held[0:PRIOR, :] = jnp.zeros((PRIOR, held.shape[1]), held.dtype)

    @pl.when(step > 0)
    def _():
        held[0:PRIOR, :] = held[rows : rows + PRIOR, :]

    for start in range(0, 3 * width, width):
        columns = slice(start, start + width)
        part = (product(normed, qkv_weight[:, columns]) + qkv_bias[:, columns]).astype(jnp.bfloat16)
        held[PRIOR:, columns] = part
        projected_ref[:, columns] = part

    def attend(frame, query_start, query_count, key_start, key_count, bias):
        query_rows = pl.ds(PRIOR + frame * FRAME + query_start, query_count)
        key_rows = pl.ds(PRIOR + frame * FRAME + key_start, key_count)
        for pair in range(0, width, 128):
            mixed_ref[pl.ds(frame * FRAME + query_start, query_count), pair : pair + 128] = attend_pair(
                held[query_rows, pair : pair + 128],
                held[key_rows, width + pair : width + pair + 128],
                held[key_rows, 2 * width + pair : 2 * width + pair + 128],
                bias,
            )

    @pl.when(is_video)
    def _():
        place = lax.broadcasted_iota(jnp.int32, (FRAME, FRAME), 1)
        bias = jnp.where(place <= TPF, 0.0, -1e30)
        for frame in range(frames):
            attend(frame, 0, FRAME, 0, FRAME, bias)

    @pl.when(jnp.logical_not(is_video))
    def _():
        for frame in range(frames):
            for query_start, query_count, key_start, key_count in SUB_BLOCKS:
                base = step * rows + frame * FRAME
                shape = (query_count, key_count)
                key_place = base + key_start + lax.broadcasted_iota(jnp.int32, shape, 1)
                query_place = base + query_start + lax.broadcasted_iota(jnp.int32, shape, 0)
                first = first_ref[pl.ds(frame * FRAME + query_start, query_count), :]
                allowed = (key_place >= first) & (key_place <= query_place)
                bias = jnp.where(allowed, 0.0, -1e30)
                attend(frame, query_start, query_count, key_start, key_count, bias)

    @pl.when(step == 0)
    def _():
        for load in loads[1:]:
            load.wait()

    middle = hidden + product(mixed_ref[...], proj_weight[...]) + proj_bias[...]
    middle_ref[...] = middle.astype(jnp.bfloat16)
    unit, _ = norm_parts(middle)
    normed = (unit * gain_two[...] + shift_two[...]).astype(jnp.bfloat16)
    normed_two_ref[...] = normed
    total = middle + fc_out_bias[...]
    for start in range(0, fc_in_weight.shape[1], width):
        columns = slice(start, start + width)
        pre = product(normed, fc_in_weight[:, columns]) + fc_in_bias[:, columns]
        gate = 0.5 + 0.5 * jnp.tanh(0.851 * pre)
        value = pre * gate
        act = value.astype(jnp.bfloat16)
        act_ref[:, columns] = act
        slope_ref[:, columns] = (gate + 1.702 * value * (1.0 - gate)).astype(jnp.bfloat16)
        total = total + product(act, fc_out_weight[columns, :])
        if start == 0:
            prepare(jnp.minimum(step + 1, last))
    for frame in range(frames):
        start = frame_start(is_video, step * frames + frame)
        store_rows(target, start, total[frame * FRAME : (frame + 1) * FRAME])

    @pl.when(step == last)
    def _():
        block_ref[...] = target[0:count, :]


def whole(shape):
    return pl.BlockSpec(
        shape, lambda *_: (0,) * len(shape), pipeline_mode=pl.Buffered(buffer_count=1)
    )


def forward(flag, tokens, message, first, params, frames=2):
    token_count, width = tokens.shape
    count = token_count // TPF * FRAME
    rows = frames * FRAME
    hidden = params[8].shape[1]

    def by_rows(columns):
        return pl.BlockSpec((rows, columns), lambda i, _: (i, 0))

    widths = (width, 3 * width, width, width, width, hidden, hidden, width)
    return pl.pallas_call(
        functools.partial(forward_kernel, frames),
        grid_spec=pltpu.PrefetchScalarGridSpec(
            num_scalar_prefetch=1,
            grid=(count // rows,),
            in_specs=[whole(tokens.shape), whole(message.shape), by_rows(1)]
            + [in_hbm(1)[0] if member.shape[0] > 1 else whole(member.shape) for member in params],
            out_specs=[by_rows(columns) for columns in widths] + [whole(tokens.shape)],
            scratch_shapes=[
                pltpu.VMEM((rows + PRIOR, 3 * width), jnp.bfloat16),
                pltpu.VMEM((count + 32, width), jnp.bfloat16),
                pltpu.VMEM((count + 32, width), jnp.bfloat16),
                pltpu.VMEM((rows, width), jnp.float32),
                pltpu.VMEM((rows, width), jnp.bfloat16),
            ]
            + [pltpu.VMEM(member.shape, member.dtype) for member in params if member.shape[0] > 1]
            + [pltpu.SemaphoreType.DMA((4,))],
        ),
        out_shape=[jax.ShapeDtypeStruct((count, columns), jnp.bfloat16) for columns in widths]
        + [jax.ShapeDtypeStruct(tokens.shape, jnp.bfloat16)],
        compiler_params=pltpu.CompilerParams(vmem_limit_bytes=VMEM_BYTES),
        cost_estimate=cost(2 * count * width * (4 * width + 2 * hidden), 2 * count * sum(widths)),
        name="forward",
    )(flag, tokens, message, first, *params)


def out_weight_kernel(me_ref, act_ref, grad_ref, bias_ref, *refs):
    outs, (stage, sems) = refs[:4], refs[4:]
    step = pl.program_id(0)
    rows = stage.shape[3]
    part = product_tn(act_ref[...], grad_ref[...]).astype(jnp.bfloat16)
    for index in range(part.shape[0] // rows):
        block = step * (part.shape[0] // rows) + index
        for side in range(2):
            values = part[index * rows : (index + 1) * rows, side * CHUNK : (side + 1) * CHUNK]
            store_block(stage, side, block, me_ref[0], 0, values)

    @pl.when(step == 0)
    def _():
        bias_ref[...] = column_sum(grad_ref[...].astype(jnp.float32))

    @pl.when(step == pl.num_programs(0) - 1)
    def _():
        copies = [
            pltpu.make_async_copy(stage.at[index // 2, index % 2], outs[index + 1 - 2 * (index % 2)], sems.at[0, index])
            for index in range(4)
        ]
        for copy in copies:
            copy.start()
        for copy in copies:
            copy.wait()


def out_weight_grad(me, size, act, grad, tile=768):
    count, hidden = act.shape
    width = grad.shape[1]
    rows = hidden // size
    return pl.pallas_call(
        out_weight_kernel,
        grid_spec=pltpu.PrefetchScalarGridSpec(
            num_scalar_prefetch=1,
            grid=(hidden // tile,),
            in_specs=[pl.BlockSpec((count, tile), lambda i, _: (0, i)), whole(grad.shape)],
            out_specs=[whole((1, width))] + in_hbm(4),
            scratch_shapes=stage_shapes(size, rows, 1),
        ),
        out_shape=[jax.ShapeDtypeStruct((1, width), jnp.float32)] + split_shapes(size, rows),
        compiler_params=pltpu.CompilerParams(vmem_limit_bytes=52 * 2**20),
        cost_estimate=cost(2 * count * hidden * width, 2 * count * hidden),
        name="out_weight_grad",
    )(me, act, grad)


def pre_grad_kernel(grad_ref, slope_ref, weight_ref, out_ref, bias_ref):
    hidden = weight_ref.shape[0]

    @pl.when(pl.program_id(0) == 0)
    def _():
        bias_ref[...] = jnp.zeros(bias_ref.shape, bias_ref.dtype)

    for start in range(0, hidden, 768):
        columns = slice(start, start + 768)
        part = product_nt(grad_ref[...], weight_ref[columns, :])
        part = (part * slope_ref[:, columns].astype(jnp.float32)).astype(jnp.bfloat16)
        out_ref[:, columns] = part
        bias_ref[:, columns] = bias_ref[:, columns] + column_sum(part.astype(jnp.float32))


def pre_grad(grad, slope, weight):
    count, width = grad.shape
    hidden = slope.shape[1]
    rows = 2 * FRAME
    return pl.pallas_call(
        pre_grad_kernel,
        grid=(count // rows,),
        in_specs=[
            pl.BlockSpec((rows, width), lambda i: (i, 0)),
            pl.BlockSpec((rows, hidden), lambda i: (i, 0)),
            whole(weight.shape),
        ],
        out_specs=[pl.BlockSpec((rows, hidden), lambda i: (i, 0)), whole((1, hidden))],
        out_shape=[
            jax.ShapeDtypeStruct((count, hidden), jnp.bfloat16),
            jax.ShapeDtypeStruct((1, hidden), jnp.float32),
        ],
        compiler_params=pltpu.CompilerParams(vmem_limit_bytes=52 * 2**20),
        cost_estimate=cost(2 * count * hidden * width, 4 * count * hidden),
        name="pre_grad",
    )(grad, slope, weight)


def middle_grad_kernel(grad_pre_ref, grad_ref, middle_ref, in_weight, proj_weight, gain_ref, out_ref, mixed_ref, vector_ref):
    back = product_nt(grad_pre_ref[...], in_weight[...])
    unit, spread = norm_parts(middle_ref[...].astype(jnp.float32))
    grad = norm_back(unit, spread, gain_ref[...], back) + grad_ref[...].astype(jnp.float32)
    grad = grad.astype(jnp.bfloat16)
    out_ref[...] = grad
    mixed_ref[...] = product_nt(grad, proj_weight[...]).astype(jnp.bfloat16)
    sums = [column_sum(part) for part in (back * unit, back, grad.astype(jnp.float32))]
    sums = jnp.concatenate(sums, axis=0)

    @pl.when(pl.program_id(0) == 0)
    def _():
        vector_ref[...] = sums

    @pl.when(pl.program_id(0) > 0)
    def _():
        vector_ref[...] = vector_ref[...] + sums


def middle_grad(grad_pre, grad, middle, in_weight, proj_weight, gain):
    count, width = grad.shape
    hidden = grad_pre.shape[1]
    rows = 2 * FRAME

    def by_rows(columns):
        return pl.BlockSpec((rows, columns), lambda i: (i, 0))

    return pl.pallas_call(
        middle_grad_kernel,
        grid=(count // rows,),
        in_specs=[by_rows(hidden), by_rows(width), by_rows(width)]
        + [whole(value.shape) for value in (in_weight, proj_weight, gain)],
        out_specs=[by_rows(width), by_rows(width), whole((3, width))],
        out_shape=[
            jax.ShapeDtypeStruct((count, width), jnp.bfloat16),
            jax.ShapeDtypeStruct((count, width), jnp.bfloat16),
            jax.ShapeDtypeStruct((3, width), jnp.float32),
        ],
        compiler_params=pltpu.CompilerParams(vmem_limit_bytes=52 * 2**20),
        cost_estimate=cost(2 * count * width * (hidden + width), 2 * count * hidden),
        name="middle_grad",
    )(grad_pre, grad, middle, in_weight, proj_weight, gain)


def in_weight_kernel(me_ref, normed_ref, grad_pre_ref, mixed_ref, grad_ref, *refs):
    outs, (stage, sems) = refs[:4], refs[4:]
    step = pl.program_id(0)
    steps = pl.num_programs(0)
    blocks = 2 * stage.shape[2]
    own = normed_ref.shape[1] // blocks
    spaced = padded_rows(own)
    chunks = grad_pre_ref.shape[1] // CHUNK
    per_half = (stage.shape[3] // spaced - 1) // chunks
    side = step // per_half
    first_row = (step - side * per_half) * chunks * spaced

    @pl.when(step < steps - 1)
    def _():
        part = product_tn(normed_ref[...], grad_pre_ref[...]).astype(jnp.bfloat16)
        for chunk in range(chunks):
            row = pl.multiple_of(first_row + chunk * spaced, 16)
            columns = slice(chunk * CHUNK, (chunk + 1) * CHUNK)
            for block in range(blocks):
                values = part[block * own : (block + 1) * own, columns]
                store_block(stage, side, block, me_ref[0], row, values)
        start_rows(stage, outs, sems, step, side, pl.multiple_of(first_row, 16), chunks * spaced)

    @pl.when(step == steps - 1)
    def _():
        part = product_tn(mixed_ref[...], grad_ref[...]).astype(jnp.bfloat16)
        row = stage.shape[3] - spaced
        for block in range(blocks):
            for half in range(2):
                values = part[block * own : (block + 1) * own, half * CHUNK : (half + 1) * CHUNK]
                store_block(stage, half, block, me_ref[0], row, values)
        last = []
        for half in range(2):
            last += rows_out(stage, outs, sems, 2 * per_half + half, half, row, spaced)
        for copy in last:
            copy.start()
        for done in range(2 * per_half):
            first = done % per_half * chunks * spaced
            wait_rows(stage, outs, sems, done, done // per_half, first, chunks * spaced)
        for copy in last:
            copy.wait()


def in_weight_grad(me, size, normed, grad_pre, mixed, grad_middle, tile=768):
    count, width = normed.shape
    hidden = grad_pre.shape[1]
    own = (hidden // (2 * CHUNK) + width // (2 * CHUNK)) * padded_rows(width // size)
    steps = hidden // tile
    return pl.pallas_call(
        in_weight_kernel,
        grid_spec=pltpu.PrefetchScalarGridSpec(
            num_scalar_prefetch=1,
            grid=(steps + 1,),
            in_specs=[
                whole(normed.shape),
                pl.BlockSpec((count, tile), lambda i, _: (0, jnp.minimum(i, steps - 1))),
                whole(mixed.shape),
                whole(grad_middle.shape),
            ],
            out_specs=in_hbm(4),
            scratch_shapes=stage_shapes(size, own, steps + 2),
        ),
        out_shape=split_shapes(size, own),
        compiler_params=pltpu.CompilerParams(vmem_limit_bytes=52 * 2**20),
        cost_estimate=cost(2 * count * width * (hidden + width), 2 * count * hidden),
        name="in_weight_grad",
    )(me, normed, grad_pre, mixed, grad_middle)


def attend_back_kernel(flag_ref, projected_ref, grad_ref, first_ref, out_ref, held, pending, carry):
    step = pl.program_id(0)
    blocks = pl.num_programs(0) - 1
    is_video = flag_ref[0] == 0
    width = grad_ref.shape[1]

    @pl.when(step == 0)
    def _():
        held[...] = jnp.zeros(held.shape, held.dtype)
        carry[...] = jnp.zeros(carry.shape, carry.dtype)

    @pl.when(step > 0)
    def _():
        out_ref[...] = pending[...]

    def add_prior(columns, values):
        rows = slice(FRAME - PRIOR, FRAME)
        out_ref[rows, columns] = (carry[:, columns] + values).astype(jnp.bfloat16)

    @pl.when((step < blocks) & is_video)
    def _():
        place = lax.broadcasted_iota(jnp.int32, (FRAME, 2 * FRAME), 0)
        bias = jnp.where(place <= TPF, 0.0, -1e30)
        for first_pair in range(0, width, 128 * 3):
            pairs = range(first_pair, first_pair + 128 * 3, 128)
            places = [
                [slice(start + pair, start + pair + 128) for start in (0, width, 2 * width)] for pair in pairs
            ]
            parts = [
                tuple((projected_ref[:, columns] for columns in place)) + (grad_ref[:, place[0]], bias)
                for place in places
            ]
            for place, grads in zip(places, attend_back_group(parts)):
                for columns, values in zip(place, grads):
                    pending[:, columns] = values.astype(jnp.bfloat16)

    @pl.when((step < blocks) & jnp.logical_not(is_video))
    def _():
        held[PRIOR:, :] = projected_ref[...]
        biases = []
        for query_start, query_count, key_start, key_count in SUB_BLOCKS:
            base = step * FRAME
            shape = (key_count, query_count)
            key_place = base + key_start + lax.broadcasted_iota(jnp.int32, shape, 0)
            query_place = base + query_start + lax.broadcasted_iota(jnp.int32, shape, 1)
            first = first_ref[0, :, query_start : query_start + query_count]
            allowed = (key_place >= first) & (key_place <= query_place)
            bias = jnp.where(allowed, 0.0, -1e30)
            biases.append(jnp.concatenate([bias, bias], axis=1))
        for first_pair in range(0, width, 128 * 3):
            pairs = range(first_pair, first_pair + 128 * 3, 128)
            places, parts = [], []
            for pair in pairs:
                place = [slice(start + pair, start + pair + 128) for start in (0, width, 2 * width)]
                places.append(place)
                for bias, block in zip(biases, SUB_BLOCKS):
                    query_start, query_count, key_start, key_count = block
                    key_rows = slice(PRIOR + key_start, PRIOR + key_start + key_count)
                    query_rows = slice(query_start, query_start + query_count)
                    parts.append(
                        (
                            projected_ref[query_rows, place[0]],
                            held[key_rows, place[1]],
                            held[key_rows, place[2]],
                            grad_ref[query_rows, place[0]],
                            bias,
                        )
                    )
            results = attend_back_group(parts)
            for index, place in enumerate(places):
                pair_results = results[2 * index : 2 * index + 2]
                for grads, block in zip(pair_results, SUB_BLOCKS):
                    pending[block[0] : block[0] + block[1], place[0]] = grads[0].astype(jnp.bfloat16)
                for kind in (1, 2):
                    early, late = pair_results[0][kind], pair_results[1][kind]
                    overlap = SUB_BLOCKS[1][2]
                    reach = SUB_BLOCKS[0][1]
                    own = jnp.concatenate(
                        [
                            early[PRIOR : PRIOR + overlap],
                            early[PRIOR + overlap :] + late[: reach - overlap],
                            late[reach - overlap :],
                        ],
                        axis=0,
                    )
                    add_prior(place[kind], early[:PRIOR])
                    pending[:, place[kind]] = own.astype(jnp.bfloat16)
                    carry[:, place[kind]] = own[FRAME - PRIOR :]
        held[0:PRIOR, :] = projected_ref[FRAME - PRIOR :, :]


def attend_back(flag, projected, grad_mixed, first):
    count, wide = projected.shape
    width = grad_mixed.shape[1]
    blocks = count // FRAME

    def ahead(i, _):
        return (jnp.minimum(i, blocks - 1), 0)

    return pl.pallas_call(
        attend_back_kernel,
        grid_spec=pltpu.PrefetchScalarGridSpec(
            num_scalar_prefetch=1,
            grid=(blocks + 1,),
            in_specs=[
                pl.BlockSpec((FRAME, wide), ahead),
                pl.BlockSpec((FRAME, width), ahead),
                pl.BlockSpec((1, 1, FRAME), lambda i, _: (jnp.minimum(i, blocks - 1), 0, 0)),
            ],
            out_specs=pl.BlockSpec((FRAME, wide), lambda i, _: (jnp.maximum(i - 1, 0), 0)),
            scratch_shapes=[
                pltpu.VMEM((FRAME + PRIOR, wide), jnp.bfloat16),
                pltpu.VMEM((FRAME, wide), jnp.bfloat16),
                pltpu.VMEM((PRIOR, wide), jnp.float32),
            ],
        ),
        out_shape=jax.ShapeDtypeStruct((count, wide), jnp.bfloat16),
        compiler_params=pltpu.CompilerParams(vmem_limit_bytes=52 * 2**20),
        cost_estimate=cost(2 * count * width * 5 * FRAME * 4, 4 * count * wide),
        name="attend_back",
    )(flag, projected, grad_mixed, first)


def two_terms(values):
    high = values.astype(jnp.bfloat16)
    return (high, (values - high.astype(jnp.float32)).astype(jnp.bfloat16))


def row_product(values, weight):
    spread = [jnp.broadcast_to(one, (8, one.shape[1])) for one in two_terms(values)]
    return (product_nt(spread[0], weight) + product_nt(spread[1], weight))[0:1]


def qkv_weight_kernel(me_ref, normed_ref, grad_ref, weight_ref, gain_ref, shift_ref, bias_ref, vector_ref, *refs):
    outs, (sums, stage, sems) = refs[:4], refs[4:]
    step = pl.program_id(0)
    last = pl.num_programs(0) - 1
    part = product_tn(normed_ref[...], grad_ref[...])
    bias = column_sum(grad_ref[...].astype(jnp.float32))
    bias_ref[...] = bias
    weight = weight_ref[...]
    shift = row_product(bias, weight)
    ones = jnp.ones((8, part.shape[1]), jnp.bfloat16)
    high, lower = two_terms(part * weight.astype(jnp.float32))
    scaled = (product_nt(ones, high) + product_nt(ones, lower))[0:1]
    both = jnp.concatenate([scaled, shift], axis=0)

    @pl.when(step == 0)
    def _():
        sums[...] = both

    @pl.when(step > 0)
    def _():
        sums[...] = sums[...] + both

    part = part.astype(jnp.bfloat16)
    blocks = 2 * stage.shape[2]
    rows = part.shape[0] // blocks
    spaced = padded_rows(rows)
    half = stage.shape[3] // spaced
    chunks = part.shape[1] // CHUNK
    for chunk in range(chunks):
        index = step * chunks + chunk
        side = index // half
        row = pl.multiple_of((index - side * half) * spaced, 16)
        columns = slice(chunk * CHUNK, (chunk + 1) * CHUNK)
        for block in range(blocks):
            store_block(stage, side, block, me_ref[0], row, part[block * rows : (block + 1) * rows, columns])
        start_rows(stage, outs, sems, index, side, row, spaced)

    @pl.when(step == last)
    def _():
        shift_total = sums[1:2, :]
        gain_total = (sums[0:1, :] - shift_ref[...] * shift_total) / gain_ref[...]
        vector_ref[...] = jnp.concatenate([gain_total, shift_total], axis=0)
        for done in range(2 * half):
            wait_rows(stage, outs, sems, done, done // half, done % half * spaced, spaced)


def qkv_weight_grad(me, size, normed, grad, weight, gain, shift, tile=768):
    count, width = normed.shape
    wide = grad.shape[1]
    own = wide // (2 * CHUNK) * padded_rows(width // size)
    return pl.pallas_call(
        qkv_weight_kernel,
        grid_spec=pltpu.PrefetchScalarGridSpec(
            num_scalar_prefetch=1,
            grid=(wide // tile,),
            in_specs=[
                whole(normed.shape),
                pl.BlockSpec((count, tile), lambda i, _: (0, i)),
                pl.BlockSpec((width, tile), lambda i, _: (0, i)),
                whole(gain.shape),
                whole(shift.shape),
            ],
            out_specs=[pl.BlockSpec((1, tile), lambda i, _: (0, i)), whole((2, width))] + in_hbm(4),
            scratch_shapes=[pltpu.VMEM((2, width), jnp.float32)]
            + stage_shapes(size, own, wide // CHUNK),
        ),
        out_shape=[
            jax.ShapeDtypeStruct((1, wide), jnp.float32),
            jax.ShapeDtypeStruct((2, width), jnp.float32),
        ]
        + split_shapes(size, own),
        compiler_params=pltpu.CompilerParams(vmem_limit_bytes=52 * 2**20),
        cost_estimate=cost(2 * count * width * wide, 2 * count * wide),
        name="qkv_weight_grad",
    )(me, normed, grad, weight, gain, shift)


def token_grad_kernel(
    part, split, flag_ref, grad_ref, hidden_ref, middle_ref, source_ref, weight_ref, gain_ref, *refs
):
    if part == 0:
        out_ref, shared_ref, target, sem = refs
    else:
        before_ref, other_ref, out_ref, target, sem = refs
    frames = source_ref.shape[0] // 2
    is_video = flag_ref[0] == 0
    origin = part * split
    step = pl.program_id(0)
    if part == 1:

        @pl.when(step == 0)
        def _():
            target[0 : before_ref.shape[0], :] = before_ref[...]

    back = product_nt(grad_ref[...], weight_ref[...])
    unit, spread = norm_parts(hidden_ref[...].astype(jnp.float32))
    grads = norm_back(unit, spread, gain_ref[...], back) + middle_ref[...].astype(jnp.float32)
    per_step = grads.shape[0] // FRAME
    for frame in range(per_step):
        rows = grads[frame * FRAME : (frame + 1) * FRAME]
        index = part * frames + step * per_step + frame
        place = lax.broadcasted_iota(jnp.int32, (8, rows.shape[1]), 0)
        extra = jnp.where(is_video & (place == 0), source_ref[pl.ds(index, 1), :], 0.0)
        rows = jnp.concatenate([rows[:8] + extra, rows[8:]], axis=0)
        store_rows(target, frame_start(is_video, index) - origin, rows)

    @pl.when(step == pl.num_programs(0) - 1)
    def _():
        count = split if part == 0 else out_ref.shape[0] - split
        copy = pltpu.make_async_copy(
            target.at[pl.ds(0, count)], out_ref.at[pl.ds(origin, count)], sem
        )
        copy.start()
        if part == 0:
            shared_ref[...] = target[split : split + shared_ref.shape[0], :]
        copy.wait()


def token_grad(part, flag, grad, hidden, grad_middle, grad_source, weight, gain, before=None, frames=2):
    count, width = hidden.shape
    rows = frames * FRAME
    tokens = (count // FRAME * TPF, width)
    steps = count // rows // 2
    split = grad_source.shape[0] // 2 * TPF // 16 * 16
    shared = (-(-(grad_source.shape[0] // 2 * FRAME - split) // 16) * 16, width)
    more = () if part == 0 else before

    def by_rows(columns):
        return pl.BlockSpec((rows, columns), lambda i, _: (i + part * steps, 0))

    out_shape = [jax.ShapeDtypeStruct(tokens, jnp.float32)]
    out_specs = in_hbm(1)
    if part == 0:
        out_shape.append(jax.ShapeDtypeStruct(shared, jnp.float32))
        out_specs = out_specs + [whole(shared)]
    results = pl.pallas_call(
        functools.partial(token_grad_kernel, part, split),
        grid_spec=pltpu.PrefetchScalarGridSpec(
            num_scalar_prefetch=1,
            grid=(steps,),
            in_specs=[
                by_rows(grad.shape[1]),
                by_rows(width),
                by_rows(width),
                whole(grad_source.shape),
                whole(weight.shape),
                whole(gain.shape),
            ]
            + ([whole(shared)] + in_hbm(1) if part == 1 else []),
            out_specs=out_specs,
            scratch_shapes=[
                pltpu.VMEM((count // 2 + FRAME, width), jnp.float32),
                pltpu.SemaphoreType.DMA(()),
            ],
        ),
        out_shape=out_shape,
        input_output_aliases={8: 0} if part == 1 else {},
        compiler_params=pltpu.CompilerParams(vmem_limit_bytes=52 * 2**20),
        cost_estimate=cost(count * width * 3 * width, 2 * count * width),
        name="token_grad",
    )(flag, grad, hidden, grad_middle, grad_source, weight, gain, *more)
    return (results[1], results[0]) if part == 0 else results[0]


def message_kernel(flag_ref, token_ref, ids_row, ids_column, in_source, in_bias, gain, shift, qkv_source, out_source, message_ref, packed_ref, start_ref, projected_ref, tokens, in_weight, qkv_weight, out_weight, sems):
    frames, width = message_ref.shape

    @pl.when(flag_ref[0] == 0)
    def _():
        rows = [frame * TPF // 16 * 16 for frame in range(frames)]
        loads = [
            pltpu.make_async_copy(token_ref.at[pl.ds(row, 16)], tokens.at[frame], sems.at[3])
            for frame, row in enumerate(rows)
        ]
        weights = ((in_source, in_weight), (qkv_source, qkv_weight), (out_source, out_weight))
        copies = [
            pltpu.make_async_copy(origin, place, sems.at[index])
            for index, (origin, place) in enumerate(weights)
        ]
        for copy in loads + copies:
            copy.start()
        for copy in loads:
            copy.wait()
        copies[0].wait()
        parts = []
        for frame in range(frames):
            row = frame * TPF
            base = row // 16 * 16
            tile = tokens[frame].astype(jnp.float32)
            parts.append(tile[row - base : row - base + 1])
        source = jnp.concatenate(parts, axis=0).astype(jnp.bfloat16)
        start = product(source, in_weight[...]) + in_bias[...]
        unit, _ = norm_parts(start)
        normed = (unit * gain[...] + shift[...]).astype(jnp.bfloat16)
        copies[1].wait()
        projected = product(normed, qkv_weight[...]).astype(jnp.bfloat16)
        mixed = side_attend(
            projected[:, :width],
            projected[:, width : 2 * width],
            projected[:, 2 * width :],
            ids_column[...] == ids_row[...],
        )
        copies[2].wait()
        message = start + product(mixed, out_weight[...])
        message_ref[...] = message
        start_ref[...] = start
        projected_ref[...] = projected
        packed_ref[...] = jnp.concatenate([message.astype(jnp.bfloat16), source, normed, mixed], axis=1)

    @pl.when(flag_ref[0] != 0)
    def _():
        message_ref[...] = jnp.zeros(message_ref.shape, message_ref.dtype)
        packed_ref[...] = jnp.zeros(packed_ref.shape, packed_ref.dtype)
        start_ref[...] = jnp.zeros(start_ref.shape, start_ref.dtype)
        projected_ref[...] = jnp.zeros(projected_ref.shape, projected_ref.dtype)


def call_once(kernel, name, flops, scalars, operands, shapes):
    return pl.pallas_call(
        kernel,
        in_specs=[pl.BlockSpec(memory_space=pltpu.SMEM) for _ in scalars] + in_vmem(len(operands)),
        out_specs=in_vmem(len(shapes)),
        out_shape=[jax.ShapeDtypeStruct(shape, dtype) for shape, dtype in shapes],
        compiler_params=pltpu.CompilerParams(vmem_limit_bytes=VMEM_BYTES),
        cost_estimate=cost(flops, sum(value.size * 2 for value in operands)),
        name=name,
    )(*scalars, *operands)


def make_message(flag, tokens, frame_ids, side_params):
    frames = frame_ids.shape[0]
    width = tokens.shape[1]
    shapes = [
        ((frames, width), jnp.float32),
        ((frames, 4 * width), jnp.bfloat16),
        ((frames, width), jnp.float32),
        ((frames, 3 * width), jnp.bfloat16),
    ]
    operands = (tokens, frame_ids[None, :], frame_ids[:, None]) + side_params
    held = (side_params[0], side_params[4], side_params[5])
    return pl.pallas_call(
        message_kernel,
        in_specs=[pl.BlockSpec(memory_space=pltpu.SMEM)]
        + [in_hbm(1)[0] if max(value.shape) > 700 and value.shape[0] > 1 else in_vmem(1)[0] for value in operands],
        out_specs=in_vmem(len(shapes)),
        out_shape=[jax.ShapeDtypeStruct(shape, dtype) for shape, dtype in shapes],
        scratch_shapes=[pltpu.VMEM((frames, 16, width), jnp.bfloat16)]
        + [pltpu.VMEM(value.shape, value.dtype) for value in held]
        + [pltpu.SemaphoreType.DMA((4,))],
        compiler_params=pltpu.CompilerParams(vmem_limit_bytes=VMEM_BYTES),
        cost_estimate=cost(1e10, 10**7),
        name="message",
    )(flag, *operands)


def prompt_kernel(
    flag_ref,
    me_ref,
    block_ref,
    cotangent_ref,
    context_ref,
    ends_column,
    caption_ids,
    frame_ids,
    in_weight,
    in_bias,
    gain,
    shift,
    qkv_weight,
    out_weight,
    out_ref,
    grad_out_ref,
    vector_ref,
    send_ref,
    keep_ref,
    padded,
):
    count, width = block_ref.shape
    frames = count // TPF
    is_video = flag_ref[0] == 0

    @pl.when(is_video)
    def _():
        out_ref[...] = block_ref[...]
        padded[0:count, :] = cotangent_ref[...]
        padded[count:, :] = jnp.zeros((padded.shape[0] - count, width), padded.dtype)
        for frame in range(frames):
            rows = load_rows(padded, frame * TPF)
            rows = frame_tail(rows, True, 0.0)
            grad_out_ref[frame * FRAME : (frame + 1) * FRAME, :] = rows.astype(jnp.bfloat16)
        vector_ref[...] = jnp.zeros(vector_ref.shape, vector_ref.dtype)

    @pl.when(jnp.logical_not(is_video))
    def _():
        captions = ends_column.shape[0]
        place = lax.broadcasted_iota(jnp.int32, (captions, count), 1)
        chosen = (place == ends_column[...]).astype(jnp.bfloat16)
        source = product(chosen, block_ref[...]).astype(jnp.bfloat16)
        grad_ends = product(chosen, cotangent_ref[...])
        start = product(source, in_weight[...]) + in_bias[...]
        unit, spread = norm_parts(start)
        normed = (unit * gain[...] + shift[...]).astype(jnp.bfloat16)
        query = product(normed, qkv_weight[:, :width]).astype(jnp.bfloat16)
        context = context_ref[:, :width]
        pair = product(context, qkv_weight[:, width:]).astype(jnp.bfloat16)
        key, value = pair[:, :width], pair[:, width:]
        allowed = caption_ids[...] == frame_ids[...]
        mixed = side_attend(query, key, value, allowed)
        prompt = start + product(mixed, out_weight[...])
        high = prompt.astype(jnp.bfloat16)
        lower = (prompt - high.astype(jnp.float32)).astype(jnp.bfloat16)
        added = product_tn(chosen, jnp.concatenate([high, lower], axis=1))
        added = added[:, :width] + added[:, width:]
        out_ref[...] = (block_ref[...].astype(jnp.float32) + added).astype(jnp.bfloat16)
        grad_round = grad_ends.astype(jnp.bfloat16)
        grad_mixed = product_nt(grad_round, out_weight[...]).astype(jnp.bfloat16)
        grad_query, grad_key, grad_value = side_attend_back(query, key, value, allowed, grad_mixed)
        grad_query = grad_query.astype(jnp.bfloat16)
        mine = (me_ref[0] >> 1) & 1

        def put(block, row, values):
            place = ((block >> 2) << 1) | (block & 1)
            values = values.astype(jnp.bfloat16)

            @pl.when(((block >> 1) & 1) != mine)
            def _():
                send_ref[place, row : row + values.shape[0], :] = values

            @pl.when(((block >> 1) & 1) == mine)
            def _():
                keep_ref[place, row : row + values.shape[0], :] = values

        blocks = 2 * send_ref.shape[0]
        own = context_ref.shape[0] // blocks
        chunks = width // CHUNK
        grad_pair = jnp.concatenate([grad_key, grad_value], axis=1)
        devices = gathered_offsets(blocks)
        for block in range(blocks):
            part = grad_pair[block * own : (block + 1) * own]
            parts = [part[:, chunk * CHUNK : (chunk + 1) * CHUNK] for chunk in range(2 * chunks)]
            put(devices[block] ^ me_ref[0], send_ref.shape[1] - 2 * chunks * own, jnp.concatenate(parts, axis=0))
        grad_normed = product_nt(grad_query, qkv_weight[:, :width])
        grad_start = norm_back(unit, spread, gain[...], grad_normed) + grad_round.astype(jnp.float32)
        grad_start = grad_start.astype(jnp.bfloat16)
        vector_ref[...] = jnp.concatenate(
            [
                column_sum(grad_start.astype(jnp.float32)),
                column_sum(grad_normed * unit),
                column_sum(grad_normed),
            ],
            axis=0,
        )
        grad_source = product_nt(grad_start, in_weight[...])
        added = product_tn(chosen, grad_source.astype(jnp.bfloat16))
        grad_out_ref[0:count, :] = (cotangent_ref[...].astype(jnp.float32) + added).astype(jnp.bfloat16)
        grad_out_ref[count:, :] = jnp.zeros((frames * FRAME - count, width), jnp.bfloat16)
        rows = width // blocks
        for third, (left, right) in enumerate(
            ((source, grad_start), (normed, grad_query), (mixed, grad_round))
        ):
            part = product_tn(left, right).astype(jnp.bfloat16)
            for chunk in range(chunks):
                row = (third * chunks + chunk) * padded_rows(rows)
                columns = slice(chunk * CHUNK, (chunk + 1) * CHUNK)
                for block in range(blocks):
                    put(block, row, part[block * rows : (block + 1) * rows, columns])


def make_prompt(flag, me, size, block, cotangent, context, ends, caption_ids, frame_ids, side_params):
    count, width = block.shape
    padded = count // TPF * FRAME
    chunks = width // CHUNK
    rows = 3 * chunks * padded_rows(width // size) + 2 * chunks * (context.shape[0] // size)
    split = (size // 2, rows, CHUNK)
    shapes = [
        ((count, width), jnp.bfloat16),
        ((padded, width), jnp.bfloat16),
        ((3, width), jnp.float32),
        (split, jnp.bfloat16),
        (split, jnp.bfloat16),
    ]
    spare = -ends.shape[0] % 16
    ends = jnp.pad(ends, (0, spare), constant_values=-1)[:, None]
    caption_ids = jnp.pad(caption_ids, (0, spare), constant_values=-1)[:, None]
    operands = (block, cotangent, context, ends, caption_ids, frame_ids[None, :]) + side_params
    return pl.pallas_call(
        prompt_kernel,
        in_specs=[pl.BlockSpec(memory_space=pltpu.SMEM)] * 2 + in_vmem(len(operands)),
        out_specs=in_vmem(len(shapes)),
        out_shape=[jax.ShapeDtypeStruct(shape, dtype) for shape, dtype in shapes],
        scratch_shapes=[pltpu.VMEM((padded + 32, width), jnp.bfloat16)],
        compiler_params=pltpu.CompilerParams(vmem_limit_bytes=VMEM_BYTES),
        cost_estimate=cost(1e10, 2 * count * width * 8),
        name="prompt",
    )(flag, me, *operands)


def message_back_kernel(frames, flag_ref, *refs):
    grads, middles, rest = refs[:frames], refs[frames : 2 * frames], refs[2 * frames :]
    (
        message_ref,
        received_ref,
        start_ref,
        projected_ref,
        ids_row,
        ids_column,
        main_weight,
        main_gain,
        in_weight,
        gain,
        qkv_weight,
        out_weight,
        pair_ref,
        source_ref,
        line_ref,
    ) = rest
    width = message_ref.shape[1]

    @pl.when(flag_ref[0] == 0)
    def _():
        row = TPF % 16
        grad = jnp.concatenate(
            [one[...].astype(jnp.float32)[row : row + 1] for one in grads], axis=0
        ).astype(jnp.bfloat16)
        middle = jnp.concatenate(
            [one[...].astype(jnp.float32)[row : row + 1] for one in middles], axis=0
        )
        unit, spread = norm_parts(message_ref[...])
        back = norm_back(unit, spread, main_gain[...], product_nt(grad, main_weight[...]))
        grad_round = (back + middle + received_ref[...]).astype(jnp.bfloat16)
        grad_mixed = product_nt(grad_round, out_weight[...]).astype(jnp.bfloat16)
        projected = projected_ref[...]
        grad_parts = side_attend_back(
            projected[:, :width],
            projected[:, width : 2 * width],
            projected[:, 2 * width :],
            ids_column[...] == ids_row[...],
            grad_mixed,
        )
        grad_projected = jnp.concatenate(grad_parts, axis=1).astype(jnp.bfloat16)
        unit, spread = norm_parts(start_ref[...])
        grad_normed = product_nt(grad_projected, qkv_weight[...])
        grad_start = norm_back(unit, spread, gain[...], grad_normed) + grad_round.astype(jnp.float32)
        grad_start = grad_start.astype(jnp.bfloat16)
        source_ref[...] = product_nt(grad_start, in_weight[...])
        line_ref[...] = jnp.concatenate([grad_start, grad_projected, grad_round], axis=1)

    @pl.when(flag_ref[0] != 0)
    def _():
        source_ref[...] = jnp.zeros(source_ref.shape, source_ref.dtype)
        line_ref[:, : 2 * width] = pair_ref[...]
        line_ref[:, 2 * width :] = jnp.zeros((line_ref.shape[0], 3 * width), line_ref.dtype)


def message_back(flag, grad_projected, grad_middle, operands):
    width = grad_middle.shape[1]
    frames = grad_middle.shape[0] // FRAME
    shapes = [
        jax.ShapeDtypeStruct((frames, width), jnp.float32),
        jax.ShapeDtypeStruct((frames, 5 * width), jnp.bfloat16),
    ]

    def last_rows(columns):
        return [
            pl.BlockSpec(
                (16, columns),
                functools.partial(lambda place, *_: (place, 0), (frame * FRAME + TPF) // 16),
                pipeline_mode=pl.Buffered(buffer_count=1),
            )
            for frame in range(frames)
        ]

    return pl.pallas_call(
        functools.partial(message_back_kernel, frames),
        grid_spec=pltpu.PrefetchScalarGridSpec(
            num_scalar_prefetch=1,
            grid=(1,),
            in_specs=last_rows(3 * width)
            + last_rows(width)
            + [whole(value.shape) for value in operands],
            out_specs=[whole(shape.shape) for shape in shapes],
        ),
        out_shape=shapes,
        compiler_params=pltpu.CompilerParams(vmem_limit_bytes=52 * 2**20),
        cost_estimate=cost(1e10, 10**7),
        name="message_back",
    )(flag, *([grad_projected] * frames), *([grad_middle] * frames), *operands)


def pair_kernel(flag_ref, side_ref, weight_ref, pair_ref, context_ref):
    rows, width = context_ref.shape
    chunks = pair_ref.shape[1] // CHUNK
    first = side_ref.shape[0] - chunks * rows

    @pl.when(flag_ref[0] != 0)
    def _():
        parts = [side_ref[first + rows * chunk : first + rows * (chunk + 1), :] for chunk in range(chunks)]
        pair = jnp.concatenate(parts, axis=1).astype(jnp.bfloat16)
        pair_ref[...] = pair
        context_ref[...] = product_nt(pair, weight_ref[:, width:])

    @pl.when(flag_ref[0] == 0)
    def _():
        pair_ref[...] = jnp.zeros(pair_ref.shape, pair_ref.dtype)
        context_ref[...] = jnp.zeros(context_ref.shape, context_ref.dtype)


def pair_grad(flag, side, weight, frames):
    width = weight.shape[0]
    shapes = [((frames, 2 * width), jnp.bfloat16), ((frames, width), jnp.float32)]
    return call_once(pair_kernel, "pair_grad", 1e9, (flag,), (side, weight), shapes)


def pack_kernel(*refs):
    start = 0
    for one in refs[:-1]:
        for row in range(one.shape[0]):
            refs[-1][:, start : start + one.shape[1]] = one[row : row + 1, :]
            start += one.shape[1]


def pack_vectors(vectors):
    shapes = [((1, sum(one.size for one in vectors)), jnp.float32)]
    return call_once(pack_kernel, "pack_vectors", 1e6, (), vectors, shapes)[0]


def side_weight_kernel(
    flag_ref,
    me_ref,
    packed_ref,
    line_ref,
    side_ref,
    weight_ref,
    gain_ref,
    shift_ref,
    in_ref,
    qkv_ref,
    out_ref,
    vector_ref,
):
    own, width = in_ref.shape

    def own_columns(place):
        part = packed_ref[:, place * width : (place + 1) * width].astype(jnp.float32)
        return pltpu.roll(part, (width - me_ref[0] * own) % width, axis=1)[:, :own].astype(jnp.bfloat16)

    @pl.when(flag_ref[0] == 0)
    def _():
        in_ref[...] = product_tn(own_columns(1), line_ref[:, :width])
        qkv_ref[...] = product_tn(own_columns(2), line_ref[:, width : 4 * width])
        out_ref[...] = product_tn(own_columns(3), line_ref[:, 4 * width :])
        lines = line_ref[...].astype(jnp.float32)
        vector_ref[0:1, :] = column_sum(lines[:, :width])
        unit = packed_ref[:, 2 * width : 3 * width].astype(jnp.float32) - shift_ref[...]
        grad_normed = product_nt(line_ref[:, width : 4 * width], weight_ref[...])
        vector_ref[1:2, :] = column_sum(grad_normed * unit) / gain_ref[...]
        vector_ref[2:3, :] = column_sum(grad_normed)

    @pl.when(flag_ref[0] != 0)
    def _():
        chunks = width // CHUNK
        spaced = padded_rows(own)

        def matrix(third):
            rows = [(third * chunks + chunk) * spaced for chunk in range(chunks)]
            return jnp.concatenate([side_ref[row : row + own, :] for row in rows], axis=1)

        in_ref[...] = matrix(0)
        qkv_ref[:, :width] = matrix(1)
        qkv_ref[:, width:] = product_tn(own_columns(0), line_ref[:, : 2 * width])
        out_ref[...] = matrix(2)
        vector_ref[...] = jnp.zeros(vector_ref.shape, vector_ref.dtype)


def side_weight_grads(flag, me, size, packed, lines, side, weight, gain, shift):
    width = packed.shape[1] // 4
    own = width // size
    shapes = [
        ((own, width), jnp.float32),
        ((own, 3 * width), jnp.float32),
        ((own, width), jnp.float32),
        ((3, width), jnp.float32),
    ]
    operands = (packed, lines, side, weight, gain, shift)
    return call_once(side_weight_kernel, "side_weight_grads", 1e9, (flag, me), operands, shapes)


def vector_kernel(size, widths, flag_ref, me_ref, line_ref, side_ref, *out_refs):
    start = 0
    third = out_refs[0].shape[1] * size
    for place, (width, out_ref) in enumerate(zip(widths, out_refs)):
        total = line_ref[:, start : start + width]
        start += width
        if place == 2:
            total = jnp.concatenate([total[:, :third], total[:, 2 * third :]], axis=1)
            width = 2 * third
        own = width // size
        side = place - (len(widths) - 3)
        if side >= 0:
            total = jnp.where(flag_ref[0] == 0, side_ref[side : side + 1, :], total)
        total = jnp.broadcast_to(total, (8, width))
        out_ref[...] = pltpu.roll(total, (width - me_ref[0] * own) % width, axis=1)[0:1, :own]


def own_vectors(flag, me, size, line, side, widths):
    shapes = [((1, width // size), jnp.float32) for width in widths]
    shapes[2] = ((1, 2 * widths[0] // size), jnp.float32)
    kernel = functools.partial(vector_kernel, size, tuple(widths))
    return call_once(kernel, "own_vectors", 1e6, (flag, me), (line, side), shapes)


def pair_list(size, distance):
    return [(place, place ^ distance) for place in range(size)]


def group_pairs(size, distance, group):
    return [(group * size + place, group * size + (place ^ distance)) for place in range(size)]


def bit_count(size):
    return size.bit_length() - 1


def gather_order(size):
    return list(range(bit_count(size)))[::-1]


def gathered_offsets(size):
    return [
        sum((((place >> step) & 1) << bit for step, bit in enumerate(gather_order(size))))
        for place in range(size)
    ]


def gathered_devices(me, size):
    return me ^ jnp.array(gathered_offsets(size), jnp.int32)


def double_gather(values, size, send):
    for bit in gather_order(size):
        values = jnp.concatenate([values, send(values, 1 << bit)], axis=0)
    return values


class Sum:
    def __init__(self, size, send, parts, layout, fan=False):
        self.send, self.layout, self.fan = send, layout, fan
        self.bits = list(range(2, bit_count(size)))
        self.orders = [[0, 1], [1, 0]]
        self.keeps, self.arrived = [], []
        for side in range(2):
            self.launch(parts[2 * side], parts[2 * side + 1], self.orders[side].pop(0))

    def launch(self, sent, kept, bit):
        self.keeps.append(kept)
        self.arrived.append(self.send(sent, 1 << bit))

    def values(self):
        return [value for pair in zip(self.keeps, self.arrived) for value in pair]

    def items(self):
        if self.orders[0]:
            values = self.values()
            return [("split", values[2 * side : 2 * side + 2], self.orders[side][0]) for side in range(2)]
        if self.bits:
            kind = "fan" if self.fan and len(self.bits) == 2 else "split"
            return [(kind, self.values(), self.bits[0])]
        return [("end", self.keeps + self.arrived, self.layout)]

    def take(self, results):
        fan = self.fan and len(self.bits) == 2 and not self.orders[0]
        self.keeps, self.arrived = [], []
        if self.orders[0]:
            for side in range(2):
                self.launch(results.pop(0), results.pop(0), self.orders[side].pop(0))
        elif fan:
            self.keeps = [results.pop(0)]
            first = self.bits[0]
            self.arrived = [self.send(results.pop(0), offset << first) for offset in (1, 2, 3)]
            self.bits = []
        elif self.bits:
            self.launch(results.pop(0), results.pop(0), self.bits.pop(0))
        else:
            self.result = [results.pop(0) for _ in self.layout]


class PlainSum:
    def __init__(self, size, send, send_small, sent, kept):
        self.send, self.send_small, self.kept = send, send_small, kept
        self.bits = [bit for bit in range(bit_count(size)) if bit != 1]
        self.arrived = send(sent, 2)
        self.steps = 1

    def items(self):
        if self.bits:
            return [("split", [self.kept, self.arrived], self.bits[0])]
        return [("raw", [self.kept, self.arrived], None)]

    def take(self, results):
        if self.bits:
            sent, self.kept = results.pop(0), results.pop(0)
            send = self.send if self.steps < 2 else self.send_small
            self.arrived = send(sent, 1 << self.bits.pop(0))
            self.steps += 1
        else:
            self.result = results.pop(0)


class Spread:
    def __init__(self, size, send, values, kind, plane=False):
        self.kind, self.send, self.held = kind, send, values
        self.steps = [[1 << bit] for bit in gather_order(size)]
        if plane:
            self.steps = self.steps[:-2] + [[2, 1, 3]]
        self.launch()

    def launch(self):
        self.arrived = [self.send(self.held, distance) for distance in self.steps.pop(0)]

    def items(self):
        return [(self.kind, [self.held] + self.arrived, None)]

    def take(self, results):
        self.held = results.pop(0)
        if self.steps:
            self.launch()
        else:
            self.result = self.held


def tie(first, second):
    return lax.optimization_barrier((first, second))


def advance(me, streams, after, before=None):
    streams = [one for one in streams if not hasattr(one, "result")]
    if not streams:
        return (after, before)
    items = [one.items() for one in streams]
    flat = [item for one in items for item in one]
    operands, after = tie([item[1] for item in flat], after)
    results = combine(me, [(item[0], values, item[2]) for item, values in zip(flat, operands)])
    results, before = tie(list(results), before)
    for one in streams:
        one.take(results)
    return (after, before)


def on_device(
    size,
    tokens,
    frame_video,
    caption_video,
    caption_len,
    attn_norm_gain,
    attn_norm_shift,
    qkv_weight,
    query_value_bias,
    proj_weight,
    proj_bias,
    mlp_norm_gain,
    mlp_norm_shift,
    fc_in_weight,
    fc_in_bias,
    fc_out_weight,
    fc_out_bias,
    side_in_weight,
    side_in_bias,
    side_norm_gain,
    side_norm_shift,
    side_qkv_weight,
    side_out_weight,
    cotangent,
):
    main_params = tuple(
        (
            member[0]
            for member in (
                attn_norm_gain,
                attn_norm_shift,
                qkv_weight,
                query_value_bias,
                proj_weight,
                proj_bias,
                mlp_norm_gain,
                mlp_norm_shift,
                fc_in_weight,
                fc_in_bias,
                fc_out_weight,
                fc_out_bias,
            )
        )
    )
    side_params = tuple(
        (
            member[0]
            for member in (
                side_in_weight,
                side_in_bias,
                side_norm_gain,
                side_norm_shift,
                side_qkv_weight,
                side_out_weight,
            )
        )
    )
    token_rows = tokens[0]
    cotangent_rows = cotangent[0]
    row_count, model_width = token_rows.shape
    frame_count = row_count // TPF
    me = lax.axis_index("dp")
    is_video = lax.axis_index("grp") == 0

    def to_text(values):
        return lax.ppermute(values, ("grp", "dp"), [(i, size + i) for i in range(size)])

    def to_video(values):
        return lax.ppermute(values, ("grp", "dp"), [(size + i, i) for i in range(size)])

    def in_all(values, distance):
        return lax.ppermute(values, "dp", pair_list(size, distance))

    def in_video(values, distance):
        return lax.ppermute(values, ("grp", "dp"), group_pairs(size, distance, 0))

    def in_text(values, distance):
        return lax.ppermute(values, ("grp", "dp"), group_pairs(size, distance, 1))

    flag = lax.axis_index("grp").astype(jnp.int32).reshape(1)
    me_one = me.astype(jnp.int32).reshape(1)
    side_rows = tuple((member if member.ndim == 2 else member[None] for member in side_params))
    frame_order = frame_video.reshape(size, frame_count)[gathered_devices(me, size)]
    frame_ids = frame_order[0]
    message, packed, side_start, side_projected = make_message(
        flag, token_rows, frame_ids, side_rows
    )
    arrived = to_text(packed[:, :model_width])
    packed = jnp.concatenate([arrived, packed[:, model_width:]], axis=1)
    caption_ends = jnp.cumsum(caption_len[0]) - 1
    places = jnp.arange(frame_count * FRAME, dtype=jnp.int32)
    caption_starts = jnp.concatenate([caption_ends + 1 - caption_len[0], jnp.full((1,), row_count)])
    first = jnp.max(
        jnp.where(places[:, None] >= caption_starts[None, :], caption_starts[None, :], 0), axis=1
    ).astype(jnp.int32)
    bias = main_params[3]
    full_bias = jnp.concatenate(
        [bias[:model_width], jnp.zeros((model_width,), jnp.float32), bias[model_width:]]
    )
    params = tuple(
        (
            member if member.ndim == 2 else member[None]
            for member in main_params[:3] + (full_bias,) + main_params[4:]
        )
    )
    normed, projected, mixed, middle, normed_two, act, slope, hidden, block_rows = forward(
        flag, token_rows, message, first[:, None], params
    )
    packed = double_gather(packed, size, in_all)
    out_rows, grad_out, text_vectors, *parts = make_prompt(
        flag,
        me_one,
        size,
        block_rows,
        cotangent_rows,
        packed,
        caption_ends,
        caption_video,
        frame_order.reshape(-1),
        side_rows,
    )
    own_width = model_width // size
    side_sum = PlainSum(size, in_text, in_all, parts[0], parts[1])
    grad_fc_out_bias, *parts = out_weight_grad(me_one, size, act, grad_out)
    parts, grad_out = tie(parts, grad_out)
    out_sum = Sum(size, in_all, parts, [(fc_out_weight.shape[1] // size, 1)])
    grad_pre, grad_fc_in_bias = pre_grad(grad_out, slope, params[10])
    grad_pre, _ = advance(me_one, [side_sum], grad_pre)
    grad_middle, grad_mixed, middle_vectors = middle_grad(
        grad_pre, grad_out, middle, params[8], params[4], params[6]
    )
    grad_middle, normed_two = advance(
        me_one, [out_sum, side_sum], grad_middle, normed_two
    )
    parts = in_weight_grad(me_one, size, normed_two, grad_pre, mixed, grad_middle)
    chunks = model_width // (2 * CHUNK)
    parts, grad_mixed = tie(parts, grad_mixed)
    in_sum = Sum(size, in_all, parts, [(own_width, 4 * chunks), (own_width, chunks)])
    _, grad_mixed = advance(me_one, [out_sum, side_sum], parts, grad_mixed)
    grad_projected = attend_back(flag, projected, grad_mixed, first.reshape(frame_count, 1, FRAME))
    grad_projected, normed = advance(
        me_one, [out_sum, in_sum, side_sum], grad_projected, normed
    )
    while not hasattr(side_sum, "result"):
        advance(me_one, [side_sum], grad_projected)
    pair_rows, context_grad = pair_grad(flag, side_sum.result, side_rows[4], frame_count)
    received = to_video(context_grad)
    grad_source, grad_lines = message_back(
        flag,
        grad_projected,
        grad_middle,
        (message, received, side_start, side_projected, frame_ids[None, :], frame_ids[:, None])
        + (params[2], params[0], side_rows[0], side_rows[2], side_rows[4], side_rows[5], pair_rows),
    )
    grad_lines, normed = tie(grad_lines, normed)
    all_lines = Spread(size, in_all, grad_lines, "stack", plane=True)
    bias_totals, first_vectors, *parts = qkv_weight_grad(
        me_one, size, normed, grad_projected, params[2], params[0], params[1]
    )
    qkv_sum = Sum(size, in_all, parts, [(own_width, 3 * chunks)], fan=True)
    line = pack_vectors(
        (
            first_vectors,
            bias_totals,
            middle_vectors,
            grad_fc_in_bias,
            grad_fc_out_bias,
            text_vectors,
        )
    )
    widths = [model_width] * 2 + [3 * model_width] + [model_width] * 3
    widths += [grad_fc_in_bias.shape[1]] + [model_width] * 4
    line_sum = Spread(size, in_all, line, "add", plane=True)
    streams = [out_sum, in_sum, all_lines]
    _, grad_source = advance(me_one, streams, bias_totals, grad_source)
    token_operands = (hidden, grad_middle, grad_source, params[2], params[0])
    before = token_grad(0, flag, grad_projected, *token_operands)
    streams = [out_sum, in_sum, qkv_sum, line_sum, all_lines]
    before, _ = advance(me_one, streams, before)
    grad_tokens = token_grad(1, flag, grad_projected, *token_operands, before=before)
    while not all((hasattr(one, "result") for one in streams)):
        grad_tokens, _ = advance(me_one, streams, grad_tokens)
    grad_in_weight, grad_side_qkv, grad_side_out, video_vectors = side_weight_grads(
        flag,
        me_one,
        size,
        packed,
        all_lines.result,
        side_sum.result,
        side_rows[4],
        side_rows[2],
        side_rows[3],
    )
    (
        grad_attn_gain,
        grad_attn_shift,
        grad_qv_bias,
        grad_mlp_gain,
        grad_mlp_shift,
        grad_proj_bias,
        grad_fc_in_bias,
        grad_fc_out_bias,
        grad_in_bias,
        grad_side_gain,
        grad_side_shift,
    ) = own_vectors(flag, me_one, size, line_sum.result, video_vectors, widths)
    summed = (
        grad_attn_gain,
        grad_attn_shift,
        qkv_sum.result[0][None],
        grad_qv_bias,
        in_sum.result[1][None],
        grad_proj_bias,
        grad_mlp_gain,
        grad_mlp_shift,
        in_sum.result[0][None],
        grad_fc_in_bias,
        out_sum.result[0][None],
        grad_fc_out_bias,
        grad_in_weight[None],
        grad_in_bias,
        grad_side_gain,
        grad_side_shift,
        grad_side_qkv[None],
        grad_side_out[None],
    )
    return tuple([out_rows[None], grad_tokens[None]] + list(summed))


def solution(mesh):
    placed = (
        P("grp", "dp", None),
        P(),
        P("dp"),
        P("dp", None),
        P("grp", None),
        P("grp", None),
        P("grp", None, None),
        P("grp", None),
        P("grp", None, None),
        P("grp", None),
        P("grp", None),
        P("grp", None),
        P("grp", None, None),
        P("grp", None),
        P("grp", None, None),
        P("grp", None),
        P("grp", None, None),
        P("grp", None),
        P("grp", None),
        P("grp", None),
        P("grp", None, None),
        P("grp", None, None),
        P("grp", "dp", None),
    )
    return jax.shard_map(
        functools.partial(on_device, mesh.shape["dp"]),
        mesh=mesh,
        in_specs=placed,
        out_specs=(
            P("grp", "dp", None),
            P("grp", "dp", None),
            P("grp", "dp"),
            P("grp", "dp"),
            P("grp", "dp", None),
            P("grp", "dp"),
            P("grp", "dp", None),
            P("grp", "dp"),
            P("grp", "dp"),
            P("grp", "dp"),
            P("grp", "dp", None),
            P("grp", "dp"),
            P("grp", "dp", None),
            P("grp", "dp"),
            P("grp", "dp", None),
            P("grp", "dp"),
            P("grp", "dp"),
            P("grp", "dp"),
            P("grp", "dp", None),
            P("grp", "dp", None),
        ),
        check_vma=False,
    )
```

```python
import functools

import jax
import jax.numpy as jnp
from jax import lax
from jax.experimental import pallas as pl
from jax.experimental.pallas import tpu as pltpu
from jax.sharding import PartitionSpec as P

HEADS = 12
HD = 64
TPF = 197
FRAME = 208
PRIOR = 80
CHUNK = 384
VMEM_BYTES = 58 * 2**20
SUB_BLOCKS = ((0, 112, -80, 192), (112, 96, 32, 176))


def product(left_side, right_side):
    return jnp.dot(left_side, right_side, preferred_element_type=jnp.float32)


def product_tn(left_side, right_side):
    return lax.dot_general(
        left_side, right_side, (((0,), (0,)), ((), ())), preferred_element_type=jnp.float32
    )


def product_nt(left_side, right_side):
    return lax.dot_general(
        left_side, right_side, (((1,), (1,)), ((), ())), preferred_element_type=jnp.float32
    )


def cost(flops, size):
    return pl.CostEstimate(flops=int(flops), bytes_accessed=int(size), transcendentals=0)


def padded_rows(rows):
    return -(-rows // 16) * 16


def split_shapes(size, rows):
    return [jax.ShapeDtypeStruct((size // 2, rows, CHUNK), jnp.bfloat16) for _ in range(4)]


def store_block(stage, side, block, me, row, values):
    differs = block ^ me
    right = side == 1
    sent = jnp.where(right, (differs >> 1) & 1, differs & 1)
    place = jnp.where(right, ((block >> 2) << 1) | (block & 1), block >> 1)
    stage[side, sent, place, pl.ds(row, values.shape[0]), :] = values


def stage_shapes(size, rows, steps):
    return [
        pltpu.VMEM((2, 2, size // 2, rows, CHUNK), jnp.bfloat16),
        pltpu.SemaphoreType.DMA((steps, 4)),
    ]


def rows_out(stage, outs, sems, step, side, row, count):
    rows = pl.ds(row, count)
    return [
        pltpu.make_async_copy(
            stage.at[side, sent, :, rows, :],
            outs[2 * side + 1 - sent].at[:, rows, :],
            sems.at[step, sent],
        )
        for sent in range(2)
    ]


def start_rows(stage, outs, sems, step, side, row, count):
    for index in range(2):

        @pl.when(side == index)
        def _():
            for copy in rows_out(stage, outs, sems, step, index, row, count):
                copy.start()


def wait_rows(stage, outs, sems, step, side, row, count):
    for copy in rows_out(stage, outs, sems, step, side, row, count):
        copy.wait()


def in_hbm(count):
    return [pl.BlockSpec(memory_space=pl.ANY) for _ in range(count)]


def combine_kernel(kinds, me_ref, *refs):
    refs = list(refs)
    sources = [[refs.pop(0) for _ in range(kind[1])] for kind in kinds]
    for (name, _, detail), parts in zip(kinds, sources):

        def total(side, index):
            keep, arrived = parts[2 * side], parts[2 * side + 1]
            return keep[index].astype(jnp.float32) + arrived[index].astype(jnp.float32)

        if name == "raw":
            refs.pop(0)[...] = total(0, 0)
        elif name == "add":
            refs.pop(0)[...] = sum((part[...] for part in parts[1:]), parts[0][...])
        elif name == "stack":
            refs.pop(0)[...] = jnp.concatenate([part[...] for part in parts], axis=0)
        elif name == "fan":
            mine = (me_ref[0] >> detail) & 3
            rows = parts[0].shape[1]
            for offset in range(4):
                out = refs.pop(0)
                for side in range(len(parts) // 2):
                    value = total(side, mine ^ offset)
                    out[side * rows : (side + 1) * rows, :] = value.astype(out.dtype)
        elif name == "end":
            if len(parts[0].shape) == 2:
                value = sum((part[...].astype(jnp.float32) for part in parts[1:]), parts[0][...].astype(jnp.float32))
            else:
                value = total(0, 0)
            half = value.shape[0] // 2
            start = 0
            for rows, chunks in detail:
                out = refs.pop(0)
                for side in range(2):
                    for chunk in range(chunks):
                        row = side * half + start + chunk * padded_rows(rows)
                        column = (side * chunks + chunk) * CHUNK
                        out[:, column : column + CHUNK] = value[row : row + rows]
                start += chunks * padded_rows(rows)
        else:
            send, held = refs.pop(0), refs.pop(0)
            mine = (me_ref[0] >> detail) & 1
            rows = parts[0].shape[1]
            for side in range(len(parts) // 2):
                place = slice(side * rows, (side + 1) * rows)
                for index in range(held.shape[0]):
                    held[index, place, :] = total(side, 2 * index + mine).astype(held.dtype)
                    send[index, place, :] = total(side, 2 * index + 1 - mine).astype(send.dtype)


def combine(me, items):
    shapes, kinds, operands = [], [], []
    for name, values, detail in items:
        kinds.append((name, len(values), detail))
        operands += values
        rows = values[0].shape[1]
        if name == "fan":
            shape = (len(values) // 2 * rows, CHUNK)
            shapes += [jax.ShapeDtypeStruct(shape, jnp.bfloat16)] * 4
        elif name == "raw":
            shapes.append(jax.ShapeDtypeStruct((rows, CHUNK), jnp.float32))
        elif name in ("add", "stack"):
            times = len(values) if name == "stack" else 1
            shape = (times * values[0].shape[0], values[0].shape[1])
            shapes.append(jax.ShapeDtypeStruct(shape, values[0].dtype))
        elif name == "end":
            for own, chunks in detail:
                shapes.append(jax.ShapeDtypeStruct((own, 2 * chunks * CHUNK), jnp.float32))
        else:
            sides = len(values) // 2
            half = (values[0].shape[0] // 2, sides * rows, CHUNK)
            shapes += [jax.ShapeDtypeStruct(half, jnp.bfloat16)] * 2
    size = 3 * sum(value.size for value in operands)
    return pl.pallas_call(
        functools.partial(combine_kernel, tuple(kinds)),
        in_specs=[pl.BlockSpec(memory_space=pltpu.SMEM)] + in_vmem(len(operands)),
        out_specs=in_vmem(len(shapes)),
        out_shape=shapes,
        compiler_params=pltpu.CompilerParams(vmem_limit_bytes=30 * 2**20),
        cost_estimate=cost(size, size),
        name="combine",
    )(me, *operands)


def in_vmem(count):
    return [pl.BlockSpec(memory_space=pltpu.VMEM) for _ in range(count)]


def norm_parts(values):
    center = values - jnp.mean(values, axis=-1, keepdims=True)
    spread = lax.rsqrt(jnp.mean(center * center, axis=-1, keepdims=True) + 1e-05)
    return (center * spread, spread)


def norm_back(unit, spread, gain, grad):
    grad_unit = grad * gain
    first = jnp.mean(grad_unit, axis=-1, keepdims=True)
    second = jnp.mean(grad_unit * unit, axis=-1, keepdims=True)
    return spread * (grad_unit - first - unit * second)


def column_sum(values):
    return jnp.sum(values, axis=0, keepdims=True)


def lane_is_low(shape):
    return lax.broadcasted_iota(jnp.int32, shape, len(shape) - 1) < HD


def frame_start(is_video, frame):
    return jnp.where(is_video, TPF, FRAME) * frame


def load_rows(buffer, start):
    base = start // 16 * 16
    window = buffer[pl.ds(pl.multiple_of(base, 16), FRAME + 24), :].astype(jnp.float32)
    return pltpu.roll(window, (FRAME + 24 - (start - base)) % (FRAME + 24), axis=0)[:FRAME]


def store_rows(buffer, start, values):
    base = pl.multiple_of(start // 16 * 16, 16)
    pad = jnp.zeros((24, values.shape[1]), jnp.float32)
    moved = pltpu.roll(jnp.concatenate([values, pad], axis=0), start - base, axis=0)
    old = buffer[pl.ds(base, 16), :].astype(jnp.float32)
    place = lax.broadcasted_iota(jnp.int32, old.shape, 0)
    first = jnp.where(place < start - base, old, moved[:16])
    buffer[pl.ds(base, 16), :] = first.astype(buffer.dtype)
    buffer[pl.ds(base + 16, FRAME), :] = moved[16 : FRAME + 16].astype(buffer.dtype)


def frame_tail(rows, is_video, last_row):
    first = TPF // 8 * 8
    tail = rows[first:]
    place = lax.broadcasted_iota(jnp.int32, tail.shape, 0) + first
    video = jnp.where(place == TPF, last_row, jnp.where(place < TPF, tail, 0.0))
    return jnp.concatenate([rows[:first], jnp.where(is_video, video, tail)], axis=0)


def head_mask(shape, head):
    lane = lax.broadcasted_iota(jnp.int32, shape, len(shape) - 1)
    return (lane >= head * HD) & (lane < (head + 1) * HD)


def stack_heads(rows):
    zero = jnp.zeros_like(rows)
    return jnp.concatenate(
        [jnp.where(head_mask(rows.shape, head), rows, zero) for head in range(HEADS)], axis=0
    )


def pick_heads(stacked):
    count = stacked.shape[0] // HEADS
    total = jnp.zeros((count, stacked.shape[1]), jnp.float32)
    for head in range(HEADS):
        part = stacked[head * count : (head + 1) * count]
        total = total + jnp.where(head_mask(part.shape, head), part, 0.0)
    return total


def side_weights(query, key, allowed):
    stacked = stack_heads(query * jnp.asarray(HD**-0.5, query.dtype))
    bias = jnp.where(allowed, 0.0, -1e30)
    scores = product_nt(stacked, key) + jnp.concatenate([bias] * HEADS, axis=0)
    weights = jnp.exp(scores - jnp.max(scores, axis=-1, keepdims=True))
    return (stacked, weights / jnp.sum(weights, axis=-1, keepdims=True))


def side_attend(query, key, value, allowed):
    _, weights = side_weights(query, key, allowed)
    return pick_heads(product(weights.astype(jnp.bfloat16), value)).astype(jnp.bfloat16)


def side_attend_back(query, key, value, allowed, grad):
    stacked, weights = side_weights(query, key, allowed)
    grads = stack_heads(grad)
    grad_soft = product_nt(grads, value)
    inner = jnp.sum(weights * grad_soft, axis=-1, keepdims=True)
    grad_scores = (weights * (grad_soft - inner)).astype(jnp.bfloat16)
    return (
        pick_heads(product(grad_scores, key)) * HD**-0.5,
        product_tn(grad_scores, stacked),
        product_tn(weights.astype(jnp.bfloat16), grads),
    )


def attend_pair(query, key, value, bias):
    count = query.shape[0]
    low = lane_is_low(query.shape)
    query = query * jnp.asarray(HD**-0.5, query.dtype)
    zero = jnp.zeros_like(query)
    stacked = jnp.concatenate([jnp.where(low, query, zero), jnp.where(low, zero, query)], axis=0)
    scores = product_nt(stacked, key)
    weights = []
    for head in range(2):
        one = scores[head * count : (head + 1) * count] + bias
        weights.append(jnp.exp(one - jnp.max(one, axis=-1, keepdims=True)).astype(jnp.bfloat16))
    wide = jnp.concatenate([value, jnp.ones_like(value)], axis=1)
    summed = product(jnp.concatenate(weights, axis=0), wide)
    mixed = summed[:, :128] / summed[:, 128:]
    return jnp.where(low, mixed[:count], mixed[count:]).astype(jnp.bfloat16)


def attend_back_group(parts):
    masked, scores, softs, grad_scores = [], [], [], []
    for query, key, value, grad, bias in parts:
        low = lane_is_low(query.shape)
        query = query * jnp.asarray(HD**-0.5, query.dtype)
        zero = jnp.zeros_like(query)
        queries = jnp.concatenate([jnp.where(low, query, zero), jnp.where(low, zero, query)], axis=0)
        grads = jnp.concatenate([jnp.where(low, grad, zero), jnp.where(low, zero, grad)], axis=0)
        masked.append((queries, grads))
    for (query, key, value, grad, bias), (queries, grads) in zip(parts, masked):
        scores.append((product_nt(key, queries) + bias, product_nt(value, grads)))
    for one, grad_soft in scores:
        soft = jnp.exp(one - jnp.max(one, axis=0, keepdims=True))
        soft = soft * (1.0 / column_sum(soft))
        inner = soft * grad_soft
        grad_scores.append((inner - soft * column_sum(inner)).astype(jnp.bfloat16))
        softs.append(soft.astype(jnp.bfloat16))
    results = []
    for (query, key, value, grad, bias), (queries, grads), soft, back in zip(parts, masked, softs, grad_scores):
        count = query.shape[0]
        grad_query = product_tn(back, key) * HD**-0.5
        grad_query = jnp.where(lane_is_low(query.shape), grad_query[:count], grad_query[count:])
        results.append((grad_query, product(back, queries), product(soft, grads)))
    return results


def forward_kernel(
    frames,
    flag_ref,
    token_ref,
    message_ref,
    first_ref,
    gain_one,
    shift_one,
    qkv_source,
    qkv_bias,
    proj_source,
    proj_bias,
    gain_two,
    shift_two,
    fc_in_source,
    fc_in_bias,
    fc_out_source,
    fc_out_bias,
    normed_ref,
    projected_ref,
    mixed_ref,
    middle_ref,
    normed_two_ref,
    act_ref,
    slope_ref,
    hidden_ref,
    block_ref,
    held,
    source,
    target,
    next_hidden,
    next_normed,
    qkv_weight,
    proj_weight,
    fc_in_weight,
    fc_out_weight,
    sems,
):
    step = pl.program_id(0)
    last = pl.num_programs(0) - 1
    is_video = flag_ref[0] == 0
    count, width = token_ref.shape
    rows = frames * FRAME
    loads = [
        pltpu.make_async_copy(origin, place, sems.at[index])
        for index, (origin, place) in enumerate(
            (
                (qkv_source, qkv_weight),
                (proj_source, proj_weight),
                (fc_in_source, fc_in_weight),
                (fc_out_source, fc_out_weight),
            )
        )
    ]

    def prepare(index):
        for frame in range(frames):
            part = load_rows(source, frame_start(is_video, index * frames + frame))
            message = message_ref[pl.ds(index * frames + frame, 1), :]
            part = frame_tail(part, is_video, message)
            place = slice(frame * FRAME, (frame + 1) * FRAME)
            next_hidden[place, :] = part
            unit, _ = norm_parts(part)
            next_normed[place, :] = (unit * gain_one[...] + shift_one[...]).astype(jnp.bfloat16)

    @pl.when(step == 0)
    def _():
        for load in loads:
            load.start()
        source[0:count, :] = token_ref[...]
        source[count:, :] = jnp.zeros((source.shape[0] - count, width), source.dtype)
        prepare(0)
        loads[0].wait()

    hidden = next_hidden[...]
    hidden_ref[...] = hidden.astype(jnp.bfloat16)
    normed = next_normed[...]
    normed_ref[...] = normed

    @pl.when(step == 0)
    def _():
        held[0:PRIOR, :] = jnp.zeros((PRIOR, held.shape[1]), held.dtype)

    @pl.when(step > 0)
    def _():
        held[0:PRIOR, :] = held[rows : rows + PRIOR, :]

    for start in range(0, 3 * width, width):
        columns = slice(start, start + width)
        part = (product(normed, qkv_weight[:, columns]) + qkv_bias[:, columns]).astype(jnp.bfloat16)
        held[PRIOR:, columns] = part
        projected_ref[:, columns] = part

    def attend(frame, query_start, query_count, key_start, key_count, bias):
        query_rows = pl.ds(PRIOR + frame * FRAME + query_start, query_count)
        key_rows = pl.ds(PRIOR + frame * FRAME + key_start, key_count)
        for pair in range(0, width, 128):
            mixed_ref[pl.ds(frame * FRAME + query_start, query_count), pair : pair + 128] = attend_pair(
                held[query_rows, pair : pair + 128],
                held[key_rows, width + pair : width + pair + 128],
                held[key_rows, 2 * width + pair : 2 * width + pair + 128],
                bias,
            )

    @pl.when(is_video)
    def _():
        place = lax.broadcasted_iota(jnp.int32, (FRAME, FRAME), 1)
        bias = jnp.where(place <= TPF, 0.0, -1e30)
        for frame in range(frames):
            attend(frame, 0, FRAME, 0, FRAME, bias)

    @pl.when(jnp.logical_not(is_video))
    def _():
        for frame in range(frames):
            for query_start, query_count, key_start, key_count in SUB_BLOCKS:
                base = step * rows + frame * FRAME
                shape = (query_count, key_count)
                key_place = base + key_start + lax.broadcasted_iota(jnp.int32, shape, 1)
                query_place = base + query_start + lax.broadcasted_iota(jnp.int32, shape, 0)
                first = first_ref[pl.ds(frame * FRAME + query_start, query_count), :]
                allowed = (key_place >= first) & (key_place <= query_place)
                bias = jnp.where(allowed, 0.0, -1e30)
                attend(frame, query_start, query_count, key_start, key_count, bias)

    @pl.when(step == 0)
    def _():
        for load in loads[1:]:
            load.wait()

    middle = hidden + product(mixed_ref[...], proj_weight[...]) + proj_bias[...]
    middle_ref[...] = middle.astype(jnp.bfloat16)
    unit, _ = norm_parts(middle)
    normed = (unit * gain_two[...] + shift_two[...]).astype(jnp.bfloat16)
    normed_two_ref[...] = normed
    total = middle + fc_out_bias[...]
    for start in range(0, fc_in_weight.shape[1], width):
        columns = slice(start, start + width)
        pre = product(normed, fc_in_weight[:, columns]) + fc_in_bias[:, columns]
        gate = 0.5 + 0.5 * jnp.tanh(0.851 * pre)
        value = pre * gate
        act = value.astype(jnp.bfloat16)
        act_ref[:, columns] = act
        slope_ref[:, columns] = (gate + 1.702 * value * (1.0 - gate)).astype(jnp.bfloat16)
        total = total + product(act, fc_out_weight[columns, :])
        if start == 0:
            prepare(jnp.minimum(step + 1, last))
    for frame in range(frames):
        start = frame_start(is_video, step * frames + frame)
        store_rows(target, start, total[frame * FRAME : (frame + 1) * FRAME])

    @pl.when(step == last)
    def _():
        block_ref[...] = target[0:count, :]


def whole(shape):
    return pl.BlockSpec(
        shape, lambda *_: (0,) * len(shape), pipeline_mode=pl.Buffered(buffer_count=1)
    )


def forward(flag, tokens, message, first, params, frames=2):
    token_count, width = tokens.shape
    count = token_count // TPF * FRAME
    rows = frames * FRAME
    hidden = params[8].shape[1]

    def by_rows(columns):
        return pl.BlockSpec((rows, columns), lambda i, _: (i, 0))

    widths = (width, 3 * width, width, width, width, hidden, hidden, width)
    return pl.pallas_call(
        functools.partial(forward_kernel, frames),
        grid_spec=pltpu.PrefetchScalarGridSpec(
            num_scalar_prefetch=1,
            grid=(count // rows,),
            in_specs=[whole(tokens.shape), whole(message.shape), by_rows(1)]
            + [in_hbm(1)[0] if member.shape[0] > 1 else whole(member.shape) for member in params],
            out_specs=[by_rows(columns) for columns in widths] + [whole(tokens.shape)],
            scratch_shapes=[
                pltpu.VMEM((rows + PRIOR, 3 * width), jnp.bfloat16),
                pltpu.VMEM((count + 32, width), jnp.bfloat16),
                pltpu.VMEM((count + 32, width), jnp.bfloat16),
                pltpu.VMEM((rows, width), jnp.float32),
                pltpu.VMEM((rows, width), jnp.bfloat16),
            ]
            + [pltpu.VMEM(member.shape, member.dtype) for member in params if member.shape[0] > 1]
            + [pltpu.SemaphoreType.DMA((4,))],
        ),
        out_shape=[jax.ShapeDtypeStruct((count, columns), jnp.bfloat16) for columns in widths]
        + [jax.ShapeDtypeStruct(tokens.shape, jnp.bfloat16)],
        compiler_params=pltpu.CompilerParams(vmem_limit_bytes=VMEM_BYTES),
        cost_estimate=cost(2 * count * width * (4 * width + 2 * hidden), 2 * count * sum(widths)),
        name="forward",
    )(flag, tokens, message, first, *params)


def out_weight_kernel(me_ref, act_ref, grad_ref, bias_ref, *refs):
    outs, (stage, sems) = refs[:4], refs[4:]
    step = pl.program_id(0)
    rows = stage.shape[3]
    part = product_tn(act_ref[...], grad_ref[...]).astype(jnp.bfloat16)
    for index in range(part.shape[0] // rows):
        block = step * (part.shape[0] // rows) + index
        for side in range(2):
            values = part[index * rows : (index + 1) * rows, side * CHUNK : (side + 1) * CHUNK]
            store_block(stage, side, block, me_ref[0], 0, values)

    @pl.when(step == 0)
    def _():
        bias_ref[...] = column_sum(grad_ref[...].astype(jnp.float32))

    @pl.when(step == pl.num_programs(0) - 1)
    def _():
        copies = [
            pltpu.make_async_copy(stage.at[index // 2, index % 2], outs[index + 1 - 2 * (index % 2)], sems.at[0, index])
            for index in range(4)
        ]
        for copy in copies:
            copy.start()
        for copy in copies:
            copy.wait()


def out_weight_grad(me, size, act, grad, tile=768):
    count, hidden = act.shape
    width = grad.shape[1]
    rows = hidden // size
    return pl.pallas_call(
        out_weight_kernel,
        grid_spec=pltpu.PrefetchScalarGridSpec(
            num_scalar_prefetch=1,
            grid=(hidden // tile,),
            in_specs=[pl.BlockSpec((count, tile), lambda i, _: (0, i)), whole(grad.shape)],
            out_specs=[whole((1, width))] + in_hbm(4),
            scratch_shapes=stage_shapes(size, rows, 1),
        ),
        out_shape=[jax.ShapeDtypeStruct((1, width), jnp.float32)] + split_shapes(size, rows),
        compiler_params=pltpu.CompilerParams(vmem_limit_bytes=52 * 2**20),
        cost_estimate=cost(2 * count * hidden * width, 2 * count * hidden),
        name="out_weight_grad",
    )(me, act, grad)


def pre_grad_kernel(grad_ref, slope_ref, weight_ref, out_ref, bias_ref):
    hidden = weight_ref.shape[0]

    @pl.when(pl.program_id(0) == 0)
    def _():
        bias_ref[...] = jnp.zeros(bias_ref.shape, bias_ref.dtype)

    for start in range(0, hidden, 768):
        columns = slice(start, start + 768)
        part = product_nt(grad_ref[...], weight_ref[columns, :])
        part = (part * slope_ref[:, columns].astype(jnp.float32)).astype(jnp.bfloat16)
        out_ref[:, columns] = part
        bias_ref[:, columns] = bias_ref[:, columns] + column_sum(part.astype(jnp.float32))


def pre_grad(grad, slope, weight):
    count, width = grad.shape
    hidden = slope.shape[1]
    rows = 2 * FRAME
    return pl.pallas_call(
        pre_grad_kernel,
        grid=(count // rows,),
        in_specs=[
            pl.BlockSpec((rows, width), lambda i: (i, 0)),
            pl.BlockSpec((rows, hidden), lambda i: (i, 0)),
            whole(weight.shape),
        ],
        out_specs=[pl.BlockSpec((rows, hidden), lambda i: (i, 0)), whole((1, hidden))],
        out_shape=[
            jax.ShapeDtypeStruct((count, hidden), jnp.bfloat16),
            jax.ShapeDtypeStruct((1, hidden), jnp.float32),
        ],
        compiler_params=pltpu.CompilerParams(vmem_limit_bytes=52 * 2**20),
        cost_estimate=cost(2 * count * hidden * width, 4 * count * hidden),
        name="pre_grad",
    )(grad, slope, weight)


def middle_grad_kernel(grad_pre_ref, grad_ref, middle_ref, in_weight, proj_weight, gain_ref, out_ref, mixed_ref, vector_ref):
    back = product_nt(grad_pre_ref[...], in_weight[...])
    unit, spread = norm_parts(middle_ref[...].astype(jnp.float32))
    grad = norm_back(unit, spread, gain_ref[...], back) + grad_ref[...].astype(jnp.float32)
    grad = grad.astype(jnp.bfloat16)
    out_ref[...] = grad
    mixed_ref[...] = product_nt(grad, proj_weight[...]).astype(jnp.bfloat16)
    sums = [column_sum(part) for part in (back * unit, back, grad.astype(jnp.float32))]
    sums = jnp.concatenate(sums, axis=0)

    @pl.when(pl.program_id(0) == 0)
    def _():
        vector_ref[...] = sums

    @pl.when(pl.program_id(0) > 0)
    def _():
        vector_ref[...] = vector_ref[...] + sums


def middle_grad(grad_pre, grad, middle, in_weight, proj_weight, gain):
    count, width = grad.shape
    hidden = grad_pre.shape[1]
    rows = 2 * FRAME

    def by_rows(columns):
        return pl.BlockSpec((rows, columns), lambda i: (i, 0))

    return pl.pallas_call(
        middle_grad_kernel,
        grid=(count // rows,),
        in_specs=[by_rows(hidden), by_rows(width), by_rows(width)]
        + [whole(value.shape) for value in (in_weight, proj_weight, gain)],
        out_specs=[by_rows(width), by_rows(width), whole((3, width))],
        out_shape=[
            jax.ShapeDtypeStruct((count, width), jnp.bfloat16),
            jax.ShapeDtypeStruct((count, width), jnp.bfloat16),
            jax.ShapeDtypeStruct((3, width), jnp.float32),
        ],
        compiler_params=pltpu.CompilerParams(vmem_limit_bytes=52 * 2**20),
        cost_estimate=cost(2 * count * width * (hidden + width), 2 * count * hidden),
        name="middle_grad",
    )(grad_pre, grad, middle, in_weight, proj_weight, gain)


def in_weight_kernel(me_ref, normed_ref, grad_pre_ref, mixed_ref, grad_ref, *refs):
    outs, (stage, sems) = refs[:4], refs[4:]
    step = pl.program_id(0)
    steps = pl.num_programs(0)
    blocks = 2 * stage.shape[2]
    own = normed_ref.shape[1] // blocks
    spaced = padded_rows(own)
    chunks = grad_pre_ref.shape[1] // CHUNK
    per_half = (stage.shape[3] // spaced - 1) // chunks
    side = step // per_half
    first_row = (step - side * per_half) * chunks * spaced

    @pl.when(step < steps - 1)
    def _():
        part = product_tn(normed_ref[...], grad_pre_ref[...]).astype(jnp.bfloat16)
        for chunk in range(chunks):
            row = pl.multiple_of(first_row + chunk * spaced, 16)
            columns = slice(chunk * CHUNK, (chunk + 1) * CHUNK)
            for block in range(blocks):
                values = part[block * own : (block + 1) * own, columns]
                store_block(stage, side, block, me_ref[0], row, values)
        start_rows(stage, outs, sems, step, side, pl.multiple_of(first_row, 16), chunks * spaced)

    @pl.when(step == steps - 1)
    def _():
        part = product_tn(mixed_ref[...], grad_ref[...]).astype(jnp.bfloat16)
        row = stage.shape[3] - spaced
        for block in range(blocks):
            for half in range(2):
                values = part[block * own : (block + 1) * own, half * CHUNK : (half + 1) * CHUNK]
                store_block(stage, half, block, me_ref[0], row, values)
        last = []
        for half in range(2):
            last += rows_out(stage, outs, sems, 2 * per_half + half, half, row, spaced)
        for copy in last:
            copy.start()
        for done in range(2 * per_half):
            first = done % per_half * chunks * spaced
            wait_rows(stage, outs, sems, done, done // per_half, first, chunks * spaced)
        for copy in last:
            copy.wait()


def in_weight_grad(me, size, normed, grad_pre, mixed, grad_middle, tile=768):
    count, width = normed.shape
    hidden = grad_pre.shape[1]
    own = (hidden // (2 * CHUNK) + width // (2 * CHUNK)) * padded_rows(width // size)
    steps = hidden // tile
    return pl.pallas_call(
        in_weight_kernel,
        grid_spec=pltpu.PrefetchScalarGridSpec(
            num_scalar_prefetch=1,
            grid=(steps + 1,),
            in_specs=[
                whole(normed.shape),
                pl.BlockSpec((count, tile), lambda i, _: (0, jnp.minimum(i, steps - 1))),
                whole(mixed.shape),
                whole(grad_middle.shape),
            ],
            out_specs=in_hbm(4),
            scratch_shapes=stage_shapes(size, own, steps + 2),
        ),
        out_shape=split_shapes(size, own),
        compiler_params=pltpu.CompilerParams(vmem_limit_bytes=52 * 2**20),
        cost_estimate=cost(2 * count * width * (hidden + width), 2 * count * hidden),
        name="in_weight_grad",
    )(me, normed, grad_pre, mixed, grad_middle)


def attend_back_kernel(flag_ref, projected_ref, grad_ref, first_ref, out_ref, held, pending, carry):
    step = pl.program_id(0)
    blocks = pl.num_programs(0) - 1
    is_video = flag_ref[0] == 0
    width = grad_ref.shape[1]

    @pl.when(step == 0)
    def _():
        held[...] = jnp.zeros(held.shape, held.dtype)
        carry[...] = jnp.zeros(carry.shape, carry.dtype)

    @pl.when(step > 0)
    def _():
        out_ref[...] = pending[...]

    def add_prior(columns, values):
        rows = slice(FRAME - PRIOR, FRAME)
        out_ref[rows, columns] = (carry[:, columns] + values).astype(jnp.bfloat16)

    @pl.when((step < blocks) & is_video)
    def _():
        place = lax.broadcasted_iota(jnp.int32, (FRAME, 2 * FRAME), 0)
        bias = jnp.where(place <= TPF, 0.0, -1e30)
        for first_pair in range(0, width, 128 * 3):
            pairs = range(first_pair, first_pair + 128 * 3, 128)
            places = [
                [slice(start + pair, start + pair + 128) for start in (0, width, 2 * width)] for pair in pairs
            ]
            parts = [
                tuple((projected_ref[:, columns] for columns in place)) + (grad_ref[:, place[0]], bias)
                for place in places
            ]
            for place, grads in zip(places, attend_back_group(parts)):
                for columns, values in zip(place, grads):
                    pending[:, columns] = values.astype(jnp.bfloat16)

    @pl.when((step < blocks) & jnp.logical_not(is_video))
    def _():
        held[PRIOR:, :] = projected_ref[...]
        biases = []
        for query_start, query_count, key_start, key_count in SUB_BLOCKS:
            base = step * FRAME
            shape = (key_count, query_count)
            key_place = base + key_start + lax.broadcasted_iota(jnp.int32, shape, 0)
            query_place = base + query_start + lax.broadcasted_iota(jnp.int32, shape, 1)
            first = first_ref[0, :, query_start : query_start + query_count]
            allowed = (key_place >= first) & (key_place <= query_place)
            bias = jnp.where(allowed, 0.0, -1e30)
            biases.append(jnp.concatenate([bias, bias], axis=1))
        for first_pair in range(0, width, 128 * 3):
            pairs = range(first_pair, first_pair + 128 * 3, 128)
            places, parts = [], []
            for pair in pairs:
                place = [slice(start + pair, start + pair + 128) for start in (0, width, 2 * width)]
                places.append(place)
                for bias, block in zip(biases, SUB_BLOCKS):
                    query_start, query_count, key_start, key_count = block
                    key_rows = slice(PRIOR + key_start, PRIOR + key_start + key_count)
                    query_rows = slice(query_start, query_start + query_count)
                    parts.append(
                        (
                            projected_ref[query_rows, place[0]],
                            held[key_rows, place[1]],
                            held[key_rows, place[2]],
                            grad_ref[query_rows, place[0]],
                            bias,
                        )
                    )
            results = attend_back_group(parts)
            for index, place in enumerate(places):
                pair_results = results[2 * index : 2 * index + 2]
                for grads, block in zip(pair_results, SUB_BLOCKS):
                    pending[block[0] : block[0] + block[1], place[0]] = grads[0].astype(jnp.bfloat16)
                for kind in (1, 2):
                    early, late = pair_results[0][kind], pair_results[1][kind]
                    overlap = SUB_BLOCKS[1][2]
                    reach = SUB_BLOCKS[0][1]
                    own = jnp.concatenate(
                        [
                            early[PRIOR : PRIOR + overlap],
                            early[PRIOR + overlap :] + late[: reach - overlap],
                            late[reach - overlap :],
                        ],
                        axis=0,
                    )
                    add_prior(place[kind], early[:PRIOR])
                    pending[:, place[kind]] = own.astype(jnp.bfloat16)
                    carry[:, place[kind]] = own[FRAME - PRIOR :]
        held[0:PRIOR, :] = projected_ref[FRAME - PRIOR :, :]


def attend_back(flag, projected, grad_mixed, first):
    count, wide = projected.shape
    width = grad_mixed.shape[1]
    blocks = count // FRAME

    def ahead(i, _):
        return (jnp.minimum(i, blocks - 1), 0)

    return pl.pallas_call(
        attend_back_kernel,
        grid_spec=pltpu.PrefetchScalarGridSpec(
            num_scalar_prefetch=1,
            grid=(blocks + 1,),
            in_specs=[
                pl.BlockSpec((FRAME, wide), ahead),
                pl.BlockSpec((FRAME, width), ahead),
                pl.BlockSpec((1, 1, FRAME), lambda i, _: (jnp.minimum(i, blocks - 1), 0, 0)),
            ],
            out_specs=pl.BlockSpec((FRAME, wide), lambda i, _: (jnp.maximum(i - 1, 0), 0)),
            scratch_shapes=[
                pltpu.VMEM((FRAME + PRIOR, wide), jnp.bfloat16),
                pltpu.VMEM((FRAME, wide), jnp.bfloat16),
                pltpu.VMEM((PRIOR, wide), jnp.float32),
            ],
        ),
        out_shape=jax.ShapeDtypeStruct((count, wide), jnp.bfloat16),
        compiler_params=pltpu.CompilerParams(vmem_limit_bytes=52 * 2**20),
        cost_estimate=cost(2 * count * width * 5 * FRAME * 4, 4 * count * wide),
        name="attend_back",
    )(flag, projected, grad_mixed, first)


def two_terms(values):
    high = values.astype(jnp.bfloat16)
    return (high, (values - high.astype(jnp.float32)).astype(jnp.bfloat16))


def row_product(values, weight):
    spread = [jnp.broadcast_to(one, (8, one.shape[1])) for one in two_terms(values)]
    return (product_nt(spread[0], weight) + product_nt(spread[1], weight))[0:1]


def qkv_weight_kernel(me_ref, normed_ref, grad_ref, weight_ref, gain_ref, shift_ref, bias_ref, vector_ref, *refs):
    outs, (sums, stage, sems) = refs[:4], refs[4:]
    step = pl.program_id(0)
    last = pl.num_programs(0) - 1
    part = product_tn(normed_ref[...], grad_ref[...])
    bias = column_sum(grad_ref[...].astype(jnp.float32))
    bias_ref[...] = bias
    weight = weight_ref[...]
    shift = row_product(bias, weight)
    ones = jnp.ones((8, part.shape[1]), jnp.bfloat16)
    high, lower = two_terms(part * weight.astype(jnp.float32))
    scaled = (product_nt(ones, high) + product_nt(ones, lower))[0:1]
    both = jnp.concatenate([scaled, shift], axis=0)

    @pl.when(step == 0)
    def _():
        sums[...] = both

    @pl.when(step > 0)
    def _():
        sums[...] = sums[...] + both

    part = part.astype(jnp.bfloat16)
    blocks = 2 * stage.shape[2]
    rows = part.shape[0] // blocks
    spaced = padded_rows(rows)
    half = stage.shape[3] // spaced
    chunks = part.shape[1] // CHUNK
    for chunk in range(chunks):
        index = step * chunks + chunk
        side = index // half
        row = pl.multiple_of((index - side * half) * spaced, 16)
        columns = slice(chunk * CHUNK, (chunk + 1) * CHUNK)
        for block in range(blocks):
            store_block(stage, side, block, me_ref[0], row, part[block * rows : (block + 1) * rows, columns])
        start_rows(stage, outs, sems, index, side, row, spaced)

    @pl.when(step == last)
    def _():
        shift_total = sums[1:2, :]
        gain_total = (sums[0:1, :] - shift_ref[...] * shift_total) / gain_ref[...]
        vector_ref[...] = jnp.concatenate([gain_total, shift_total], axis=0)
        for done in range(2 * half):
            wait_rows(stage, outs, sems, done, done // half, done % half * spaced, spaced)


def qkv_weight_grad(me, size, normed, grad, weight, gain, shift, tile=768):
    count, width = normed.shape
    wide = grad.shape[1]
    own = wide // (2 * CHUNK) * padded_rows(width // size)
    return pl.pallas_call(
        qkv_weight_kernel,
        grid_spec=pltpu.PrefetchScalarGridSpec(
            num_scalar_prefetch=1,
            grid=(wide // tile,),
            in_specs=[
                whole(normed.shape),
                pl.BlockSpec((count, tile), lambda i, _: (0, i)),
                pl.BlockSpec((width, tile), lambda i, _: (0, i)),
                whole(gain.shape),
                whole(shift.shape),
            ],
            out_specs=[pl.BlockSpec((1, tile), lambda i, _: (0, i)), whole((2, width))] + in_hbm(4),
            scratch_shapes=[pltpu.VMEM((2, width), jnp.float32)]
            + stage_shapes(size, own, wide // CHUNK),
        ),
        out_shape=[
            jax.ShapeDtypeStruct((1, wide), jnp.float32),
            jax.ShapeDtypeStruct((2, width), jnp.float32),
        ]
        + split_shapes(size, own),
        compiler_params=pltpu.CompilerParams(vmem_limit_bytes=52 * 2**20),
        cost_estimate=cost(2 * count * width * wide, 2 * count * wide),
        name="qkv_weight_grad",
    )(me, normed, grad, weight, gain, shift)


def token_grad_kernel(
    part, split, flag_ref, grad_ref, hidden_ref, middle_ref, source_ref, weight_ref, gain_ref, *refs
):
    if part == 0:
        out_ref, shared_ref, target, sem = refs
    else:
        before_ref, other_ref, out_ref, target, sem = refs
    frames = source_ref.shape[0] // 2
    is_video = flag_ref[0] == 0
    origin = part * split
    step = pl.program_id(0)
    if part == 1:

        @pl.when(step == 0)
        def _():
            target[0 : before_ref.shape[0], :] = before_ref[...]

    back = product_nt(grad_ref[...], weight_ref[...])
    unit, spread = norm_parts(hidden_ref[...].astype(jnp.float32))
    grads = norm_back(unit, spread, gain_ref[...], back) + middle_ref[...].astype(jnp.float32)
    per_step = grads.shape[0] // FRAME
    for frame in range(per_step):
        rows = grads[frame * FRAME : (frame + 1) * FRAME]
        index = part * frames + step * per_step + frame
        place = lax.broadcasted_iota(jnp.int32, (8, rows.shape[1]), 0)
        extra = jnp.where(is_video & (place == 0), source_ref[pl.ds(index, 1), :], 0.0)
        rows = jnp.concatenate([rows[:8] + extra, rows[8:]], axis=0)
        store_rows(target, frame_start(is_video, index) - origin, rows)

    @pl.when(step == pl.num_programs(0) - 1)
    def _():
        count = split if part == 0 else out_ref.shape[0] - split
        copy = pltpu.make_async_copy(
            target.at[pl.ds(0, count)], out_ref.at[pl.ds(origin, count)], sem
        )
        copy.start()
        if part == 0:
            shared_ref[...] = target[split : split + shared_ref.shape[0], :]
        copy.wait()


def token_grad(part, flag, grad, hidden, grad_middle, grad_source, weight, gain, before=None, frames=2):
    count, width = hidden.shape
    rows = frames * FRAME
    tokens = (count // FRAME * TPF, width)
    steps = count // rows // 2
    split = grad_source.shape[0] // 2 * TPF // 16 * 16
    shared = (-(-(grad_source.shape[0] // 2 * FRAME - split) // 16) * 16, width)
    more = () if part == 0 else before

    def by_rows(columns):
        return pl.BlockSpec((rows, columns), lambda i, _: (i + part * steps, 0))

    out_shape = [jax.ShapeDtypeStruct(tokens, jnp.float32)]
    out_specs = in_hbm(1)
    if part == 0:
        out_shape.append(jax.ShapeDtypeStruct(shared, jnp.float32))
        out_specs = out_specs + [whole(shared)]
    results = pl.pallas_call(
        functools.partial(token_grad_kernel, part, split),
        grid_spec=pltpu.PrefetchScalarGridSpec(
            num_scalar_prefetch=1,
            grid=(steps,),
            in_specs=[
                by_rows(grad.shape[1]),
                by_rows(width),
                by_rows(width),
                whole(grad_source.shape),
                whole(weight.shape),
                whole(gain.shape),
            ]
            + ([whole(shared)] + in_hbm(1) if part == 1 else []),
            out_specs=out_specs,
            scratch_shapes=[
                pltpu.VMEM((count // 2 + FRAME, width), jnp.float32),
                pltpu.SemaphoreType.DMA(()),
            ],
        ),
        out_shape=out_shape,
        input_output_aliases={8: 0} if part == 1 else {},
        compiler_params=pltpu.CompilerParams(vmem_limit_bytes=52 * 2**20),
        cost_estimate=cost(count * width * 3 * width, 2 * count * width),
        name="token_grad",
    )(flag, grad, hidden, grad_middle, grad_source, weight, gain, *more)
    return (results[1], results[0]) if part == 0 else results[0]


def message_kernel(flag_ref, token_ref, ids_row, ids_column, in_source, in_bias, gain, shift, qkv_source, out_source, message_ref, packed_ref, start_ref, projected_ref, tokens, in_weight, qkv_weight, out_weight, sems):
    frames, width = message_ref.shape

    @pl.when(flag_ref[0] == 0)
    def _():
        rows = [frame * TPF // 16 * 16 for frame in range(frames)]
        loads = [
            pltpu.make_async_copy(token_ref.at[pl.ds(row, 16)], tokens.at[frame], sems.at[3])
            for frame, row in enumerate(rows)
        ]
        weights = ((in_source, in_weight), (qkv_source, qkv_weight), (out_source, out_weight))
        copies = [
            pltpu.make_async_copy(origin, place, sems.at[index])
            for index, (origin, place) in enumerate(weights)
        ]
        for copy in loads + copies:
            copy.start()
        for copy in loads:
            copy.wait()
        copies[0].wait()
        parts = []
        for frame in range(frames):
            row = frame * TPF
            base = row // 16 * 16
            tile = tokens[frame].astype(jnp.float32)
            parts.append(tile[row - base : row - base + 1])
        source = jnp.concatenate(parts, axis=0).astype(jnp.bfloat16)
        start = product(source, in_weight[...]) + in_bias[...]
        unit, _ = norm_parts(start)
        normed = (unit * gain[...] + shift[...]).astype(jnp.bfloat16)
        copies[1].wait()
        projected = product(normed, qkv_weight[...]).astype(jnp.bfloat16)
        mixed = side_attend(
            projected[:, :width],
            projected[:, width : 2 * width],
            projected[:, 2 * width :],
            ids_column[...] == ids_row[...],
        )
        copies[2].wait()
        message = start + product(mixed, out_weight[...])
        message_ref[...] = message
        start_ref[...] = start
        projected_ref[...] = projected
        packed_ref[...] = jnp.concatenate([message.astype(jnp.bfloat16), source, mixed], axis=1)

    @pl.when(flag_ref[0] != 0)
    def _():
        message_ref[...] = jnp.zeros(message_ref.shape, message_ref.dtype)
        packed_ref[...] = jnp.zeros(packed_ref.shape, packed_ref.dtype)
        start_ref[...] = jnp.zeros(start_ref.shape, start_ref.dtype)
        projected_ref[...] = jnp.zeros(projected_ref.shape, projected_ref.dtype)


def call_once(kernel, name, flops, scalars, operands, shapes):
    return pl.pallas_call(
        kernel,
        in_specs=[pl.BlockSpec(memory_space=pltpu.SMEM) for _ in scalars] + in_vmem(len(operands)),
        out_specs=in_vmem(len(shapes)),
        out_shape=[jax.ShapeDtypeStruct(shape, dtype) for shape, dtype in shapes],
        compiler_params=pltpu.CompilerParams(vmem_limit_bytes=VMEM_BYTES),
        cost_estimate=cost(flops, sum(value.size * 2 for value in operands)),
        name=name,
    )(*scalars, *operands)


def make_message(flag, tokens, frame_ids, side_params):
    frames = frame_ids.shape[0]
    width = tokens.shape[1]
    shapes = [
        ((frames, width), jnp.float32),
        ((frames, 3 * width), jnp.bfloat16),
        ((frames, width), jnp.float32),
        ((frames, 3 * width), jnp.bfloat16),
    ]
    operands = (tokens, frame_ids[None, :], frame_ids[:, None]) + side_params
    held = (side_params[0], side_params[4], side_params[5])
    return pl.pallas_call(
        message_kernel,
        in_specs=[pl.BlockSpec(memory_space=pltpu.SMEM)]
        + [in_hbm(1)[0] if max(value.shape) > 700 and value.shape[0] > 1 else in_vmem(1)[0] for value in operands],
        out_specs=in_vmem(len(shapes)),
        out_shape=[jax.ShapeDtypeStruct(shape, dtype) for shape, dtype in shapes],
        scratch_shapes=[pltpu.VMEM((frames, 16, width), jnp.bfloat16)]
        + [pltpu.VMEM(value.shape, value.dtype) for value in held]
        + [pltpu.SemaphoreType.DMA((4,))],
        compiler_params=pltpu.CompilerParams(vmem_limit_bytes=VMEM_BYTES),
        cost_estimate=cost(1e10, 10**7),
        name="message",
    )(flag, *operands)


def prompt_kernel(
    flag_ref,
    me_ref,
    block_source,
    cotangent_source,
    context_ref,
    ends_column,
    caption_ids,
    frame_ids,
    in_source,
    in_bias,
    gain,
    shift,
    qkv_source,
    out_source,
    out_target,
    grad_out_target,
    vector_ref,
    send_target,
    keep_target,
    padded,
    block_ref,
    cotangent_ref,
    in_weight,
    qkv_weight,
    out_weight,
    out_ref,
    grad_out_ref,
    send_ref,
    keep_ref,
    sems,
):
    count, width = block_ref.shape
    frames = count // TPF
    is_video = flag_ref[0] == 0
    pairs = (
        (cotangent_source, cotangent_ref),
        (block_source, block_ref),
        (in_source, in_weight),
        (qkv_source, qkv_weight),
        (out_source, out_weight),
        (out_ref, out_target),
        (grad_out_ref, grad_out_target),
        (send_ref, send_target),
        (keep_ref, keep_target),
    )
    copies = [
        pltpu.make_async_copy(origin, place, sems.at[index])
        for index, (origin, place) in enumerate(pairs)
    ]
    copies[0].start()

    @pl.when(is_video)
    def _():
        copies[1].start()
        direct = pltpu.make_async_copy(block_ref, out_target, sems.at[5])
        copies[0].wait()
        padded[0:count, :] = cotangent_ref[...]
        padded[count:, :] = jnp.zeros((padded.shape[0] - count, width), padded.dtype)
        for frame in range(frames):
            rows = load_rows(padded, frame * TPF)
            rows = frame_tail(rows, True, 0.0)
            grad_out_ref[frame * FRAME : (frame + 1) * FRAME, :] = rows.astype(jnp.bfloat16)
        copies[6].start()
        copies[1].wait()
        direct.start()
        vector_ref[...] = jnp.zeros(vector_ref.shape, vector_ref.dtype)
        direct.wait()
        copies[6].wait()

    @pl.when(jnp.logical_not(is_video))
    def _():
        for copy in copies[1:5]:
            copy.start()
        copies[0].wait()
        copies[1].wait()
        captions = ends_column.shape[0]
        place = lax.broadcasted_iota(jnp.int32, (captions, count), 1)
        chosen = (place == ends_column[...]).astype(jnp.bfloat16)
        source = product(chosen, block_ref[...]).astype(jnp.bfloat16)
        grad_ends = product(chosen, cotangent_ref[...])
        copies[2].wait()
        start = product(source, in_weight[...]) + in_bias[...]
        unit, spread = norm_parts(start)
        normed = (unit * gain[...] + shift[...]).astype(jnp.bfloat16)
        copies[3].wait()
        query = product(normed, qkv_weight[:, :width]).astype(jnp.bfloat16)
        context = context_ref[:, :width]
        pair = product(context, qkv_weight[:, width:]).astype(jnp.bfloat16)
        key, value = pair[:, :width], pair[:, width:]
        allowed = caption_ids[...] == frame_ids[...]
        mixed = side_attend(query, key, value, allowed)
        copies[4].wait()
        prompt = start + product(mixed, out_weight[...])
        high = prompt.astype(jnp.bfloat16)
        lower = (prompt - high.astype(jnp.float32)).astype(jnp.bfloat16)
        added = product_tn(chosen, jnp.concatenate([high, lower], axis=1))
        added = added[:, :width] + added[:, width:]
        out_ref[...] = (block_ref[...].astype(jnp.float32) + added).astype(jnp.bfloat16)
        copies[5].start()
        grad_round = grad_ends.astype(jnp.bfloat16)
        grad_mixed = product_nt(grad_round, out_weight[...]).astype(jnp.bfloat16)
        grad_query, grad_key, grad_value = side_attend_back(query, key, value, allowed, grad_mixed)
        grad_query = grad_query.astype(jnp.bfloat16)
        mine = (me_ref[0] >> 1) & 1

        def put(block, row, values):
            place = ((block >> 2) << 1) | (block & 1)
            values = values.astype(jnp.bfloat16)

            @pl.when(((block >> 1) & 1) != mine)
            def _():
                send_ref[place, row : row + values.shape[0], :] = values

            @pl.when(((block >> 1) & 1) == mine)
            def _():
                keep_ref[place, row : row + values.shape[0], :] = values

        blocks = 2 * send_ref.shape[0]
        own = context_ref.shape[0] // blocks
        chunks = width // CHUNK
        grad_pair = jnp.concatenate([grad_key, grad_value], axis=1)
        devices = gathered_offsets(blocks)
        for block in range(blocks):
            part = grad_pair[block * own : (block + 1) * own]
            parts = [part[:, chunk * CHUNK : (chunk + 1) * CHUNK] for chunk in range(2 * chunks)]
            put(devices[block] ^ me_ref[0], send_ref.shape[1] - 2 * chunks * own, jnp.concatenate(parts, axis=0))
        grad_normed = product_nt(grad_query, qkv_weight[:, :width])
        grad_start = norm_back(unit, spread, gain[...], grad_normed) + grad_round.astype(jnp.float32)
        grad_start = grad_start.astype(jnp.bfloat16)
        vector_ref[...] = jnp.concatenate(
            [
                column_sum(grad_start.astype(jnp.float32)),
                column_sum(grad_normed * unit),
                column_sum(grad_normed),
            ],
            axis=0,
        )
        grad_source = product_nt(grad_start, in_weight[...])
        added = product_tn(chosen, grad_source.astype(jnp.bfloat16))
        grad_out_ref[0:count, :] = (cotangent_ref[...].astype(jnp.float32) + added).astype(jnp.bfloat16)
        grad_out_ref[count:, :] = jnp.zeros((frames * FRAME - count, width), jnp.bfloat16)
        copies[6].start()
        rows = width // blocks
        for third, (left, right) in enumerate(
            ((source, grad_start), (normed, grad_query), (mixed, grad_round))
        ):
            part = product_tn(left, right).astype(jnp.bfloat16)
            for chunk in range(chunks):
                row = (third * chunks + chunk) * padded_rows(rows)
                columns = slice(chunk * CHUNK, (chunk + 1) * CHUNK)
                for block in range(blocks):
                    put(block, row, part[block * rows : (block + 1) * rows, columns])
        for copy in copies[7:]:
            copy.start()
        for copy in copies[5:]:
            copy.wait()


def make_prompt(flag, me, size, block, cotangent, context, ends, caption_ids, frame_ids, side_params):
    count, width = block.shape
    padded = count // TPF * FRAME
    chunks = width // CHUNK
    rows = 3 * chunks * padded_rows(width // size) + 2 * chunks * (context.shape[0] // size)
    split = (size // 2, rows, CHUNK)
    shapes = [
        ((count, width), jnp.bfloat16),
        ((padded, width), jnp.bfloat16),
        ((3, width), jnp.float32),
        (split, jnp.bfloat16),
        (split, jnp.bfloat16),
    ]
    spare = -ends.shape[0] % 16
    ends = jnp.pad(ends, (0, spare), constant_values=-1)[:, None]
    caption_ids = jnp.pad(caption_ids, (0, spare), constant_values=-1)[:, None]
    operands = (block, cotangent, context, ends, caption_ids, frame_ids[None, :]) + side_params
    weights = [place for place, value in enumerate(operands) if place > 5 and value.shape[0] > 1]
    held = [operands[place] for place in [0, 1] + weights]
    placed = [
        (in_hbm if place in [0, 1] + weights else in_vmem)(1)[0] for place in range(len(operands))
    ]
    outs = [in_vmem(1)[0] if place == 2 else in_hbm(1)[0] for place in range(len(shapes))]
    return pl.pallas_call(
        prompt_kernel,
        in_specs=[pl.BlockSpec(memory_space=pltpu.SMEM)] * 2 + placed,
        out_specs=outs,
        out_shape=[jax.ShapeDtypeStruct(shape, dtype) for shape, dtype in shapes],
        scratch_shapes=[pltpu.VMEM((padded + 32, width), jnp.bfloat16)]
        + [pltpu.VMEM(value.shape, value.dtype) for value in held]
        + [pltpu.VMEM(*shapes[place]) for place in (0, 1, 3, 4)]
        + [pltpu.SemaphoreType.DMA((9,))],
        compiler_params=pltpu.CompilerParams(vmem_limit_bytes=VMEM_BYTES),
        cost_estimate=cost(1e10, 2 * count * width * 8),
        name="prompt",
    )(flag, me, *operands)


def message_back_kernel(frames, flag_ref, *refs):
    grads, middles, rest = refs[:frames], refs[frames : 2 * frames], refs[2 * frames :]
    (
        message_ref,
        received_ref,
        start_ref,
        projected_ref,
        ids_row,
        ids_column,
        main_weight,
        main_gain,
        in_weight,
        gain,
        qkv_weight,
        out_weight,
        pair_ref,
        source_ref,
        line_ref,
    ) = rest
    width = message_ref.shape[1]

    @pl.when(flag_ref[0] == 0)
    def _():
        row = TPF % 16
        grad = jnp.concatenate(
            [one[...].astype(jnp.float32)[row : row + 1] for one in grads], axis=0
        ).astype(jnp.bfloat16)
        middle = jnp.concatenate(
            [one[...].astype(jnp.float32)[row : row + 1] for one in middles], axis=0
        )
        unit, spread = norm_parts(message_ref[...])
        back = norm_back(unit, spread, main_gain[...], product_nt(grad, main_weight[...]))
        grad_round = (back + middle + received_ref[...]).astype(jnp.bfloat16)
        grad_mixed = product_nt(grad_round, out_weight[...]).astype(jnp.bfloat16)
        projected = projected_ref[...]
        grad_parts = side_attend_back(
            projected[:, :width],
            projected[:, width : 2 * width],
            projected[:, 2 * width :],
            ids_column[...] == ids_row[...],
            grad_mixed,
        )
        grad_projected = jnp.concatenate(grad_parts, axis=1).astype(jnp.bfloat16)
        unit, spread = norm_parts(start_ref[...])
        grad_normed = product_nt(grad_projected, qkv_weight[...])
        grad_start = norm_back(unit, spread, gain[...], grad_normed) + grad_round.astype(jnp.float32)
        grad_start = grad_start.astype(jnp.bfloat16)
        source_ref[...] = product_nt(grad_start, in_weight[...])
        line_ref[...] = jnp.concatenate([grad_start, grad_projected, grad_round], axis=1)

    @pl.when(flag_ref[0] != 0)
    def _():
        source_ref[...] = jnp.zeros(source_ref.shape, source_ref.dtype)
        line_ref[:, : 2 * width] = pair_ref[...]
        line_ref[:, 2 * width :] = jnp.zeros((line_ref.shape[0], 3 * width), line_ref.dtype)


def message_back(flag, grad_projected, grad_middle, operands):
    width = grad_middle.shape[1]
    frames = grad_middle.shape[0] // FRAME
    shapes = [
        jax.ShapeDtypeStruct((frames, width), jnp.float32),
        jax.ShapeDtypeStruct((frames, 5 * width), jnp.bfloat16),
    ]

    def last_rows(columns):
        return [
            pl.BlockSpec(
                (16, columns),
                functools.partial(lambda place, *_: (place, 0), (frame * FRAME + TPF) // 16),
                pipeline_mode=pl.Buffered(buffer_count=1),
            )
            for frame in range(frames)
        ]

    return pl.pallas_call(
        functools.partial(message_back_kernel, frames),
        grid_spec=pltpu.PrefetchScalarGridSpec(
            num_scalar_prefetch=1,
            grid=(1,),
            in_specs=last_rows(3 * width)
            + last_rows(width)
            + [whole(value.shape) for value in operands],
            out_specs=[whole(shape.shape) for shape in shapes],
        ),
        out_shape=shapes,
        compiler_params=pltpu.CompilerParams(vmem_limit_bytes=52 * 2**20),
        cost_estimate=cost(1e10, 10**7),
        name="message_back",
    )(flag, *([grad_projected] * frames), *([grad_middle] * frames), *operands)


def pair_kernel(flag_ref, side_ref, source_ref, pair_ref, context_ref, weight, sem):
    rows, width = context_ref.shape
    chunks = pair_ref.shape[1] // CHUNK
    first = side_ref.shape[0] - chunks * rows
    load = pltpu.make_async_copy(source_ref, weight, sem)

    @pl.when(flag_ref[0] != 0)
    def _():
        load.start()
        parts = [side_ref[first + rows * chunk : first + rows * (chunk + 1), :] for chunk in range(chunks)]
        pair = jnp.concatenate(parts, axis=1).astype(jnp.bfloat16)
        pair_ref[...] = pair
        load.wait()
        context_ref[...] = product_nt(pair, weight[:, width:])

    @pl.when(flag_ref[0] == 0)
    def _():
        pair_ref[...] = jnp.zeros(pair_ref.shape, pair_ref.dtype)
        context_ref[...] = jnp.zeros(context_ref.shape, context_ref.dtype)


def pair_grad(flag, side, weight, frames):
    width = weight.shape[0]
    return pl.pallas_call(
        pair_kernel,
        in_specs=[pl.BlockSpec(memory_space=pltpu.SMEM)] + in_vmem(1) + in_hbm(1),
        out_specs=in_vmem(2),
        out_shape=[
            jax.ShapeDtypeStruct((frames, 2 * width), jnp.bfloat16),
            jax.ShapeDtypeStruct((frames, width), jnp.float32),
        ],
        scratch_shapes=[pltpu.VMEM(weight.shape, weight.dtype), pltpu.SemaphoreType.DMA(())],
        compiler_params=pltpu.CompilerParams(vmem_limit_bytes=52 * 2**20),
        cost_estimate=cost(1e9, 10**7),
        name="pair_grad",
    )(flag, side, weight)


def pack_kernel(*refs):
    start = 0
    for one in refs[:-1]:
        for row in range(one.shape[0]):
            refs[-1][:, start : start + one.shape[1]] = one[row : row + 1, :]
            start += one.shape[1]


def pack_vectors(vectors):
    shapes = [((1, sum(one.size for one in vectors)), jnp.float32)]
    return call_once(pack_kernel, "pack_vectors", 1e6, (), vectors, shapes)[0]


def side_weight_kernel(
    flag_ref,
    me_ref,
    packed_ref,
    line_ref,
    side_ref,
    weight_ref,
    gain_ref,
    shift_ref,
    in_source,
    in_bias,
    in_ref,
    qkv_ref,
    out_ref,
    vector_ref,
    in_weight,
    sem,
):
    own, width = in_ref.shape
    load = pltpu.make_async_copy(in_source, in_weight, sem)

    def own_columns(place):
        return cut_columns(packed_ref[:, place * width : (place + 1) * width].astype(jnp.float32))

    def cut_columns(part):
        return pltpu.roll(part, (width - me_ref[0] * own) % width, axis=1)[:, :own].astype(jnp.bfloat16)

    @pl.when(flag_ref[0] == 0)
    def _():
        load.start()
        in_ref[...] = product_tn(own_columns(0), line_ref[:, :width])
        out_ref[...] = product_tn(own_columns(1), line_ref[:, 4 * width :])
        lines = line_ref[...].astype(jnp.float32)
        grad_normed = product_nt(line_ref[:, width : 4 * width], weight_ref[...])
        load.wait()
        start = product(packed_ref[:, :width], in_weight[...]) + in_bias[...]
        unit, _ = norm_parts(start)
        normed = (unit * gain_ref[...] + shift_ref[...]).astype(jnp.bfloat16)
        normed = cut_columns(normed.astype(jnp.float32))
        qkv_ref[...] = product_tn(normed, line_ref[:, width : 4 * width])
        vector_ref[0:1, :] = column_sum(lines[:, :width])
        vector_ref[1:2, :] = column_sum(grad_normed * unit)
        vector_ref[2:3, :] = column_sum(grad_normed)

    @pl.when(flag_ref[0] != 0)
    def _():
        chunks = width // CHUNK
        spaced = padded_rows(own)

        def matrix(third):
            rows = [(third * chunks + chunk) * spaced for chunk in range(chunks)]
            return jnp.concatenate([side_ref[row : row + own, :] for row in rows], axis=1)

        in_ref[...] = matrix(0)
        qkv_ref[:, :width] = matrix(1)
        qkv_ref[:, width:] = product_tn(own_columns(0), line_ref[:, : 2 * width])
        out_ref[...] = matrix(2)
        vector_ref[...] = jnp.zeros(vector_ref.shape, vector_ref.dtype)


def side_weight_grads(flag, me, size, packed, lines, side, weight, gain, shift, in_weight, in_bias):
    width = in_weight.shape[0]
    own = width // size
    shapes = [
        ((own, width), jnp.float32),
        ((own, 3 * width), jnp.float32),
        ((own, width), jnp.float32),
        ((3, width), jnp.float32),
    ]
    operands = (packed, lines, side, weight, gain, shift, in_weight, in_bias)
    return pl.pallas_call(
        side_weight_kernel,
        in_specs=[pl.BlockSpec(memory_space=pltpu.SMEM)] * 2 + in_vmem(6) + in_hbm(1) + in_vmem(1),
        out_specs=in_vmem(len(shapes)),
        out_shape=[jax.ShapeDtypeStruct(shape, dtype) for shape, dtype in shapes],
        scratch_shapes=[pltpu.VMEM(in_weight.shape, in_weight.dtype), pltpu.SemaphoreType.DMA(())],
        compiler_params=pltpu.CompilerParams(vmem_limit_bytes=VMEM_BYTES),
        cost_estimate=cost(1e9, 10**7),
        name="side_weight_grads",
    )(flag, me, *operands)


def vector_kernel(size, widths, flag_ref, me_ref, line_ref, side_ref, *out_refs):
    start = 0
    third = out_refs[0].shape[1] * size
    for place, (width, out_ref) in enumerate(zip(widths, out_refs)):
        total = line_ref[:, start : start + width]
        start += width
        if place == 2:
            total = jnp.concatenate([total[:, :third], total[:, 2 * third :]], axis=1)
            width = 2 * third
        own = width // size
        side = place - (len(widths) - 3)
        if side >= 0:
            total = jnp.where(flag_ref[0] == 0, side_ref[side : side + 1, :], total)
        total = jnp.broadcast_to(total, (8, width))
        out_ref[...] = pltpu.roll(total, (width - me_ref[0] * own) % width, axis=1)[0:1, :own]


def own_vectors(flag, me, size, line, side, widths):
    shapes = [((1, width // size), jnp.float32) for width in widths]
    shapes[2] = ((1, 2 * widths[0] // size), jnp.float32)
    kernel = functools.partial(vector_kernel, size, tuple(widths))
    return call_once(kernel, "own_vectors", 1e6, (flag, me), (line, side), shapes)


def pair_list(size, distance):
    return [(place, place ^ distance) for place in range(size)]


def group_pairs(size, distance, group):
    return [(group * size + place, group * size + (place ^ distance)) for place in range(size)]


def bit_count(size):
    return size.bit_length() - 1


def gather_order(size):
    return list(range(bit_count(size)))[::-1]


def gathered_offsets(size):
    return [
        sum((((place >> step) & 1) << bit for step, bit in enumerate(gather_order(size))))
        for place in range(size)
    ]


def gathered_devices(me, size):
    return me ^ jnp.array(gathered_offsets(size), jnp.int32)


def double_gather(values, size, send):
    for bit in gather_order(size):
        values = jnp.concatenate([values, send(values, 1 << bit)], axis=0)
    return values


class Sum:
    def __init__(self, size, send, parts, layout, fan=False):
        self.send, self.layout, self.fan = send, layout, fan
        self.bits = list(range(2, bit_count(size)))
        self.orders = [[0, 1], [1, 0]]
        self.keeps, self.arrived = [], []
        for side in range(2):
            self.launch(parts[2 * side], parts[2 * side + 1], self.orders[side].pop(0))

    def launch(self, sent, kept, bit):
        self.keeps.append(kept)
        self.arrived.append(self.send(sent, 1 << bit))

    def values(self):
        return [value for pair in zip(self.keeps, self.arrived) for value in pair]

    def items(self):
        if self.orders[0]:
            values = self.values()
            return [("split", values[2 * side : 2 * side + 2], self.orders[side][0]) for side in range(2)]
        if self.bits:
            kind = "fan" if self.fan and len(self.bits) == 2 else "split"
            return [(kind, self.values(), self.bits[0])]
        return [("end", self.keeps + self.arrived, self.layout)]

    def take(self, results):
        fan = self.fan and len(self.bits) == 2 and not self.orders[0]
        self.keeps, self.arrived = [], []
        if self.orders[0]:
            for side in range(2):
                self.launch(results.pop(0), results.pop(0), self.orders[side].pop(0))
        elif fan:
            self.keeps = [results.pop(0)]
            first = self.bits[0]
            self.arrived = [self.send(results.pop(0), offset << first) for offset in (1, 2, 3)]
            self.bits = []
        elif self.bits:
            self.launch(results.pop(0), results.pop(0), self.bits.pop(0))
        else:
            self.result = [results.pop(0) for _ in self.layout]


class PlainSum:
    def __init__(self, size, send, send_small, sent, kept):
        self.send, self.send_small, self.kept = send, send_small, kept
        self.bits = [bit for bit in range(bit_count(size)) if bit != 1]
        self.arrived = send(sent, 2)
        self.steps = 1

    def items(self):
        if self.bits:
            return [("split", [self.kept, self.arrived], self.bits[0])]
        return [("raw", [self.kept, self.arrived], None)]

    def take(self, results):
        if self.bits:
            sent, self.kept = results.pop(0), results.pop(0)
            send = self.send if self.steps < 2 else self.send_small
            self.arrived = send(sent, 1 << self.bits.pop(0))
            self.steps += 1
        else:
            self.result = results.pop(0)


class Spread:
    def __init__(self, size, send, values, kind, plane=False):
        self.kind, self.send, self.held = kind, send, values
        self.steps = [[1 << bit] for bit in gather_order(size)]
        if plane:
            self.steps = self.steps[:-2] + [[2, 1, 3]]
        self.launch()

    def launch(self):
        self.arrived = [self.send(self.held, distance) for distance in self.steps.pop(0)]

    def items(self):
        return [(self.kind, [self.held] + self.arrived, None)]

    def take(self, results):
        self.held = results.pop(0)
        if self.steps:
            self.launch()
        else:
            self.result = self.held


def tie(first, second):
    return lax.optimization_barrier((first, second))


def advance(me, streams, after, before=None):
    streams = [one for one in streams if not hasattr(one, "result")]
    if not streams:
        return (after, before)
    items = [one.items() for one in streams]
    flat = [item for one in items for item in one]
    operands, after = tie([item[1] for item in flat], after)
    results = combine(me, [(item[0], values, item[2]) for item, values in zip(flat, operands)])
    results, before = tie(list(results), before)
    for one in streams:
        one.take(results)
    return (after, before)


def on_device(
    size,
    tokens,
    frame_video,
    caption_video,
    caption_len,
    attn_norm_gain,
    attn_norm_shift,
    qkv_weight,
    query_value_bias,
    proj_weight,
    proj_bias,
    mlp_norm_gain,
    mlp_norm_shift,
    fc_in_weight,
    fc_in_bias,
    fc_out_weight,
    fc_out_bias,
    side_in_weight,
    side_in_bias,
    side_norm_gain,
    side_norm_shift,
    side_qkv_weight,
    side_out_weight,
    cotangent,
):
    main_params = tuple(
        (
            member[0]
            for member in (
                attn_norm_gain,
                attn_norm_shift,
                qkv_weight,
                query_value_bias,
                proj_weight,
                proj_bias,
                mlp_norm_gain,
                mlp_norm_shift,
                fc_in_weight,
                fc_in_bias,
                fc_out_weight,
                fc_out_bias,
            )
        )
    )
    side_params = tuple(
        (
            member[0]
            for member in (
                side_in_weight,
                side_in_bias,
                side_norm_gain,
                side_norm_shift,
                side_qkv_weight,
                side_out_weight,
            )
        )
    )
    token_rows = tokens[0]
    cotangent_rows = cotangent[0]
    row_count, model_width = token_rows.shape
    frame_count = row_count // TPF
    me = lax.axis_index("dp")
    is_video = lax.axis_index("grp") == 0

    def to_text(values):
        return lax.ppermute(values, ("grp", "dp"), [(i, size + i) for i in range(size)])

    def to_video(values):
        return lax.ppermute(values, ("grp", "dp"), [(size + i, i) for i in range(size)])

    def in_all(values, distance):
        return lax.ppermute(values, "dp", pair_list(size, distance))

    def in_video(values, distance):
        return lax.ppermute(values, ("grp", "dp"), group_pairs(size, distance, 0))

    def in_text(values, distance):
        return lax.ppermute(values, ("grp", "dp"), group_pairs(size, distance, 1))

    flag = lax.axis_index("grp").astype(jnp.int32).reshape(1)
    me_one = me.astype(jnp.int32).reshape(1)
    side_rows = tuple((member if member.ndim == 2 else member[None] for member in side_params))
    frame_order = frame_video.reshape(size, frame_count)[gathered_devices(me, size)]
    frame_ids = frame_order[0]
    message, packed, side_start, side_projected = make_message(
        flag, token_rows, frame_ids, side_rows
    )
    arrived = to_text(packed[:, :model_width])
    arrived = jnp.concatenate([arrived, arrived], axis=1)
    packed = jnp.where(is_video, packed[:, model_width:], arrived)
    caption_ends = jnp.cumsum(caption_len[0]) - 1
    places = jnp.arange(frame_count * FRAME, dtype=jnp.int32)
    caption_starts = jnp.concatenate([caption_ends + 1 - caption_len[0], jnp.full((1,), row_count)])
    first = jnp.max(
        jnp.where(places[:, None] >= caption_starts[None, :], caption_starts[None, :], 0), axis=1
    ).astype(jnp.int32)
    bias = main_params[3]
    full_bias = jnp.concatenate(
        [bias[:model_width], jnp.zeros((model_width,), jnp.float32), bias[model_width:]]
    )
    params = tuple(
        (
            member if member.ndim == 2 else member[None]
            for member in main_params[:3] + (full_bias,) + main_params[4:]
        )
    )
    normed, projected, mixed, middle, normed_two, act, slope, hidden, block_rows = forward(
        flag, token_rows, message, first[:, None], params
    )
    packed = double_gather(packed, size, in_all)
    out_rows, grad_out, text_vectors, *parts = make_prompt(
        flag,
        me_one,
        size,
        block_rows,
        cotangent_rows,
        packed,
        caption_ends,
        caption_video,
        frame_order.reshape(-1),
        side_rows,
    )
    own_width = model_width // size
    side_sum = PlainSum(size, in_text, in_all, parts[0], parts[1])
    grad_fc_out_bias, *parts = out_weight_grad(me_one, size, act, grad_out)
    parts, grad_out = tie(parts, grad_out)
    out_sum = Sum(size, in_all, parts, [(fc_out_weight.shape[1] // size, 1)])
    grad_pre, grad_fc_in_bias = pre_grad(grad_out, slope, params[10])
    grad_pre, _ = advance(me_one, [side_sum], grad_pre)
    grad_middle, grad_mixed, middle_vectors = middle_grad(
        grad_pre, grad_out, middle, params[8], params[4], params[6]
    )
    grad_middle, normed_two = advance(
        me_one, [out_sum, side_sum], grad_middle, normed_two
    )
    parts = in_weight_grad(me_one, size, normed_two, grad_pre, mixed, grad_middle)
    chunks = model_width // (2 * CHUNK)
    parts, grad_mixed = tie(parts, grad_mixed)
    in_sum = Sum(size, in_all, parts, [(own_width, 4 * chunks), (own_width, chunks)])
    _, grad_mixed = advance(me_one, [out_sum, side_sum], parts, grad_mixed)
    grad_projected = attend_back(flag, projected, grad_mixed, first.reshape(frame_count, 1, FRAME))
    grad_projected, normed = advance(
        me_one, [out_sum, in_sum, side_sum], grad_projected, normed
    )
    while not hasattr(side_sum, "result"):
        advance(me_one, [side_sum], grad_projected)
    pair_rows, context_grad = pair_grad(flag, side_sum.result, side_rows[4], frame_count)
    received = to_video(context_grad)
    grad_source, grad_lines = message_back(
        flag,
        grad_projected,
        grad_middle,
        (message, received, side_start, side_projected, frame_ids[None, :], frame_ids[:, None])
        + (params[2], params[0], side_rows[0], side_rows[2], side_rows[4], side_rows[5], pair_rows),
    )
    grad_lines, normed = tie(grad_lines, normed)
    all_lines = Spread(size, in_all, grad_lines, "stack", plane=True)
    bias_totals, first_vectors, *parts = qkv_weight_grad(
        me_one, size, normed, grad_projected, params[2], params[0], params[1]
    )
    qkv_sum = Sum(size, in_all, parts, [(own_width, 3 * chunks)], fan=True)
    line = pack_vectors(
        (
            first_vectors,
            bias_totals,
            middle_vectors,
            grad_fc_in_bias,
            grad_fc_out_bias,
            text_vectors,
        )
    )
    widths = [model_width] * 2 + [3 * model_width] + [model_width] * 3
    widths += [grad_fc_in_bias.shape[1]] + [model_width] * 4
    line_sum = Spread(size, in_all, line, "add", plane=True)
    streams = [out_sum, in_sum, all_lines]
    _, grad_source = advance(me_one, streams, bias_totals, grad_source)
    token_operands = (hidden, grad_middle, grad_source, params[2], params[0])
    before = token_grad(0, flag, grad_projected, *token_operands)
    streams = [out_sum, in_sum, qkv_sum, line_sum, all_lines]
    before, _ = advance(me_one, streams, before)
    grad_tokens = token_grad(1, flag, grad_projected, *token_operands, before=before)
    while not all((hasattr(one, "result") for one in streams)):
        grad_tokens, _ = advance(me_one, streams, grad_tokens)
    grad_in_weight, grad_side_qkv, grad_side_out, video_vectors = side_weight_grads(
        flag,
        me_one,
        size,
        packed,
        all_lines.result,
        side_sum.result,
        side_rows[4],
        side_rows[2],
        side_rows[3],
        side_rows[0],
        side_rows[1],
    )
    (
        grad_attn_gain,
        grad_attn_shift,
        grad_qv_bias,
        grad_mlp_gain,
        grad_mlp_shift,
        grad_proj_bias,
        grad_fc_in_bias,
        grad_fc_out_bias,
        grad_in_bias,
        grad_side_gain,
        grad_side_shift,
    ) = own_vectors(flag, me_one, size, line_sum.result, video_vectors, widths)
    summed = (
        grad_attn_gain,
        grad_attn_shift,
        qkv_sum.result[0][None],
        grad_qv_bias,
        in_sum.result[1][None],
        grad_proj_bias,
        grad_mlp_gain,
        grad_mlp_shift,
        in_sum.result[0][None],
        grad_fc_in_bias,
        out_sum.result[0][None],
        grad_fc_out_bias,
        grad_in_weight[None],
        grad_in_bias,
        grad_side_gain,
        grad_side_shift,
        grad_side_qkv[None],
        grad_side_out[None],
    )
    return tuple([out_rows[None], grad_tokens[None]] + list(summed))


def solution(mesh):
    placed = (
        P("grp", "dp", None),
        P(),
        P("dp"),
        P("dp", None),
        P("grp", None),
        P("grp", None),
        P("grp", None, None),
        P("grp", None),
        P("grp", None, None),
        P("grp", None),
        P("grp", None),
        P("grp", None),
        P("grp", None, None),
        P("grp", None),
        P("grp", None, None),
        P("grp", None),
        P("grp", None, None),
        P("grp", None),
        P("grp", None),
        P("grp", None),
        P("grp", None, None),
        P("grp", None, None),
        P("grp", "dp", None),
    )
    return jax.shard_map(
        functools.partial(on_device, mesh.shape["dp"]),
        mesh=mesh,
        in_specs=placed,
        out_specs=(
            P("grp", "dp", None),
            P("grp", "dp", None),
            P("grp", "dp"),
            P("grp", "dp"),
            P("grp", "dp", None),
            P("grp", "dp"),
            P("grp", "dp", None),
            P("grp", "dp"),
            P("grp", "dp"),
            P("grp", "dp"),
            P("grp", "dp", None),
            P("grp", "dp"),
            P("grp", "dp", None),
            P("grp", "dp"),
            P("grp", "dp", None),
            P("grp", "dp"),
            P("grp", "dp"),
            P("grp", "dp"),
            P("grp", "dp", None),
            P("grp", "dp", None),
        ),
        check_vma=False,
    )
```

```python
import functools

import jax
import jax.numpy as jnp
from jax import lax
from jax.experimental import pallas as pl
from jax.experimental.pallas import tpu as pltpu
from jax.sharding import PartitionSpec as P

HEADS = 12
HD = 64
TPF = 197
FRAME = 208
PRIOR = 80
CHUNK = 384
VMEM_BYTES = 58 * 2**20
SUB_BLOCKS = ((0, 112, -80, 192), (112, 96, 32, 176))


def product(left_side, right_side):
    return jnp.dot(left_side, right_side, preferred_element_type=jnp.float32)


def product_tn(left_side, right_side):
    return lax.dot_general(
        left_side, right_side, (((0,), (0,)), ((), ())), preferred_element_type=jnp.float32
    )


def product_nt(left_side, right_side):
    return lax.dot_general(
        left_side, right_side, (((1,), (1,)), ((), ())), preferred_element_type=jnp.float32
    )


def cost(flops, size):
    return pl.CostEstimate(flops=int(flops), bytes_accessed=int(size), transcendentals=0)


def padded_rows(rows):
    return -(-rows // 16) * 16


def split_shapes(size, rows):
    return [jax.ShapeDtypeStruct((size // 2, rows, CHUNK), jnp.bfloat16) for _ in range(4)]


def store_block(stage, side, block, me, row, values):
    differs = block ^ me
    right = side == 1
    sent = jnp.where(right, (differs >> 1) & 1, differs & 1)
    place = jnp.where(right, ((block >> 2) << 1) | (block & 1), block >> 1)
    stage[side, sent, place, pl.ds(row, values.shape[0]), :] = values


def stage_shapes(size, rows, steps):
    return [
        pltpu.VMEM((2, 2, size // 2, rows, CHUNK), jnp.bfloat16),
        pltpu.SemaphoreType.DMA((steps, 4)),
    ]


def rows_out(stage, outs, sems, step, side, row, count):
    rows = pl.ds(row, count)
    return [
        pltpu.make_async_copy(
            stage.at[side, sent, :, rows, :],
            outs[2 * side + 1 - sent].at[:, rows, :],
            sems.at[step, sent],
        )
        for sent in range(2)
    ]


def start_rows(stage, outs, sems, step, side, row, count):
    for index in range(2):

        @pl.when(side == index)
        def _():
            for copy in rows_out(stage, outs, sems, step, index, row, count):
                copy.start()


def wait_rows(stage, outs, sems, step, side, row, count):
    for copy in rows_out(stage, outs, sems, step, side, row, count):
        copy.wait()


def in_hbm(count):
    return [pl.BlockSpec(memory_space=pl.ANY) for _ in range(count)]


def combine_kernel(kinds, me_ref, *refs):
    refs = list(refs)
    sources = [[refs.pop(0) for _ in range(kind[1])] for kind in kinds]
    for (name, _, detail), parts in zip(kinds, sources):

        def total(side, index):
            keep, arrived = parts[2 * side], parts[2 * side + 1]
            return keep[index].astype(jnp.float32) + arrived[index].astype(jnp.float32)

        if name == "raw":
            refs.pop(0)[...] = total(0, 0)
        elif name == "add":
            refs.pop(0)[...] = sum((part[...] for part in parts[1:]), parts[0][...])
        elif name == "stack":
            refs.pop(0)[...] = jnp.concatenate([part[...] for part in parts], axis=0)
        elif name == "fan":
            mine = (me_ref[0] >> detail) & 3
            rows = parts[0].shape[1]
            for offset in range(4):
                out = refs.pop(0)
                for side in range(len(parts) // 2):
                    value = total(side, mine ^ offset)
                    out[side * rows : (side + 1) * rows, :] = value.astype(out.dtype)
        elif name == "end":
            if len(parts[0].shape) == 2:
                value = sum((part[...].astype(jnp.float32) for part in parts[1:]), parts[0][...].astype(jnp.float32))
            else:
                value = total(0, 0)
            half = value.shape[0] // 2
            start = 0
            for rows, chunks in detail:
                out = refs.pop(0)
                for side in range(2):
                    for chunk in range(chunks):
                        row = side * half + start + chunk * padded_rows(rows)
                        column = (side * chunks + chunk) * CHUNK
                        out[:, column : column + CHUNK] = value[row : row + rows]
                start += chunks * padded_rows(rows)
        else:
            send, held = refs.pop(0), refs.pop(0)
            mine = (me_ref[0] >> detail) & 1
            rows = parts[0].shape[1]
            for side in range(len(parts) // 2):
                place = slice(side * rows, (side + 1) * rows)
                for index in range(held.shape[0]):
                    held[index, place, :] = total(side, 2 * index + mine).astype(held.dtype)
                    send[index, place, :] = total(side, 2 * index + 1 - mine).astype(send.dtype)


def combine(me, items):
    shapes, kinds, operands = [], [], []
    for name, values, detail in items:
        kinds.append((name, len(values), detail))
        operands += values
        rows = values[0].shape[1]
        if name == "fan":
            shape = (len(values) // 2 * rows, CHUNK)
            shapes += [jax.ShapeDtypeStruct(shape, jnp.bfloat16)] * 4
        elif name == "raw":
            shapes.append(jax.ShapeDtypeStruct((rows, CHUNK), jnp.float32))
        elif name in ("add", "stack"):
            times = len(values) if name == "stack" else 1
            shape = (times * values[0].shape[0], values[0].shape[1])
            shapes.append(jax.ShapeDtypeStruct(shape, values[0].dtype))
        elif name == "end":
            for own, chunks in detail:
                shapes.append(jax.ShapeDtypeStruct((own, 2 * chunks * CHUNK), jnp.float32))
        else:
            sides = len(values) // 2
            half = (values[0].shape[0] // 2, sides * rows, CHUNK)
            shapes += [jax.ShapeDtypeStruct(half, jnp.bfloat16)] * 2
    size = 3 * sum(value.size for value in operands)
    return pl.pallas_call(
        functools.partial(combine_kernel, tuple(kinds)),
        in_specs=[pl.BlockSpec(memory_space=pltpu.SMEM)] + in_vmem(len(operands)),
        out_specs=in_vmem(len(shapes)),
        out_shape=shapes,
        compiler_params=pltpu.CompilerParams(vmem_limit_bytes=30 * 2**20),
        cost_estimate=cost(size, size),
        name="combine",
    )(me, *operands)


def in_vmem(count):
    return [pl.BlockSpec(memory_space=pltpu.VMEM) for _ in range(count)]


def norm_parts(values):
    center = values - jnp.mean(values, axis=-1, keepdims=True)
    spread = lax.rsqrt(jnp.mean(center * center, axis=-1, keepdims=True) + 1e-05)
    return (center * spread, spread)


def norm_back(unit, spread, gain, grad):
    grad_unit = grad * gain
    first = jnp.mean(grad_unit, axis=-1, keepdims=True)
    second = jnp.mean(grad_unit * unit, axis=-1, keepdims=True)
    return spread * (grad_unit - first - unit * second)


def column_sum(values):
    return jnp.sum(values, axis=0, keepdims=True)


def lane_is_low(shape):
    return lax.broadcasted_iota(jnp.int32, shape, len(shape) - 1) < HD


def frame_start(is_video, frame):
    return jnp.where(is_video, TPF, FRAME) * frame


def load_rows(buffer, start):
    base = start // 16 * 16
    window = buffer[pl.ds(pl.multiple_of(base, 16), FRAME + 24), :].astype(jnp.float32)
    return pltpu.roll(window, (FRAME + 24 - (start - base)) % (FRAME + 24), axis=0)[:FRAME]


def store_rows(buffer, start, values):
    base = pl.multiple_of(start // 16 * 16, 16)
    pad = jnp.zeros((24, values.shape[1]), jnp.float32)
    moved = pltpu.roll(jnp.concatenate([values, pad], axis=0), start - base, axis=0)
    old = buffer[pl.ds(base, 16), :].astype(jnp.float32)
    place = lax.broadcasted_iota(jnp.int32, old.shape, 0)
    first = jnp.where(place < start - base, old, moved[:16])
    buffer[pl.ds(base, 16), :] = first.astype(buffer.dtype)
    buffer[pl.ds(base + 16, FRAME), :] = moved[16 : FRAME + 16].astype(buffer.dtype)


def frame_tail(rows, is_video, last_row):
    first = TPF // 8 * 8
    tail = rows[first:]
    place = lax.broadcasted_iota(jnp.int32, tail.shape, 0) + first
    video = jnp.where(place == TPF, last_row, jnp.where(place < TPF, tail, 0.0))
    return jnp.concatenate([rows[:first], jnp.where(is_video, video, tail)], axis=0)


def head_mask(shape, head):
    lane = lax.broadcasted_iota(jnp.int32, shape, len(shape) - 1)
    return (lane >= head * HD) & (lane < (head + 1) * HD)


def stack_heads(rows):
    zero = jnp.zeros_like(rows)
    return jnp.concatenate(
        [jnp.where(head_mask(rows.shape, head), rows, zero) for head in range(HEADS)], axis=0
    )


def pick_heads(stacked):
    count = stacked.shape[0] // HEADS
    total = jnp.zeros((count, stacked.shape[1]), jnp.float32)
    for head in range(HEADS):
        part = stacked[head * count : (head + 1) * count]
        total = total + jnp.where(head_mask(part.shape, head), part, 0.0)
    return total


def side_weights(query, key, allowed):
    stacked = stack_heads(query * jnp.asarray(HD**-0.5, query.dtype))
    bias = jnp.where(allowed, 0.0, -1e30)
    scores = product_nt(stacked, key) + jnp.concatenate([bias] * HEADS, axis=0)
    weights = jnp.exp(scores - jnp.max(scores, axis=-1, keepdims=True))
    return (stacked, weights / jnp.sum(weights, axis=-1, keepdims=True))


def side_attend(query, key, value, allowed):
    _, weights = side_weights(query, key, allowed)
    return pick_heads(product(weights.astype(jnp.bfloat16), value)).astype(jnp.bfloat16)


def side_attend_back(query, key, value, allowed, grad):
    stacked, weights = side_weights(query, key, allowed)
    grads = stack_heads(grad)
    grad_soft = product_nt(grads, value)
    inner = jnp.sum(weights * grad_soft, axis=-1, keepdims=True)
    grad_scores = (weights * (grad_soft - inner)).astype(jnp.bfloat16)
    return (
        pick_heads(product(grad_scores, key)) * HD**-0.5,
        product_tn(grad_scores, stacked),
        product_tn(weights.astype(jnp.bfloat16), grads),
    )


def attend_pair(query, key, value, bias):
    count = query.shape[0]
    low = lane_is_low(query.shape)
    query = query * jnp.asarray(HD**-0.5, query.dtype)
    zero = jnp.zeros_like(query)
    stacked = jnp.concatenate([jnp.where(low, query, zero), jnp.where(low, zero, query)], axis=0)
    scores = product_nt(stacked, key)
    weights = []
    for head in range(2):
        one = scores[head * count : (head + 1) * count] + bias
        weights.append(jnp.exp(one - jnp.max(one, axis=-1, keepdims=True)).astype(jnp.bfloat16))
    wide = jnp.concatenate([value, jnp.ones_like(value)], axis=1)
    summed = product(jnp.concatenate(weights, axis=0), wide)
    mixed = summed[:, :128] / summed[:, 128:]
    return jnp.where(low, mixed[:count], mixed[count:]).astype(jnp.bfloat16)


def attend_back_group(parts):
    masked, scores, softs, grad_scores = [], [], [], []
    for query, key, value, grad, bias in parts:
        low = lane_is_low(query.shape)
        query = query * jnp.asarray(HD**-0.5, query.dtype)
        zero = jnp.zeros_like(query)
        queries = jnp.concatenate([jnp.where(low, query, zero), jnp.where(low, zero, query)], axis=0)
        grads = jnp.concatenate([jnp.where(low, grad, zero), jnp.where(low, zero, grad)], axis=0)
        masked.append((queries, grads))
    for (query, key, value, grad, bias), (queries, grads) in zip(parts, masked):
        scores.append((product_nt(key, queries) + bias, product_nt(value, grads)))
    for one, grad_soft in scores:
        soft = jnp.exp(one - jnp.max(one, axis=0, keepdims=True))
        soft = soft * (1.0 / column_sum(soft))
        inner = soft * grad_soft
        grad_scores.append((inner - soft * column_sum(inner)).astype(jnp.bfloat16))
        softs.append(soft.astype(jnp.bfloat16))
    results = []
    for (query, key, value, grad, bias), (queries, grads), soft, back in zip(parts, masked, softs, grad_scores):
        count = query.shape[0]
        grad_query = product_tn(back, key) * HD**-0.5
        grad_query = jnp.where(lane_is_low(query.shape), grad_query[:count], grad_query[count:])
        results.append((grad_query, product(back, queries), product(soft, grads)))
    return results


def forward_kernel(
    frames,
    flag_ref,
    token_ref,
    message_ref,
    first_ref,
    gain_one,
    shift_one,
    qkv_source,
    qkv_bias,
    proj_source,
    proj_bias,
    gain_two,
    shift_two,
    fc_in_source,
    fc_in_bias,
    fc_out_source,
    fc_out_bias,
    normed_ref,
    projected_ref,
    mixed_ref,
    middle_ref,
    normed_two_ref,
    act_ref,
    slope_ref,
    hidden_ref,
    block_ref,
    held,
    source,
    target,
    next_hidden,
    next_normed,
    qkv_weight,
    proj_weight,
    fc_in_weight,
    fc_out_weight,
    sems,
):
    step = pl.program_id(0)
    last = pl.num_programs(0) - 1
    is_video = flag_ref[0] == 0
    count, width = token_ref.shape
    rows = frames * FRAME
    loads = [
        pltpu.make_async_copy(origin, place, sems.at[index])
        for index, (origin, place) in enumerate(
            (
                (qkv_source, qkv_weight),
                (proj_source, proj_weight),
                (fc_in_source, fc_in_weight),
                (fc_out_source, fc_out_weight),
            )
        )
    ]

    def prepare(index):
        for frame in range(frames):
            part = load_rows(source, frame_start(is_video, index * frames + frame))
            message = message_ref[pl.ds(index * frames + frame, 1), :]
            part = frame_tail(part, is_video, message)
            place = slice(frame * FRAME, (frame + 1) * FRAME)
            next_hidden[place, :] = part
            unit, _ = norm_parts(part)
            next_normed[place, :] = (unit * gain_one[...] + shift_one[...]).astype(jnp.bfloat16)

    @pl.when(step == 0)
    def _():
        for load in loads:
            load.start()
        source[0:count, :] = token_ref[...]
        source[count:, :] = jnp.zeros((source.shape[0] - count, width), source.dtype)
        prepare(0)
        loads[0].wait()

    hidden = next_hidden[...]
    hidden_ref[...] = hidden.astype(jnp.bfloat16)
    normed = next_normed[...]
    normed_ref[...] = normed

    @pl.when(step == 0)
    def _():
        held[0:PRIOR, :] = jnp.zeros((PRIOR, held.shape[1]), held.dtype)

    @pl.when(step > 0)
    def _():
        held[0:PRIOR, :] = held[rows : rows + PRIOR, :]

    for start in range(0, 3 * width, width):
        columns = slice(start, start + width)
        part = (product(normed, qkv_weight[:, columns]) + qkv_bias[:, columns]).astype(jnp.bfloat16)
        held[PRIOR:, columns] = part
        projected_ref[:, columns] = part

    def attend(frame, query_start, query_count, key_start, key_count, bias):
        query_rows = pl.ds(PRIOR + frame * FRAME + query_start, query_count)
        key_rows = pl.ds(PRIOR + frame * FRAME + key_start, key_count)
        for pair in range(0, width, 128):
            mixed_ref[pl.ds(frame * FRAME + query_start, query_count), pair : pair + 128] = attend_pair(
                held[query_rows, pair : pair + 128],
                held[key_rows, width + pair : width + pair + 128],
                held[key_rows, 2 * width + pair : 2 * width + pair + 128],
                bias,
            )

    @pl.when(is_video)
    def _():
        place = lax.broadcasted_iota(jnp.int32, (FRAME, FRAME), 1)
        bias = jnp.where(place <= TPF, 0.0, -1e30)
        for frame in range(frames):
            attend(frame, 0, FRAME, 0, FRAME, bias)

    @pl.when(jnp.logical_not(is_video))
    def _():
        for frame in range(frames):
            for query_start, query_count, key_start, key_count in SUB_BLOCKS:
                base = step * rows + frame * FRAME
                shape = (query_count, key_count)
                key_place = base + key_start + lax.broadcasted_iota(jnp.int32, shape, 1)
                query_place = base + query_start + lax.broadcasted_iota(jnp.int32, shape, 0)
                first = first_ref[pl.ds(frame * FRAME + query_start, query_count), :]
                allowed = (key_place >= first) & (key_place <= query_place)
                bias = jnp.where(allowed, 0.0, -1e30)
                attend(frame, query_start, query_count, key_start, key_count, bias)

    @pl.when(step == 0)
    def _():
        for load in loads[1:]:
            load.wait()

    middle = hidden + product(mixed_ref[...], proj_weight[...]) + proj_bias[...]
    middle_ref[...] = middle.astype(jnp.bfloat16)
    unit, _ = norm_parts(middle)
    normed = (unit * gain_two[...] + shift_two[...]).astype(jnp.bfloat16)
    normed_two_ref[...] = normed
    total = middle + fc_out_bias[...]
    for start in range(0, fc_in_weight.shape[1], width):
        columns = slice(start, start + width)
        pre = product(normed, fc_in_weight[:, columns]) + fc_in_bias[:, columns]
        gate = 0.5 + 0.5 * jnp.tanh(0.851 * pre)
        value = pre * gate
        act = value.astype(jnp.bfloat16)
        act_ref[:, columns] = act
        slope_ref[:, columns] = (gate + 1.702 * value * (1.0 - gate)).astype(jnp.bfloat16)
        total = total + product(act, fc_out_weight[columns, :])
        if start == 0:
            prepare(jnp.minimum(step + 1, last))
    for frame in range(frames):
        start = frame_start(is_video, step * frames + frame)
        store_rows(target, start, total[frame * FRAME : (frame + 1) * FRAME])

    @pl.when(step == last)
    def _():
        block_ref[...] = target[0:count, :]


def whole(shape):
    return pl.BlockSpec(
        shape, lambda *_: (0,) * len(shape), pipeline_mode=pl.Buffered(buffer_count=1)
    )


def forward(flag, tokens, message, first, params, frames=2):
    token_count, width = tokens.shape
    count = token_count // TPF * FRAME
    rows = frames * FRAME
    hidden = params[8].shape[1]

    def by_rows(columns):
        return pl.BlockSpec((rows, columns), lambda i, _: (i, 0))

    widths = (width, 3 * width, width, width, width, hidden, hidden, width)
    return pl.pallas_call(
        functools.partial(forward_kernel, frames),
        grid_spec=pltpu.PrefetchScalarGridSpec(
            num_scalar_prefetch=1,
            grid=(count // rows,),
            in_specs=[whole(tokens.shape), whole(message.shape), by_rows(1)]
            + [in_hbm(1)[0] if member.shape[0] > 1 else whole(member.shape) for member in params],
            out_specs=[by_rows(columns) for columns in widths] + [whole(tokens.shape)],
            scratch_shapes=[
                pltpu.VMEM((rows + PRIOR, 3 * width), jnp.bfloat16),
                pltpu.VMEM((count + 32, width), jnp.bfloat16),
                pltpu.VMEM((count + 32, width), jnp.bfloat16),
                pltpu.VMEM((rows, width), jnp.float32),
                pltpu.VMEM((rows, width), jnp.bfloat16),
            ]
            + [pltpu.VMEM(member.shape, member.dtype) for member in params if member.shape[0] > 1]
            + [pltpu.SemaphoreType.DMA((4,))],
        ),
        out_shape=[jax.ShapeDtypeStruct((count, columns), jnp.bfloat16) for columns in widths]
        + [jax.ShapeDtypeStruct(tokens.shape, jnp.bfloat16)],
        compiler_params=pltpu.CompilerParams(vmem_limit_bytes=VMEM_BYTES),
        cost_estimate=cost(2 * count * width * (4 * width + 2 * hidden), 2 * count * sum(widths)),
        name="forward",
    )(flag, tokens, message, first, *params)


def out_weight_kernel(me_ref, act_ref, grad_ref, bias_ref, *refs):
    outs, (stage, sems) = refs[:4], refs[4:]
    step = pl.program_id(0)
    rows = stage.shape[3]
    part = product_tn(act_ref[...], grad_ref[...]).astype(jnp.bfloat16)
    for index in range(part.shape[0] // rows):
        block = step * (part.shape[0] // rows) + index
        for side in range(2):
            values = part[index * rows : (index + 1) * rows, side * CHUNK : (side + 1) * CHUNK]
            store_block(stage, side, block, me_ref[0], 0, values)

    @pl.when(step == 0)
    def _():
        bias_ref[...] = column_sum(grad_ref[...].astype(jnp.float32))

    @pl.when(step == pl.num_programs(0) - 1)
    def _():
        copies = [
            pltpu.make_async_copy(stage.at[index // 2, index % 2], outs[index + 1 - 2 * (index % 2)], sems.at[0, index])
            for index in range(4)
        ]
        for copy in copies:
            copy.start()
        for copy in copies:
            copy.wait()


def out_weight_grad(me, size, act, grad, tile=768):
    count, hidden = act.shape
    width = grad.shape[1]
    rows = hidden // size
    return pl.pallas_call(
        out_weight_kernel,
        grid_spec=pltpu.PrefetchScalarGridSpec(
            num_scalar_prefetch=1,
            grid=(hidden // tile,),
            in_specs=[pl.BlockSpec((count, tile), lambda i, _: (0, i)), whole(grad.shape)],
            out_specs=[whole((1, width))] + in_hbm(4),
            scratch_shapes=stage_shapes(size, rows, 1),
        ),
        out_shape=[jax.ShapeDtypeStruct((1, width), jnp.float32)] + split_shapes(size, rows),
        compiler_params=pltpu.CompilerParams(vmem_limit_bytes=52 * 2**20),
        cost_estimate=cost(2 * count * hidden * width, 2 * count * hidden),
        name="out_weight_grad",
    )(me, act, grad)


def pre_grad_kernel(grad_ref, slope_ref, weight_ref, out_ref, bias_ref):
    hidden = weight_ref.shape[0]

    @pl.when(pl.program_id(0) == 0)
    def _():
        bias_ref[...] = jnp.zeros(bias_ref.shape, bias_ref.dtype)

    for start in range(0, hidden, 768):
        columns = slice(start, start + 768)
        part = product_nt(grad_ref[...], weight_ref[columns, :])
        part = (part * slope_ref[:, columns].astype(jnp.float32)).astype(jnp.bfloat16)
        out_ref[:, columns] = part
        bias_ref[:, columns] = bias_ref[:, columns] + column_sum(part.astype(jnp.float32))


def pre_grad(grad, slope, weight):
    count, width = grad.shape
    hidden = slope.shape[1]
    rows = 2 * FRAME
    return pl.pallas_call(
        pre_grad_kernel,
        grid=(count // rows,),
        in_specs=[
            pl.BlockSpec((rows, width), lambda i: (i, 0)),
            pl.BlockSpec((rows, hidden), lambda i: (i, 0)),
            whole(weight.shape),
        ],
        out_specs=[pl.BlockSpec((rows, hidden), lambda i: (i, 0)), whole((1, hidden))],
        out_shape=[
            jax.ShapeDtypeStruct((count, hidden), jnp.bfloat16),
            jax.ShapeDtypeStruct((1, hidden), jnp.float32),
        ],
        compiler_params=pltpu.CompilerParams(vmem_limit_bytes=52 * 2**20),
        cost_estimate=cost(2 * count * hidden * width, 4 * count * hidden),
        name="pre_grad",
    )(grad, slope, weight)


def middle_grad_kernel(grad_pre_ref, grad_ref, middle_ref, in_weight, proj_weight, gain_ref, out_ref, mixed_ref, vector_ref):
    back = product_nt(grad_pre_ref[...], in_weight[...])
    unit, spread = norm_parts(middle_ref[...].astype(jnp.float32))
    grad = norm_back(unit, spread, gain_ref[...], back) + grad_ref[...].astype(jnp.float32)
    grad = grad.astype(jnp.bfloat16)
    out_ref[...] = grad
    mixed_ref[...] = product_nt(grad, proj_weight[...]).astype(jnp.bfloat16)
    sums = [column_sum(part) for part in (back * unit, back, grad.astype(jnp.float32))]
    sums = jnp.concatenate(sums, axis=0)

    @pl.when(pl.program_id(0) == 0)
    def _():
        vector_ref[...] = sums

    @pl.when(pl.program_id(0) > 0)
    def _():
        vector_ref[...] = vector_ref[...] + sums


def middle_grad(grad_pre, grad, middle, in_weight, proj_weight, gain):
    count, width = grad.shape
    hidden = grad_pre.shape[1]
    rows = 2 * FRAME

    def by_rows(columns):
        return pl.BlockSpec((rows, columns), lambda i: (i, 0))

    return pl.pallas_call(
        middle_grad_kernel,
        grid=(count // rows,),
        in_specs=[by_rows(hidden), by_rows(width), by_rows(width)]
        + [whole(value.shape) for value in (in_weight, proj_weight, gain)],
        out_specs=[by_rows(width), by_rows(width), whole((3, width))],
        out_shape=[
            jax.ShapeDtypeStruct((count, width), jnp.bfloat16),
            jax.ShapeDtypeStruct((count, width), jnp.bfloat16),
            jax.ShapeDtypeStruct((3, width), jnp.float32),
        ],
        compiler_params=pltpu.CompilerParams(vmem_limit_bytes=52 * 2**20),
        cost_estimate=cost(2 * count * width * (hidden + width), 2 * count * hidden),
        name="middle_grad",
    )(grad_pre, grad, middle, in_weight, proj_weight, gain)


def in_weight_kernel(me_ref, normed_ref, grad_pre_ref, mixed_ref, grad_ref, *refs):
    outs, (stage, sems) = refs[:4], refs[4:]
    step = pl.program_id(0)
    steps = pl.num_programs(0)
    blocks = 2 * stage.shape[2]
    own = normed_ref.shape[1] // blocks
    spaced = padded_rows(own)
    chunks = grad_pre_ref.shape[1] // CHUNK
    per_half = (stage.shape[3] // spaced - 1) // chunks
    side = step // per_half
    first_row = (step - side * per_half) * chunks * spaced

    @pl.when(step < steps - 1)
    def _():
        part = product_tn(normed_ref[...], grad_pre_ref[...]).astype(jnp.bfloat16)
        for chunk in range(chunks):
            row = pl.multiple_of(first_row + chunk * spaced, 16)
            columns = slice(chunk * CHUNK, (chunk + 1) * CHUNK)
            for block in range(blocks):
                values = part[block * own : (block + 1) * own, columns]
                store_block(stage, side, block, me_ref[0], row, values)
        start_rows(stage, outs, sems, step, side, pl.multiple_of(first_row, 16), chunks * spaced)

    @pl.when(step == steps - 1)
    def _():
        part = product_tn(mixed_ref[...], grad_ref[...]).astype(jnp.bfloat16)
        row = stage.shape[3] - spaced
        for block in range(blocks):
            for half in range(2):
                values = part[block * own : (block + 1) * own, half * CHUNK : (half + 1) * CHUNK]
                store_block(stage, half, block, me_ref[0], row, values)
        last = []
        for half in range(2):
            last += rows_out(stage, outs, sems, 2 * per_half + half, half, row, spaced)
        for copy in last:
            copy.start()
        for done in range(2 * per_half):
            first = done % per_half * chunks * spaced
            wait_rows(stage, outs, sems, done, done // per_half, first, chunks * spaced)
        for copy in last:
            copy.wait()


def in_weight_grad(me, size, normed, grad_pre, mixed, grad_middle, tile=768):
    count, width = normed.shape
    hidden = grad_pre.shape[1]
    own = (hidden // (2 * CHUNK) + width // (2 * CHUNK)) * padded_rows(width // size)
    steps = hidden // tile
    return pl.pallas_call(
        in_weight_kernel,
        grid_spec=pltpu.PrefetchScalarGridSpec(
            num_scalar_prefetch=1,
            grid=(steps + 1,),
            in_specs=[
                whole(normed.shape),
                pl.BlockSpec((count, tile), lambda i, _: (0, jnp.minimum(i, steps - 1))),
                whole(mixed.shape),
                whole(grad_middle.shape),
            ],
            out_specs=in_hbm(4),
            scratch_shapes=stage_shapes(size, own, steps + 2),
        ),
        out_shape=split_shapes(size, own),
        compiler_params=pltpu.CompilerParams(vmem_limit_bytes=52 * 2**20),
        cost_estimate=cost(2 * count * width * (hidden + width), 2 * count * hidden),
        name="in_weight_grad",
    )(me, normed, grad_pre, mixed, grad_middle)


def attend_back_kernel(flag_ref, projected_ref, grad_ref, first_ref, out_ref, held, pending, carry):
    step = pl.program_id(0)
    blocks = pl.num_programs(0) - 1
    is_video = flag_ref[0] == 0
    width = grad_ref.shape[1]

    @pl.when(step == 0)
    def _():
        held[...] = jnp.zeros(held.shape, held.dtype)
        carry[...] = jnp.zeros(carry.shape, carry.dtype)

    @pl.when(step > 0)
    def _():
        out_ref[...] = pending[...]

    def add_prior(columns, values):
        rows = slice(FRAME - PRIOR, FRAME)
        out_ref[rows, columns] = (carry[:, columns] + values).astype(jnp.bfloat16)

    @pl.when((step < blocks) & is_video)
    def _():
        place = lax.broadcasted_iota(jnp.int32, (FRAME, 2 * FRAME), 0)
        bias = jnp.where(place <= TPF, 0.0, -1e30)
        for first_pair in range(0, width, 128 * 3):
            pairs = range(first_pair, first_pair + 128 * 3, 128)
            places = [
                [slice(start + pair, start + pair + 128) for start in (0, width, 2 * width)] for pair in pairs
            ]
            parts = [
                tuple((projected_ref[:, columns] for columns in place)) + (grad_ref[:, place[0]], bias)
                for place in places
            ]
            for place, grads in zip(places, attend_back_group(parts)):
                for columns, values in zip(place, grads):
                    pending[:, columns] = values.astype(jnp.bfloat16)

    @pl.when((step < blocks) & jnp.logical_not(is_video))
    def _():
        held[PRIOR:, :] = projected_ref[...]
        biases = []
        for query_start, query_count, key_start, key_count in SUB_BLOCKS:
            base = step * FRAME
            shape = (key_count, query_count)
            key_place = base + key_start + lax.broadcasted_iota(jnp.int32, shape, 0)
            query_place = base + query_start + lax.broadcasted_iota(jnp.int32, shape, 1)
            first = first_ref[0, :, query_start : query_start + query_count]
            allowed = (key_place >= first) & (key_place <= query_place)
            bias = jnp.where(allowed, 0.0, -1e30)
            biases.append(jnp.concatenate([bias, bias], axis=1))
        for first_pair in range(0, width, 128 * 3):
            pairs = range(first_pair, first_pair + 128 * 3, 128)
            places, parts = [], []
            for pair in pairs:
                place = [slice(start + pair, start + pair + 128) for start in (0, width, 2 * width)]
                places.append(place)
                for bias, block in zip(biases, SUB_BLOCKS):
                    query_start, query_count, key_start, key_count = block
                    key_rows = slice(PRIOR + key_start, PRIOR + key_start + key_count)
                    query_rows = slice(query_start, query_start + query_count)
                    parts.append(
                        (
                            projected_ref[query_rows, place[0]],
                            held[key_rows, place[1]],
                            held[key_rows, place[2]],
                            grad_ref[query_rows, place[0]],
                            bias,
                        )
                    )
            results = attend_back_group(parts)
            for index, place in enumerate(places):
                pair_results = results[2 * index : 2 * index + 2]
                for grads, block in zip(pair_results, SUB_BLOCKS):
                    pending[block[0] : block[0] + block[1], place[0]] = grads[0].astype(jnp.bfloat16)
                for kind in (1, 2):
                    early, late = pair_results[0][kind], pair_results[1][kind]
                    overlap = SUB_BLOCKS[1][2]
                    reach = SUB_BLOCKS[0][1]
                    own = jnp.concatenate(
                        [
                            early[PRIOR : PRIOR + overlap],
                            early[PRIOR + overlap :] + late[: reach - overlap],
                            late[reach - overlap :],
                        ],
                        axis=0,
                    )
                    add_prior(place[kind], early[:PRIOR])
                    pending[:, place[kind]] = own.astype(jnp.bfloat16)
                    carry[:, place[kind]] = own[FRAME - PRIOR :]
        held[0:PRIOR, :] = projected_ref[FRAME - PRIOR :, :]


def attend_back(flag, projected, grad_mixed, first):
    count, wide = projected.shape
    width = grad_mixed.shape[1]
    blocks = count // FRAME

    def ahead(i, _):
        return (jnp.minimum(i, blocks - 1), 0)

    return pl.pallas_call(
        attend_back_kernel,
        grid_spec=pltpu.PrefetchScalarGridSpec(
            num_scalar_prefetch=1,
            grid=(blocks + 1,),
            in_specs=[
                pl.BlockSpec((FRAME, wide), ahead),
                pl.BlockSpec((FRAME, width), ahead),
                pl.BlockSpec((1, 1, FRAME), lambda i, _: (jnp.minimum(i, blocks - 1), 0, 0)),
            ],
            out_specs=pl.BlockSpec((FRAME, wide), lambda i, _: (jnp.maximum(i - 1, 0), 0)),
            scratch_shapes=[
                pltpu.VMEM((FRAME + PRIOR, wide), jnp.bfloat16),
                pltpu.VMEM((FRAME, wide), jnp.bfloat16),
                pltpu.VMEM((PRIOR, wide), jnp.float32),
            ],
        ),
        out_shape=jax.ShapeDtypeStruct((count, wide), jnp.bfloat16),
        compiler_params=pltpu.CompilerParams(vmem_limit_bytes=52 * 2**20),
        cost_estimate=cost(2 * count * width * 5 * FRAME * 4, 4 * count * wide),
        name="attend_back",
    )(flag, projected, grad_mixed, first)


def two_terms(values):
    high = values.astype(jnp.bfloat16)
    return (high, (values - high.astype(jnp.float32)).astype(jnp.bfloat16))


def row_product(values, weight):
    spread = [jnp.broadcast_to(one, (8, one.shape[1])) for one in two_terms(values)]
    return (product_nt(spread[0], weight) + product_nt(spread[1], weight))[0:1]


def qkv_weight_kernel(me_ref, normed_ref, grad_ref, weight_ref, gain_ref, shift_ref, bias_ref, vector_ref, *refs):
    outs, (sums, stage, sems) = refs[:4], refs[4:]
    step = pl.program_id(0)
    last = pl.num_programs(0) - 1
    part = product_tn(normed_ref[...], grad_ref[...])
    bias = column_sum(grad_ref[...].astype(jnp.float32))
    bias_ref[...] = bias
    weight = weight_ref[...]
    shift = row_product(bias, weight)
    ones = jnp.ones((8, part.shape[1]), jnp.bfloat16)
    high, lower = two_terms(part * weight.astype(jnp.float32))
    scaled = (product_nt(ones, high) + product_nt(ones, lower))[0:1]
    both = jnp.concatenate([scaled, shift], axis=0)

    @pl.when(step == 0)
    def _():
        sums[...] = both

    @pl.when(step > 0)
    def _():
        sums[...] = sums[...] + both

    part = part.astype(jnp.bfloat16)
    blocks = 2 * stage.shape[2]
    rows = part.shape[0] // blocks
    spaced = padded_rows(rows)
    half = stage.shape[3] // spaced
    chunks = part.shape[1] // CHUNK
    for chunk in range(chunks):
        index = step * chunks + chunk
        side = index // half
        row = pl.multiple_of((index - side * half) * spaced, 16)
        columns = slice(chunk * CHUNK, (chunk + 1) * CHUNK)
        for block in range(blocks):
            store_block(stage, side, block, me_ref[0], row, part[block * rows : (block + 1) * rows, columns])
        start_rows(stage, outs, sems, index, side, row, spaced)

    @pl.when(step == last)
    def _():
        shift_total = sums[1:2, :]
        gain_total = (sums[0:1, :] - shift_ref[...] * shift_total) / gain_ref[...]
        vector_ref[...] = jnp.concatenate([gain_total, shift_total], axis=0)
        for done in range(2 * half):
            wait_rows(stage, outs, sems, done, done // half, done % half * spaced, spaced)


def qkv_weight_grad(me, size, normed, grad, weight, gain, shift, tile=768):
    count, width = normed.shape
    wide = grad.shape[1]
    own = wide // (2 * CHUNK) * padded_rows(width // size)
    return pl.pallas_call(
        qkv_weight_kernel,
        grid_spec=pltpu.PrefetchScalarGridSpec(
            num_scalar_prefetch=1,
            grid=(wide // tile,),
            in_specs=[
                whole(normed.shape),
                pl.BlockSpec((count, tile), lambda i, _: (0, i)),
                pl.BlockSpec((width, tile), lambda i, _: (0, i)),
                whole(gain.shape),
                whole(shift.shape),
            ],
            out_specs=[pl.BlockSpec((1, tile), lambda i, _: (0, i)), whole((2, width))] + in_hbm(4),
            scratch_shapes=[pltpu.VMEM((2, width), jnp.float32)]
            + stage_shapes(size, own, wide // CHUNK),
        ),
        out_shape=[
            jax.ShapeDtypeStruct((1, wide), jnp.float32),
            jax.ShapeDtypeStruct((2, width), jnp.float32),
        ]
        + split_shapes(size, own),
        compiler_params=pltpu.CompilerParams(vmem_limit_bytes=52 * 2**20),
        cost_estimate=cost(2 * count * width * wide, 2 * count * wide),
        name="qkv_weight_grad",
    )(me, normed, grad, weight, gain, shift)


def token_grad_kernel(
    part, split, flag_ref, grad_ref, hidden_ref, middle_ref, source_ref, weight_ref, gain_ref, *refs
):
    if part == 0:
        out_ref, shared_ref, target, sem = refs
    else:
        before_ref, other_ref, out_ref, target, sem = refs
    frames = source_ref.shape[0] // 2
    is_video = flag_ref[0] == 0
    origin = part * split
    step = pl.program_id(0)
    if part == 1:

        @pl.when(step == 0)
        def _():
            target[0 : before_ref.shape[0], :] = before_ref[...]

    back = product_nt(grad_ref[...], weight_ref[...])
    unit, spread = norm_parts(hidden_ref[...].astype(jnp.float32))
    grads = norm_back(unit, spread, gain_ref[...], back) + middle_ref[...].astype(jnp.float32)
    per_step = grads.shape[0] // FRAME
    for frame in range(per_step):
        rows = grads[frame * FRAME : (frame + 1) * FRAME]
        index = part * frames + step * per_step + frame
        place = lax.broadcasted_iota(jnp.int32, (8, rows.shape[1]), 0)
        extra = jnp.where(is_video & (place == 0), source_ref[pl.ds(index, 1), :], 0.0)
        rows = jnp.concatenate([rows[:8] + extra, rows[8:]], axis=0)
        store_rows(target, frame_start(is_video, index) - origin, rows)

    @pl.when(step == pl.num_programs(0) - 1)
    def _():
        count = split if part == 0 else out_ref.shape[0] - split
        copy = pltpu.make_async_copy(
            target.at[pl.ds(0, count)], out_ref.at[pl.ds(origin, count)], sem
        )
        copy.start()
        if part == 0:
            shared_ref[...] = target[split : split + shared_ref.shape[0], :]
        copy.wait()


def token_grad(part, flag, grad, hidden, grad_middle, grad_source, weight, gain, before=None, frames=2):
    count, width = hidden.shape
    rows = frames * FRAME
    tokens = (count // FRAME * TPF, width)
    steps = count // rows // 2
    split = grad_source.shape[0] // 2 * TPF // 16 * 16
    shared = (-(-(grad_source.shape[0] // 2 * FRAME - split) // 16) * 16, width)
    more = () if part == 0 else before

    def by_rows(columns):
        return pl.BlockSpec((rows, columns), lambda i, _: (i + part * steps, 0))

    out_shape = [jax.ShapeDtypeStruct(tokens, jnp.float32)]
    out_specs = in_hbm(1)
    if part == 0:
        out_shape.append(jax.ShapeDtypeStruct(shared, jnp.float32))
        out_specs = out_specs + [whole(shared)]
    results = pl.pallas_call(
        functools.partial(token_grad_kernel, part, split),
        grid_spec=pltpu.PrefetchScalarGridSpec(
            num_scalar_prefetch=1,
            grid=(steps,),
            in_specs=[
                by_rows(grad.shape[1]),
                by_rows(width),
                by_rows(width),
                whole(grad_source.shape),
                whole(weight.shape),
                whole(gain.shape),
            ]
            + ([whole(shared)] + in_hbm(1) if part == 1 else []),
            out_specs=out_specs,
            scratch_shapes=[
                pltpu.VMEM((count // 2 + FRAME, width), jnp.float32),
                pltpu.SemaphoreType.DMA(()),
            ],
        ),
        out_shape=out_shape,
        input_output_aliases={8: 0} if part == 1 else {},
        compiler_params=pltpu.CompilerParams(vmem_limit_bytes=52 * 2**20),
        cost_estimate=cost(count * width * 3 * width, 2 * count * width),
        name="token_grad",
    )(flag, grad, hidden, grad_middle, grad_source, weight, gain, *more)
    return (results[1], results[0]) if part == 0 else results[0]


def message_kernel(flag_ref, token_ref, ids_row, ids_column, in_source, in_bias, gain, shift, qkv_source, out_source, message_ref, packed_ref, start_ref, projected_ref, tokens, in_weight, qkv_weight, out_weight, sems):
    frames, width = message_ref.shape

    @pl.when(flag_ref[0] == 0)
    def _():
        rows = [frame * TPF // 16 * 16 for frame in range(frames)]
        loads = [
            pltpu.make_async_copy(token_ref.at[pl.ds(row, 16)], tokens.at[frame], sems.at[3])
            for frame, row in enumerate(rows)
        ]
        weights = ((in_source, in_weight), (qkv_source, qkv_weight), (out_source, out_weight))
        copies = [
            pltpu.make_async_copy(origin, place, sems.at[index])
            for index, (origin, place) in enumerate(weights)
        ]
        for copy in loads + copies:
            copy.start()
        for copy in loads:
            copy.wait()
        copies[0].wait()
        parts = []
        for frame in range(frames):
            row = frame * TPF
            base = row // 16 * 16
            tile = tokens[frame].astype(jnp.float32)
            parts.append(tile[row - base : row - base + 1])
        source = jnp.concatenate(parts, axis=0).astype(jnp.bfloat16)
        start = product(source, in_weight[...]) + in_bias[...]
        unit, _ = norm_parts(start)
        normed = (unit * gain[...] + shift[...]).astype(jnp.bfloat16)
        copies[1].wait()
        projected = product(normed, qkv_weight[...]).astype(jnp.bfloat16)
        mixed = side_attend(
            projected[:, :width],
            projected[:, width : 2 * width],
            projected[:, 2 * width :],
            ids_column[...] == ids_row[...],
        )
        copies[2].wait()
        message = start + product(mixed, out_weight[...])
        message_ref[...] = message
        start_ref[...] = start
        projected_ref[...] = projected
        packed_ref[...] = jnp.concatenate([message.astype(jnp.bfloat16), source, mixed], axis=1)

    @pl.when(flag_ref[0] != 0)
    def _():
        message_ref[...] = jnp.zeros(message_ref.shape, message_ref.dtype)
        packed_ref[...] = jnp.zeros(packed_ref.shape, packed_ref.dtype)
        start_ref[...] = jnp.zeros(start_ref.shape, start_ref.dtype)
        projected_ref[...] = jnp.zeros(projected_ref.shape, projected_ref.dtype)


def call_once(kernel, name, flops, scalars, operands, shapes):
    return pl.pallas_call(
        kernel,
        in_specs=[pl.BlockSpec(memory_space=pltpu.SMEM) for _ in scalars] + in_vmem(len(operands)),
        out_specs=in_vmem(len(shapes)),
        out_shape=[jax.ShapeDtypeStruct(shape, dtype) for shape, dtype in shapes],
        compiler_params=pltpu.CompilerParams(vmem_limit_bytes=VMEM_BYTES),
        cost_estimate=cost(flops, sum(value.size * 2 for value in operands)),
        name=name,
    )(*scalars, *operands)


def make_message(flag, tokens, frame_ids, side_params):
    frames = frame_ids.shape[0]
    width = tokens.shape[1]
    shapes = [
        ((frames, width), jnp.float32),
        ((frames, 3 * width), jnp.bfloat16),
        ((frames, width), jnp.float32),
        ((frames, 3 * width), jnp.bfloat16),
    ]
    operands = (tokens, frame_ids[None, :], frame_ids[:, None]) + side_params
    held = (side_params[0], side_params[4], side_params[5])
    return pl.pallas_call(
        message_kernel,
        in_specs=[pl.BlockSpec(memory_space=pltpu.SMEM)]
        + [in_hbm(1)[0] if max(value.shape) > 700 and value.shape[0] > 1 else in_vmem(1)[0] for value in operands],
        out_specs=in_vmem(len(shapes)),
        out_shape=[jax.ShapeDtypeStruct(shape, dtype) for shape, dtype in shapes],
        scratch_shapes=[pltpu.VMEM((frames, 16, width), jnp.bfloat16)]
        + [pltpu.VMEM(value.shape, value.dtype) for value in held]
        + [pltpu.SemaphoreType.DMA((4,))],
        compiler_params=pltpu.CompilerParams(vmem_limit_bytes=VMEM_BYTES),
        cost_estimate=cost(1e10, 10**7),
        name="message",
    )(flag, *operands)


def prompt_kernel(
    flag_ref,
    me_ref,
    block_source,
    cotangent_source,
    context_ref,
    ends_column,
    caption_ids,
    frame_ids,
    in_source,
    in_bias,
    gain,
    shift,
    qkv_source,
    out_source,
    out_target,
    grad_out_target,
    vector_ref,
    send_target,
    keep_target,
    padded,
    block_ref,
    cotangent_ref,
    in_weight,
    qkv_weight,
    out_weight,
    out_ref,
    grad_out_ref,
    send_ref,
    keep_ref,
    sems,
):
    count, width = block_ref.shape
    frames = count // TPF
    is_video = flag_ref[0] == 0
    pairs = (
        (cotangent_source, cotangent_ref),
        (block_source, block_ref),
        (in_source, in_weight),
        (qkv_source, qkv_weight),
        (out_source, out_weight),
        (out_ref, out_target),
        (grad_out_ref, grad_out_target),
        (send_ref, send_target),
        (keep_ref, keep_target),
    )
    copies = [
        pltpu.make_async_copy(origin, place, sems.at[index])
        for index, (origin, place) in enumerate(pairs)
    ]
    copies[0].start()

    @pl.when(is_video)
    def _():
        copies[1].start()
        direct = pltpu.make_async_copy(block_ref, out_target, sems.at[5])
        copies[0].wait()
        padded[0:count, :] = cotangent_ref[...]
        padded[count:, :] = jnp.zeros((padded.shape[0] - count, width), padded.dtype)
        for frame in range(frames):
            rows = load_rows(padded, frame * TPF)
            rows = frame_tail(rows, True, 0.0)
            grad_out_ref[frame * FRAME : (frame + 1) * FRAME, :] = rows.astype(jnp.bfloat16)
        copies[6].start()
        copies[1].wait()
        direct.start()
        vector_ref[...] = jnp.zeros(vector_ref.shape, vector_ref.dtype)
        direct.wait()
        copies[6].wait()

    @pl.when(jnp.logical_not(is_video))
    def _():
        for copy in copies[1:5]:
            copy.start()
        copies[0].wait()
        copies[1].wait()
        captions = ends_column.shape[0]
        place = lax.broadcasted_iota(jnp.int32, (captions, count), 1)
        chosen = (place == ends_column[...]).astype(jnp.bfloat16)
        source = product(chosen, block_ref[...]).astype(jnp.bfloat16)
        grad_ends = product(chosen, cotangent_ref[...])
        copies[2].wait()
        start = product(source, in_weight[...]) + in_bias[...]
        unit, spread = norm_parts(start)
        normed = (unit * gain[...] + shift[...]).astype(jnp.bfloat16)
        copies[3].wait()
        query = product(normed, qkv_weight[:, :width]).astype(jnp.bfloat16)
        context = context_ref[:, :width]
        pair = product(context, qkv_weight[:, width:]).astype(jnp.bfloat16)
        key, value = pair[:, :width], pair[:, width:]
        allowed = caption_ids[...] == frame_ids[...]
        mixed = side_attend(query, key, value, allowed)
        copies[4].wait()
        prompt = start + product(mixed, out_weight[...])
        high = prompt.astype(jnp.bfloat16)
        lower = (prompt - high.astype(jnp.float32)).astype(jnp.bfloat16)
        added = product_tn(chosen, jnp.concatenate([high, lower], axis=1))
        added = added[:, :width] + added[:, width:]
        out_ref[...] = (block_ref[...].astype(jnp.float32) + added).astype(jnp.bfloat16)
        copies[5].start()
        grad_round = grad_ends.astype(jnp.bfloat16)
        grad_mixed = product_nt(grad_round, out_weight[...]).astype(jnp.bfloat16)
        grad_query, grad_key, grad_value = side_attend_back(query, key, value, allowed, grad_mixed)
        grad_query = grad_query.astype(jnp.bfloat16)
        mine = (me_ref[0] >> 1) & 1

        def put(block, row, values):
            place = ((block >> 2) << 1) | (block & 1)
            values = values.astype(jnp.bfloat16)

            @pl.when(((block >> 1) & 1) != mine)
            def _():
                send_ref[place, row : row + values.shape[0], :] = values

            @pl.when(((block >> 1) & 1) == mine)
            def _():
                keep_ref[place, row : row + values.shape[0], :] = values

        blocks = 2 * send_ref.shape[0]
        own = context_ref.shape[0] // blocks
        chunks = width // CHUNK
        grad_pair = jnp.concatenate([grad_key, grad_value], axis=1)
        devices = gathered_offsets(blocks)
        for block in range(blocks):
            part = grad_pair[block * own : (block + 1) * own]
            parts = [part[:, chunk * CHUNK : (chunk + 1) * CHUNK] for chunk in range(2 * chunks)]
            put(devices[block] ^ me_ref[0], send_ref.shape[1] - 2 * chunks * own, jnp.concatenate(parts, axis=0))
        grad_normed = product_nt(grad_query, qkv_weight[:, :width])
        grad_start = norm_back(unit, spread, gain[...], grad_normed) + grad_round.astype(jnp.float32)
        grad_start = grad_start.astype(jnp.bfloat16)
        vector_ref[...] = jnp.concatenate(
            [
                column_sum(grad_start.astype(jnp.float32)),
                column_sum(grad_normed * unit),
                column_sum(grad_normed),
            ],
            axis=0,
        )
        grad_source = product_nt(grad_start, in_weight[...])
        added = product_tn(chosen, grad_source.astype(jnp.bfloat16))
        grad_out_ref[0:count, :] = (cotangent_ref[...].astype(jnp.float32) + added).astype(jnp.bfloat16)
        grad_out_ref[count:, :] = jnp.zeros((frames * FRAME - count, width), jnp.bfloat16)
        copies[6].start()
        rows = width // blocks
        for third, (left, right) in enumerate(
            ((source, grad_start), (normed, grad_query), (mixed, grad_round))
        ):
            part = product_tn(left, right).astype(jnp.bfloat16)
            for chunk in range(chunks):
                row = (third * chunks + chunk) * padded_rows(rows)
                columns = slice(chunk * CHUNK, (chunk + 1) * CHUNK)
                for block in range(blocks):
                    put(block, row, part[block * rows : (block + 1) * rows, columns])
        for copy in copies[7:]:
            copy.start()
        for copy in copies[5:]:
            copy.wait()


def make_prompt(flag, me, size, block, cotangent, context, ends, caption_ids, frame_ids, side_params):
    count, width = block.shape
    padded = count // TPF * FRAME
    chunks = width // CHUNK
    rows = 3 * chunks * padded_rows(width // size) + 2 * chunks * (context.shape[0] // size)
    split = (size // 2, rows, CHUNK)
    shapes = [
        ((count, width), jnp.bfloat16),
        ((padded, width), jnp.bfloat16),
        ((3, width), jnp.float32),
        (split, jnp.bfloat16),
        (split, jnp.bfloat16),
    ]
    spare = -ends.shape[0] % 16
    ends = jnp.pad(ends, (0, spare), constant_values=-1)[:, None]
    caption_ids = jnp.pad(caption_ids, (0, spare), constant_values=-1)[:, None]
    operands = (block, cotangent, context, ends, caption_ids, frame_ids[None, :]) + side_params
    weights = [place for place, value in enumerate(operands) if place > 5 and value.shape[0] > 1]
    held = [operands[place] for place in [0, 1] + weights]
    placed = [
        (in_hbm if place in [0, 1] + weights else in_vmem)(1)[0] for place in range(len(operands))
    ]
    outs = [in_vmem(1)[0] if place == 2 else in_hbm(1)[0] for place in range(len(shapes))]
    return pl.pallas_call(
        prompt_kernel,
        in_specs=[pl.BlockSpec(memory_space=pltpu.SMEM)] * 2 + placed,
        out_specs=outs,
        out_shape=[jax.ShapeDtypeStruct(shape, dtype) for shape, dtype in shapes],
        scratch_shapes=[pltpu.VMEM((padded + 32, width), jnp.bfloat16)]
        + [pltpu.VMEM(value.shape, value.dtype) for value in held]
        + [pltpu.VMEM(*shapes[place]) for place in (0, 1, 3, 4)]
        + [pltpu.SemaphoreType.DMA((9,))],
        compiler_params=pltpu.CompilerParams(vmem_limit_bytes=VMEM_BYTES),
        cost_estimate=cost(1e10, 2 * count * width * 8),
        name="prompt",
    )(flag, me, *operands)


def message_back_kernel(frames, flag_ref, *refs):
    grads, middles, rest = refs[:frames], refs[frames : 2 * frames], refs[2 * frames :]
    (
        message_ref,
        received_ref,
        start_ref,
        projected_ref,
        ids_row,
        ids_column,
        main_source,
        main_gain,
        in_source,
        gain,
        qkv_source,
        out_source,
        pair_ref,
        source_ref,
        line_ref,
        main_weight,
        in_weight,
        qkv_weight,
        out_weight,
        sems,
    ) = rest
    width = message_ref.shape[1]

    @pl.when(flag_ref[0] == 0)
    def _():
        pairs = (
            (main_source, main_weight),
            (out_source, out_weight),
            (qkv_source, qkv_weight),
            (in_source, in_weight),
        )
        loads = [
            pltpu.make_async_copy(origin, place, sems.at[index])
            for index, (origin, place) in enumerate(pairs)
        ]
        for load in loads:
            load.start()
        row = TPF % 16
        grad = jnp.concatenate(
            [one[...].astype(jnp.float32)[row : row + 1] for one in grads], axis=0
        ).astype(jnp.bfloat16)
        middle = jnp.concatenate(
            [one[...].astype(jnp.float32)[row : row + 1] for one in middles], axis=0
        )
        loads[0].wait()
        unit, spread = norm_parts(message_ref[...])
        back = norm_back(unit, spread, main_gain[...], product_nt(grad, main_weight[...]))
        grad_round = (back + middle + received_ref[...]).astype(jnp.bfloat16)
        loads[1].wait()
        grad_mixed = product_nt(grad_round, out_weight[...]).astype(jnp.bfloat16)
        projected = projected_ref[...]
        grad_parts = side_attend_back(
            projected[:, :width],
            projected[:, width : 2 * width],
            projected[:, 2 * width :],
            ids_column[...] == ids_row[...],
            grad_mixed,
        )
        grad_projected = jnp.concatenate(grad_parts, axis=1).astype(jnp.bfloat16)
        unit, spread = norm_parts(start_ref[...])
        loads[2].wait()
        grad_normed = product_nt(grad_projected, qkv_weight[...])
        grad_start = norm_back(unit, spread, gain[...], grad_normed) + grad_round.astype(jnp.float32)
        grad_start = grad_start.astype(jnp.bfloat16)
        loads[3].wait()
        source_ref[...] = product_nt(grad_start, in_weight[...])
        line_ref[...] = jnp.concatenate([grad_start, grad_projected, grad_round], axis=1)

    @pl.when(flag_ref[0] != 0)
    def _():
        source_ref[...] = jnp.zeros(source_ref.shape, source_ref.dtype)
        line_ref[:, : 2 * width] = pair_ref[...]
        line_ref[:, 2 * width :] = jnp.zeros((line_ref.shape[0], 3 * width), line_ref.dtype)


def message_back(flag, grad_projected, grad_middle, operands):
    width = grad_middle.shape[1]
    frames = grad_middle.shape[0] // FRAME
    shapes = [
        jax.ShapeDtypeStruct((frames, width), jnp.float32),
        jax.ShapeDtypeStruct((frames, 5 * width), jnp.bfloat16),
    ]

    def last_rows(columns):
        return [
            pl.BlockSpec(
                (16, columns),
                functools.partial(lambda place, *_: (place, 0), (frame * FRAME + TPF) // 16),
                pipeline_mode=pl.Buffered(buffer_count=1),
            )
            for frame in range(frames)
        ]

    return pl.pallas_call(
        functools.partial(message_back_kernel, frames),
        grid_spec=pltpu.PrefetchScalarGridSpec(
            num_scalar_prefetch=1,
            grid=(1,),
            in_specs=last_rows(3 * width)
            + last_rows(width)
            + [in_hbm(1)[0] if value.shape[0] == width else whole(value.shape) for value in operands],
            out_specs=[whole(shape.shape) for shape in shapes],
            scratch_shapes=[
                pltpu.VMEM(value.shape, value.dtype) for value in operands if value.shape[0] == width
            ]
            + [pltpu.SemaphoreType.DMA((4,))],
        ),
        out_shape=shapes,
        compiler_params=pltpu.CompilerParams(vmem_limit_bytes=52 * 2**20),
        cost_estimate=cost(1e10, 10**7),
        name="message_back",
    )(flag, *([grad_projected] * frames), *([grad_middle] * frames), *operands)


def pair_kernel(flag_ref, side_ref, source_ref, pair_ref, context_ref, weight, sem):
    rows, width = context_ref.shape
    chunks = pair_ref.shape[1] // CHUNK
    first = side_ref.shape[0] - chunks * rows
    load = pltpu.make_async_copy(source_ref, weight, sem)

    @pl.when(flag_ref[0] != 0)
    def _():
        load.start()
        parts = [side_ref[first + rows * chunk : first + rows * (chunk + 1), :] for chunk in range(chunks)]
        pair = jnp.concatenate(parts, axis=1).astype(jnp.bfloat16)
        pair_ref[...] = pair
        load.wait()
        context_ref[...] = product_nt(pair, weight[:, width:])

    @pl.when(flag_ref[0] == 0)
    def _():
        pair_ref[...] = jnp.zeros(pair_ref.shape, pair_ref.dtype)
        context_ref[...] = jnp.zeros(context_ref.shape, context_ref.dtype)


def pair_grad(flag, side, weight, frames):
    width = weight.shape[0]
    return pl.pallas_call(
        pair_kernel,
        in_specs=[pl.BlockSpec(memory_space=pltpu.SMEM)] + in_vmem(1) + in_hbm(1),
        out_specs=in_vmem(2),
        out_shape=[
            jax.ShapeDtypeStruct((frames, 2 * width), jnp.bfloat16),
            jax.ShapeDtypeStruct((frames, width), jnp.float32),
        ],
        scratch_shapes=[pltpu.VMEM(weight.shape, weight.dtype), pltpu.SemaphoreType.DMA(())],
        compiler_params=pltpu.CompilerParams(vmem_limit_bytes=52 * 2**20),
        cost_estimate=cost(1e9, 10**7),
        name="pair_grad",
    )(flag, side, weight)


def pack_kernel(*refs):
    start = 0
    for one in refs[:-1]:
        for row in range(one.shape[0]):
            refs[-1][:, start : start + one.shape[1]] = one[row : row + 1, :]
            start += one.shape[1]


def pack_vectors(vectors):
    shapes = [((1, sum(one.size for one in vectors)), jnp.float32)]
    return call_once(pack_kernel, "pack_vectors", 1e6, (), vectors, shapes)[0]


def side_weight_kernel(
    flag_ref,
    me_ref,
    packed_ref,
    line_ref,
    side_ref,
    weight_ref,
    gain_ref,
    shift_ref,
    in_source,
    in_bias,
    in_ref,
    qkv_ref,
    out_ref,
    vector_ref,
    in_weight,
    sem,
):
    own, width = in_ref.shape
    load = pltpu.make_async_copy(in_source, in_weight, sem)

    def own_columns(place):
        return cut_columns(packed_ref[:, place * width : (place + 1) * width].astype(jnp.float32))

    def cut_columns(part):
        return pltpu.roll(part, (width - me_ref[0] * own) % width, axis=1)[:, :own].astype(jnp.bfloat16)

    @pl.when(flag_ref[0] == 0)
    def _():
        load.start()
        in_ref[...] = product_tn(own_columns(0), line_ref[:, :width])
        out_ref[...] = product_tn(own_columns(1), line_ref[:, 4 * width :])
        lines = line_ref[...].astype(jnp.float32)
        grad_normed = product_nt(line_ref[:, width : 4 * width], weight_ref[...])
        load.wait()
        start = product(packed_ref[:, :width], in_weight[...]) + in_bias[...]
        unit, _ = norm_parts(start)
        normed = (unit * gain_ref[...] + shift_ref[...]).astype(jnp.bfloat16)
        normed = cut_columns(normed.astype(jnp.float32))
        qkv_ref[...] = product_tn(normed, line_ref[:, width : 4 * width])
        vector_ref[0:1, :] = column_sum(lines[:, :width])
        vector_ref[1:2, :] = column_sum(grad_normed * unit)
        vector_ref[2:3, :] = column_sum(grad_normed)

    @pl.when(flag_ref[0] != 0)
    def _():
        chunks = width // CHUNK
        spaced = padded_rows(own)

        def matrix(third):
            rows = [(third * chunks + chunk) * spaced for chunk in range(chunks)]
            return jnp.concatenate([side_ref[row : row + own, :] for row in rows], axis=1)

        in_ref[...] = matrix(0)
        qkv_ref[:, :width] = matrix(1)
        qkv_ref[:, width:] = product_tn(own_columns(0), line_ref[:, : 2 * width])
        out_ref[...] = matrix(2)
        vector_ref[...] = jnp.zeros(vector_ref.shape, vector_ref.dtype)


def side_weight_grads(flag, me, size, packed, lines, side, weight, gain, shift, in_weight, in_bias):
    width = in_weight.shape[0]
    own = width // size
    shapes = [
        ((own, width), jnp.float32),
        ((own, 3 * width), jnp.float32),
        ((own, width), jnp.float32),
        ((3, width), jnp.float32),
    ]
    operands = (packed, lines, side, weight, gain, shift, in_weight, in_bias)
    return pl.pallas_call(
        side_weight_kernel,
        in_specs=[pl.BlockSpec(memory_space=pltpu.SMEM)] * 2 + in_vmem(6) + in_hbm(1) + in_vmem(1),
        out_specs=in_vmem(len(shapes)),
        out_shape=[jax.ShapeDtypeStruct(shape, dtype) for shape, dtype in shapes],
        scratch_shapes=[pltpu.VMEM(in_weight.shape, in_weight.dtype), pltpu.SemaphoreType.DMA(())],
        compiler_params=pltpu.CompilerParams(vmem_limit_bytes=VMEM_BYTES),
        cost_estimate=cost(1e9, 10**7),
        name="side_weight_grads",
    )(flag, me, *operands)


def vector_kernel(size, widths, flag_ref, me_ref, line_ref, side_ref, *out_refs):
    start = 0
    third = out_refs[0].shape[1] * size
    for place, (width, out_ref) in enumerate(zip(widths, out_refs)):
        total = line_ref[:, start : start + width]
        start += width
        if place == 2:
            total = jnp.concatenate([total[:, :third], total[:, 2 * third :]], axis=1)
            width = 2 * third
        own = width // size
        side = place - (len(widths) - 3)
        if side >= 0:
            total = jnp.where(flag_ref[0] == 0, side_ref[side : side + 1, :], total)
        total = jnp.broadcast_to(total, (8, width))
        out_ref[...] = pltpu.roll(total, (width - me_ref[0] * own) % width, axis=1)[0:1, :own]


def own_vectors(flag, me, size, line, side, widths):
    shapes = [((1, width // size), jnp.float32) for width in widths]
    shapes[2] = ((1, 2 * widths[0] // size), jnp.float32)
    kernel = functools.partial(vector_kernel, size, tuple(widths))
    return call_once(kernel, "own_vectors", 1e6, (flag, me), (line, side), shapes)


def pair_list(size, distance):
    return [(place, place ^ distance) for place in range(size)]


def group_pairs(size, distance, group):
    return [(group * size + place, group * size + (place ^ distance)) for place in range(size)]


def bit_count(size):
    return size.bit_length() - 1


def gather_order(size):
    return list(range(bit_count(size)))[::-1]


def gathered_offsets(size):
    return [
        sum((((place >> step) & 1) << bit for step, bit in enumerate(gather_order(size))))
        for place in range(size)
    ]


def gathered_devices(me, size):
    return me ^ jnp.array(gathered_offsets(size), jnp.int32)


def double_gather(values, size, send):
    for bit in gather_order(size):
        values = jnp.concatenate([values, send(values, 1 << bit)], axis=0)
    return values


class Sum:
    def __init__(self, size, send, parts, layout, fan=False):
        self.send, self.layout, self.fan = send, layout, fan
        self.bits = list(range(2, bit_count(size)))
        self.orders = [[0, 1], [1, 0]]
        self.keeps, self.arrived = [], []
        for side in range(2):
            self.launch(parts[2 * side], parts[2 * side + 1], self.orders[side].pop(0))

    def launch(self, sent, kept, bit):
        self.keeps.append(kept)
        self.arrived.append(self.send(sent, 1 << bit))

    def values(self):
        return [value for pair in zip(self.keeps, self.arrived) for value in pair]

    def items(self):
        if self.orders[0]:
            values = self.values()
            return [("split", values[2 * side : 2 * side + 2], self.orders[side][0]) for side in range(2)]
        if self.bits:
            kind = "fan" if self.fan and len(self.bits) == 2 else "split"
            return [(kind, self.values(), self.bits[0])]
        return [("end", self.keeps + self.arrived, self.layout)]

    def take(self, results):
        fan = self.fan and len(self.bits) == 2 and not self.orders[0]
        self.keeps, self.arrived = [], []
        if self.orders[0]:
            for side in range(2):
                self.launch(results.pop(0), results.pop(0), self.orders[side].pop(0))
        elif fan:
            self.keeps = [results.pop(0)]
            first = self.bits[0]
            self.arrived = [self.send(results.pop(0), offset << first) for offset in (1, 2, 3)]
            self.bits = []
        elif self.bits:
            self.launch(results.pop(0), results.pop(0), self.bits.pop(0))
        else:
            self.result = [results.pop(0) for _ in self.layout]


class PlainSum:
    def __init__(self, size, send, send_small, sent, kept):
        self.send, self.send_small, self.kept = send, send_small, kept
        self.bits = [bit for bit in range(bit_count(size)) if bit != 1]
        self.arrived = send(sent, 2)
        self.steps = 1

    def items(self):
        if self.bits:
            return [("split", [self.kept, self.arrived], self.bits[0])]
        return [("raw", [self.kept, self.arrived], None)]

    def take(self, results):
        if self.bits:
            sent, self.kept = results.pop(0), results.pop(0)
            send = self.send if self.steps < 2 else self.send_small
            self.arrived = send(sent, 1 << self.bits.pop(0))
            self.steps += 1
        else:
            self.result = results.pop(0)


class Spread:
    def __init__(self, size, send, values, kind, plane=False):
        self.kind, self.send, self.held = kind, send, values
        self.steps = [[1 << bit] for bit in gather_order(size)]
        if plane:
            self.steps = self.steps[:-2] + [[2, 1, 3]]
        self.launch()

    def launch(self):
        self.arrived = [self.send(self.held, distance) for distance in self.steps.pop(0)]

    def items(self):
        return [(self.kind, [self.held] + self.arrived, None)]

    def take(self, results):
        self.held = results.pop(0)
        if self.steps:
            self.launch()
        else:
            self.result = self.held


def tie(first, second):
    return lax.optimization_barrier((first, second))


def advance(me, streams, after, before=None):
    streams = [one for one in streams if not hasattr(one, "result")]
    if not streams:
        return (after, before)
    items = [one.items() for one in streams]
    flat = [item for one in items for item in one]
    operands, after = tie([item[1] for item in flat], after)
    results = combine(me, [(item[0], values, item[2]) for item, values in zip(flat, operands)])
    results, before = tie(list(results), before)
    for one in streams:
        one.take(results)
    return (after, before)


def on_device(
    size,
    tokens,
    frame_video,
    caption_video,
    caption_len,
    attn_norm_gain,
    attn_norm_shift,
    qkv_weight,
    query_value_bias,
    proj_weight,
    proj_bias,
    mlp_norm_gain,
    mlp_norm_shift,
    fc_in_weight,
    fc_in_bias,
    fc_out_weight,
    fc_out_bias,
    side_in_weight,
    side_in_bias,
    side_norm_gain,
    side_norm_shift,
    side_qkv_weight,
    side_out_weight,
    cotangent,
):
    main_params = tuple(
        (
            member[0]
            for member in (
                attn_norm_gain,
                attn_norm_shift,
                qkv_weight,
                query_value_bias,
                proj_weight,
                proj_bias,
                mlp_norm_gain,
                mlp_norm_shift,
                fc_in_weight,
                fc_in_bias,
                fc_out_weight,
                fc_out_bias,
            )
        )
    )
    side_params = tuple(
        (
            member[0]
            for member in (
                side_in_weight,
                side_in_bias,
                side_norm_gain,
                side_norm_shift,
                side_qkv_weight,
                side_out_weight,
            )
        )
    )
    token_rows = tokens[0]
    cotangent_rows = cotangent[0]
    row_count, model_width = token_rows.shape
    frame_count = row_count // TPF
    me = lax.axis_index("dp")
    is_video = lax.axis_index("grp") == 0

    def to_text(values):
        return lax.ppermute(values, ("grp", "dp"), [(i, size + i) for i in range(size)])

    def to_video(values):
        return lax.ppermute(values, ("grp", "dp"), [(size + i, i) for i in range(size)])

    def in_all(values, distance):
        return lax.ppermute(values, "dp", pair_list(size, distance))

    def in_video(values, distance):
        return lax.ppermute(values, ("grp", "dp"), group_pairs(size, distance, 0))

    def in_text(values, distance):
        return lax.ppermute(values, ("grp", "dp"), group_pairs(size, distance, 1))

    flag = lax.axis_index("grp").astype(jnp.int32).reshape(1)
    me_one = me.astype(jnp.int32).reshape(1)
    side_rows = tuple((member if member.ndim == 2 else member[None] for member in side_params))
    frame_order = frame_video.reshape(size, frame_count)[gathered_devices(me, size)]
    frame_ids = frame_order[0]
    message, packed, side_start, side_projected = make_message(
        flag, token_rows, frame_ids, side_rows
    )
    arrived = to_text(packed[:, :model_width])
    arrived = jnp.concatenate([arrived, arrived], axis=1)
    packed = jnp.where(is_video, packed[:, model_width:], arrived)
    caption_ends = jnp.cumsum(caption_len[0]) - 1
    places = jnp.arange(frame_count * FRAME, dtype=jnp.int32)
    caption_starts = jnp.concatenate([caption_ends + 1 - caption_len[0], jnp.full((1,), row_count)])
    first = jnp.max(
        jnp.where(places[:, None] >= caption_starts[None, :], caption_starts[None, :], 0), axis=1
    ).astype(jnp.int32)
    bias = main_params[3]
    full_bias = jnp.concatenate(
        [bias[:model_width], jnp.zeros((model_width,), jnp.float32), bias[model_width:]]
    )
    params = tuple(
        (
            member if member.ndim == 2 else member[None]
            for member in main_params[:3] + (full_bias,) + main_params[4:]
        )
    )
    normed, projected, mixed, middle, normed_two, act, slope, hidden, block_rows = forward(
        flag, token_rows, message, first[:, None], params
    )
    packed = double_gather(packed, size, in_all)
    out_rows, grad_out, text_vectors, *parts = make_prompt(
        flag,
        me_one,
        size,
        block_rows,
        cotangent_rows,
        packed,
        caption_ends,
        caption_video,
        frame_order.reshape(-1),
        side_rows,
    )
    own_width = model_width // size
    side_sum = PlainSum(size, in_text, in_all, parts[0], parts[1])
    grad_fc_out_bias, *parts = out_weight_grad(me_one, size, act, grad_out)
    parts, grad_out = tie(parts, grad_out)
    out_sum = Sum(size, in_all, parts, [(fc_out_weight.shape[1] // size, 1)])
    grad_pre, grad_fc_in_bias = pre_grad(grad_out, slope, params[10])
    grad_pre, _ = advance(me_one, [side_sum], grad_pre)
    grad_middle, grad_mixed, middle_vectors = middle_grad(
        grad_pre, grad_out, middle, params[8], params[4], params[6]
    )
    grad_middle, normed_two = advance(
        me_one, [out_sum, side_sum], grad_middle, normed_two
    )
    parts = in_weight_grad(me_one, size, normed_two, grad_pre, mixed, grad_middle)
    chunks = model_width // (2 * CHUNK)
    parts, grad_mixed = tie(parts, grad_mixed)
    in_sum = Sum(size, in_all, parts, [(own_width, 4 * chunks), (own_width, chunks)])
    _, grad_mixed = advance(me_one, [out_sum, side_sum], parts, grad_mixed)
    grad_projected = attend_back(flag, projected, grad_mixed, first.reshape(frame_count, 1, FRAME))
    grad_projected, normed = advance(
        me_one, [out_sum, in_sum, side_sum], grad_projected, normed
    )
    while not hasattr(side_sum, "result"):
        advance(me_one, [side_sum], grad_projected)
    pair_rows, context_grad = pair_grad(flag, side_sum.result, side_rows[4], frame_count)
    received = to_video(context_grad)
    grad_source, grad_lines = message_back(
        flag,
        grad_projected,
        grad_middle,
        (message, received, side_start, side_projected, frame_ids[None, :], frame_ids[:, None])
        + (params[2], params[0], side_rows[0], side_rows[2], side_rows[4], side_rows[5], pair_rows),
    )
    grad_lines, normed = tie(grad_lines, normed)
    all_lines = Spread(size, in_all, grad_lines, "stack", plane=True)
    bias_totals, first_vectors, *parts = qkv_weight_grad(
        me_one, size, normed, grad_projected, params[2], params[0], params[1]
    )
    qkv_sum = Sum(size, in_all, parts, [(own_width, 3 * chunks)], fan=True)
    line = pack_vectors(
        (
            first_vectors,
            bias_totals,
            middle_vectors,
            grad_fc_in_bias,
            grad_fc_out_bias,
            text_vectors,
        )
    )
    widths = [model_width] * 2 + [3 * model_width] + [model_width] * 3
    widths += [grad_fc_in_bias.shape[1]] + [model_width] * 4
    line_sum = Spread(size, in_all, line, "add", plane=True)
    streams = [out_sum, in_sum, all_lines]
    _, grad_source = advance(me_one, streams, bias_totals, grad_source)
    token_operands = (hidden, grad_middle, grad_source, params[2], params[0])
    before = token_grad(0, flag, grad_projected, *token_operands)
    streams = [out_sum, in_sum, qkv_sum, line_sum, all_lines]
    before, _ = advance(me_one, streams, before)
    grad_tokens = token_grad(1, flag, grad_projected, *token_operands, before=before)
    while not all((hasattr(one, "result") for one in streams)):
        grad_tokens, _ = advance(me_one, streams, grad_tokens)
    grad_in_weight, grad_side_qkv, grad_side_out, video_vectors = side_weight_grads(
        flag,
        me_one,
        size,
        packed,
        all_lines.result,
        side_sum.result,
        side_rows[4],
        side_rows[2],
        side_rows[3],
        side_rows[0],
        side_rows[1],
    )
    (
        grad_attn_gain,
        grad_attn_shift,
        grad_qv_bias,
        grad_mlp_gain,
        grad_mlp_shift,
        grad_proj_bias,
        grad_fc_in_bias,
        grad_fc_out_bias,
        grad_in_bias,
        grad_side_gain,
        grad_side_shift,
    ) = own_vectors(flag, me_one, size, line_sum.result, video_vectors, widths)
    summed = (
        grad_attn_gain,
        grad_attn_shift,
        qkv_sum.result[0][None],
        grad_qv_bias,
        in_sum.result[1][None],
        grad_proj_bias,
        grad_mlp_gain,
        grad_mlp_shift,
        in_sum.result[0][None],
        grad_fc_in_bias,
        out_sum.result[0][None],
        grad_fc_out_bias,
        grad_in_weight[None],
        grad_in_bias,
        grad_side_gain,
        grad_side_shift,
        grad_side_qkv[None],
        grad_side_out[None],
    )
    return tuple([out_rows[None], grad_tokens[None]] + list(summed))


def solution(mesh):
    placed = (
        P("grp", "dp", None),
        P(),
        P("dp"),
        P("dp", None),
        P("grp", None),
        P("grp", None),
        P("grp", None, None),
        P("grp", None),
        P("grp", None, None),
        P("grp", None),
        P("grp", None),
        P("grp", None),
        P("grp", None, None),
        P("grp", None),
        P("grp", None, None),
        P("grp", None),
        P("grp", None, None),
        P("grp", None),
        P("grp", None),
        P("grp", None),
        P("grp", None, None),
        P("grp", None, None),
        P("grp", "dp", None),
    )
    return jax.shard_map(
        functools.partial(on_device, mesh.shape["dp"]),
        mesh=mesh,
        in_specs=placed,
        out_specs=(
            P("grp", "dp", None),
            P("grp", "dp", None),
            P("grp", "dp"),
            P("grp", "dp"),
            P("grp", "dp", None),
            P("grp", "dp"),
            P("grp", "dp", None),
            P("grp", "dp"),
            P("grp", "dp"),
            P("grp", "dp"),
            P("grp", "dp", None),
            P("grp", "dp"),
            P("grp", "dp", None),
            P("grp", "dp"),
            P("grp", "dp", None),
            P("grp", "dp"),
            P("grp", "dp"),
            P("grp", "dp"),
            P("grp", "dp", None),
            P("grp", "dp", None),
        ),
        check_vma=False,
    )
```
